32 devices in a mesh: dp: 4 (over y, x), tensor: 8 (over z, core).
Axes of the slice: x: 2, y: 2, z: 4, core: 2. Of those that a mesh axis runs over, the one named last changes fastest.
Arguments:
- inputs: bfloat16 [8192, 2048], P(('dp', 'tensor')), may hold values from -6 to 6
- cotangent: bfloat16 [8192, 2048], P(('dp', 'tensor')), may hold values from -6 to 6
- lengths: int32 [4], P('dp'), may hold values from 1024 to 2048, as said below
- positions: int32 [8192], P('dp'), may hold values from 0 to 4094, as said below
- qkv_master: float32 [3, 2048, 2048], P(None, 'dp', 'tensor'), may hold values from -0.125 to 0.125
- gate_up_master: float32 [2, 2048, 5632], P(None, 'dp', 'tensor'), may hold values from -0.125 to 0.125
- out_master: float32 [2048, 2048], P('tensor', 'dp'), may hold values from -1 to 1
- down_master: float32 [5632, 2048], P('tensor', 'dp'), may hold values from -0.25 to 0.25
- bias_master: float32 [3, 32, 64], P(None, 'tensor', 'dp'), may hold values from -3 to 3
- norm_master: float32 [4, 2048], replicated
- qkv_first: float32 [3, 2048, 2048], P(None, 'dp', 'tensor'), may hold values from -48 to 48
- gate_up_first: float32 [2, 2048, 5632], P(None, 'dp', 'tensor'), may hold values from -64 to 64
- out_first: float32 [2048, 2048], P('tensor', 'dp'), may hold values from -20 to 20
- down_first: float32 [5632, 2048], P('tensor', 'dp'), may hold values from -20 to 20
- bias_first: float32 [3, 32, 64], P(None, 'tensor', 'dp'), may hold values from -96 to 96
- norm_first: float32 [4, 2048], replicated, may hold values from -48 to 48
- qkv_second: float32 [3, 2048, 2048], P(None, 'dp', 'tensor'), may hold values from 131.072 to 2048
- gate_up_second: float32 [2, 2048, 5632], P(None, 'dp', 'tensor'), may hold values from 221.184 to 3686.4
- out_second: float32 [2048, 2048], P('tensor', 'dp'), may hold values from 24.576 to 409.6
- down_second: float32 [5632, 2048], P('tensor', 'dp'), may hold values from 24.576 to 409.6
- bias_second: float32 [3, 32, 64], P(None, 'tensor', 'dp'), may hold values from 491.52 to 8192
- norm_second: float32 [4, 2048], replicated, may hold values from 131.072 to 2048
Outputs:
- block_output: bfloat16 [8192, 2048], P(('dp', 'tensor'))
- input_grad: float32 [8192, 2048], P(('dp', 'tensor'))
- qkv_new: float32 [3, 2048, 2048], P(None, 'dp', 'tensor')
- qkv_first_new: float32 [3, 2048, 2048], P(None, 'dp', 'tensor')
- qkv_second_new: float32 [3, 2048, 2048], P(None, 'dp', 'tensor')
- gate_up_new: float32 [2, 2048, 5632], P(None, 'dp', 'tensor')
- gate_up_first_new: float32 [2, 2048, 5632], P(None, 'dp', 'tensor')
- gate_up_second_new: float32 [2, 2048, 5632], P(None, 'dp', 'tensor')
- out_new: float32 [2048, 2048], P('tensor', 'dp')
- out_first_new: float32 [2048, 2048], P('tensor', 'dp')
- out_second_new: float32 [2048, 2048], P('tensor', 'dp')
- down_new: float32 [5632, 2048], P('tensor', 'dp')
- down_first_new: float32 [5632, 2048], P('tensor', 'dp')
- down_second_new: float32 [5632, 2048], P('tensor', 'dp')
- bias_new: float32 [3, 32, 64], P(None, 'tensor', 'dp')
- bias_first_new: float32 [3, 32, 64], P(None, 'tensor', 'dp')
- bias_second_new: float32 [3, 32, 64], P(None, 'tensor', 'dp')
- norm_new: float32 [4, 2048], replicated
- norm_first_new: float32 [4, 2048], replicated
- norm_second_new: float32 [4, 2048], replicated
The draws below stay inside these ranges and needn't reach their ends.
Inputs may be any that keep to these rules, and one draw needn't show every extreme that they name: `lengths`: each row holds one sequence in its first slots and padding after it; some row has exactly 2048 tokens. `positions`: 0 at the first slot of every row and rising by 1 or 2 from slot to slot within a row; the first row rises by 2 at every slot.
All inputs are finite; a program needn't handle non-finite values.
Results may differ from the reference program's by a relative error of at most 0.012.
Values may be sent and summed in bfloat16 or wider, within the bound.
A program may use at most 256 MiB of HBM per device.

```python
import math
import jax
import jax.numpy as jnp
from jax import lax

D = 2048
HEADS = 32
HEAD_DIM = 64
ROTARY = 16
FF = 5632
ROWS = 1
LROW = 2048
TOKENS = 8192
ALL_ROWS = 4
N_DP = 4


def draw_lengths(key, part):
    spread = jax.random.randint(key, (ALL_ROWS,), 0, 64)
    extra_len = spread * spread * spread * (LROW - LROW // 2) // 250047
    drawn = LROW // 2 + extra_len
    return drawn.at[0].set(LROW).astype(jnp.int32)


def draw_positions(key, part):
    increments = 1 + jax.random.randint(key, (ALL_ROWS, LROW), 0, 2)
    increments = increments.at[0].set(2)
    running = jnp.cumsum(increments, axis=1) - increments[:, :1]
    return running.reshape(ALL_ROWS * LROW).astype(jnp.int32)


def draw_norm_master(key, part):
    gain_key = jax.random.fold_in(key, 11)
    shift_key = jax.random.fold_in(key, 12)
    gains = 1.0 + 0.15 * jax.random.normal(gain_key, (2, D), jnp.float32)
    shifts = 0.3 * jax.random.normal(shift_key, (2, D), jnp.float32)
    return jnp.stack([gains[0], shifts[0], gains[1], shifts[1]]).astype(jnp.float32)


def steps_of(key, dims, split, low, top_value):
    level = 1.0
    for position, blocks in split:
        steps = jax.random.uniform(jax.random.fold_in(jax.random.fold_in(key, 6), position), (blocks,), jnp.float32, low / len(split), top_value / len(split))
        level = level * jnp.repeat(jnp.exp(steps), dims[position] // blocks).reshape((-1,) + (1,) * (len(dims) - 1 - position))
    return level


def gaussian(stream_key, dims, deviation, most, split=(), held_as=jnp.bfloat16):
    values = jax.random.normal(stream_key, dims, jnp.float32) * deviation
    if len(split) > 0:
        values = steps_of(stream_key, dims, split, -0.22, 0.18) * values
    return jnp.clip(values, min=-most, max=most).astype(held_as)


def setup_inputs(seed: int = 0) -> dict:
    key_of = jax.random.split(jax.random.key(seed), 23)
    return {
        "inputs": gaussian(key_of[0], (TOKENS, D), 1.0, 6.0, ((0, 32),)),
        "cotangent": gaussian(key_of[1], (TOKENS, D), 1.0, 6.0, ((0, 32),)),
        "lengths": draw_lengths(jax.random.fold_in(key_of[22], 71), 0),
        "positions": draw_positions(jax.random.fold_in(key_of[22], 71), 0),
        "qkv_master": gaussian(key_of[4], (3, D, HEADS * HEAD_DIM), D ** -0.5, 0.125, ((1, 4), (2, 8)), jnp.float32),
        "gate_up_master": gaussian(key_of[5], (2, D, FF), D ** -0.5, 0.125, ((1, 4), (2, 8)), jnp.float32),
        "out_master": gaussian(key_of[6], (HEADS * HEAD_DIM, D), (HEADS * HEAD_DIM // 64) ** -0.5, 1.0, ((0, 8), (1, 4)), jnp.float32),
        "down_master": gaussian(key_of[7], (FF, D), (FF // 9) ** -0.5, 0.25, ((0, 8), (1, 4)), jnp.float32),
        "bias_master": gaussian(key_of[8], (3, HEADS, HEAD_DIM), 0.5, 3.0, ((1, 8), (2, 4)), jnp.float32),
        "norm_master": draw_norm_master(jax.random.fold_in(key_of[22], 71), 0),
        "qkv_first": gaussian(key_of[10], (3, D, HEADS * HEAD_DIM), (0.09 * TOKENS ** 0.5), 48.0, ((1, 4), (2, 8)), jnp.float32),
        "gate_up_first": gaussian(key_of[11], (2, D, FF), (0.12 * TOKENS ** 0.5), 64.0, ((1, 4), (2, 8)), jnp.float32),
        "out_first": gaussian(key_of[12], (HEADS * HEAD_DIM, D), (0.04 * TOKENS ** 0.5), 20.0, ((0, 8), (1, 4)), jnp.float32),
        "down_first": gaussian(key_of[13], (FF, D), (0.04 * TOKENS ** 0.5), 20.0, ((0, 8), (1, 4)), jnp.float32),
        "bias_first": gaussian(key_of[14], (3, HEADS, HEAD_DIM), (0.17 * TOKENS ** 0.5), 96.0, ((1, 8), (2, 4)), jnp.float32),
        "norm_first": gaussian(key_of[15], (4, D), (0.09 * TOKENS ** 0.5), 48.0, (), jnp.float32),
        "qkv_second": jnp.clip(jnp.exp(math.log(2048.0) - 2.748872 * jax.random.uniform(key_of[16], (3, D, HEADS * HEAD_DIM), jnp.float32) ** steps_of(key_of[16], (3, D, HEADS * HEAD_DIM), ((1, 4), (2, 8)), -0.2, 0.2)), 131.072, 2048.0),
        "gate_up_second": jnp.clip(jnp.exp(math.log(3686.4) - 2.8134107 * jax.random.uniform(key_of[17], (2, D, FF), jnp.float32) ** steps_of(key_of[17], (2, D, FF), ((1, 4), (2, 8)), -0.2, 0.2)), 221.184, 3686.4),
        "out_second": jnp.clip(jnp.exp(math.log(409.6) - 2.8134107 * jax.random.uniform(key_of[18], (HEADS * HEAD_DIM, D), jnp.float32) ** steps_of(key_of[18], (HEADS * HEAD_DIM, D), ((0, 8), (1, 4)), -0.2, 0.2)), 24.576, 409.6),
        "down_second": jnp.clip(jnp.exp(math.log(409.6) - 2.8134107 * jax.random.uniform(key_of[19], (FF, D), jnp.float32) ** steps_of(key_of[19], (FF, D), ((0, 8), (1, 4)), -0.2, 0.2)), 24.576, 409.6),
        "bias_second": jnp.clip(jnp.exp(math.log(8192.0) - 2.8134107 * jax.random.uniform(key_of[20], (3, HEADS, HEAD_DIM), jnp.float32) ** steps_of(key_of[20], (3, HEADS, HEAD_DIM), ((1, 8), (2, 4)), -0.2, 0.2)), 491.52, 8192.0),
        "norm_second": jnp.clip(jnp.exp(jax.random.uniform(key_of[21], (4, D), jnp.float32, math.log(131.072), math.log(2048.0))), 131.072, 2048.0),
    }


@jax.custom_vjp
def low(v):
    return lax.optimization_barrier(v.astype(jnp.bfloat16)).astype(jnp.float32)

@jax.custom_vjp
def low_back(v):
    return v

def low_keep(v):
    return (low(v), None)

def low_pass(kept, grad):
    return (grad,)

def back_keep(v):
    return (v, None)

def back_low(kept, grad):
    return (low(grad),)
low.defvjp(low_keep, low_pass)
low_back.defvjp(back_keep, back_low)
norm_eps = 1e-05
beta_one = 0.9
beta_two = 0.95
adam_eps = 1e-08
adam_steps = 10
decay_rate = 0.1
rope_base = 10000.0
score_scale = 0.125
mask_fill = -1e+30

def product(left_side, right_side):
    return jnp.dot(left_side, right_side, precision=lax.Precision.HIGHEST, preferred_element_type=jnp.float32)

def layer_norm(values, gain_row, shift_row):
    average = lax.optimization_barrier(jnp.mean(values, axis=-1, keepdims=True))
    centred = values - average
    spread = lax.optimization_barrier(jnp.mean(centred * centred, axis=-1, keepdims=True))
    return centred * lax.rsqrt(spread + norm_eps) * gain_row + shift_row

def rotate(values, cosine, sine_part):
    half_rot = ROTARY // 2
    first_half = values[..., :half_rot]
    second_half = values[..., half_rot:ROTARY]
    cosine_wide = cosine[:, None, :]
    sine_wide = sine_part[:, None, :]
    return jnp.concatenate([first_half * cosine_wide - second_half * sine_wide, second_half * cosine_wide + first_half * sine_wide, values[..., ROTARY:]], axis=-1)

def head_attention(head_pack):
    query_rows, key_rows, value_rows, row_size = head_pack
    slots = jnp.arange(LROW)
    allowed = (slots[None, :] <= slots[:, None]) & (slots[None, :] < row_size)
    scores = low_back(product(query_rows, key_rows.T) * score_scale)
    masked = jnp.where(allowed, scores, mask_fill)
    highest = lax.optimization_barrier(jnp.max(masked, axis=1, keepdims=True))
    weights = jnp.exp(masked - highest)
    normalized = weights / lax.optimization_barrier(jnp.sum(weights, axis=1, keepdims=True))
    return low(low_back(product(low(normalized), value_rows)))

def block(inputs, qkv_master, gate_up_master, out_master, down_master, bias_master, norm_master, lengths, positions):
    token_count = inputs.shape[0]
    row_total = token_count // LROW
    width = HEADS * HEAD_DIM
    qkv_copy = low(qkv_master)
    gate_up_copy = low(gate_up_master)
    out_copy = low(out_master)
    down_copy = low(down_master)
    bias_copy = low(bias_master).reshape(3, width)
    normed_one = low(layer_norm(inputs, norm_master[0], norm_master[1]))
    pre_query = low_back(product(normed_one, qkv_copy[0]) + bias_copy[0])
    pre_key = low_back(product(normed_one, qkv_copy[1]) + bias_copy[1])
    pre_value = low_back(product(normed_one, qkv_copy[2]) + bias_copy[2])
    frequency = rope_base ** (-(2.0 * jnp.arange(ROTARY // 2, dtype=jnp.float32)) / ROTARY)
    angles = positions.astype(jnp.float32)[:, None] * frequency[None, :]
    cosine = jnp.cos(angles)
    sine_part = jnp.sin(angles)
    queries = low(rotate(pre_query.reshape(token_count, HEADS, HEAD_DIM), cosine, sine_part))
    keys_rot = low(rotate(pre_key.reshape(token_count, HEADS, HEAD_DIM), cosine, sine_part))
    values_low = low(pre_value).reshape(token_count, HEADS, HEAD_DIM)

    def to_heads(array):
        return array.reshape(row_total, LROW, HEADS, HEAD_DIM).transpose(0, 2, 1, 3).reshape(row_total * HEADS, LROW, HEAD_DIM)
    head_lengths = jnp.repeat(lengths, HEADS)
    attended = lax.map(jax.checkpoint(head_attention), (to_heads(queries), to_heads(keys_rot), to_heads(values_low), head_lengths))
    attended = attended.reshape(row_total, HEADS, LROW, HEAD_DIM).transpose(0, 2, 1, 3).reshape(token_count, width)
    middle = inputs + low_back(product(attended, out_copy))
    normed_two = low(layer_norm(middle, norm_master[2], norm_master[3]))
    gate = low_back(product(normed_two, gate_up_copy[0]))
    up_part = low_back(product(normed_two, gate_up_copy[1]))
    hidden = low(jax.nn.silu(gate) * up_part)
    return middle + low_back(product(hidden, down_copy))

def adamw(weight_old, first_old, second_old, gradient, step_rate, decay_part):
    first_new = beta_one * first_old + (1.0 - beta_one) * gradient
    second_new = beta_two * second_old + (1.0 - beta_two) * gradient * gradient
    correct_one = 1.0 - beta_one ** adam_steps
    correct_two = 1.0 - beta_two ** adam_steps
    update = first_new / correct_one / (jnp.sqrt(second_new / correct_two) + adam_eps)
    return (weight_old - step_rate * (update + decay_part * weight_old), first_new, second_new)

def reference(inputs, cotangent, lengths, positions, qkv_master, gate_up_master, out_master, down_master, bias_master, norm_master, qkv_first, gate_up_first, out_first, down_first, bias_first, norm_first, qkv_second, gate_up_second, out_second, down_second, bias_second, norm_second):
    group_tokens = ROWS * LROW
    token_index = jnp.arange(TOKENS)
    slots = token_index % LROW
    row_index = token_index // LROW
    valid = (slots < lengths[row_index]).astype(jnp.float32)
    weighting = cotangent.astype(jnp.float32) * valid[:, None]
    params = (qkv_master, gate_up_master, out_master, down_master, bias_master, norm_master)

    def group_step(carry, group_pack):
        group_inputs, group_weighting, group_lengths, group_positions = group_pack

        def apply_block(values, qkv_w, gate_up_w, out_w, down_w, bias_w, norm_w):
            return block(values, qkv_w, gate_up_w, out_w, down_w, bias_w, norm_w, group_lengths, group_positions)
        result, pullback = jax.vjp(apply_block, group_inputs, qkv_master, gate_up_master, out_master, down_master, bias_master, norm_master)
        gradients = pullback(group_weighting)
        summed = jax.tree.map(jnp.add, carry, tuple(gradients[1:]))
        return (summed, (result.astype(jnp.bfloat16), gradients[0]))
    start_carry = tuple((jnp.zeros_like(item) for item in params))
    totals, outputs = lax.scan(group_step, start_carry, (inputs.astype(jnp.float32).reshape(N_DP, group_tokens, D), weighting.reshape(N_DP, group_tokens, D), lengths.reshape(N_DP, ROWS), positions.reshape(N_DP, group_tokens)))
    block_output = outputs[0].reshape(TOKENS, D)
    input_grad = outputs[1].reshape(TOKENS, D)
    qkv_new = adamw(qkv_master, qkv_first, qkv_second, totals[0], 2.0 / math.sqrt(D), decay_rate)
    gate_up_new = adamw(gate_up_master, gate_up_first, gate_up_second, totals[1], 2.0 / math.sqrt(D), decay_rate)
    out_new = adamw(out_master, out_first, out_second, totals[2], 16.0 / math.sqrt(HEADS * HEAD_DIM), decay_rate)
    down_new = adamw(down_master, down_first, down_second, totals[3], 6.0 / math.sqrt(FF), decay_rate)
    bias_new = adamw(bias_master, bias_first, bias_second, totals[4], 1.5, 0.0)
    norm_new = adamw(norm_master, norm_first, norm_second, totals[5], 0.7, 0.0)
    return (block_output, input_grad, qkv_new[0], qkv_new[1], qkv_new[2], gate_up_new[0], gate_up_new[1], gate_up_new[2], out_new[0], out_new[1], out_new[2], down_new[0], down_new[1], down_new[2], bias_new[0], bias_new[1], bias_new[2], norm_new[0], norm_new[1], norm_new[2])
```

```python
import functools
import math

import jax
import jax.numpy as jnp
from jax import lax
from jax.experimental import pallas as pl
from jax.experimental.pallas import tpu as pltpu
from jax.sharding import PartitionSpec as P

D = 2048
HEADS = 32
HEAD_DIM = 64
ROTARY = 16
FF = 5632


norm_eps = 1e-05
beta_one = 0.9
beta_two = 0.95
adam_eps = 1e-08
adam_steps = 10
decay_rate = 0.1
rope_base = 10000.0
score_scale = 0.125
mask_fill = -1e30
log2_e = math.log2(math.e)
LANES = 128
VMEM_LIMIT = 58 * 1024 * 1024


def norm_forward(values, gain_row, shift_row):
    average = jnp.mean(values, axis=-1, keepdims=True)
    centred = values - average
    spread = jnp.mean(centred * centred, axis=-1, keepdims=True)
    return centred * lax.rsqrt(spread + norm_eps) * gain_row + shift_row


def norm_backward(values, gain_row, grad_rows):
    average = jnp.mean(values, axis=-1, keepdims=True)
    centred = values - average
    spread = jnp.mean(centred * centred, axis=-1, keepdims=True)
    inverse = lax.rsqrt(spread + norm_eps)
    normal = centred * inverse
    grad_normal = grad_rows * gain_row
    grad_values = inverse * (
        grad_normal
        - jnp.mean(grad_normal, axis=-1, keepdims=True)
        - normal * jnp.mean(grad_normal * normal, axis=-1, keepdims=True)
    )
    return (grad_values, jnp.sum(grad_rows * normal, axis=0), jnp.sum(grad_rows, axis=0))


def rotary_tables(positions):
    half_rot = ROTARY // 2
    frequency = rope_base ** (-(2.0 * jnp.arange(half_rot, dtype=jnp.float32)) / ROTARY)
    angles = positions.astype(jnp.float32)[:, None] * frequency[None, :]
    cosine = jnp.cos(angles)
    sine_part = jnp.sin(angles)
    count = positions.shape[0]
    still = HEAD_DIM - ROTARY
    none = jnp.zeros((count, half_rot), jnp.float32)
    rest = jnp.zeros((count, still), jnp.float32)
    keep = [cosine, cosine, jnp.ones((count, still), jnp.float32)]
    ahead = [-sine_part, none, rest]
    behind = [none, sine_part, rest]
    copies = LANES // HEAD_DIM
    return tuple(jnp.concatenate(part * copies, axis=1) for part in (keep, ahead, behind))


def sum_rows(partial):
    return lax.psum_scatter(
        partial.astype(jnp.bfloat16), "tensor", scatter_dimension=0, tiled=True
    ).astype(jnp.float32)


def sum_shard(gradient, dimension):
    return lax.psum_scatter(
        gradient.astype(jnp.bfloat16), "dp", scatter_dimension=dimension, tiled=True
    ).astype(jnp.float32)


def swiglu(gate_part, up_part):
    return jax.nn.silu(gate_part) * up_part


def adamw(weight_old, first_old, second_old, gradient, step_rate, decay_part):
    first_new = beta_one * first_old + (1.0 - beta_one) * gradient
    second_new = beta_two * second_old + (1.0 - beta_two) * gradient * gradient
    correct_one = 1.0 - beta_one**adam_steps
    correct_two = 1.0 - beta_two**adam_steps
    update = first_new / correct_one / (jnp.sqrt(second_new / correct_two) + adam_eps)
    return (weight_old - step_rate * (update + decay_part * weight_old), first_new, second_new)


def spin(x, keep, ahead, behind):
    return x * keep + pltpu.roll(x, LANES - ROTARY // 2, 1) * ahead + pltpu.roll(x, ROTARY // 2, 1) * behind


def dot_nt(a, b):
    return lax.dot_general(a, b, (((1,), (1,)), ((), ())), preferred_element_type=jnp.float32)


def dot_nn(a, b):
    return lax.dot_general(a, b, (((1,), (0,)), ((), ())), preferred_element_type=jnp.float32)


def masked_scores(s, key_start, query_start, length, causal):
    key_slots = key_start + lax.broadcasted_iota(jnp.int32, s.shape, 0)
    allowed = key_slots < length
    if causal:
        query_slots = query_start + lax.broadcasted_iota(jnp.int32, s.shape, 1)
        allowed = allowed & (key_slots <= query_slots)
    return jnp.where(allowed, s, mask_fill)


def forward_kernel(block, length_ref, pre_ref, keep_ref, ahead_ref, behind_ref,
                   q_ref, k_ref, v_ref, kt_ref, o_ref, lse_ref, vt_ref):
    heads, rows, _ = q_ref.shape
    width = heads * HEAD_DIM
    groups = width // LANES
    per_group = LANES // HEAD_DIM
    blocks = rows // block
    length = length_ref[0]

    def prepare(i, _):
        at = pl.ds(pl.multiple_of(i * block, block), block)
        keep, ahead, behind = keep_ref[at, :], ahead_ref[at, :], behind_ref[at, :]
        for g in range(groups):
            lanes = slice(g * LANES, (g + 1) * LANES)
            q = spin(pre_ref[at, g * LANES:(g + 1) * LANES], keep, ahead, behind)
            k = spin(pre_ref[at, width + g * LANES:width + (g + 1) * LANES], keep, ahead, behind)
            v = pre_ref[at, 2 * width + g * LANES:2 * width + (g + 1) * LANES]
            kt_ref[lanes, at] = k.T.astype(jnp.bfloat16)
            vt_ref[lanes, at] = v.T.astype(jnp.bfloat16)
            for p in range(per_group):
                cut = slice(p * HEAD_DIM, (p + 1) * HEAD_DIM)
                q_ref[g * per_group + p, at, :] = q[:, cut].astype(jnp.bfloat16)
                k_ref[g * per_group + p, at, :] = k[:, cut].astype(jnp.bfloat16)
                v_ref[g * per_group + p, at, :] = v[:, cut].astype(jnp.bfloat16)
        return 0

    lax.fori_loop(0, blocks, prepare, 0)
    full_blocks = length // block
    used_blocks = (length + block - 1) // block

    def query_block(i, _):
        at = pl.ds(pl.multiple_of(i * block, block), block)
        queries = [q_ref[h, at, :] for h in range(heads)]

        def key_block(j, carry, kind):
            key_start = pl.multiple_of(j * block, block)
            keys_at = pl.ds(key_start, block)
            out = []
            for h in range(heads):
                top, total, mixed = carry[h]
                s = dot_nt(k_ref[h, keys_at, :], queries[h]) * (score_scale * log2_e)
                if kind > 0:
                    s = masked_scores(s, key_start, i * block, length, kind == 2)
                new_top = jnp.maximum(top, jnp.max(s, axis=0, keepdims=True))
                shrink = jnp.exp2(top - new_top)
                p = jnp.exp2(s - new_top)
                total = total * shrink + jnp.sum(p, axis=0, keepdims=True)
                mixed = mixed * shrink + dot_nn(
                    vt_ref[h * HEAD_DIM:(h + 1) * HEAD_DIM, keys_at], p.astype(jnp.bfloat16))
                out.append((new_top, total, mixed))
            return tuple(out)

        start = tuple(
            (jnp.full((1, block), mask_fill, jnp.float32), jnp.zeros((1, block), jnp.float32),
             jnp.zeros((HEAD_DIM, block), jnp.float32)) for _ in range(heads))
        plain = jnp.minimum(i, full_blocks)
        carry = lax.fori_loop(0, plain, lambda j, c: key_block(j, c, 0), start)
        carry = lax.fori_loop(plain, jnp.minimum(i, used_blocks), lambda j, c: key_block(j, c, 1), carry)
        carry = key_block(i, carry, 2)
        for h in range(heads):
            top, total, mixed = carry[h]
            lse_ref[h:h + 1, at] = top + jnp.log2(total)
        for g in range(groups):
            pair = [carry[g * per_group + p][2] * (1.0 / carry[g * per_group + p][1]) for p in range(per_group)]
            o_ref[at, g * LANES:(g + 1) * LANES] = jnp.concatenate(pair, axis=0).T.astype(jnp.bfloat16)
        return 0

    lax.fori_loop(0, blocks, query_block, 0)


def attention_forward(lengths, projected, keep, ahead, behind, heads, block):
    rows = projected.shape[0]
    width = heads * HEAD_DIM
    vm = pl.BlockSpec(memory_space=pltpu.VMEM)
    split = jax.ShapeDtypeStruct((heads, rows, HEAD_DIM), jnp.bfloat16)
    return pl.pallas_call(
        functools.partial(forward_kernel, block),
        out_shape=(split, split, split,
                   jax.ShapeDtypeStruct((width, rows), jnp.bfloat16),
                   jax.ShapeDtypeStruct((rows, width), jnp.bfloat16),
                   jax.ShapeDtypeStruct((heads, rows), jnp.float32)),
        in_specs=[pl.BlockSpec(memory_space=pltpu.SMEM)] + [vm] * 4,
        out_specs=(vm,) * 6,
        scratch_shapes=[pltpu.VMEM((width, rows), jnp.bfloat16)],
        compiler_params=pltpu.CompilerParams(vmem_limit_bytes=VMEM_LIMIT),
        cost_estimate=pl.CostEstimate(flops=heads * rows * rows * HEAD_DIM * 8, bytes_accessed=rows * width * 30, transcendentals=heads * rows * rows),
        name="attention_forward",
    )(lengths, projected, keep, ahead, behind)


def backward_kernel(block, length_ref, q_ref, k_ref, v_ref, kt_ref, o_ref, lse_ref, do_ref,
                    keep_ref, ahead_ref, behind_ref, out_ref, bias_ref,
                    dos_ref, delta_ref, dqt_ref, dk_ref, dv_ref):
    heads, rows, _ = q_ref.shape
    width = heads * HEAD_DIM
    groups = width // LANES
    per_group = LANES // HEAD_DIM
    blocks = rows // block
    length = length_ref[0]

    def prepare(i, _):
        at = pl.ds(pl.multiple_of(i * block, block), block)
        for g in range(groups):
            lanes = slice(g * LANES, (g + 1) * LANES)
            grad = do_ref[at, lanes]
            for p in range(per_group):
                dos_ref[g * per_group + p, at, :] = grad[:, p * HEAD_DIM:(p + 1) * HEAD_DIM]
            both = (grad.astype(jnp.float32) * o_ref[at, lanes].astype(jnp.float32)).T
            for p in range(per_group):
                h = g * per_group + p
                delta_ref[h:h + 1, at] = jnp.sum(both[p * HEAD_DIM:(p + 1) * HEAD_DIM], axis=0, keepdims=True)
        dqt_ref[:, at] = jnp.zeros((width, block), jnp.float32)
        return 0

    lax.fori_loop(0, blocks, prepare, 0)

    def key_block(j, _):
        key_start = pl.multiple_of(j * block, block)
        keys_at = pl.ds(key_start, block)

        def query_block(i, carry, kind):
            at = pl.ds(pl.multiple_of(i * block, block), block)
            out = []
            for h in range(heads):
                dk, dv = carry[h]
                keys, queries, grad = k_ref[h, keys_at, :], q_ref[h, at, :], dos_ref[h, at, :]
                s = dot_nt(keys, queries) * (score_scale * log2_e)
                if kind > 0:
                    s = masked_scores(s, key_start, i * block, length, kind == 2)
                p = jnp.exp2(s - lse_ref[h:h + 1, at])
                dp = dot_nt(v_ref[h, keys_at, :], grad)
                ds = (p * (dp - delta_ref[h:h + 1, at])).astype(jnp.bfloat16)
                dv = dv + dot_nn(p.astype(jnp.bfloat16), grad)
                dk = dk + dot_nn(ds, queries)
                here = slice(h * HEAD_DIM, (h + 1) * HEAD_DIM)
                dqt_ref[here, at] += dot_nn(kt_ref[here, keys_at], ds)
                out.append((dk, dv))
            return tuple(out)

        zero = jnp.zeros((block, HEAD_DIM), jnp.float32)
        carry = query_block(j, tuple((zero, zero) for _ in range(heads)), 2)
        whole = key_start + block <= length
        carry = lax.fori_loop(j + 1, jnp.where(whole, blocks, j + 1), lambda i, c: query_block(i, c, 0), carry)
        carry = lax.fori_loop(j + 1, jnp.where(whole, j + 1, blocks), lambda i, c: query_block(i, c, 1), carry)
        for h in range(heads):
            dk_ref[h, keys_at, :] = carry[h][0]
            dv_ref[h, keys_at, :] = carry[h][1]
        return 0

    lax.fori_loop(0, blocks, key_block, 0)
    bias_ref[...] = jnp.zeros(bias_ref.shape, jnp.float32)

    def finish(i, _):
        at = pl.ds(pl.multiple_of(i * block, block), block)
        keep, ahead, behind = keep_ref[at, :], -ahead_ref[at, :], -behind_ref[at, :]
        for g in range(groups):
            lanes = slice(g * LANES, (g + 1) * LANES)
            dq = dqt_ref[lanes, at].T
            dk = jnp.concatenate([dk_ref[g * per_group + p, at, :] for p in range(per_group)], axis=1)
            dv = jnp.concatenate([dv_ref[g * per_group + p, at, :] for p in range(per_group)], axis=1)
            parts = (spin(dq * score_scale, keep, ahead, behind), spin(dk * score_scale, keep, ahead, behind), dv)
            for c in range(3):
                low = parts[c].astype(jnp.bfloat16)
                place = slice(c * width + g * LANES, c * width + (g + 1) * LANES)
                out_ref[at, place] = low
                bias_ref[:, place] += jnp.sum(low.astype(jnp.float32), axis=0, keepdims=True)
        return 0

    lax.fori_loop(0, blocks, finish, 0)


def attention_backward(lengths, q, k, v, kt, o, lse, grad, keep, ahead, behind, block):
    heads, rows, _ = q.shape
    width = heads * HEAD_DIM
    vm = pl.BlockSpec(memory_space=pltpu.VMEM)
    return pl.pallas_call(
        functools.partial(backward_kernel, block),
        out_shape=(jax.ShapeDtypeStruct((rows, 3 * width), jnp.bfloat16),
                   jax.ShapeDtypeStruct((1, 3 * width), jnp.float32)),
        in_specs=[pl.BlockSpec(memory_space=pltpu.SMEM)] + [vm] * 10,
        out_specs=(vm,) * 2,
        scratch_shapes=[
            pltpu.VMEM((heads, rows, HEAD_DIM), jnp.bfloat16),
            pltpu.VMEM((heads, rows), jnp.float32),
            pltpu.VMEM((width, rows), jnp.float32),
            pltpu.VMEM((heads, rows, HEAD_DIM), jnp.float32),
            pltpu.VMEM((heads, rows, HEAD_DIM), jnp.float32),
        ],
        compiler_params=pltpu.CompilerParams(vmem_limit_bytes=VMEM_LIMIT),
        cost_estimate=pl.CostEstimate(flops=heads * rows * rows * HEAD_DIM * 20, bytes_accessed=rows * width * 30, transcendentals=heads * rows * rows),
        name="attention_backward",
    )(lengths, q, k, v, kt, o, lse, grad, keep, ahead, behind)


def local(
    inputs,
    cotangent,
    lengths,
    positions,
    qkv_master,
    gate_up_master,
    out_master,
    down_master,
    bias_master,
    norm_master,
    qkv_first,
    gate_up_first,
    out_first,
    down_first,
    bias_first,
    norm_first,
    qkv_second,
    gate_up_second,
    out_second,
    down_second,
    bias_second,
    norm_second,
):
    tensor_count = lax.axis_size("tensor")
    local_tokens = inputs.shape[0]
    group_tokens = local_tokens * tensor_count
    row_count = lengths.shape[0]
    row_length = group_tokens // row_count
    block_rows = min(256, row_length)
    heads_here = bias_master.shape[1]
    width_here = heads_here * HEAD_DIM
    own_start = lax.axis_index("tensor") * local_tokens
    qkv_copy, gate_up_copy, out_copy, down_copy, bias_copy = (
        lax.all_gather(qkv_master.astype(jnp.bfloat16), "dp", axis=1, tiled=True),
        lax.all_gather(gate_up_master.astype(jnp.bfloat16), "dp", axis=1, tiled=True),
        lax.all_gather(out_master.astype(jnp.bfloat16), "dp", axis=1, tiled=True),
        lax.all_gather(down_master.astype(jnp.bfloat16), "dp", axis=1, tiled=True),
        lax.all_gather(bias_master.astype(jnp.bfloat16), "dp", axis=2, tiled=True),
    )
    qkv_flat = jnp.transpose(qkv_copy, (1, 0, 2)).reshape(qkv_copy.shape[1], 3 * width_here)
    inputs_wide = inputs.astype(jnp.float32)
    normed_one = norm_forward(inputs_wide, norm_master[0], norm_master[1]).astype(jnp.bfloat16)
    gathered_one = lax.all_gather(normed_one, "tensor", axis=0, tiled=True)
    projected = jnp.dot(
        gathered_one, qkv_flat, preferred_element_type=jnp.float32
    ) + bias_copy.reshape(1, 3 * width_here).astype(jnp.float32)
    keep, ahead, behind = rotary_tables(positions)
    queries, keys, values, keys_flipped, mixed_low, log_totals = attention_forward(
        lengths, projected, keep, ahead, behind, heads_here, block_rows
    )
    rows_part = mixed_low
    branch_one = sum_rows(jnp.dot(rows_part, out_copy, preferred_element_type=jnp.float32))
    middle = inputs_wide + branch_one
    normed_two = norm_forward(middle, norm_master[2], norm_master[3]).astype(jnp.bfloat16)
    gathered_two = lax.all_gather(normed_two, "tensor", axis=0, tiled=True)
    gate_up = jnp.einsum(
        "td,cdf->ctf", gathered_two, gate_up_copy, preferred_element_type=jnp.float32
    )
    hidden_wide, swiglu_pull = jax.vjp(swiglu, gate_up[0], gate_up[1])
    hidden = hidden_wide.astype(jnp.bfloat16)
    rows_part = hidden
    branch_two = sum_rows(jnp.dot(rows_part, down_copy, preferred_element_type=jnp.float32))
    block_output = (middle + branch_two).astype(jnp.bfloat16)
    group_index = own_start + jnp.arange(local_tokens, dtype=jnp.int32)
    row_of = group_index // row_length
    slot_of = group_index % row_length
    row_match = row_of[:, None] == jnp.arange(row_count, dtype=jnp.int32)[None, :]
    length_of = jnp.sum(jnp.where(row_match, lengths[None, :], 0), axis=1)
    valid = (slot_of < length_of).astype(jnp.float32)
    grad_result = cotangent.astype(jnp.float32) * valid[:, None]
    gathered_grad = lax.all_gather(grad_result.astype(jnp.bfloat16), "tensor", axis=0, tiled=True)
    grad_down = jnp.einsum("tf,td->fd", hidden, gathered_grad, preferred_element_type=jnp.float32)
    grad_hidden = jnp.einsum(
        "td,fd->tf", gathered_grad, down_copy, preferred_element_type=jnp.float32
    )
    grad_gate, grad_up = swiglu_pull(grad_hidden)
    grad_gate_up = jnp.stack([grad_gate, grad_up]).astype(jnp.bfloat16)
    grad_gate_up_w = jnp.einsum(
        "td,ctf->cdf", gathered_two, grad_gate_up, preferred_element_type=jnp.float32
    )
    rows_part = grad_gate_up
    grad_normed_two = sum_rows(jnp.einsum("ctf,cdf->td", rows_part, gate_up_copy, preferred_element_type=jnp.float32))
    grad_middle_norm, gain_two, shift_two = norm_backward(middle, norm_master[2], grad_normed_two)
    grad_middle = grad_result + grad_middle_norm
    gathered_mid = lax.all_gather(grad_middle.astype(jnp.bfloat16), "tensor", axis=0, tiled=True)
    grad_out_w = jnp.einsum(
        "tw,td->wd", mixed_low, gathered_mid, preferred_element_type=jnp.float32
    )
    grad_mixed = jnp.einsum(
        "td,wd->tw", gathered_mid, out_copy, preferred_element_type=jnp.float32
    ).astype(jnp.bfloat16)

    grad_projected, grad_bias = attention_backward(
        lengths, queries, keys, values, keys_flipped, mixed_low, log_totals, grad_mixed, keep, ahead, behind, block_rows
    )
    grad_bias = grad_bias.reshape(3, heads_here, HEAD_DIM)
    grad_qkv_w = jnp.einsum(
        "td,tcw->cdw",
        gathered_one,
        grad_projected.reshape(group_tokens, 3, width_here),
        preferred_element_type=jnp.float32,
    )
    rows_part = grad_projected
    grad_normed_one = sum_rows(jnp.einsum("tc,dc->td", rows_part, qkv_flat, preferred_element_type=jnp.float32))
    grad_input_norm, gain_one, shift_one = norm_backward(
        inputs_wide, norm_master[0], grad_normed_one
    )
    input_grad = grad_middle + grad_input_norm
    norm_grads = lax.psum(jnp.stack([gain_one, shift_one, gain_two, shift_two]), ("dp", "tensor"))
    qkv_grad, gate_up_grad, out_grad, down_grad, bias_grad = (
        sum_shard(grad_qkv_w, 1),
        sum_shard(grad_gate_up_w, 1),
        sum_shard(grad_out_w, 1),
        sum_shard(grad_down, 1),
        lax.psum_scatter(grad_bias, "dp", scatter_dimension=2, tiled=True),
    )
    qkv_new = adamw(qkv_master, qkv_first, qkv_second, qkv_grad, 2.0 / math.sqrt(D), decay_rate)
    gate_up_new = adamw(
        gate_up_master, gate_up_first, gate_up_second, gate_up_grad, 2.0 / math.sqrt(D), decay_rate
    )
    out_new = adamw(
        out_master, out_first, out_second, out_grad, 16.0 / math.sqrt(HEADS * HEAD_DIM), decay_rate
    )
    down_new = adamw(
        down_master, down_first, down_second, down_grad, 6.0 / math.sqrt(FF), decay_rate
    )
    bias_new = adamw(bias_master, bias_first, bias_second, bias_grad, 1.5, 0.0)
    norm_new = adamw(norm_master, norm_first, norm_second, norm_grads, 0.7, 0.0)
    return (
        block_output,
        input_grad,
        qkv_new[0],
        qkv_new[1],
        qkv_new[2],
        gate_up_new[0],
        gate_up_new[1],
        gate_up_new[2],
        out_new[0],
        out_new[1],
        out_new[2],
        down_new[0],
        down_new[1],
        down_new[2],
        bias_new[0],
        bias_new[1],
        bias_new[2],
        norm_new[0],
        norm_new[1],
        norm_new[2],
    )


def solution(mesh):
    return jax.shard_map(
        local,
        mesh=mesh,
        in_specs=(
            P(("dp", "tensor"), None),
            P(("dp", "tensor"), None),
            P("dp"),
            P("dp"),
            P(None, "dp", "tensor"),
            P(None, "dp", "tensor"),
            P("tensor", "dp"),
            P("tensor", "dp"),
            P(None, "tensor", "dp"),
            P(),
            P(None, "dp", "tensor"),
            P(None, "dp", "tensor"),
            P("tensor", "dp"),
            P("tensor", "dp"),
            P(None, "tensor", "dp"),
            P(),
            P(None, "dp", "tensor"),
            P(None, "dp", "tensor"),
            P("tensor", "dp"),
            P("tensor", "dp"),
            P(None, "tensor", "dp"),
            P(),
        ),
        out_specs=(
            P(("dp", "tensor"), None),
            P(("dp", "tensor"), None),
            P(None, "dp", "tensor"),
            P(None, "dp", "tensor"),
            P(None, "dp", "tensor"),
            P(None, "dp", "tensor"),
            P(None, "dp", "tensor"),
            P(None, "dp", "tensor"),
            P("tensor", "dp"),
            P("tensor", "dp"),
            P("tensor", "dp"),
            P("tensor", "dp"),
            P("tensor", "dp"),
            P("tensor", "dp"),
            P(None, "tensor", "dp"),
            P(None, "tensor", "dp"),
            P(None, "tensor", "dp"),
            P(),
            P(),
            P(),
        ),
        check_vma=False,
    )
```

```python
import functools
import math

import jax
import jax.numpy as jnp
from jax import lax
from jax.experimental import pallas as pl
from jax.experimental.pallas import tpu as pltpu
from jax.sharding import PartitionSpec as P

D = 2048
HEADS = 32
HEAD_DIM = 64
ROTARY = 16
FF = 5632


norm_eps = 1e-05
beta_one = 0.9
beta_two = 0.95
adam_eps = 1e-08
adam_steps = 10
decay_rate = 0.1
rope_base = 10000.0
score_scale = 0.125
mask_fill = -1e30
log2_e = math.log2(math.e)
LANES = 128
VMEM_LIMIT = 60 * 1024 * 1024


def norm_forward(values, gain_row, shift_row):
    average = jnp.mean(values, axis=-1, keepdims=True)
    centred = values - average
    spread = jnp.mean(centred * centred, axis=-1, keepdims=True)
    return centred * lax.rsqrt(spread + norm_eps) * gain_row + shift_row


def norm_backward(values, gain_row, grad_rows):
    average = jnp.mean(values, axis=-1, keepdims=True)
    centred = values - average
    spread = jnp.mean(centred * centred, axis=-1, keepdims=True)
    inverse = lax.rsqrt(spread + norm_eps)
    normal = centred * inverse
    grad_normal = grad_rows * gain_row
    grad_values = inverse * (
        grad_normal
        - jnp.mean(grad_normal, axis=-1, keepdims=True)
        - normal * jnp.mean(grad_normal * normal, axis=-1, keepdims=True)
    )
    return (
        grad_values,
        jnp.sum(grad_rows * normal, axis=0, keepdims=True),
        jnp.sum(grad_rows, axis=0, keepdims=True),
    )


def rotary_tables(positions):
    half_rot = ROTARY // 2
    frequency = rope_base ** (-(2.0 * jnp.arange(half_rot, dtype=jnp.float32)) / ROTARY)
    angles = positions.astype(jnp.float32)[:, None] * frequency[None, :]
    cosine = jnp.cos(angles)
    sine_part = jnp.sin(angles)
    count = positions.shape[0]
    still = HEAD_DIM - ROTARY
    none = jnp.zeros((count, half_rot), jnp.float32)
    rest = jnp.zeros((count, still), jnp.float32)
    keep = [cosine, cosine, jnp.ones((count, still), jnp.float32)]
    ahead = [-sine_part, none, rest]
    behind = [none, sine_part, rest]
    copies = LANES // HEAD_DIM
    return tuple(jnp.concatenate(part * copies, axis=1) for part in (keep, ahead, behind))


def sum_shard(gradient, dimension):
    return lax.psum_scatter(
        gradient.astype(jnp.bfloat16), "dp", scatter_dimension=dimension, tiled=True
    ).astype(jnp.float32)


def adamw(weight_old, first_old, second_old, gradient, step_rate, decay_part):
    first_new = beta_one * first_old + (1.0 - beta_one) * gradient
    second_new = beta_two * second_old + (1.0 - beta_two) * gradient * gradient
    correct_one = 1.0 - beta_one**adam_steps
    correct_two = 1.0 - beta_two**adam_steps
    update = first_new / correct_one / (jnp.sqrt(second_new / correct_two) + adam_eps)
    return (weight_old - step_rate * (update + decay_part * weight_old), first_new, second_new)


def spin(x, keep, ahead, behind):
    return x * keep + pltpu.roll(x, LANES - ROTARY // 2, 1) * ahead + pltpu.roll(x, ROTARY // 2, 1) * behind


def dot_nt(a, b):
    return lax.dot_general(a, b, (((1,), (1,)), ((), ())), preferred_element_type=jnp.float32)


def dot_nn(a, b):
    return lax.dot_general(a, b, (((1,), (0,)), ((), ())), preferred_element_type=jnp.float32)


def masked_scores(s, key_start, query_start, length, causal):
    key_slots = key_start + lax.broadcasted_iota(jnp.int32, s.shape, 0)
    allowed = key_slots < length
    if causal:
        query_slots = query_start + lax.broadcasted_iota(jnp.int32, s.shape, 1)
        allowed = allowed & (key_slots <= query_slots)
    return jnp.where(allowed, s, mask_fill)


def forward_kernel(block, length_ref, pre_ref, keep_ref, ahead_ref, behind_ref,
                   q_ref, k_ref, v_ref, kt_ref, o_ref, lse_ref, vt_ref):
    heads, rows, _ = q_ref.shape
    width = heads * HEAD_DIM
    groups = width // LANES
    per_group = LANES // HEAD_DIM
    blocks = rows // block
    length = length_ref[0]

    def prepare(i, _):
        at = pl.ds(pl.multiple_of(i * block, block), block)
        keep, ahead, behind = keep_ref[at, :], ahead_ref[at, :], behind_ref[at, :]
        for g in range(groups):
            lanes = slice(g * LANES, (g + 1) * LANES)
            q = spin(pre_ref[at, g * LANES:(g + 1) * LANES], keep, ahead, behind)
            k = spin(pre_ref[at, width + g * LANES:width + (g + 1) * LANES], keep, ahead, behind)
            v = pre_ref[at, 2 * width + g * LANES:2 * width + (g + 1) * LANES]
            kt_ref[lanes, at] = k.T.astype(jnp.bfloat16)
            vt_ref[lanes, at] = v.T.astype(jnp.bfloat16)
            for p in range(per_group):
                cut = slice(p * HEAD_DIM, (p + 1) * HEAD_DIM)
                q_ref[g * per_group + p, at, :] = q[:, cut].astype(jnp.bfloat16)
                k_ref[g * per_group + p, at, :] = k[:, cut].astype(jnp.bfloat16)
                v_ref[g * per_group + p, at, :] = v[:, cut].astype(jnp.bfloat16)
        return 0

    lax.fori_loop(0, blocks, prepare, 0)
    full_blocks = length // block
    used_blocks = (length + block - 1) // block

    def query_block(i, _):
        at = pl.ds(pl.multiple_of(i * block, block), block)
        queries = [q_ref[h, at, :] for h in range(heads)]

        def key_block(j, carry, kind):
            key_start = pl.multiple_of(j * block, block)
            keys_at = pl.ds(key_start, block)
            out = []
            for h in range(heads):
                top, total, mixed = carry[h]
                s = dot_nt(k_ref[h, keys_at, :], queries[h]) * (score_scale * log2_e)
                if kind > 0:
                    s = masked_scores(s, key_start, i * block, length, kind == 2)
                new_top = jnp.maximum(top, jnp.max(s, axis=0, keepdims=True))
                shrink = jnp.exp2(top - new_top)
                p = jnp.exp2(s - new_top)
                total = total * shrink + jnp.sum(p, axis=0, keepdims=True)
                mixed = mixed * shrink + dot_nn(
                    vt_ref[h * HEAD_DIM:(h + 1) * HEAD_DIM, keys_at], p.astype(jnp.bfloat16))
                out.append((new_top, total, mixed))
            return tuple(out)

        start = tuple(
            (jnp.full((1, block), mask_fill, jnp.float32), jnp.zeros((1, block), jnp.float32),
             jnp.zeros((HEAD_DIM, block), jnp.float32)) for _ in range(heads))
        plain = jnp.minimum(i, full_blocks)
        carry = lax.fori_loop(0, plain, lambda j, c: key_block(j, c, 0), start)
        carry = lax.fori_loop(plain, jnp.minimum(i, used_blocks), lambda j, c: key_block(j, c, 1), carry)
        carry = key_block(i, carry, 2)
        for h in range(heads):
            top, total, mixed = carry[h]
            lse_ref[h:h + 1, at] = top + jnp.log2(total)
        for g in range(groups):
            pair = [carry[g * per_group + p][2] * (1.0 / carry[g * per_group + p][1]) for p in range(per_group)]
            o_ref[at, g * LANES:(g + 1) * LANES] = jnp.concatenate(pair, axis=0).T.astype(jnp.bfloat16)
        return 0

    lax.fori_loop(0, blocks, query_block, 0)


def attention_forward(lengths, projected, keep, ahead, behind, heads, block):
    rows = projected.shape[0]
    width = heads * HEAD_DIM
    vm = pl.BlockSpec(memory_space=pltpu.VMEM)
    split = jax.ShapeDtypeStruct((heads, rows, HEAD_DIM), jnp.bfloat16)
    return pl.pallas_call(
        functools.partial(forward_kernel, block),
        out_shape=(split, split, split,
                   jax.ShapeDtypeStruct((width, rows), jnp.bfloat16),
                   jax.ShapeDtypeStruct((rows, width), jnp.bfloat16),
                   jax.ShapeDtypeStruct((heads, rows), jnp.float32)),
        in_specs=[pl.BlockSpec(memory_space=pltpu.SMEM)] + [vm] * 4,
        out_specs=(vm,) * 6,
        scratch_shapes=[pltpu.VMEM((width, rows), jnp.bfloat16)],
        compiler_params=pltpu.CompilerParams(vmem_limit_bytes=VMEM_LIMIT),
        cost_estimate=pl.CostEstimate(flops=heads * rows * rows * HEAD_DIM * 8, bytes_accessed=rows * width * 30, transcendentals=heads * rows * rows),
        name="attention_forward",
    )(lengths, projected, keep, ahead, behind)


def backward_kernel(block, length_ref, q_ref, k_ref, v_ref, kt_ref, o_ref, lse_ref, do_ref,
                    keep_ref, ahead_ref, behind_ref, out_ref, bias_ref,
                    dos_ref, delta_ref, dqt_ref, dk_ref, dv_ref):
    heads, rows, _ = q_ref.shape
    width = heads * HEAD_DIM
    groups = width // LANES
    per_group = LANES // HEAD_DIM
    blocks = rows // block
    length = length_ref[0]

    def prepare(i, _):
        at = pl.ds(pl.multiple_of(i * block, block), block)
        for g in range(groups):
            lanes = slice(g * LANES, (g + 1) * LANES)
            grad = do_ref[at, lanes]
            for p in range(per_group):
                dos_ref[g * per_group + p, at, :] = grad[:, p * HEAD_DIM:(p + 1) * HEAD_DIM]
            both = (grad.astype(jnp.float32) * o_ref[at, lanes].astype(jnp.float32)).T
            for p in range(per_group):
                h = g * per_group + p
                delta_ref[h:h + 1, at] = jnp.sum(both[p * HEAD_DIM:(p + 1) * HEAD_DIM], axis=0, keepdims=True)
        dqt_ref[:, at] = jnp.zeros((width, block), jnp.float32)
        return 0

    lax.fori_loop(0, blocks, prepare, 0)

    def key_block(j, _):
        key_start = pl.multiple_of(j * block, block)
        keys_at = pl.ds(key_start, block)

        def query_block(i, carry, kind):
            at = pl.ds(pl.multiple_of(i * block, block), block)
            out = []
            for h in range(heads):
                dk, dv = carry[h]
                keys, queries, grad = k_ref[h, keys_at, :], q_ref[h, at, :], dos_ref[h, at, :]
                s = dot_nt(keys, queries) * (score_scale * log2_e)
                if kind > 0:
                    s = masked_scores(s, key_start, i * block, length, kind == 2)
                p = jnp.exp2(s - lse_ref[h:h + 1, at])
                dp = dot_nt(v_ref[h, keys_at, :], grad)
                ds = (p * (dp - delta_ref[h:h + 1, at])).astype(jnp.bfloat16)
                dv = dv + dot_nn(p.astype(jnp.bfloat16), grad)
                dk = dk + dot_nn(ds, queries)
                here = slice(h * HEAD_DIM, (h + 1) * HEAD_DIM)
                dqt_ref[here, at] += dot_nn(kt_ref[here, keys_at], ds)
                out.append((dk, dv))
            return tuple(out)

        zero = jnp.zeros((block, HEAD_DIM), jnp.float32)
        carry = query_block(j, tuple((zero, zero) for _ in range(heads)), 2)
        whole = key_start + block <= length
        carry = lax.fori_loop(j + 1, jnp.where(whole, blocks, j + 1), lambda i, c: query_block(i, c, 0), carry)
        carry = lax.fori_loop(j + 1, jnp.where(whole, j + 1, blocks), lambda i, c: query_block(i, c, 1), carry)
        for h in range(heads):
            dk_ref[h, keys_at, :] = carry[h][0]
            dv_ref[h, keys_at, :] = carry[h][1]
        return 0

    lax.fori_loop(0, blocks, key_block, 0)
    bias_ref[...] = jnp.zeros(bias_ref.shape, jnp.float32)

    def finish(i, _):
        at = pl.ds(pl.multiple_of(i * block, block), block)
        keep, ahead, behind = keep_ref[at, :], -ahead_ref[at, :], -behind_ref[at, :]
        for g in range(groups):
            lanes = slice(g * LANES, (g + 1) * LANES)
            dq = dqt_ref[lanes, at].T
            dk = jnp.concatenate([dk_ref[g * per_group + p, at, :] for p in range(per_group)], axis=1)
            dv = jnp.concatenate([dv_ref[g * per_group + p, at, :] for p in range(per_group)], axis=1)
            parts = (spin(dq * score_scale, keep, ahead, behind), spin(dk * score_scale, keep, ahead, behind), dv)
            for c in range(3):
                low = parts[c].astype(jnp.bfloat16)
                place = slice(c * width + g * LANES, c * width + (g + 1) * LANES)
                out_ref[at, place] = low
                bias_ref[:, place] += jnp.sum(low.astype(jnp.float32), axis=0, keepdims=True)
        return 0

    lax.fori_loop(0, blocks, finish, 0)


def attention_backward(lengths, q, k, v, kt, o, lse, grad, keep, ahead, behind, block):
    heads, rows, _ = q.shape
    width = heads * HEAD_DIM
    vm = pl.BlockSpec(memory_space=pltpu.VMEM)
    return pl.pallas_call(
        functools.partial(backward_kernel, block),
        out_shape=(jax.ShapeDtypeStruct((rows, 3 * width), jnp.bfloat16),
                   jax.ShapeDtypeStruct((1, 3 * width), jnp.float32)),
        in_specs=[pl.BlockSpec(memory_space=pltpu.SMEM)] + [vm] * 10,
        out_specs=(vm,) * 2,
        scratch_shapes=[
            pltpu.VMEM((heads, rows, HEAD_DIM), jnp.bfloat16),
            pltpu.VMEM((heads, rows), jnp.float32),
            pltpu.VMEM((width, rows), jnp.float32),
            pltpu.VMEM((heads, rows, HEAD_DIM), jnp.float32),
            pltpu.VMEM((heads, rows, HEAD_DIM), jnp.float32),
        ],
        compiler_params=pltpu.CompilerParams(vmem_limit_bytes=VMEM_LIMIT),
        cost_estimate=pl.CostEstimate(flops=heads * rows * rows * HEAD_DIM * 20, bytes_accessed=rows * width * 30, transcendentals=heads * rows * rows),
        name="attention_backward",
    )(lengths, q, k, v, kt, o, lse, grad, keep, ahead, behind)


VM = pl.BlockSpec(memory_space=pltpu.VMEM)
MESH = pl.DeviceIdType.MESH


def params(number):
    return pltpu.CompilerParams(collective_id=number, has_side_effects=True, vmem_limit_bytes=VMEM_LIMIT)


def lasting(us):
    return pl.CostEstimate(flops=int(us * 1.1e9), bytes_accessed=0, transcendentals=0)


def place():
    t = lax.axis_index("tensor")
    return t, lax.rem(t, 2), lax.div(t, 2)


def greet(n):
    t, core, chip = place()
    barrier = pltpu.get_barrier_semaphore()

    def hail(index):
        pl.semaphore_signal(barrier, inc=1, device_id={"tensor": index}, device_id_type=MESH)

    hail(t + 1 - 2 * core)
    pl.when(chip > 0)(lambda: hail(t - 2))
    pl.when(chip < n - 1)(lambda: hail(t + 2))
    pl.semaphore_wait(barrier, 1 + jnp.minimum(chip, 1) + jnp.minimum(n - 1 - chip, 1))


def near(j, m, n):
    below, above = m, n - 1 - m
    both = jnp.minimum(below, above)
    half = lax.div(j + 1, 2)
    inside = m + jnp.where(lax.rem(j, 2) == 1, -half, half)
    outside = m + jnp.where(above > below, j - both, both - j)
    return jnp.where(j <= 2 * both, inside, outside)


class Gather:
    def __init__(self, n, own, buf, sems, pieces):
        self.n, self.own, self.buf, self.pieces = n, own, buf, pieces
        self.up, self.down, self.side, self.line_in, self.side_in = [sems.at[i] for i in range(5)]
        self.t, self.core, self.m = place()
        self.sibling = self.t + 1 - 2 * self.core
        self.rows = own.shape[0] // pieces

    def copy(self, src, k, p, core, send, recv, target):
        at = pl.ds(pl.multiple_of(p * self.rows, self.rows), self.rows)
        index = k * self.pieces + p
        return pltpu.make_async_remote_copy(
            src_ref=src.at[at], dst_ref=self.buf.at[2 * k + core, at], send_sem=send.at[index],
            recv_sem=recv.at[index], device_id={"tensor": target}, device_id_type=MESH)

    def to_up(self, k, p, src):
        return self.copy(src, k, p, self.core, self.up, self.line_in, self.t + 2)

    def to_down(self, k, p, src):
        return self.copy(src, k, p, self.core, self.down, self.line_in, self.t - 2)

    def to_side(self, k, p, src):
        return self.copy(src, k, p, self.core, self.side, self.side_in, self.sibling)

    def start(self):
        m = self.m
        for p in range(self.pieces):
            pl.when(m < self.n - 1)(lambda: self.to_up(m, p, self.own).start())
            pl.when(m > 0)(lambda: self.to_down(m, p, self.own).start())
            self.to_side(m, p, self.own).start()

    def arrive(self, d, only=None):
        m = self.m
        lo, hi = m - d, m + d
        for p in range(self.pieces) if only is None else (only,):
            @pl.when(lo >= 0)
            def _():
                src = self.buf.at[2 * lo + self.core]
                self.to_up(lo, p, src).wait_recv()
                pl.when(m < self.n - 1)(lambda: self.to_up(lo, p, src).start())
                self.to_side(lo, p, src).start()

            @pl.when(hi < self.n)
            def _():
                src = self.buf.at[2 * hi + self.core]
                self.to_down(hi, p, src).wait_recv()
                pl.when(m > 0)(lambda: self.to_down(hi, p, src).start())
                self.to_side(hi, p, src).start()

    def side_wait(self, k):
        for p in range(self.pieces):
            self.copy(self.own, k, p, 1 - self.core, self.side, self.side_in, self.sibling).wait_recv()

    def finish(self):
        m = self.m

        def one(k, _):
            for p in range(self.pieces):
                pl.when((k <= m) & (m < self.n - 1))(lambda: self.to_up(k, p, self.own).wait_send())
                pl.when((k >= m) & (m > 0))(lambda: self.to_down(k, p, self.own).wait_send())
                self.to_side(k, p, self.own).wait_send()
            return 0

        lax.fori_loop(0, self.n, one, 0)


class Scatter:
    def __init__(self, n, pieces, side_out, side_in, line_in, side_sems, line_send, line_recv):
        self.n, self.pieces = n, pieces
        self.side_out, self.side_in, self.line_in = side_out, side_in, line_in
        self.side_send, self.side_recv = side_sems.at[0], side_sems.at[1]
        self.line_send, self.line_recv = line_send, line_recv
        self.t, self.core, self.m = place()
        self.sibling = self.t + 1 - 2 * self.core
        self.rows = side_out.shape[1] // pieces
        self.step = min(32, self.rows)

    def side(self, k):
        return pltpu.make_async_remote_copy(
            src_ref=self.side_out.at[k], dst_ref=self.side_in.at[k], send_sem=self.side_send.at[k],
            recv_sem=self.side_recv.at[k], device_id={"tensor": self.sibling}, device_id_type=MESH)

    def line(self, k, p, slot, target):
        at = pl.ds(pl.multiple_of(p * self.rows, self.rows), self.rows)
        return pltpu.make_async_remote_copy(
            src_ref=self.side_in.at[k, at], dst_ref=self.line_in.at[slot, at],
            send_sem=self.line_send.at[k * self.pieces + p], recv_sem=self.line_recv.at[slot * self.pieces + p],
            device_id={"tensor": target}, device_id_type=MESH)

    def each(self, p, body):
        def one(i, _):
            body(pl.ds(pl.multiple_of(p * self.rows + i * self.step, self.step), self.step))
            return 0

        lax.fori_loop(0, self.rows // self.step, one, 0)

    def pass_on(self, k, own, between=None):
        m, n = self.m, self.n
        self.side(k).wait_recv()
        inner = ((k > m) & (m > 0)) | ((k < m) & (m < n - 1))

        def one(p, _):
            @pl.when(inner)
            def _():
                self.line(k, p, k, self.t).wait_recv()

                def add(at):
                    total = own[at, :] + self.side_in[k, at, :].astype(jnp.float32) + self.line_in[k, at, :].astype(jnp.float32)
                    self.side_in[k, at, :] = total.astype(jnp.bfloat16)

                self.each(p, add)

            @pl.when(jnp.logical_not(inner))
            def _():
                def add(at):
                    self.side_in[k, at, :] = (own[at, :] + self.side_in[k, at, :].astype(jnp.float32)).astype(jnp.bfloat16)

                self.each(p, add)

            pl.when(k > m)(lambda: self.line(k, p, k, self.t + 2).start())
            pl.when(k < m)(lambda: self.line(k, p, jnp.where(k == m - 1, n, k), self.t - 2).start())
            if between is not None:
                between(p)
            return 0

        lax.fori_loop(0, self.pieces, one, 0)

    def settle(self, own, consume):
        m, n = self.m, self.n
        self.side(m).wait_recv()

        def one(p, _):
            def first(at):
                own[at, :] += self.side_in[m, at, :].astype(jnp.float32)

            self.each(p, first)

            def more(slot):
                self.line(m, p, slot, self.t).wait_recv()

                def add(at):
                    own[at, :] += self.line_in[slot, at, :].astype(jnp.float32)

                self.each(p, add)

            pl.when(m > 0)(lambda: more(m))
            pl.when(m < n - 1)(lambda: more(n))
            self.each(p, lambda at: consume(at, own[at, :]))
            return 0

        lax.fori_loop(0, self.pieces, one, 0)

    def finish(self):
        def one(k, _):
            self.side(k).wait_send()

            @pl.when(k != self.m)
            def _():
                for p in range(self.pieces):
                    self.line(k, p, k, self.t).wait_send()

            return 0

        lax.fori_loop(0, self.n, one, 0)


def scatter_scratch(n, pieces, rows, width):
    return [
        pltpu.VMEM((n, rows, width), jnp.bfloat16), pltpu.VMEM((n, rows, width), jnp.bfloat16),
        pltpu.VMEM((n + 1, rows, width), jnp.bfloat16),
        pltpu.SemaphoreType.DMA((2, n)), pltpu.SemaphoreType.DMA((n * pieces,)), pltpu.SemaphoreType.DMA(((n + 1) * pieces,)),
    ]


def gather_kernel(n, pieces, x_ref, g_ref, sems):
    greet(n)
    g = Gather(n, x_ref, g_ref, sems, pieces)
    g.start()
    g_ref[g.t] = x_ref[...]
    for d in range(1, n):
        g.arrive(d)
    for k in range(n):
        g.side_wait(k)
    g.finish()


def gather(x, n, number, pieces=4):
    rows, d = x.shape
    return pl.pallas_call(functools.partial(gather_kernel, n, pieces),
        out_shape=jax.ShapeDtypeStruct((2 * n, rows, d), x.dtype),
        in_specs=[VM], out_specs=VM,
        scratch_shapes=[pltpu.SemaphoreType.DMA((5, n * pieces))],
        compiler_params=params(number),
        cost_estimate=lasting(78), name="gather_rows")(x)


def out_kernel(n, pieces, mixed_ref, w_ref, x_ref, norm_ref, cot_ref, middle_ref, normed_ref, cots_ref,
               acc_ref, side_out, side_in, line_in, side_sems, line_send, line_recv, gather_sems):
    greet(n)
    g = Gather(n, cot_ref, cots_ref, gather_sems, pieces)
    s = Scatter(n, pieces, side_out, side_in, line_in, side_sems, line_send, line_recv)
    g.start()
    cots_ref[g.t] = cot_ref[...]
    m, core = s.m, s.core
    width = w_ref.shape[1]
    cut = min(512, width)

    def one(j, _):
        k = near(n - 1 - j, m, n)
        for a in range(0, width, cut):
            s.side_out[k, :, a:a + cut] = dot_nn(mixed_ref[2 * k + 1 - core], w_ref[:, a:a + cut]).astype(jnp.bfloat16)
        s.side(k).start()
        for a in range(0, width, cut):
            acc_ref[:, a:a + cut] = dot_nn(mixed_ref[2 * k + core], w_ref[:, a:a + cut])
        pl.when(j < n - 1)(lambda: s.pass_on(k, acc_ref, lambda p: g.arrive(j + 1, p)))
        return 0

    lax.fori_loop(0, n, one, 0)

    def consume(at, total):
        middle = x_ref[at, :].astype(jnp.float32) + total
        middle_ref[at, :] = middle
        normed_ref[at, :] = norm_forward(middle, norm_ref[2:3, :], norm_ref[3:4, :]).astype(jnp.bfloat16)

    s.settle(acc_ref, consume)
    for k in range(n):
        g.side_wait(k)
    g.finish()
    s.finish()


def out_branch(mixed, w, x, norms, cot, n, number, pieces=4):
    rows, width = x.shape
    return pl.pallas_call(functools.partial(out_kernel, n, pieces),
        out_shape=(jax.ShapeDtypeStruct((rows, width), jnp.float32), jax.ShapeDtypeStruct((rows, width), jnp.bfloat16),
                   jax.ShapeDtypeStruct((2 * n, rows, width), jnp.bfloat16)),
        in_specs=[VM] * 5, out_specs=(VM,) * 3,
        scratch_shapes=[pltpu.VMEM((rows, width), jnp.float32)] + scatter_scratch(n, pieces, rows, width) + [pltpu.SemaphoreType.DMA((5, n * pieces))],
        compiler_params=params(number),
        cost_estimate=lasting(115), name="out_branch")(mixed.reshape(2 * n, rows, mixed.shape[1]), w, x, norms, cot)


def mlp_kernel(n, pieces, x_ref, cots_ref, gate_up_ref, down_ref, middle_ref, norm_ref,
               xs_ref, hidden_ref, grads_ref, grad_middle_ref, low_ref, sums_ref,
               acc_ref, side_out, side_in, line_in, side_sems, line_send, line_recv, gather_sems):
    greet(n)
    g = Gather(n, x_ref, xs_ref, gather_sems, pieces)
    s = Scatter(n, pieces, side_out, side_in, line_in, side_sems, line_send, line_recv)
    g.start()
    xs_ref[g.t] = x_ref[...]
    m, core = s.m, s.core

    def work(slot):
        x = xs_ref[slot]
        gate = dot_nn(x, gate_up_ref[0])
        up = dot_nn(x, gate_up_ref[1])
        grad_hidden = dot_nt(cots_ref[slot], down_ref[...])
        sig = 1.0 / (1.0 + jnp.exp(-gate))
        silu = gate * sig
        hidden_ref[slot] = (silu * up).astype(jnp.bfloat16)
        grads_ref[0, slot] = (grad_hidden * up * (sig * (1.0 + gate * (1.0 - sig)))).astype(jnp.bfloat16)
        grads_ref[1, slot] = (grad_hidden * silu).astype(jnp.bfloat16)

    def ring(d, _):
        pl.when(d > 0)(lambda: g.arrive(d))

        def one(q, _):
            other, above = lax.div(q, 2), lax.rem(q, 2)
            k = jnp.where(above == 1, m + d, m - d)

            @pl.when((k >= 0) & (k < n) & ((d > 0) | (above == 0)))
            def _():
                pl.when(other == 1)(lambda: g.side_wait(k))
                work(2 * k + jnp.where(other == 1, 1 - core, core))

            return 0

        lax.fori_loop(0, 4, one, 0)
        return 0

    lax.fori_loop(0, n, ring, 0)
    width = x_ref.shape[1]
    cut = min(512, width)

    def one(j, _):
        k = near(n - 1 - j, m, n)

        def partial(slot, a):
            return dot_nt(grads_ref[0, slot], gate_up_ref[0, a:a + cut, :]) + dot_nt(grads_ref[1, slot], gate_up_ref[1, a:a + cut, :])

        for a in range(0, width, cut):
            s.side_out[k, :, a:a + cut] = partial(2 * k + 1 - core, a).astype(jnp.bfloat16)
        s.side(k).start()
        for a in range(0, width, cut):
            acc_ref[:, a:a + cut] = partial(2 * k + core, a)
        pl.when(j < n - 1)(lambda: s.pass_on(k, acc_ref))
        return 0

    lax.fori_loop(0, n, one, 0)
    sums_ref[...] = jnp.zeros(sums_ref.shape, jnp.float32)

    def consume(at, total):
        back, gain, shift = norm_backward(middle_ref[at, :], norm_ref[2:3, :], total)
        result = cots_ref[s.t, at, :].astype(jnp.float32) + back
        grad_middle_ref[at, :] = result
        low_ref[at, :] = result.astype(jnp.bfloat16)
        sums_ref[0:1, :] += gain
        sums_ref[1:2, :] += shift

    s.settle(acc_ref, consume)
    g.finish()
    s.finish()


def mlp(x, cots, gate_up, down, middle, norms, n, number, pieces=4):
    rows, width = x.shape
    hidden = down.shape[0]
    f32, low = jnp.float32, jnp.bfloat16
    return pl.pallas_call(functools.partial(mlp_kernel, n, pieces),
        out_shape=(jax.ShapeDtypeStruct((2 * n, rows, width), low), jax.ShapeDtypeStruct((2 * n, rows, hidden), low),
                   jax.ShapeDtypeStruct((2, 2 * n, rows, hidden), low), jax.ShapeDtypeStruct((rows, width), f32),
                   jax.ShapeDtypeStruct((rows, width), low), jax.ShapeDtypeStruct((2, width), f32)),
        in_specs=[VM] * 6, out_specs=(VM,) * 6,
        scratch_shapes=[pltpu.VMEM((rows, width), f32)] + scatter_scratch(n, pieces, rows, width) + [pltpu.SemaphoreType.DMA((5, n * pieces))],
        compiler_params=params(number), cost_estimate=lasting(165), name="mlp")(x, cots, gate_up, down, middle, norms)


def down_kernel(n, pieces, hidden_ref, down_ref, middle_ref, x_ref, out_ref, block_ref, xs_ref, back_ref,
                acc_ref, side_out, side_in, line_in, side_sems, line_send, line_recv, gather_sems):
    greet(n)
    g = Gather(n, x_ref, xs_ref, gather_sems, pieces)
    s = Scatter(n, pieces, side_out, side_in, line_in, side_sems, line_send, line_recv)
    g.start()
    xs_ref[g.t] = x_ref[...]
    m, core = s.m, s.core
    width = down_ref.shape[1]
    cut = min(512, width)

    def one(j, _):
        k = near(n - 1 - j, m, n)
        for a in range(0, width, cut):
            s.side_out[k, :, a:a + cut] = dot_nn(hidden_ref[2 * k + 1 - core], down_ref[:, a:a + cut]).astype(jnp.bfloat16)
        s.side(k).start()
        for a in range(0, width, cut):
            acc_ref[:, a:a + cut] = dot_nn(hidden_ref[2 * k + core], down_ref[:, a:a + cut])
        pl.when(j < n - 1)(lambda: s.pass_on(k, acc_ref, lambda p: g.arrive(j + 1, p)))
        return 0

    lax.fori_loop(0, n, one, 0)

    def consume(at, total):
        block_ref[at, :] = (middle_ref[at, :] + total).astype(jnp.bfloat16)

    s.settle(acc_ref, consume)

    def last(k, _):
        g.side_wait(k)
        for c in range(2):
            back_ref[2 * k + c] = dot_nt(xs_ref[2 * k + c], out_ref[...]).astype(jnp.bfloat16)
        return 0

    lax.fori_loop(0, n, last, 0)
    g.finish()
    s.finish()


def down_branch(hidden, down, middle, x, out, n, number, pieces=4):
    rows, width = x.shape
    f32, low = jnp.float32, jnp.bfloat16
    return pl.pallas_call(functools.partial(down_kernel, n, pieces),
        out_shape=(jax.ShapeDtypeStruct((rows, width), low), jax.ShapeDtypeStruct((2 * n, rows, width), low),
                   jax.ShapeDtypeStruct((2 * n, rows, out.shape[0]), low)),
        in_specs=[VM] * 5, out_specs=(VM,) * 3,
        scratch_shapes=[pltpu.VMEM((rows, width), f32)] + scatter_scratch(n, pieces, rows, width) + [pltpu.SemaphoreType.DMA((5, n * pieces))],
        compiler_params=params(number), cost_estimate=lasting(115), name="down_branch")(hidden, down, middle, x, out)


def first_kernel(n, pieces, grad_ref, w_ref, x_ref, middle_ref, norm_ref, result_ref, sums_ref,
                 acc_ref, side_out, side_in, line_in, side_sems, line_send, line_recv):
    greet(n)
    s = Scatter(n, pieces, side_out, side_in, line_in, side_sems, line_send, line_recv)
    m, core = s.m, s.core
    width = w_ref.shape[0]
    cut = min(512, width)

    def one(j, _):
        k = near(n - 1 - j, m, n)
        for a in range(0, width, cut):
            s.side_out[k, :, a:a + cut] = dot_nt(grad_ref[2 * k + 1 - core], w_ref[a:a + cut, :]).astype(jnp.bfloat16)
        s.side(k).start()
        for a in range(0, width, cut):
            acc_ref[:, a:a + cut] = dot_nt(grad_ref[2 * k + core], w_ref[a:a + cut, :])
        pl.when(j < n - 1)(lambda: s.pass_on(k, acc_ref))
        return 0

    lax.fori_loop(0, n, one, 0)
    sums_ref[...] = jnp.zeros(sums_ref.shape, jnp.float32)

    def consume(at, total):
        back, gain, shift = norm_backward(x_ref[at, :].astype(jnp.float32), norm_ref[0:1, :], total)
        result_ref[at, :] = middle_ref[at, :] + back
        sums_ref[0:1, :] += gain
        sums_ref[1:2, :] += shift

    s.settle(acc_ref, consume)
    s.finish()


def first_branch(grad, w, x, grad_middle, norms, n, number, pieces=4):
    rows, width = x.shape
    f32 = jnp.float32
    return pl.pallas_call(functools.partial(first_kernel, n, pieces),
        out_shape=(jax.ShapeDtypeStruct((rows, width), f32), jax.ShapeDtypeStruct((2, width), f32)),
        in_specs=[VM] * 5, out_specs=(VM,) * 2,
        scratch_shapes=[pltpu.VMEM((rows, width), f32)] + scatter_scratch(n, pieces, rows, width),
        compiler_params=params(number), cost_estimate=lasting(85), name="first_branch")(grad.reshape(2 * n, rows, grad.shape[1]), w, x, grad_middle, norms)


def total_kernel(x_ref, out_ref, parts, groups, send_one, recv_one, send_two, recv_two, send_three, recv_three):
    t, g = lax.axis_index("tensor"), lax.axis_index("dp")
    count, group_count = parts.shape[0], groups.shape[0]
    barrier = pltpu.get_barrier_semaphore()
    for j in range(count):
        pl.when(j != t)(lambda: pl.semaphore_signal(barrier, inc=1, device_id={"tensor": j}, device_id_type=MESH))
    for i in range(group_count):
        pl.when(i != g)(lambda: pl.semaphore_signal(barrier, inc=1, device_id={"dp": i}, device_id_type=MESH))
    pl.semaphore_wait(barrier, count + group_count - 2)

    def spread(src, dst, send, recv, at, axis, peer):
        return pltpu.make_async_remote_copy(
            src_ref=src, dst_ref=dst, send_sem=send.at[peer], recv_sem=recv.at[at], device_id={axis: peer}, device_id_type=MESH)

    def exchange(me, size, make, stay):
        for j in range(size):
            pl.when(j != me)(lambda: make(j, me).start())
        stay()
        for j in range(size):
            pl.when(j != me)(lambda: make(j, j).wait_recv())
        for j in range(size):
            pl.when(j != me)(lambda: make(j, me).wait_send())

    def keep_one():
        parts[t] = x_ref[t]

    def keep_two():
        groups[g] = sum_of(parts)

    def sum_of(ref):
        total = ref[0]
        for j in range(1, ref.shape[0]):
            total = total + ref[j]
        return total

    exchange(t, count, lambda j, at: spread(x_ref.at[j], parts.at[at], send_one, recv_one, at, "tensor", j), keep_one)
    keep_two()
    exchange(g, group_count, lambda j, at: spread(groups.at[g], groups.at[at], send_two, recv_two, at, "dp", j), lambda: None)
    out_ref[t] = sum_of(groups)
    exchange(t, count, lambda j, at: spread(out_ref.at[t], out_ref.at[at], send_three, recv_three, at, "tensor", j), lambda: None)


def total_over_all(x, count, group_count, number):
    rows, width = x.shape
    piece = width // count
    shape = jax.ShapeDtypeStruct((count, rows, piece), x.dtype)
    out = pl.pallas_call(
        total_kernel, out_shape=shape, in_specs=[VM], out_specs=VM,
        scratch_shapes=[
            pltpu.VMEM((count, rows, piece), x.dtype), pltpu.VMEM((group_count, rows, piece), x.dtype),
            pltpu.SemaphoreType.DMA((count,)), pltpu.SemaphoreType.DMA((count,)),
            pltpu.SemaphoreType.DMA((group_count,)), pltpu.SemaphoreType.DMA((group_count,)),
            pltpu.SemaphoreType.DMA((count,)), pltpu.SemaphoreType.DMA((count,)),
        ],
        compiler_params=params(number), cost_estimate=lasting(12), name="total_over_all",
    )(jnp.transpose(x.reshape(rows, count, piece), (1, 0, 2)))
    return jnp.transpose(out, (1, 0, 2)).reshape(rows, width)


def local(
    inputs,
    cotangent,
    lengths,
    positions,
    qkv_master,
    gate_up_master,
    out_master,
    down_master,
    bias_master,
    norm_master,
    qkv_first,
    gate_up_first,
    out_first,
    down_first,
    bias_first,
    norm_first,
    qkv_second,
    gate_up_second,
    out_second,
    down_second,
    bias_second,
    norm_second,
):
    tensor_count = lax.axis_size("tensor")
    local_tokens = inputs.shape[0]
    group_tokens = local_tokens * tensor_count
    row_count = lengths.shape[0]
    row_length = group_tokens // row_count
    block_rows = min(256, row_length)
    heads_here = bias_master.shape[1]
    width_here = heads_here * HEAD_DIM
    own_start = lax.axis_index("tensor") * local_tokens
    chips = tensor_count // 2
    qkv_copy, gate_up_copy, out_copy, down_copy, bias_copy = (
        lax.all_gather(qkv_master.astype(jnp.bfloat16), "dp", axis=1, tiled=True),
        lax.all_gather(gate_up_master.astype(jnp.bfloat16), "dp", axis=1, tiled=True),
        lax.all_gather(out_master.astype(jnp.bfloat16), "dp", axis=1, tiled=True),
        lax.all_gather(down_master.astype(jnp.bfloat16), "dp", axis=1, tiled=True),
        lax.all_gather(bias_master.astype(jnp.bfloat16), "dp", axis=2, tiled=True),
    )
    qkv_flat = jnp.transpose(qkv_copy, (1, 0, 2)).reshape(qkv_copy.shape[1], 3 * width_here)
    inputs_wide = inputs.astype(jnp.float32)
    normed_one = norm_forward(inputs_wide, norm_master[0], norm_master[1]).astype(jnp.bfloat16)
    gathered_one = gather(normed_one, chips, 0).reshape(group_tokens, D)
    projected = jnp.dot(
        gathered_one, qkv_flat, preferred_element_type=jnp.float32
    ) + bias_copy.reshape(1, 3 * width_here).astype(jnp.float32)
    keep, ahead, behind = rotary_tables(positions)
    queries, keys, values, keys_flipped, mixed_low, log_totals = attention_forward(
        lengths, projected, keep, ahead, behind, heads_here, block_rows
    )
    group_index = own_start + jnp.arange(local_tokens, dtype=jnp.int32)
    row_of = group_index // row_length
    slot_of = group_index % row_length
    row_match = row_of[:, None] == jnp.arange(row_count, dtype=jnp.int32)[None, :]
    length_of = jnp.sum(jnp.where(row_match, lengths[None, :], 0), axis=1)
    valid = slot_of < length_of
    grad_low = jnp.where(valid[:, None], cotangent, jnp.zeros_like(cotangent))
    middle, normed_two, gathered_grad = out_branch(mixed_low, out_copy, inputs, norm_master, grad_low, chips, 1)
    gathered_two, hidden, grad_gate_up, grad_middle, grad_middle_low, sums_two = mlp(
        normed_two, gathered_grad, gate_up_copy, down_copy, middle, norm_master, chips, 2
    )
    block_output, gathered_mid, grad_mixed = down_branch(
        hidden, down_copy, middle, grad_middle_low, out_copy, chips, 3
    )
    hidden = hidden.reshape(group_tokens, hidden.shape[2])
    grad_gate_up = grad_gate_up.reshape(2, group_tokens, hidden.shape[1])
    gathered_grad = gathered_grad.reshape(group_tokens, D)
    gathered_two = gathered_two.reshape(group_tokens, D)
    gathered_mid = gathered_mid.reshape(group_tokens, D)
    grad_mixed = grad_mixed.reshape(group_tokens, width_here)
    grad_down = jnp.einsum("tf,td->fd", hidden, gathered_grad, preferred_element_type=jnp.float32)
    grad_gate_up_w = jnp.einsum(
        "td,ctf->cdf", gathered_two, grad_gate_up, preferred_element_type=jnp.float32
    )
    grad_out_w = jnp.einsum(
        "tw,td->wd", mixed_low, gathered_mid, preferred_element_type=jnp.float32
    )
    grad_projected, grad_bias = attention_backward(
        lengths, queries, keys, values, keys_flipped, mixed_low, log_totals, grad_mixed, keep, ahead, behind, block_rows
    )
    grad_bias = grad_bias.reshape(3, heads_here, HEAD_DIM)
    grad_qkv_w = jnp.einsum(
        "td,tcw->cdw",
        gathered_one,
        grad_projected.reshape(group_tokens, 3, width_here),
        preferred_element_type=jnp.float32,
    )
    input_grad, sums_one = first_branch(
        grad_projected, qkv_flat, inputs, grad_middle, norm_master, chips, 4
    )
    norm_grads = total_over_all(
        jnp.concatenate([sums_one, sums_two], axis=0), tensor_count, lax.axis_size("dp"), 5
    )
    qkv_grad, gate_up_grad, out_grad, down_grad, bias_grad = (
        sum_shard(grad_qkv_w, 1),
        sum_shard(grad_gate_up_w, 1),
        sum_shard(grad_out_w, 1),
        sum_shard(grad_down, 1),
        lax.psum_scatter(grad_bias, "dp", scatter_dimension=2, tiled=True),
    )
    qkv_new = adamw(qkv_master, qkv_first, qkv_second, qkv_grad, 2.0 / math.sqrt(D), decay_rate)
    gate_up_new = adamw(
        gate_up_master, gate_up_first, gate_up_second, gate_up_grad, 2.0 / math.sqrt(D), decay_rate
    )
    out_new = adamw(
        out_master, out_first, out_second, out_grad, 16.0 / math.sqrt(HEADS * HEAD_DIM), decay_rate
    )
    down_new = adamw(
        down_master, down_first, down_second, down_grad, 6.0 / math.sqrt(FF), decay_rate
    )
    bias_new = adamw(bias_master, bias_first, bias_second, bias_grad, 1.5, 0.0)
    norm_new = adamw(norm_master, norm_first, norm_second, norm_grads, 0.7, 0.0)
    return (
        block_output,
        input_grad,
        qkv_new[0],
        qkv_new[1],
        qkv_new[2],
        gate_up_new[0],
        gate_up_new[1],
        gate_up_new[2],
        out_new[0],
        out_new[1],
        out_new[2],
        down_new[0],
        down_new[1],
        down_new[2],
        bias_new[0],
        bias_new[1],
        bias_new[2],
        norm_new[0],
        norm_new[1],
        norm_new[2],
    )


def solution(mesh):
    return jax.shard_map(
        local,
        mesh=mesh,
        in_specs=(
            P(("dp", "tensor"), None),
            P(("dp", "tensor"), None),
            P("dp"),
            P("dp"),
            P(None, "dp", "tensor"),
            P(None, "dp", "tensor"),
            P("tensor", "dp"),
            P("tensor", "dp"),
            P(None, "tensor", "dp"),
            P(),
            P(None, "dp", "tensor"),
            P(None, "dp", "tensor"),
            P("tensor", "dp"),
            P("tensor", "dp"),
            P(None, "tensor", "dp"),
            P(),
            P(None, "dp", "tensor"),
            P(None, "dp", "tensor"),
            P("tensor", "dp"),
            P("tensor", "dp"),
            P(None, "tensor", "dp"),
            P(),
        ),
        out_specs=(
            P(("dp", "tensor"), None),
            P(("dp", "tensor"), None),
            P(None, "dp", "tensor"),
            P(None, "dp", "tensor"),
            P(None, "dp", "tensor"),
            P(None, "dp", "tensor"),
            P(None, "dp", "tensor"),
            P(None, "dp", "tensor"),
            P("tensor", "dp"),
            P("tensor", "dp"),
            P("tensor", "dp"),
            P("tensor", "dp"),
            P("tensor", "dp"),
            P("tensor", "dp"),
            P(None, "tensor", "dp"),
            P(None, "tensor", "dp"),
            P(None, "tensor", "dp"),
            P(),
            P(),
            P(),
        ),
        check_vma=False,
    )
```

```python
import functools
import math

import jax
import jax.numpy as jnp
from jax import lax
from jax.experimental import pallas as pl
from jax.experimental.pallas import tpu as pltpu
from jax.sharding import PartitionSpec as P

D = 2048
HEADS = 32
HEAD_DIM = 64
ROTARY = 16
FF = 5632


norm_eps = 1e-05
beta_one = 0.9
beta_two = 0.95
adam_eps = 1e-08
adam_steps = 10
decay_rate = 0.1
rope_base = 10000.0
score_scale = 0.125
mask_fill = -1e30
log2_e = math.log2(math.e)
LANES = 128
VMEM_LIMIT = 62 * 1024 * 1024


def norm_forward(values, gain_row, shift_row):
    average = jnp.mean(values, axis=-1, keepdims=True)
    centred = values - average
    spread = jnp.mean(centred * centred, axis=-1, keepdims=True)
    return centred * lax.rsqrt(spread + norm_eps) * gain_row + shift_row


def norm_backward(values, gain_row, grad_rows):
    average = jnp.mean(values, axis=-1, keepdims=True)
    centred = values - average
    spread = jnp.mean(centred * centred, axis=-1, keepdims=True)
    inverse = lax.rsqrt(spread + norm_eps)
    normal = centred * inverse
    grad_normal = grad_rows * gain_row
    grad_values = inverse * (
        grad_normal
        - jnp.mean(grad_normal, axis=-1, keepdims=True)
        - normal * jnp.mean(grad_normal * normal, axis=-1, keepdims=True)
    )
    return (
        grad_values,
        jnp.sum(grad_rows * normal, axis=0, keepdims=True),
        jnp.sum(grad_rows, axis=0, keepdims=True),
    )


def sum_shard(gradient, dimension):
    return lax.psum_scatter(
        gradient.astype(jnp.bfloat16), "dp", scatter_dimension=dimension, tiled=True
    ).astype(jnp.float32)


def adamw(weight_old, first_old, second_old, gradient, step_rate, decay_part):
    first_new = beta_one * first_old + (1.0 - beta_one) * gradient
    second_new = beta_two * second_old + (1.0 - beta_two) * gradient * gradient
    correct_one = 1.0 - beta_one**adam_steps
    correct_two = 1.0 - beta_two**adam_steps
    update = first_new / correct_one / (jnp.sqrt(second_new / correct_two) + adam_eps)
    return (weight_old - step_rate * (update + decay_part * weight_old), first_new, second_new)


def spin(x, keep, ahead, behind):
    return x * keep + pltpu.roll(x, LANES - ROTARY // 2, 1) * ahead + pltpu.roll(x, ROTARY // 2, 1) * behind


def dot_nt(a, b):
    return lax.dot_general(a, b, (((1,), (1,)), ((), ())), preferred_element_type=jnp.float32)


def dot_nn(a, b):
    return lax.dot_general(a, b, (((1,), (0,)), ((), ())), preferred_element_type=jnp.float32)


def masked_scores(s, key_start, query_start, length, causal):
    key_slots = key_start + lax.broadcasted_iota(jnp.int32, s.shape, 0)
    allowed = key_slots < length
    if causal:
        query_slots = query_start + lax.broadcasted_iota(jnp.int32, s.shape, 1)
        allowed = allowed & (key_slots <= query_slots)
    return jnp.where(allowed, s, mask_fill)


def backward_kernel(block, length_ref, q_ref, k_ref, v_ref, kt_ref, o_ref, lse_ref, do_ref,
                    keep_ref, ahead_ref, behind_ref, out_ref, bias_ref,
                    dos_ref, delta_ref, dqt_ref, dk_ref, dv_ref):
    heads, rows, _ = q_ref.shape
    width = heads * HEAD_DIM
    groups = width // LANES
    per_group = LANES // HEAD_DIM
    blocks = rows // block
    length = length_ref[0]

    def prepare(i, _):
        at = pl.ds(pl.multiple_of(i * block, block), block)
        for g in range(groups):
            lanes = slice(g * LANES, (g + 1) * LANES)
            grad = do_ref[at, lanes]
            for p in range(per_group):
                dos_ref[g * per_group + p, at, :] = grad[:, p * HEAD_DIM:(p + 1) * HEAD_DIM]
            both = (grad.astype(jnp.float32) * o_ref[at, lanes].astype(jnp.float32)).T
            for p in range(per_group):
                h = g * per_group + p
                delta_ref[h:h + 1, at] = jnp.sum(both[p * HEAD_DIM:(p + 1) * HEAD_DIM], axis=0, keepdims=True)
        dqt_ref[:, at] = jnp.zeros((width, block), jnp.float32)
        return 0

    lax.fori_loop(0, blocks, prepare, 0)

    def key_block(j, _):
        key_start = pl.multiple_of(j * block, block)
        keys_at = pl.ds(key_start, block)

        def query_block(i, carry, kind):
            at = pl.ds(pl.multiple_of(i * block, block), block)
            out = []
            for h in range(heads):
                dk, dv = carry[h]
                keys, queries, grad = k_ref[h, keys_at, :], q_ref[h, at, :], dos_ref[h, at, :]
                s = dot_nt(keys, queries) * (score_scale * log2_e)
                if kind > 0:
                    s = masked_scores(s, key_start, i * block, length, kind == 2)
                p = jnp.exp2(s - lse_ref[h:h + 1, at])
                dp = dot_nt(v_ref[h, keys_at, :], grad)
                ds = (p * (dp - delta_ref[h:h + 1, at])).astype(jnp.bfloat16)
                dv = dv + dot_nn(p.astype(jnp.bfloat16), grad)
                dk = dk + dot_nn(ds, queries)
                here = slice(h * HEAD_DIM, (h + 1) * HEAD_DIM)
                dqt_ref[here, at] += dot_nn(kt_ref[here, keys_at], ds)
                out.append((dk, dv))
            return tuple(out)

        zero = jnp.zeros((block, HEAD_DIM), jnp.float32)
        carry = query_block(j, tuple((zero, zero) for _ in range(heads)), 2)
        whole = key_start + block <= length
        carry = lax.fori_loop(j + 1, jnp.where(whole, blocks, j + 1), lambda i, c: query_block(i, c, 0), carry)
        carry = lax.fori_loop(j + 1, jnp.where(whole, j + 1, blocks), lambda i, c: query_block(i, c, 1), carry)
        for h in range(heads):
            dk_ref[h, keys_at, :] = carry[h][0]
            dv_ref[h, keys_at, :] = carry[h][1]
        return 0

    lax.fori_loop(0, blocks, key_block, 0)
    bias_ref[...] = jnp.zeros(bias_ref.shape, jnp.float32)

    def finish(i, _):
        at = pl.ds(pl.multiple_of(i * block, block), block)
        keep, ahead, behind = keep_ref[at, :], -ahead_ref[at, :], -behind_ref[at, :]
        for g in range(groups):
            lanes = slice(g * LANES, (g + 1) * LANES)
            dq = dqt_ref[lanes, at].T
            dk = jnp.concatenate([dk_ref[g * per_group + p, at, :] for p in range(per_group)], axis=1)
            dv = jnp.concatenate([dv_ref[g * per_group + p, at, :] for p in range(per_group)], axis=1)
            parts = (spin(dq * score_scale, keep, ahead, behind), spin(dk * score_scale, keep, ahead, behind), dv)
            for c in range(3):
                low = parts[c].astype(jnp.bfloat16)
                place = slice(c * width + g * LANES, c * width + (g + 1) * LANES)
                out_ref[at, place] = low
                bias_ref[:, place] += jnp.sum(low.astype(jnp.float32), axis=0, keepdims=True)
        return 0

    lax.fori_loop(0, blocks, finish, 0)


def attention_backward(lengths, q, k, v, kt, o, lse, grad, keep, ahead, behind, block):
    heads, rows, _ = q.shape
    width = heads * HEAD_DIM
    vm = pl.BlockSpec(memory_space=pltpu.VMEM)
    return pl.pallas_call(
        functools.partial(backward_kernel, block),
        out_shape=(jax.ShapeDtypeStruct((rows, 3 * width), jnp.bfloat16),
                   jax.ShapeDtypeStruct((1, 3 * width), jnp.float32)),
        in_specs=[pl.BlockSpec(memory_space=pltpu.SMEM)] + [vm] * 10,
        out_specs=(vm,) * 2,
        scratch_shapes=[
            pltpu.VMEM((heads, rows, HEAD_DIM), jnp.bfloat16),
            pltpu.VMEM((heads, rows), jnp.float32),
            pltpu.VMEM((width, rows), jnp.float32),
            pltpu.VMEM((heads, rows, HEAD_DIM), jnp.float32),
            pltpu.VMEM((heads, rows, HEAD_DIM), jnp.float32),
        ],
        compiler_params=pltpu.CompilerParams(vmem_limit_bytes=VMEM_LIMIT),
        cost_estimate=pl.CostEstimate(flops=heads * rows * rows * HEAD_DIM * 20, bytes_accessed=rows * width * 30, transcendentals=heads * rows * rows),
        name="attention_backward",
    )(lengths, q, k, v, kt, o, lse, grad, keep, ahead, behind)


VM = pl.BlockSpec(memory_space=pltpu.VMEM)
MESH = pl.DeviceIdType.MESH


def params(number):
    return pltpu.CompilerParams(collective_id=number, has_side_effects=True, vmem_limit_bytes=VMEM_LIMIT)


def lasting(us):
    return pl.CostEstimate(flops=int(us * 1.1e9), bytes_accessed=0, transcendentals=0)


def place():
    t = lax.axis_index("tensor")
    return t, lax.rem(t, 2), lax.div(t, 2)


def greet(n):
    t, core, chip = place()
    barrier = pltpu.get_barrier_semaphore()

    def hail(index):
        pl.semaphore_signal(barrier, inc=1, device_id={"tensor": index}, device_id_type=MESH)

    hail(t + 1 - 2 * core)
    pl.when(chip > 0)(lambda: hail(t - 2))
    pl.when(chip < n - 1)(lambda: hail(t + 2))
    pl.semaphore_wait(barrier, 1 + jnp.minimum(chip, 1) + jnp.minimum(n - 1 - chip, 1))


def near(j, m, n):
    below, above = m, n - 1 - m
    both = jnp.minimum(below, above)
    half = lax.div(j + 1, 2)
    inside = m + jnp.where(lax.rem(j, 2) == 1, -half, half)
    outside = m + jnp.where(above > below, j - both, both - j)
    return jnp.where(j <= 2 * both, inside, outside)


class Gather:
    def __init__(self, n, own, buf, sems, pieces):
        self.n, self.own, self.buf, self.pieces = n, own, buf, pieces
        self.up, self.down, self.side, self.line_in, self.side_in = [sems.at[i] for i in range(5)]
        self.t, self.core, self.m = place()
        self.sibling = self.t + 1 - 2 * self.core
        self.rows = own.shape[0] // pieces

    def copy(self, src, k, p, core, send, recv, target):
        at = pl.ds(pl.multiple_of(p * self.rows, self.rows), self.rows)
        index = k * self.pieces + p
        return pltpu.make_async_remote_copy(
            src_ref=src.at[at], dst_ref=self.buf.at[2 * k + core, at], send_sem=send.at[index],
            recv_sem=recv.at[index], device_id={"tensor": target}, device_id_type=MESH)

    def to_up(self, k, p, src):
        return self.copy(src, k, p, self.core, self.up, self.line_in, self.t + 2)

    def to_down(self, k, p, src):
        return self.copy(src, k, p, self.core, self.down, self.line_in, self.t - 2)

    def to_side(self, k, p, src):
        return self.copy(src, k, p, self.core, self.side, self.side_in, self.sibling)

    def start(self):
        m = self.m
        for p in range(self.pieces):
            pl.when(m < self.n - 1)(lambda: self.to_up(m, p, self.own).start())
            pl.when(m > 0)(lambda: self.to_down(m, p, self.own).start())
            self.to_side(m, p, self.own).start()

    def arrive(self, d, only=None):
        m = self.m
        lo, hi = m - d, m + d
        for p in range(self.pieces) if only is None else (only,):
            @pl.when(lo >= 0)
            def _():
                src = self.buf.at[2 * lo + self.core]
                self.to_up(lo, p, src).wait_recv()
                pl.when(m < self.n - 1)(lambda: self.to_up(lo, p, src).start())
                self.to_side(lo, p, src).start()

            @pl.when(hi < self.n)
            def _():
                src = self.buf.at[2 * hi + self.core]
                self.to_down(hi, p, src).wait_recv()
                pl.when(m > 0)(lambda: self.to_down(hi, p, src).start())
                self.to_side(hi, p, src).start()

    def side_wait(self, k):
        for p in range(self.pieces):
            self.copy(self.own, k, p, 1 - self.core, self.side, self.side_in, self.sibling).wait_recv()

    def finish(self):
        m = self.m

        def one(k, _):
            for p in range(self.pieces):
                pl.when((k <= m) & (m < self.n - 1))(lambda: self.to_up(k, p, self.own).wait_send())
                pl.when((k >= m) & (m > 0))(lambda: self.to_down(k, p, self.own).wait_send())
                self.to_side(k, p, self.own).wait_send()
            return 0

        lax.fori_loop(0, self.n, one, 0)


class Scatter:
    def __init__(self, n, pieces, side_out, side_in, line_in, side_sems, line_send, line_recv):
        self.n, self.pieces = n, pieces
        self.side_out, self.side_in, self.line_in = side_out, side_in, line_in
        self.side_send, self.side_recv = side_sems.at[0], side_sems.at[1]
        self.line_send, self.line_recv = line_send, line_recv
        self.t, self.core, self.m = place()
        self.sibling = self.t + 1 - 2 * self.core
        self.rows = side_out.shape[1] // pieces
        self.step = min(32, self.rows)

    def side(self, k):
        return pltpu.make_async_remote_copy(
            src_ref=self.side_out.at[k], dst_ref=self.side_in.at[k], send_sem=self.side_send.at[k],
            recv_sem=self.side_recv.at[k], device_id={"tensor": self.sibling}, device_id_type=MESH)

    def line(self, k, p, slot, target):
        at = pl.ds(pl.multiple_of(p * self.rows, self.rows), self.rows)
        return pltpu.make_async_remote_copy(
            src_ref=self.side_in.at[k, at], dst_ref=self.line_in.at[slot, at],
            send_sem=self.line_send.at[k * self.pieces + p], recv_sem=self.line_recv.at[slot * self.pieces + p],
            device_id={"tensor": target}, device_id_type=MESH)

    def each(self, p, body):
        def one(i, _):
            body(pl.ds(pl.multiple_of(p * self.rows + i * self.step, self.step), self.step))
            return 0

        lax.fori_loop(0, self.rows // self.step, one, 0)

    def pass_on(self, k, own, between=None):
        m, n = self.m, self.n
        self.side(k).wait_recv()
        inner = ((k > m) & (m > 0)) | ((k < m) & (m < n - 1))

        def one(p, _):
            @pl.when(inner)
            def _():
                self.line(k, p, k, self.t).wait_recv()

                def add(at):
                    total = own[at, :] + self.side_in[k, at, :].astype(jnp.float32) + self.line_in[k, at, :].astype(jnp.float32)
                    self.side_in[k, at, :] = total.astype(jnp.bfloat16)

                self.each(p, add)

            @pl.when(jnp.logical_not(inner))
            def _():
                def add(at):
                    self.side_in[k, at, :] = (own[at, :] + self.side_in[k, at, :].astype(jnp.float32)).astype(jnp.bfloat16)

                self.each(p, add)

            pl.when(k > m)(lambda: self.line(k, p, k, self.t + 2).start())
            pl.when(k < m)(lambda: self.line(k, p, jnp.where(k == m - 1, n, k), self.t - 2).start())
            if between is not None:
                between(p)
            return 0

        lax.fori_loop(0, self.pieces, one, 0)

    def settle(self, own, consume):
        m, n = self.m, self.n
        self.side(m).wait_recv()

        def one(p, _):
            def first(at):
                own[at, :] += self.side_in[m, at, :].astype(jnp.float32)

            self.each(p, first)

            def more(slot):
                self.line(m, p, slot, self.t).wait_recv()

                def add(at):
                    own[at, :] += self.line_in[slot, at, :].astype(jnp.float32)

                self.each(p, add)

            pl.when(m > 0)(lambda: more(m))
            pl.when(m < n - 1)(lambda: more(n))
            self.each(p, lambda at: consume(at, own[at, :]))
            return 0

        lax.fori_loop(0, self.pieces, one, 0)

    def finish(self):
        def one(k, _):
            self.side(k).wait_send()

            @pl.when(k != self.m)
            def _():
                for p in range(self.pieces):
                    self.line(k, p, k, self.t).wait_send()

            return 0

        lax.fori_loop(0, self.n, one, 0)


def scatter_scratch(n, pieces, rows, width):
    return [
        pltpu.VMEM((n, rows, width), jnp.bfloat16), pltpu.VMEM((n, rows, width), jnp.bfloat16),
        pltpu.VMEM((n + 1, rows, width), jnp.bfloat16),
        pltpu.SemaphoreType.DMA((2, n)), pltpu.SemaphoreType.DMA((n * pieces,)), pltpu.SemaphoreType.DMA(((n + 1) * pieces,)),
    ]


def greet_all(n, group_count):
    t, core, chip = place()
    g = lax.axis_index("dp")
    barrier = pltpu.get_barrier_semaphore()

    def hail(index):
        pl.semaphore_signal(barrier, inc=1, device_id={"tensor": index}, device_id_type=MESH)

    hail(t + 1 - 2 * core)
    pl.when(chip > 0)(lambda: hail(t - 2))
    pl.when(chip < n - 1)(lambda: hail(t + 2))
    for i in range(group_count):
        pl.when(i != g)(lambda: pl.semaphore_signal(barrier, inc=1, device_id={"dp": i}, device_id_type=MESH))
    pl.semaphore_wait(barrier, group_count + jnp.minimum(chip, 1) + jnp.minimum(n - 1 - chip, 1))


def forward_kernel(n, group_count, pieces, length_ref, place_ref, frequency_ref, x_ref, norm_ref, qkv_ref, out_ref, bias_ref, cot_ref,
                   xs_ref, wq_ref, wo_ref, q_ref, k_ref, v_ref, kt_ref, mixed_ref, lse_ref, keep_ref, ahead_ref, behind_ref,
                   middle_ref, normed_ref, cots_ref,
                   vt_ref, biases_ref, acc_ref, side_out, side_in, line_in, side_sems, line_send, line_recv,
                   first_sems, cot_sems, share_send, share_recv):
    greet_all(n, group_count)
    heads, total_rows, _ = q_ref.shape
    rows, features = x_ref.shape
    width = heads * HEAD_DIM
    lane_groups = width // LANES
    per_group = LANES // HEAD_DIM
    block = rows
    length = length_ref[0]
    group = lax.axis_index("dp")
    t, core, m = place()
    first = Gather(n, xs_ref.at[t], xs_ref, first_sems, pieces)
    cots = Gather(n, cot_ref, cots_ref, cot_sems, pieces)
    s = Scatter(n, pieces, side_out, side_in, line_in, side_sems, line_send, line_recv)
    step = 32

    def first_norm(i, _):
        at = pl.ds(pl.multiple_of(i * step, step), step)
        xs_ref[t, at, :] = norm_forward(x_ref[at, :].astype(jnp.float32), norm_ref[0:1, :], norm_ref[1:2, :]).astype(jnp.bfloat16)
        return 0

    lax.fori_loop(0, rows // step, first_norm, 0)
    first.start()
    depth = features // group_count
    mine = pl.ds(pl.multiple_of(group * depth, depth), depth)
    for c in range(3):
        wq_ref[c, mine, :] = qkv_ref[c].astype(jnp.bfloat16)
    wo_ref[:, mine] = out_ref[...].astype(jnp.bfloat16)
    biases_ref[group] = bias_ref[...].astype(jnp.bfloat16).astype(jnp.float32)

    def share(kind, src, owner, peer):
        ref = src(owner)
        return pltpu.make_async_remote_copy(
            src_ref=ref, dst_ref=ref, send_sem=share_send.at[kind, peer], recv_sem=share_recv.at[kind, owner],
            device_id={"dp": peer}, device_id_type=MESH)

    def part(owner):
        return pl.ds(pl.multiple_of(owner * depth, depth), depth)

    kinds = (lambda o: wq_ref.at[:, part(o), :], lambda o: biases_ref.at[o], lambda o: wo_ref.at[:, part(o)])
    for kind in range(3):
        for i in range(group_count):
            pl.when(i != group)(lambda: share(kind, kinds[kind], group, i).start())

    def tables(i, _):
        at = pl.ds(pl.multiple_of(i * block, block), block)
        angles = jnp.broadcast_to(place_ref[:, at], (LANES, block)).T * frequency_ref[...]
        cosine, sine = jnp.cos(angles), jnp.sin(angles)
        dim = lax.rem(lax.broadcasted_iota(jnp.int32, (block, LANES), 1), HEAD_DIM)
        none = jnp.zeros((block, LANES), jnp.float32)
        keep_ref[at, :] = jnp.where(dim < ROTARY, cosine, 1.0)
        ahead_ref[at, :] = jnp.where(dim < ROTARY // 2, -sine, none)
        behind_ref[at, :] = jnp.where((dim >= ROTARY // 2) & (dim < ROTARY), sine, none)
        return 0

    lax.fori_loop(0, total_rows // block, tables, 0)
    def project(slot):
        at = pl.ds(pl.multiple_of(slot * block, block), block)
        keep, ahead, behind = keep_ref[at, :], ahead_ref[at, :], behind_ref[at, :]
        x = xs_ref[slot]
        for c in range(3):
            wide = dot_nn(x, wq_ref[c]) + biases_ref[group_count, c:c + 1, :]
            for a in range(lane_groups):
                lanes = slice(a * LANES, (a + 1) * LANES)
                part_wide = wide[:, lanes]
                if c < 2:
                    part_wide = spin(part_wide, keep, ahead, behind)
                if c == 1:
                    kt_ref[lanes, at] = part_wide.T.astype(jnp.bfloat16)
                if c == 2:
                    vt_ref[lanes, at] = part_wide.T.astype(jnp.bfloat16)
                for b in range(per_group):
                    (q_ref, k_ref, v_ref)[c][a * per_group + b, at, :] = part_wide[:, b * HEAD_DIM:(b + 1) * HEAD_DIM].astype(jnp.bfloat16)

    def ring(d, _):
        def one(q, _):
            other, above = lax.div(q, 2), lax.rem(q, 2)
            k = jnp.where(above == 1, m + d, m - d)

            @pl.when((k >= 0) & (k < n) & ((d > 0) | (above == 0)))
            def _():
                pl.when(other == 1)(lambda: first.side_wait(k))
                project(2 * k + jnp.where(other == 1, 1 - core, core))

            return 0

        lax.fori_loop(0, 4, one, 0)
        pl.when(d == n - 2)(lambda: first.arrive(n - 1))
        return 0

    for d in range(1, n - 1):
        first.arrive(d)
    for kind in range(3):
        for i in range(group_count):
            pl.when(i != group)(lambda: share(kind, kinds[kind], i, i).wait_recv())
    bias = biases_ref[0]
    for i in range(1, group_count):
        bias = bias + biases_ref[i]
    biases_ref[group_count] = bias

    lax.fori_loop(0, n, ring, 0)
    cots.start()
    cots_ref[t] = cot_ref[...]
    pair = 2 * block

    def attend(i):
        at = pl.ds(pl.multiple_of(i * pair, pair), pair)
        queries = [q_ref[h, at, :] for h in range(heads)]

        def key_block(j, carry, kind):
            key_start = pl.multiple_of(j * pair, pair)
            keys_at = pl.ds(key_start, pair)
            out = []
            for h in range(heads):
                top, total, mixed = carry[h]
                scores = dot_nt(k_ref[h, keys_at, :], queries[h]) * (score_scale * log2_e)
                if kind > 0:
                    scores = masked_scores(scores, key_start, i * pair, length, kind == 2)
                new_top = jnp.maximum(top, jnp.max(scores, axis=0, keepdims=True))
                shrink = jnp.exp2(top - new_top)
                p = jnp.exp2(scores - new_top)
                total = total * shrink + jnp.sum(p, axis=0, keepdims=True)
                mixed = mixed * shrink + dot_nn(
                    vt_ref[h * HEAD_DIM:(h + 1) * HEAD_DIM, keys_at], p.astype(jnp.bfloat16))
                out.append((new_top, total, mixed))
            return tuple(out)

        start = tuple(
            (jnp.full((1, pair), mask_fill, jnp.float32), jnp.zeros((1, pair), jnp.float32),
             jnp.zeros((HEAD_DIM, pair), jnp.float32)) for _ in range(heads))
        carry = lax.fori_loop(0, i, lambda j, c: key_block(j, c, 1), start)
        carry = key_block(i, carry, 2)
        for h in range(heads):
            top, total, mixed = carry[h]
            lse_ref[h:h + 1, at] = top + jnp.log2(total)
        for a in range(lane_groups):
            both = [carry[a * per_group + b][2] * (1.0 / carry[a * per_group + b][1]) for b in range(per_group)]
            mixed_ref[at, a * LANES:(a + 1) * LANES] = jnp.concatenate(both, axis=0).T.astype(jnp.bfloat16)

    cut = min(512, features)

    def branch(j, _):
        k = near(n - 1 - j, m, n)

        attend(k)

        def attended(slot):
            return mixed_ref[pl.ds(pl.multiple_of(slot * block, block), block), :]

        low = attended(2 * k + 1 - core)
        for a in range(0, features, cut):
            s.side_out[k, :, a:a + cut] = dot_nn(low, wo_ref[:, a:a + cut]).astype(jnp.bfloat16)
        s.side(k).start()
        low = attended(2 * k + core)
        for a in range(0, features, cut):
            acc_ref[:, a:a + cut] = dot_nn(low, wo_ref[:, a:a + cut])
        pl.when(j < n - 1)(lambda: s.pass_on(k, acc_ref, lambda p: cots.arrive(j + 1, p)))
        return 0

    lax.fori_loop(0, n, branch, 0)

    def consume(at, total):
        middle = x_ref[at, :].astype(jnp.float32) + total
        middle_ref[at, :] = middle
        normed_ref[at, :] = norm_forward(middle, norm_ref[2:3, :], norm_ref[3:4, :]).astype(jnp.bfloat16)

    s.settle(acc_ref, consume)
    for k in range(n):
        cots.side_wait(k)
    first.finish()
    cots.finish()
    s.finish()
    for kind in range(3):
        for i in range(group_count):
            pl.when(i != group)(lambda: share(kind, kinds[kind], group, i).wait_send())


def forward(lengths, positions, x, norms, qkv, out, bias, cot, n, group_count, number, pieces=4):
    rows, features = x.shape
    width = qkv.shape[2]
    heads = width // HEAD_DIM
    total_rows = 2 * n * rows
    f32, low = jnp.float32, jnp.bfloat16
    shape = jax.ShapeDtypeStruct
    half_rot = ROTARY // 2
    frequency = rope_base ** (-(2.0 * jnp.arange(half_rot, dtype=jnp.float32)) / ROTARY)
    split = shape((heads, total_rows, HEAD_DIM), low)
    table = shape((total_rows, LANES), f32)
    gathered = shape((2 * n, rows, features), low)
    return pl.pallas_call(
        functools.partial(forward_kernel, n, group_count, pieces),
        out_shape=(gathered, shape((3, features, width), low), shape((width, features), low), split, split, split,
                   shape((width, total_rows), low), shape((total_rows, width), low), shape((heads, total_rows), f32),
                   table, table, table, shape((rows, features), f32), shape((rows, features), low), gathered),
        in_specs=[pl.BlockSpec(memory_space=pltpu.SMEM)] + [VM] * 8, out_specs=(VM,) * 15,
        scratch_shapes=[
            pltpu.VMEM((width, total_rows), low), pltpu.VMEM((group_count + 1, 8, width), f32), pltpu.VMEM((rows, features), f32),
        ] + scatter_scratch(n, pieces, rows, features) + [
            pltpu.SemaphoreType.DMA((5, n * pieces)), pltpu.SemaphoreType.DMA((5, n * pieces)),
            pltpu.SemaphoreType.DMA((3, group_count)), pltpu.SemaphoreType.DMA((3, group_count)),
        ],
        compiler_params=params(number), cost_estimate=lasting(200), name="forward",
    )(lengths, positions.astype(f32).reshape(1, total_rows), jnp.tile(frequency, LANES // half_rot).reshape(1, LANES),
      x, norms, qkv, out, bias, cot)


def mlp_kernel(n, pieces, x_ref, cots_ref, gate_up_ref, down_ref, middle_ref, norm_ref,
               xs_ref, hidden_ref, grads_ref, grad_middle_ref, low_ref, sums_ref,
               acc_ref, side_out, side_in, line_in, side_sems, line_send, line_recv, gather_sems):
    greet(n)
    g = Gather(n, x_ref, xs_ref, gather_sems, pieces)
    s = Scatter(n, pieces, side_out, side_in, line_in, side_sems, line_send, line_recv)
    g.start()
    xs_ref[g.t] = x_ref[...]
    m, core = s.m, s.core

    def work(slot):
        x = xs_ref[slot]
        gate = dot_nn(x, gate_up_ref[0])
        up = dot_nn(x, gate_up_ref[1])
        grad_hidden = dot_nt(cots_ref[slot], down_ref[...])
        sig = 1.0 / (1.0 + jnp.exp(-gate))
        silu = gate * sig
        hidden_ref[slot] = (silu * up).astype(jnp.bfloat16)
        grads_ref[0, slot] = (grad_hidden * up * (sig * (1.0 + gate * (1.0 - sig)))).astype(jnp.bfloat16)
        grads_ref[1, slot] = (grad_hidden * silu).astype(jnp.bfloat16)

    def ring(d, _):
        pl.when(d > 0)(lambda: g.arrive(d))

        def one(q, _):
            other, above = lax.div(q, 2), lax.rem(q, 2)
            k = jnp.where(above == 1, m + d, m - d)

            @pl.when((k >= 0) & (k < n) & ((d > 0) | (above == 0)))
            def _():
                pl.when(other == 1)(lambda: g.side_wait(k))
                work(2 * k + jnp.where(other == 1, 1 - core, core))

            return 0

        lax.fori_loop(0, 4, one, 0)
        return 0

    lax.fori_loop(0, n, ring, 0)
    width = x_ref.shape[1]
    cut = min(512, width)

    def one(j, _):
        k = near(n - 1 - j, m, n)

        def partial(slot, a):
            return dot_nt(grads_ref[0, slot], gate_up_ref[0, a:a + cut, :]) + dot_nt(grads_ref[1, slot], gate_up_ref[1, a:a + cut, :])

        for a in range(0, width, cut):
            s.side_out[k, :, a:a + cut] = partial(2 * k + 1 - core, a).astype(jnp.bfloat16)
        s.side(k).start()
        for a in range(0, width, cut):
            acc_ref[:, a:a + cut] = partial(2 * k + core, a)
        pl.when(j < n - 1)(lambda: s.pass_on(k, acc_ref))
        return 0

    lax.fori_loop(0, n, one, 0)
    sums_ref[...] = jnp.zeros(sums_ref.shape, jnp.float32)

    def consume(at, total):
        back, gain, shift = norm_backward(middle_ref[at, :], norm_ref[2:3, :], total)
        result = cots_ref[s.t, at, :].astype(jnp.float32) + back
        grad_middle_ref[at, :] = result
        low_ref[at, :] = result.astype(jnp.bfloat16)
        sums_ref[0:1, :] += gain
        sums_ref[1:2, :] += shift

    s.settle(acc_ref, consume)
    g.finish()
    s.finish()


def mlp(x, cots, gate_up, down, middle, norms, n, number, pieces=4):
    rows, width = x.shape
    hidden = down.shape[0]
    f32, low = jnp.float32, jnp.bfloat16
    return pl.pallas_call(functools.partial(mlp_kernel, n, pieces),
        out_shape=(jax.ShapeDtypeStruct((2 * n, rows, width), low), jax.ShapeDtypeStruct((2 * n, rows, hidden), low),
                   jax.ShapeDtypeStruct((2, 2 * n, rows, hidden), low), jax.ShapeDtypeStruct((rows, width), f32),
                   jax.ShapeDtypeStruct((rows, width), low), jax.ShapeDtypeStruct((2, width), f32)),
        in_specs=[VM] * 6, out_specs=(VM,) * 6,
        scratch_shapes=[pltpu.VMEM((rows, width), f32)] + scatter_scratch(n, pieces, rows, width) + [pltpu.SemaphoreType.DMA((5, n * pieces))],
        compiler_params=params(number), cost_estimate=lasting(165), name="mlp")(x, cots, gate_up, down, middle, norms)


def down_kernel(n, pieces, hidden_ref, down_ref, middle_ref, x_ref, out_ref, block_ref, xs_ref, back_ref,
                acc_ref, side_out, side_in, line_in, side_sems, line_send, line_recv, gather_sems):
    greet(n)
    g = Gather(n, x_ref, xs_ref, gather_sems, pieces)
    s = Scatter(n, pieces, side_out, side_in, line_in, side_sems, line_send, line_recv)
    g.start()
    xs_ref[g.t] = x_ref[...]
    m, core = s.m, s.core
    width = down_ref.shape[1]
    cut = min(512, width)

    def one(j, _):
        k = near(n - 1 - j, m, n)
        for a in range(0, width, cut):
            s.side_out[k, :, a:a + cut] = dot_nn(hidden_ref[2 * k + 1 - core], down_ref[:, a:a + cut]).astype(jnp.bfloat16)
        s.side(k).start()
        for a in range(0, width, cut):
            acc_ref[:, a:a + cut] = dot_nn(hidden_ref[2 * k + core], down_ref[:, a:a + cut])
        pl.when(j < n - 1)(lambda: s.pass_on(k, acc_ref, lambda p: g.arrive(j + 1, p)))
        return 0

    lax.fori_loop(0, n, one, 0)

    def consume(at, total):
        block_ref[at, :] = (middle_ref[at, :] + total).astype(jnp.bfloat16)

    s.settle(acc_ref, consume)

    def last(k, _):
        g.side_wait(k)
        for c in range(2):
            back_ref[2 * k + c] = dot_nt(xs_ref[2 * k + c], out_ref[...]).astype(jnp.bfloat16)
        return 0

    lax.fori_loop(0, n, last, 0)
    g.finish()
    s.finish()


def down_branch(hidden, down, middle, x, out, n, number, pieces=4):
    rows, width = x.shape
    f32, low = jnp.float32, jnp.bfloat16
    return pl.pallas_call(functools.partial(down_kernel, n, pieces),
        out_shape=(jax.ShapeDtypeStruct((rows, width), low), jax.ShapeDtypeStruct((2 * n, rows, width), low),
                   jax.ShapeDtypeStruct((2 * n, rows, out.shape[0]), low)),
        in_specs=[VM] * 5, out_specs=(VM,) * 3,
        scratch_shapes=[pltpu.VMEM((rows, width), f32)] + scatter_scratch(n, pieces, rows, width) + [pltpu.SemaphoreType.DMA((5, n * pieces))],
        compiler_params=params(number), cost_estimate=lasting(115), name="down_branch")(hidden, down, middle, x, out)


def first_kernel(n, pieces, grad_ref, w_ref, x_ref, middle_ref, norm_ref, result_ref, sums_ref,
                 acc_ref, side_out, side_in, line_in, side_sems, line_send, line_recv):
    greet(n)
    s = Scatter(n, pieces, side_out, side_in, line_in, side_sems, line_send, line_recv)
    m, core = s.m, s.core
    width = w_ref.shape[1]
    part = w_ref.shape[2]
    cut = min(512, width)

    def one(j, _):
        k = near(n - 1 - j, m, n)

        def partial(slot, a):
            return sum(dot_nt(grad_ref[slot, :, c * part:(c + 1) * part], w_ref[c, a:a + cut, :]) for c in range(3))

        for a in range(0, width, cut):
            s.side_out[k, :, a:a + cut] = partial(2 * k + 1 - core, a).astype(jnp.bfloat16)
        s.side(k).start()
        for a in range(0, width, cut):
            acc_ref[:, a:a + cut] = partial(2 * k + core, a)
        pl.when(j < n - 1)(lambda: s.pass_on(k, acc_ref))
        return 0

    lax.fori_loop(0, n, one, 0)
    sums_ref[...] = jnp.zeros(sums_ref.shape, jnp.float32)

    def consume(at, total):
        back, gain, shift = norm_backward(x_ref[at, :].astype(jnp.float32), norm_ref[0:1, :], total)
        result_ref[at, :] = middle_ref[at, :] + back
        sums_ref[0:1, :] += gain
        sums_ref[1:2, :] += shift

    s.settle(acc_ref, consume)
    s.finish()


def first_branch(grad, w, x, grad_middle, norms, n, number, pieces=4):
    rows, width = x.shape
    f32 = jnp.float32
    return pl.pallas_call(functools.partial(first_kernel, n, pieces),
        out_shape=(jax.ShapeDtypeStruct((rows, width), f32), jax.ShapeDtypeStruct((2, width), f32)),
        in_specs=[VM] * 5, out_specs=(VM,) * 2,
        scratch_shapes=[pltpu.VMEM((rows, width), f32)] + scatter_scratch(n, pieces, rows, width),
        compiler_params=params(number), cost_estimate=lasting(85), name="first_branch")(grad.reshape(2 * n, rows, grad.shape[1]), w, x, grad_middle, norms)


def total_kernel(x_ref, out_ref, parts, groups, send_one, recv_one, send_two, recv_two, send_three, recv_three):
    t, g = lax.axis_index("tensor"), lax.axis_index("dp")
    count, group_count = parts.shape[0], groups.shape[0]
    barrier = pltpu.get_barrier_semaphore()
    for j in range(count):
        pl.when(j != t)(lambda: pl.semaphore_signal(barrier, inc=1, device_id={"tensor": j}, device_id_type=MESH))
    for i in range(group_count):
        pl.when(i != g)(lambda: pl.semaphore_signal(barrier, inc=1, device_id={"dp": i}, device_id_type=MESH))
    pl.semaphore_wait(barrier, count + group_count - 2)

    def spread(src, dst, send, recv, at, axis, peer):
        return pltpu.make_async_remote_copy(
            src_ref=src, dst_ref=dst, send_sem=send.at[peer], recv_sem=recv.at[at], device_id={axis: peer}, device_id_type=MESH)

    def exchange(me, size, make, stay):
        for j in range(size):
            pl.when(j != me)(lambda: make(j, me).start())
        stay()
        for j in range(size):
            pl.when(j != me)(lambda: make(j, j).wait_recv())
        for j in range(size):
            pl.when(j != me)(lambda: make(j, me).wait_send())

    def keep_one():
        parts[t] = x_ref[t]

    def keep_two():
        groups[g] = sum_of(parts)

    def sum_of(ref):
        total = ref[0]
        for j in range(1, ref.shape[0]):
            total = total + ref[j]
        return total

    exchange(t, count, lambda j, at: spread(x_ref.at[j], parts.at[at], send_one, recv_one, at, "tensor", j), keep_one)
    keep_two()
    exchange(g, group_count, lambda j, at: spread(groups.at[g], groups.at[at], send_two, recv_two, at, "dp", j), lambda: None)
    out_ref[t] = sum_of(groups)
    exchange(t, count, lambda j, at: spread(out_ref.at[t], out_ref.at[at], send_three, recv_three, at, "tensor", j), lambda: None)


def total_over_all(x, count, group_count, number):
    rows, width = x.shape
    piece = width // count
    shape = jax.ShapeDtypeStruct((count, rows, piece), x.dtype)
    out = pl.pallas_call(
        total_kernel, out_shape=shape, in_specs=[VM], out_specs=VM,
        scratch_shapes=[
            pltpu.VMEM((count, rows, piece), x.dtype), pltpu.VMEM((group_count, rows, piece), x.dtype),
            pltpu.SemaphoreType.DMA((count,)), pltpu.SemaphoreType.DMA((count,)),
            pltpu.SemaphoreType.DMA((group_count,)), pltpu.SemaphoreType.DMA((group_count,)),
            pltpu.SemaphoreType.DMA((count,)), pltpu.SemaphoreType.DMA((count,)),
        ],
        compiler_params=params(number), cost_estimate=lasting(12), name="total_over_all",
    )(jnp.transpose(x.reshape(rows, count, piece), (1, 0, 2)))
    return jnp.transpose(out, (1, 0, 2)).reshape(rows, width)


def local(
    inputs,
    cotangent,
    lengths,
    positions,
    qkv_master,
    gate_up_master,
    out_master,
    down_master,
    bias_master,
    norm_master,
    qkv_first,
    gate_up_first,
    out_first,
    down_first,
    bias_first,
    norm_first,
    qkv_second,
    gate_up_second,
    out_second,
    down_second,
    bias_second,
    norm_second,
):
    tensor_count = lax.axis_size("tensor")
    local_tokens = inputs.shape[0]
    group_tokens = local_tokens * tensor_count
    row_count = lengths.shape[0]
    row_length = group_tokens // row_count
    block_rows = min(512, row_length)
    heads_here = bias_master.shape[1]
    width_here = heads_here * HEAD_DIM
    own_start = lax.axis_index("tensor") * local_tokens
    chips = tensor_count // 2
    gate_up_copy, down_copy = (
        lax.all_gather(gate_up_master.astype(jnp.bfloat16), "dp", axis=1, tiled=True),
        lax.all_gather(down_master.astype(jnp.bfloat16), "dp", axis=1, tiled=True),
    )
    group = lax.axis_index("dp")
    group_count = lax.axis_size("dp")
    group_index = own_start + jnp.arange(local_tokens, dtype=jnp.int32)
    row_of = group_index // row_length
    slot_of = group_index % row_length
    row_match = row_of[:, None] == jnp.arange(row_count, dtype=jnp.int32)[None, :]
    length_of = jnp.sum(jnp.where(row_match, lengths[None, :], 0), axis=1)
    valid = slot_of < length_of
    grad_low = jnp.where(valid[:, None], cotangent, jnp.zeros_like(cotangent))
    own_dims = jnp.arange(HEAD_DIM) // (HEAD_DIM // group_count) == group
    bias_row = jnp.where(own_dims, jnp.tile(bias_master, (1, 1, group_count)), 0.0).reshape(3, width_here)
    bias_row = jnp.concatenate([bias_row, jnp.zeros((5, width_here), jnp.float32)], axis=0)
    (
        gathered_one, qkv_copy, out_copy, queries, keys, values, keys_flipped, mixed_low, log_totals,
        keep, ahead, behind, middle, normed_two, gathered_grad,
    ) = forward(
        lengths, positions, inputs, norm_master, qkv_master, out_master, bias_row, grad_low, chips, group_count, 0
    )
    gathered_one = gathered_one.reshape(group_tokens, D)
    gathered_two, hidden, grad_gate_up, grad_middle, grad_middle_low, sums_two = mlp(
        normed_two, gathered_grad, gate_up_copy, down_copy, middle, norm_master, chips, 2
    )
    block_output, gathered_mid, grad_mixed = down_branch(
        hidden, down_copy, middle, grad_middle_low, out_copy, chips, 3
    )
    hidden = hidden.reshape(group_tokens, hidden.shape[2])
    grad_gate_up = grad_gate_up.reshape(2, group_tokens, hidden.shape[1])
    gathered_grad = gathered_grad.reshape(group_tokens, D)
    gathered_two = gathered_two.reshape(group_tokens, D)
    gathered_mid = gathered_mid.reshape(group_tokens, D)
    grad_mixed = grad_mixed.reshape(group_tokens, width_here)
    grad_down = jnp.einsum("tf,td->fd", hidden, gathered_grad, preferred_element_type=jnp.float32)
    grad_gate_up_w = jnp.einsum(
        "td,ctf->cdf", gathered_two, grad_gate_up, preferred_element_type=jnp.float32
    )
    grad_out_w = jnp.einsum(
        "tw,td->wd", mixed_low, gathered_mid, preferred_element_type=jnp.float32
    )
    grad_projected, grad_bias = attention_backward(
        lengths, queries, keys, values, keys_flipped, mixed_low, log_totals, grad_mixed, keep, ahead, behind, block_rows
    )
    grad_bias = grad_bias.reshape(3, heads_here, HEAD_DIM)
    grad_qkv_w = jnp.einsum(
        "td,tcw->cdw",
        gathered_one,
        grad_projected.reshape(group_tokens, 3, width_here),
        preferred_element_type=jnp.float32,
    )
    input_grad, sums_one = first_branch(
        grad_projected, qkv_copy, inputs, grad_middle, norm_master, chips, 4
    )
    norm_grads = total_over_all(
        jnp.concatenate([sums_one, sums_two], axis=0), tensor_count, group_count, 5
    )
    qkv_grad, gate_up_grad, out_grad, down_grad, bias_grad = (
        sum_shard(grad_qkv_w, 1),
        sum_shard(grad_gate_up_w, 1),
        sum_shard(grad_out_w, 1),
        sum_shard(grad_down, 1),
        lax.psum_scatter(grad_bias, "dp", scatter_dimension=2, tiled=True),
    )
    qkv_new = adamw(qkv_master, qkv_first, qkv_second, qkv_grad, 2.0 / math.sqrt(D), decay_rate)
    gate_up_new = adamw(
        gate_up_master, gate_up_first, gate_up_second, gate_up_grad, 2.0 / math.sqrt(D), decay_rate
    )
    out_new = adamw(
        out_master, out_first, out_second, out_grad, 16.0 / math.sqrt(HEADS * HEAD_DIM), decay_rate
    )
    down_new = adamw(
        down_master, down_first, down_second, down_grad, 6.0 / math.sqrt(FF), decay_rate
    )
    bias_new = adamw(bias_master, bias_first, bias_second, bias_grad, 1.5, 0.0)
    norm_new = adamw(norm_master, norm_first, norm_second, norm_grads, 0.7, 0.0)
    return (
        block_output,
        input_grad,
        qkv_new[0],
        qkv_new[1],
        qkv_new[2],
        gate_up_new[0],
        gate_up_new[1],
        gate_up_new[2],
        out_new[0],
        out_new[1],
        out_new[2],
        down_new[0],
        down_new[1],
        down_new[2],
        bias_new[0],
        bias_new[1],
        bias_new[2],
        norm_new[0],
        norm_new[1],
        norm_new[2],
    )


def solution(mesh):
    return jax.shard_map(
        local,
        mesh=mesh,
        in_specs=(
            P(("dp", "tensor"), None),
            P(("dp", "tensor"), None),
            P("dp"),
            P("dp"),
            P(None, "dp", "tensor"),
            P(None, "dp", "tensor"),
            P("tensor", "dp"),
            P("tensor", "dp"),
            P(None, "tensor", "dp"),
            P(),
            P(None, "dp", "tensor"),
            P(None, "dp", "tensor"),
            P("tensor", "dp"),
            P("tensor", "dp"),
            P(None, "tensor", "dp"),
            P(),
            P(None, "dp", "tensor"),
            P(None, "dp", "tensor"),
            P("tensor", "dp"),
            P("tensor", "dp"),
            P(None, "tensor", "dp"),
            P(),
        ),
        out_specs=(
            P(("dp", "tensor"), None),
            P(("dp", "tensor"), None),
            P(None, "dp", "tensor"),
            P(None, "dp", "tensor"),
            P(None, "dp", "tensor"),
            P(None, "dp", "tensor"),
            P(None, "dp", "tensor"),
            P(None, "dp", "tensor"),
            P("tensor", "dp"),
            P("tensor", "dp"),
            P("tensor", "dp"),
            P("tensor", "dp"),
            P("tensor", "dp"),
            P("tensor", "dp"),
            P(None, "tensor", "dp"),
            P(None, "tensor", "dp"),
            P(None, "tensor", "dp"),
            P(),
            P(),
            P(),
        ),
        check_vma=False,
    )
```

```python
import functools
import math

import jax
import jax.numpy as jnp
from jax import lax
from jax.experimental import pallas as pl
from jax.experimental.pallas import tpu as pltpu
from jax.sharding import PartitionSpec as P

D = 2048
HEADS = 32
HEAD_DIM = 64
ROTARY = 16
FF = 5632


norm_eps = 1e-05
beta_one = 0.9
beta_two = 0.95
adam_eps = 1e-08
adam_steps = 10
decay_rate = 0.1
rope_base = 10000.0
score_scale = 0.125
mask_fill = -1e30
log2_e = math.log2(math.e)
LANES = 128
VMEM_LIMIT = 62 * 1024 * 1024


def norm_forward(values, gain_row, shift_row):
    average = jnp.mean(values, axis=-1, keepdims=True)
    centred = values - average
    spread = jnp.mean(centred * centred, axis=-1, keepdims=True)
    return centred * lax.rsqrt(spread + norm_eps) * gain_row + shift_row


def norm_backward(values, gain_row, grad_rows):
    average = jnp.mean(values, axis=-1, keepdims=True)
    centred = values - average
    spread = jnp.mean(centred * centred, axis=-1, keepdims=True)
    inverse = lax.rsqrt(spread + norm_eps)
    normal = centred * inverse
    grad_normal = grad_rows * gain_row
    grad_values = inverse * (
        grad_normal
        - jnp.mean(grad_normal, axis=-1, keepdims=True)
        - normal * jnp.mean(grad_normal * normal, axis=-1, keepdims=True)
    )
    return (
        grad_values,
        jnp.sum(grad_rows * normal, axis=0, keepdims=True),
        jnp.sum(grad_rows, axis=0, keepdims=True),
    )


def sum_parts(parts):
    return sum(parts[i].astype(jnp.float32) for i in range(parts.shape[0]))


def adamw(weight_old, first_old, second_old, gradient, step_rate, decay_part):
    first_new = beta_one * first_old + (1.0 - beta_one) * gradient
    second_new = beta_two * second_old + (1.0 - beta_two) * gradient * gradient
    correct_one = 1.0 - beta_one**adam_steps
    correct_two = 1.0 - beta_two**adam_steps
    update = first_new / correct_one / (jnp.sqrt(second_new / correct_two) + adam_eps)
    return (weight_old - step_rate * (update + decay_part * weight_old), first_new, second_new)


def spin(x, keep, ahead, behind):
    return x * keep + pltpu.roll(x, LANES - ROTARY // 2, 1) * ahead + pltpu.roll(x, ROTARY // 2, 1) * behind


def dot_nt(a, b):
    return lax.dot_general(a, b, (((1,), (1,)), ((), ())), preferred_element_type=jnp.float32)


def dot_nn(a, b):
    return lax.dot_general(a, b, (((1,), (0,)), ((), ())), preferred_element_type=jnp.float32)


def masked_scores(s, key_start, query_start, length, causal):
    key_slots = key_start + lax.broadcasted_iota(jnp.int32, s.shape, 0)
    allowed = key_slots < length
    if causal:
        query_slots = query_start + lax.broadcasted_iota(jnp.int32, s.shape, 1)
        allowed = allowed & (key_slots <= query_slots)
    return jnp.where(allowed, s, mask_fill)


def backward_kernel(block, length_ref, q_ref, k_ref, v_ref, kt_ref, o_ref, lse_ref, do_ref,
                    keep_ref, ahead_ref, behind_ref, out_ref, bias_ref,
                    dos_ref, delta_ref, dqt_ref, dk_ref, dv_ref):
    heads, rows, _ = q_ref.shape
    width = heads * HEAD_DIM
    groups = width // LANES
    per_group = LANES // HEAD_DIM
    blocks = rows // block
    length = length_ref[0]

    def prepare(i, _):
        at = pl.ds(pl.multiple_of(i * block, block), block)
        for g in range(groups):
            lanes = slice(g * LANES, (g + 1) * LANES)
            grad = do_ref[at, lanes]
            for p in range(per_group):
                dos_ref[g * per_group + p, at, :] = grad[:, p * HEAD_DIM:(p + 1) * HEAD_DIM]
            both = (grad.astype(jnp.float32) * o_ref[at, lanes].astype(jnp.float32)).T
            for p in range(per_group):
                h = g * per_group + p
                delta_ref[h:h + 1, at] = jnp.sum(both[p * HEAD_DIM:(p + 1) * HEAD_DIM], axis=0, keepdims=True)
        dqt_ref[:, at] = jnp.zeros((width, block), jnp.float32)
        return 0

    lax.fori_loop(0, blocks, prepare, 0)

    def key_block(j, _):
        key_start = pl.multiple_of(j * block, block)
        keys_at = pl.ds(key_start, block)

        def query_block(i, carry, kind):
            at = pl.ds(pl.multiple_of(i * block, block), block)
            out = []
            for h in range(heads):
                dk, dv = carry[h]
                keys, queries, grad = k_ref[h, keys_at, :], q_ref[h, at, :], dos_ref[h, at, :]
                s = dot_nt(keys, queries) * (score_scale * log2_e)
                if kind > 0:
                    s = masked_scores(s, key_start, i * block, length, kind == 2)
                p = jnp.exp2(s - lse_ref[h:h + 1, at])
                dp = dot_nt(v_ref[h, keys_at, :], grad)
                ds = (p * (dp - delta_ref[h:h + 1, at])).astype(jnp.bfloat16)
                dv = dv + dot_nn(p.astype(jnp.bfloat16), grad)
                dk = dk + dot_nn(ds, queries)
                here = slice(h * HEAD_DIM, (h + 1) * HEAD_DIM)
                dqt_ref[here, at] += dot_nn(kt_ref[here, keys_at], ds)
                out.append((dk, dv))
            return tuple(out)

        zero = jnp.zeros((block, HEAD_DIM), jnp.float32)
        carry = query_block(j, tuple((zero, zero) for _ in range(heads)), 2)
        whole = key_start + block <= length
        carry = lax.fori_loop(j + 1, jnp.where(whole, blocks, j + 1), lambda i, c: query_block(i, c, 0), carry)
        carry = lax.fori_loop(j + 1, jnp.where(whole, j + 1, blocks), lambda i, c: query_block(i, c, 1), carry)
        for h in range(heads):
            dk_ref[h, keys_at, :] = carry[h][0]
            dv_ref[h, keys_at, :] = carry[h][1]
        return 0

    lax.fori_loop(0, blocks, key_block, 0)
    bias_ref[...] = jnp.zeros(bias_ref.shape, jnp.float32)

    def finish(i, _):
        at = pl.ds(pl.multiple_of(i * block, block), block)
        keep, ahead, behind = keep_ref[at, :], -ahead_ref[at, :], -behind_ref[at, :]
        for g in range(groups):
            lanes = slice(g * LANES, (g + 1) * LANES)
            dq = dqt_ref[lanes, at].T
            dk = jnp.concatenate([dk_ref[g * per_group + p, at, :] for p in range(per_group)], axis=1)
            dv = jnp.concatenate([dv_ref[g * per_group + p, at, :] for p in range(per_group)], axis=1)
            parts = (spin(dq * score_scale, keep, ahead, behind), spin(dk * score_scale, keep, ahead, behind), dv)
            for c in range(3):
                low = parts[c].astype(jnp.bfloat16)
                place = slice(c * width + g * LANES, c * width + (g + 1) * LANES)
                out_ref[at, place] = low
                bias_ref[:, place] += jnp.sum(low.astype(jnp.float32), axis=0, keepdims=True)
        return 0

    lax.fori_loop(0, blocks, finish, 0)


def attention_backward(lengths, q, k, v, kt, o, lse, grad, keep, ahead, behind, block):
    heads, rows, _ = q.shape
    width = heads * HEAD_DIM
    vm = pl.BlockSpec(memory_space=pltpu.VMEM)
    return pl.pallas_call(
        functools.partial(backward_kernel, block),
        out_shape=(jax.ShapeDtypeStruct((rows, 3 * width), jnp.bfloat16),
                   jax.ShapeDtypeStruct((1, 3 * width), jnp.float32)),
        in_specs=[pl.BlockSpec(memory_space=pltpu.SMEM)] + [vm] * 10,
        out_specs=(vm,) * 2,
        scratch_shapes=[
            pltpu.VMEM((heads, rows, HEAD_DIM), jnp.bfloat16),
            pltpu.VMEM((heads, rows), jnp.float32),
            pltpu.VMEM((width, rows), jnp.float32),
            pltpu.VMEM((heads, rows, HEAD_DIM), jnp.float32),
            pltpu.VMEM((heads, rows, HEAD_DIM), jnp.float32),
        ],
        compiler_params=pltpu.CompilerParams(vmem_limit_bytes=VMEM_LIMIT),
        cost_estimate=pl.CostEstimate(flops=heads * rows * rows * HEAD_DIM * 20, bytes_accessed=rows * width * 30, transcendentals=heads * rows * rows),
        name="attention_backward",
    )(lengths, q, k, v, kt, o, lse, grad, keep, ahead, behind)


VM = pl.BlockSpec(memory_space=pltpu.VMEM)
ANYWHERE = pl.BlockSpec(memory_space=pl.ANY)
MESH = pl.DeviceIdType.MESH


def params(number):
    return pltpu.CompilerParams(collective_id=number, has_side_effects=True, vmem_limit_bytes=VMEM_LIMIT)


def lasting(us):
    return pl.CostEstimate(flops=int(us * 1.1e9), bytes_accessed=0, transcendentals=0)


def place():
    t = lax.axis_index("tensor")
    return t, lax.rem(t, 2), lax.div(t, 2)


def greet(n):
    t, core, chip = place()
    barrier = pltpu.get_barrier_semaphore()

    def hail(index):
        pl.semaphore_signal(barrier, inc=1, device_id={"tensor": index}, device_id_type=MESH)

    hail(t + 1 - 2 * core)
    pl.when(chip > 0)(lambda: hail(t - 2))
    pl.when(chip < n - 1)(lambda: hail(t + 2))
    pl.semaphore_wait(barrier, 1 + jnp.minimum(chip, 1) + jnp.minimum(n - 1 - chip, 1))


def near(j, m, n):
    below, above = m, n - 1 - m
    both = jnp.minimum(below, above)
    half = lax.div(j + 1, 2)
    inside = m + jnp.where(lax.rem(j, 2) == 1, -half, half)
    outside = m + jnp.where(above > below, j - both, both - j)
    return jnp.where(j <= 2 * both, inside, outside)


class Gather:
    def __init__(self, n, own, buf, sems, pieces):
        self.n, self.own, self.buf, self.pieces = n, own, buf, pieces
        self.up, self.down, self.side, self.line_in, self.side_in = [sems.at[i] for i in range(5)]
        self.t, self.core, self.m = place()
        self.sibling = self.t + 1 - 2 * self.core
        self.rows = own.shape[0] // pieces

    def copy(self, src, k, p, core, send, recv, target):
        at = pl.ds(pl.multiple_of(p * self.rows, self.rows), self.rows)
        index = k * self.pieces + p
        return pltpu.make_async_remote_copy(
            src_ref=src.at[at], dst_ref=self.buf.at[2 * k + core, at], send_sem=send.at[index],
            recv_sem=recv.at[index], device_id={"tensor": target}, device_id_type=MESH)

    def to_up(self, k, p, src):
        return self.copy(src, k, p, self.core, self.up, self.line_in, self.t + 2)

    def to_down(self, k, p, src):
        return self.copy(src, k, p, self.core, self.down, self.line_in, self.t - 2)

    def to_side(self, k, p, src):
        return self.copy(src, k, p, self.core, self.side, self.side_in, self.sibling)

    def start(self, which=None):
        m = self.m
        for p in range(self.pieces) if which is None else which:
            pl.when(m < self.n - 1)(lambda: self.to_up(m, p, self.own).start())
            pl.when(m > 0)(lambda: self.to_down(m, p, self.own).start())
            self.to_side(m, p, self.own).start()

    def arrive(self, d, which=None):
        m = self.m
        lo, hi = m - d, m + d
        for p in range(self.pieces) if which is None else which:
            @pl.when(lo >= 0)
            def _():
                src = self.buf.at[2 * lo + self.core]
                self.to_up(lo, p, src).wait_recv()
                pl.when(m < self.n - 1)(lambda: self.to_up(lo, p, src).start())
                self.to_side(lo, p, src).start()

            @pl.when(hi < self.n)
            def _():
                src = self.buf.at[2 * hi + self.core]
                self.to_down(hi, p, src).wait_recv()
                pl.when(m > 0)(lambda: self.to_down(hi, p, src).start())
                self.to_side(hi, p, src).start()

    def side_wait(self, k, which=None):
        for p in range(self.pieces) if which is None else which:
            self.copy(self.own, k, p, 1 - self.core, self.side, self.side_in, self.sibling).wait_recv()

    def finish(self):
        m = self.m

        def one(k, _):
            for p in range(self.pieces):
                pl.when((k <= m) & (m < self.n - 1))(lambda: self.to_up(k, p, self.own).wait_send())
                pl.when((k >= m) & (m > 0))(lambda: self.to_down(k, p, self.own).wait_send())
                self.to_side(k, p, self.own).wait_send()
            return 0

        lax.fori_loop(0, self.n, one, 0)


class Scatter:
    def __init__(self, n, pieces, side_out, side_in, line_in, side_sems, line_send, line_recv):
        self.n, self.pieces = n, pieces
        self.side_out, self.side_in, self.line_in = side_out, side_in, line_in
        self.side_send, self.side_recv = side_sems.at[0], side_sems.at[1]
        self.line_send, self.line_recv = line_send, line_recv
        self.t, self.core, self.m = place()
        self.sibling = self.t + 1 - 2 * self.core
        self.rows = side_out.shape[1] // pieces
        self.step = min(32, self.rows)

    def side(self, k):
        return pltpu.make_async_remote_copy(
            src_ref=self.side_out.at[k], dst_ref=self.side_in.at[k], send_sem=self.side_send.at[k],
            recv_sem=self.side_recv.at[k], device_id={"tensor": self.sibling}, device_id_type=MESH)

    def line(self, k, p, slot, target):
        at = pl.ds(pl.multiple_of(p * self.rows, self.rows), self.rows)
        return pltpu.make_async_remote_copy(
            src_ref=self.side_in.at[k, at], dst_ref=self.line_in.at[slot, at],
            send_sem=self.line_send.at[k * self.pieces + p], recv_sem=self.line_recv.at[slot * self.pieces + p],
            device_id={"tensor": target}, device_id_type=MESH)

    def each(self, p, body):
        def one(i, _):
            body(pl.ds(pl.multiple_of(p * self.rows + i * self.step, self.step), self.step))
            return 0

        lax.fori_loop(0, self.rows // self.step, one, 0)

    def pass_on(self, k, own, between=None):
        m, n = self.m, self.n
        self.side(k).wait_recv()
        inner = ((k > m) & (m > 0)) | ((k < m) & (m < n - 1))

        def one(p, _):
            @pl.when(inner)
            def _():
                self.line(k, p, k, self.t).wait_recv()

                def add(at):
                    total = own[at, :] + self.side_in[k, at, :].astype(jnp.float32) + self.line_in[k, at, :].astype(jnp.float32)
                    self.side_in[k, at, :] = total.astype(jnp.bfloat16)

                self.each(p, add)

            @pl.when(jnp.logical_not(inner))
            def _():
                def add(at):
                    self.side_in[k, at, :] = (own[at, :] + self.side_in[k, at, :].astype(jnp.float32)).astype(jnp.bfloat16)

                self.each(p, add)

            pl.when(k > m)(lambda: self.line(k, p, k, self.t + 2).start())
            pl.when(k < m)(lambda: self.line(k, p, jnp.where(k == m - 1, n, k), self.t - 2).start())
            if between is not None:
                between(p)
            return 0

        lax.fori_loop(0, self.pieces, one, 0)

    def settle(self, own, consume):
        m, n = self.m, self.n
        self.side(m).wait_recv()

        def one(p, _):
            def first(at):
                own[at, :] += self.side_in[m, at, :].astype(jnp.float32)

            self.each(p, first)

            def more(slot):
                self.line(m, p, slot, self.t).wait_recv()

                def add(at):
                    own[at, :] += self.line_in[slot, at, :].astype(jnp.float32)

                self.each(p, add)

            pl.when(m > 0)(lambda: more(m))
            pl.when(m < n - 1)(lambda: more(n))
            self.each(p, lambda at: consume(at, own[at, :]))
            return 0

        lax.fori_loop(0, self.pieces, one, 0)

    def finish(self):
        def one(k, _):
            self.side(k).wait_send()
            self.finish_line(k)
            return 0

        lax.fori_loop(0, self.n, one, 0)

    def finish_line(self, k):
        @pl.when(k != self.m)
        def _():
            for p in range(self.pieces):
                self.line(k, p, k, self.t).wait_send()


def scatter_scratch(n, pieces, rows, width):
    return [
        pltpu.VMEM((n, rows, width), jnp.bfloat16), pltpu.VMEM((n, rows, width), jnp.bfloat16),
        pltpu.VMEM((n + 1, rows, width), jnp.bfloat16),
        pltpu.SemaphoreType.DMA((2, n)), pltpu.SemaphoreType.DMA((n * pieces,)), pltpu.SemaphoreType.DMA(((n + 1) * pieces,)),
    ]


class Exchange:
    def __init__(self, group_count, pairs, local_sems, send, recv):
        self.group, self.count, self.pairs = lax.axis_index("dp"), group_count, pairs
        self.local_sems, self.send, self.recv = local_sems, send, recv

    def stay(self, index):
        src, dst = self.pairs[index]
        return pltpu.make_async_copy(src.at[self.group], dst.at[self.group], self.local_sems.at[index])

    def copy(self, index, peer, slot):
        src, dst = self.pairs[index]
        return pltpu.make_async_remote_copy(
            src_ref=src.at[peer], dst_ref=dst.at[slot], send_sem=self.send.at[index, peer],
            recv_sem=self.recv.at[index, slot], device_id={"dp": peer}, device_id_type=MESH)

    def others(self, body):
        for index in range(len(self.pairs)):
            for i in range(self.count):
                pl.when(i != self.group)(lambda: body(index, i))

    def start(self):
        self.others(lambda index, i: self.copy(index, i, self.group).start())
        for index in range(len(self.pairs)):
            self.stay(index).start()

    def finish(self):
        for index in range(len(self.pairs)):
            self.stay(index).wait()
        self.others(lambda index, i: self.copy(index, i, i).wait_recv())
        self.others(lambda index, i: self.copy(index, i, self.group).wait_send())


def exchange_scratch(pairs, group_count):
    dma = pltpu.SemaphoreType.DMA
    return [dma((pairs,)), dma((pairs, group_count)), dma((pairs, group_count))]


def greet_all(n, group_count):
    t, core, chip = place()
    g = lax.axis_index("dp")
    barrier = pltpu.get_barrier_semaphore()

    def hail(index):
        pl.semaphore_signal(barrier, inc=1, device_id={"tensor": index}, device_id_type=MESH)

    hail(t + 1 - 2 * core)
    pl.when(chip > 0)(lambda: hail(t - 2))
    pl.when(chip < n - 1)(lambda: hail(t + 2))
    for i in range(group_count):
        pl.when(i != g)(lambda: pl.semaphore_signal(barrier, inc=1, device_id={"dp": i}, device_id_type=MESH))
    pl.semaphore_wait(barrier, group_count + jnp.minimum(chip, 1) + jnp.minimum(n - 1 - chip, 1))


def forward_kernel(n, group_count, pieces, length_ref, place_ref, frequency_ref, x_ref, norm_ref, qkv_ref, out_ref, bias_ref, cot_ref,
                   xs_ref, wq_ref, wo_ref, q_ref, k_ref, v_ref, kt_ref, mixed_ref, lse_ref, keep_ref, ahead_ref, behind_ref,
                   middle_ref, normed_ref, cots_ref,
                   vt_ref, biases_ref, acc_ref, side_out, side_in, line_in, side_sems, line_send, line_recv,
                   first_sems, cot_sems, share_send, share_recv):
    greet_all(n, group_count)
    heads, total_rows, _ = q_ref.shape
    rows, features = x_ref.shape
    width = heads * HEAD_DIM
    lane_groups = width // LANES
    per_group = LANES // HEAD_DIM
    block = rows
    length = length_ref[0]
    group = lax.axis_index("dp")
    t, core, m = place()
    first = Gather(n, xs_ref.at[t], xs_ref, first_sems, pieces)
    cots = Gather(n, cot_ref, cots_ref, cot_sems, pieces)
    s = Scatter(n, pieces, side_out, side_in, line_in, side_sems, line_send, line_recv)
    step = 32

    def first_norm(i, _):
        at = pl.ds(pl.multiple_of(i * step, step), step)
        xs_ref[t, at, :] = norm_forward(x_ref[at, :].astype(jnp.float32), norm_ref[0:1, :], norm_ref[1:2, :]).astype(jnp.bfloat16)
        return 0

    lax.fori_loop(0, rows // step, first_norm, 0)
    first.start()
    depth = features // group_count
    mine = pl.ds(pl.multiple_of(group * depth, depth), depth)
    for c in range(3):
        wq_ref[c, mine, :] = qkv_ref[c].astype(jnp.bfloat16)
    wo_ref[:, mine] = out_ref[...].astype(jnp.bfloat16)
    biases_ref[group] = bias_ref[...].astype(jnp.bfloat16).astype(jnp.float32)

    def share(kind, src, owner, peer):
        ref = src(owner)
        return pltpu.make_async_remote_copy(
            src_ref=ref, dst_ref=ref, send_sem=share_send.at[kind, peer], recv_sem=share_recv.at[kind, owner],
            device_id={"dp": peer}, device_id_type=MESH)

    def part(owner):
        return pl.ds(pl.multiple_of(owner * depth, depth), depth)

    kinds = (lambda o: wq_ref.at[:, part(o), :], lambda o: biases_ref.at[o], lambda o: wo_ref.at[:, part(o)])
    for kind in range(3):
        for i in range(group_count):
            pl.when(i != group)(lambda: share(kind, kinds[kind], group, i).start())

    def tables(i, _):
        at = pl.ds(pl.multiple_of(i * block, block), block)
        angles = jnp.broadcast_to(place_ref[:, at], (LANES, block)).T * frequency_ref[...]
        cosine, sine = jnp.cos(angles), jnp.sin(angles)
        dim = lax.rem(lax.broadcasted_iota(jnp.int32, (block, LANES), 1), HEAD_DIM)
        none = jnp.zeros((block, LANES), jnp.float32)
        keep_ref[at, :] = jnp.where(dim < ROTARY, cosine, 1.0)
        ahead_ref[at, :] = jnp.where(dim < ROTARY // 2, -sine, none)
        behind_ref[at, :] = jnp.where((dim >= ROTARY // 2) & (dim < ROTARY), sine, none)
        return 0

    lax.fori_loop(0, total_rows // block, tables, 0)
    def project(slot):
        at = pl.ds(pl.multiple_of(slot * block, block), block)
        keep, ahead, behind = keep_ref[at, :], ahead_ref[at, :], behind_ref[at, :]
        x = xs_ref[slot]
        for c in range(3):
            wide = dot_nn(x, wq_ref[c]) + biases_ref[group_count, c:c + 1, :]
            for a in range(lane_groups):
                lanes = slice(a * LANES, (a + 1) * LANES)
                part_wide = wide[:, lanes]
                if c < 2:
                    part_wide = spin(part_wide, keep, ahead, behind)
                if c == 1:
                    kt_ref[lanes, at] = part_wide.T.astype(jnp.bfloat16)
                if c == 2:
                    vt_ref[lanes, at] = part_wide.T.astype(jnp.bfloat16)
                for b in range(per_group):
                    (q_ref, k_ref, v_ref)[c][a * per_group + b, at, :] = part_wide[:, b * HEAD_DIM:(b + 1) * HEAD_DIM].astype(jnp.bfloat16)

    def ring(d, _):
        def one(q, _):
            other, above = lax.div(q, 2), lax.rem(q, 2)
            k = jnp.where(above == 1, m + d, m - d)

            @pl.when((k >= 0) & (k < n) & ((d > 0) | (above == 0)))
            def _():
                pl.when(other == 1)(lambda: first.side_wait(k))
                project(2 * k + jnp.where(other == 1, 1 - core, core))

            return 0

        lax.fori_loop(0, 4, one, 0)
        pl.when(d == n - 2)(lambda: first.arrive(n - 1))
        return 0

    for d in range(1, n - 1):
        first.arrive(d)
    for kind in range(3):
        for i in range(group_count):
            pl.when(i != group)(lambda: share(kind, kinds[kind], i, i).wait_recv())
    bias = biases_ref[0]
    for i in range(1, group_count):
        bias = bias + biases_ref[i]
    biases_ref[group_count] = bias

    lax.fori_loop(0, n, ring, 0)
    cots.start()
    cots_ref[t] = cot_ref[...]
    pair = 2 * block

    def attend(i):
        at = pl.ds(pl.multiple_of(i * pair, pair), pair)
        queries = [q_ref[h, at, :] for h in range(heads)]

        def key_block(j, carry, kind):
            key_start = pl.multiple_of(j * pair, pair)
            keys_at = pl.ds(key_start, pair)
            out = []
            for h in range(heads):
                top, total, mixed = carry[h]
                scores = dot_nt(k_ref[h, keys_at, :], queries[h]) * (score_scale * log2_e)
                if kind > 0:
                    scores = masked_scores(scores, key_start, i * pair, length, kind == 2)
                new_top = jnp.maximum(top, jnp.max(scores, axis=0, keepdims=True))
                shrink = jnp.exp2(top - new_top)
                p = jnp.exp2(scores - new_top)
                total = total * shrink + jnp.sum(p, axis=0, keepdims=True)
                mixed = mixed * shrink + dot_nn(
                    vt_ref[h * HEAD_DIM:(h + 1) * HEAD_DIM, keys_at], p.astype(jnp.bfloat16))
                out.append((new_top, total, mixed))
            return tuple(out)

        start = tuple(
            (jnp.full((1, pair), mask_fill, jnp.float32), jnp.zeros((1, pair), jnp.float32),
             jnp.zeros((HEAD_DIM, pair), jnp.float32)) for _ in range(heads))
        carry = lax.fori_loop(0, i, lambda j, c: key_block(j, c, 1), start)
        carry = key_block(i, carry, 2)
        for h in range(heads):
            top, total, mixed = carry[h]
            lse_ref[h:h + 1, at] = top + jnp.log2(total)
        for a in range(lane_groups):
            both = [carry[a * per_group + b][2] * (1.0 / carry[a * per_group + b][1]) for b in range(per_group)]
            mixed_ref[at, a * LANES:(a + 1) * LANES] = jnp.concatenate(both, axis=0).T.astype(jnp.bfloat16)

    cut = min(512, features)

    def branch(j, _):
        k = near(n - 1 - j, m, n)

        attend(k)

        def attended(slot):
            return mixed_ref[pl.ds(pl.multiple_of(slot * block, block), block), :]

        low = attended(2 * k + 1 - core)
        for a in range(0, features, cut):
            s.side_out[k, :, a:a + cut] = dot_nn(low, wo_ref[:, a:a + cut]).astype(jnp.bfloat16)
        s.side(k).start()
        low = attended(2 * k + core)
        for a in range(0, features, cut):
            acc_ref[:, a:a + cut] = dot_nn(low, wo_ref[:, a:a + cut])
        pl.when(j < n - 1)(lambda: s.pass_on(k, acc_ref, lambda p: cots.arrive(j + 1, (p,))))
        return 0

    lax.fori_loop(0, n, branch, 0)

    def consume(at, total):
        middle = x_ref[at, :].astype(jnp.float32) + total
        middle_ref[at, :] = middle
        normed_ref[at, :] = norm_forward(middle, norm_ref[2:3, :], norm_ref[3:4, :]).astype(jnp.bfloat16)

    s.settle(acc_ref, consume)
    for k in range(n):
        cots.side_wait(k)
    first.finish()
    cots.finish()
    s.finish()
    for kind in range(3):
        for i in range(group_count):
            pl.when(i != group)(lambda: share(kind, kinds[kind], group, i).wait_send())


def forward(lengths, positions, x, norms, qkv, out, bias, cot, n, group_count, number, pieces=4):
    rows, features = x.shape
    width = qkv.shape[2]
    heads = width // HEAD_DIM
    total_rows = 2 * n * rows
    f32, low = jnp.float32, jnp.bfloat16
    shape = jax.ShapeDtypeStruct
    half_rot = ROTARY // 2
    frequency = rope_base ** (-(2.0 * jnp.arange(half_rot, dtype=jnp.float32)) / ROTARY)
    split = shape((heads, total_rows, HEAD_DIM), low)
    table = shape((total_rows, LANES), f32)
    gathered = shape((2 * n, rows, features), low)
    return pl.pallas_call(
        functools.partial(forward_kernel, n, group_count, pieces),
        out_shape=(gathered, shape((3, features, width), low), shape((width, features), low), split, split, split,
                   shape((width, total_rows), low), shape((total_rows, width), low), shape((heads, total_rows), f32),
                   table, table, table, shape((rows, features), f32), shape((rows, features), low), gathered),
        in_specs=[pl.BlockSpec(memory_space=pltpu.SMEM)] + [VM] * 8, out_specs=(VM,) * 15,
        scratch_shapes=[
            pltpu.VMEM((width, total_rows), low), pltpu.VMEM((group_count + 1, 8, width), f32), pltpu.VMEM((rows, features), f32),
        ] + scatter_scratch(n, pieces, rows, features) + [
            pltpu.SemaphoreType.DMA((5, n * pieces)), pltpu.SemaphoreType.DMA((5, n * pieces)),
            pltpu.SemaphoreType.DMA((3, group_count)), pltpu.SemaphoreType.DMA((3, group_count)),
        ],
        compiler_params=params(number), cost_estimate=lasting(200), name="forward",
    )(lengths, positions.astype(f32).reshape(1, total_rows), jnp.tile(frequency, LANES // half_rot).reshape(1, LANES),
      x, norms, qkv, out, bias, cot)


def mlp_kernel(n, pieces, x_ref, cots_hbm, gate_up_hbm, down_hbm, middle_hbm, norm_ref,
               hidden_ref, grad_middle_ref, sums_ref, grad_gate_up_ref, grad_down_ref,
               cots_ref, gate_up_ref, down_ref, middle_ref, xs_ref, grads_ref, load_sems,
               acc_ref, side_out, side_in, line_in, side_sems, line_send, line_recv, gather_sems,
               wide_stage, down_stage, wide_sem, down_sem):
    loads = [
        pltpu.make_async_copy(src, dst, load_sems.at[i])
        for i, (src, dst) in enumerate(
            ((gate_up_hbm, gate_up_ref), (cots_hbm, cots_ref), (down_hbm, down_ref), (middle_hbm, middle_ref)))
    ]
    for load in loads:
        load.start()
    greet(n)
    g = Gather(n, x_ref, xs_ref, gather_sems, pieces)
    halves = tuple(
        Scatter(n, pieces // 2, side_out, side_in.at[h], line_in.at[h], side_sems.at[h], line_send.at[h], line_recv.at[h])
        for h in range(2))
    m, core = g.m, g.core
    rows, width = x_ref.shape
    half = rows // 2
    group_count, hidden_units, depth = down_ref.shape
    cut = min(512, depth)
    places = [(f, min(256, hidden_units - f)) for f in range(0, hidden_units, 256)]
    early, late = tuple(range(pieces // 2)), tuple(range(pieces // 2, pieces))
    g.start(early)
    xs_ref[g.t] = x_ref[...]
    for load in loads:
        load.wait()

    def work(k, h):
        both = pl.ds(2 * k, 2)
        at = slice(h * half, (h + 1) * half)
        x = xs_ref[both, at, :].reshape(2 * half, width)
        cot = cots_ref[both, at, :].reshape(2 * half, width)
        for place, size in places:
            units = slice(place, place + size)
            shape = (2, half, size)

            def product(left, right):
                return sum(dot_nt(left[:, o * depth:(o + 1) * depth], right(o)) for o in range(group_count))

            gate = product(x, lambda o: gate_up_ref[o, 0, units, :])
            up = product(x, lambda o: gate_up_ref[o, 1, units, :])
            grad_hidden = product(cot, lambda o: down_ref[o, units, :])
            sig = 1.0 / (1.0 + jnp.exp(-gate))
            silu = gate * sig
            hidden_ref[both, at, units] = (silu * up).astype(jnp.bfloat16).reshape(shape)
            grads_ref[0, both, at, units] = (grad_hidden * up * (sig * (1.0 + gate * (1.0 - sig)))).astype(jnp.bfloat16).reshape(shape)
            grads_ref[1, both, at, units] = (grad_hidden * silu).astype(jnp.bfloat16).reshape(shape)

    def work_at(d, h, which):
        def one(above, _):
            k = jnp.where(above == 1, m + d, m - d)

            @pl.when((k >= 0) & (k < n) & ((d > 0) | (above == 0)))
            def _():
                g.side_wait(k, which)
                work(k, h)

            return 0

        lax.fori_loop(0, 2, one, 0)

    def ring(d, _):
        pl.when(d > 0)(lambda: g.arrive(d, early))
        pl.when(d == n - 2)(lambda: g.start(late))
        work_at(d, 0, early)
        return 0

    lax.fori_loop(0, n, ring, 0)

    def partials(k, h):
        at = slice(h * half, (h + 1) * half)
        both = pl.ds(2 * k, 2)
        for a in range(0, width, cut):
            acc_ref[h, :, :, a:a + cut] = sum(
                dot_nn(grads_ref[c, both, at, :].reshape(2 * half, hidden_units), gate_up_ref[a // depth, c, :, a % depth:a % depth + cut])
                for c in range(2)
            ).reshape(2, half, cut)
        if h == 1:
            halves[0].side(k).wait_send()
        step = min(32, half)

        def lower(i, _):
            here = pl.ds(pl.multiple_of(i * step, step), step)
            side_out[k, here, :] = acc_ref[h, 1 - core, here, :].astype(jnp.bfloat16)
            return 0

        lax.fori_loop(0, half // step, lower, 0)
        halves[h].side(k).start()

    def one(j, _):
        k = near(n - 1 - j, m, n)
        partials(k, 0)
        pl.when(j < n - 1)(
            lambda: halves[0].pass_on(k, acc_ref.at[0, core], lambda p: g.arrive(j + 1, (late[0] + p,))))
        work_at(j, 1, late)
        return 0

    lax.fori_loop(0, n, one, 0)
    wide_cut = min(256, depth)
    per = -(-(width // wide_cut) // n)
    tokens = 2 * n * rows

    def wide_copy(place, slot):
        lanes = pl.ds(pl.multiple_of(lax.rem(place, depth), wide_cut), wide_cut)
        return pltpu.make_async_copy(
            wide_stage.at[slot], grad_gate_up_ref.at[lax.div(place, depth), :, :, lanes], wide_sem.at[slot])

    def wide_gradient(u, j):
        place = (j * per + u) * wide_cut

        @pl.when(place < width)
        def _():
            pl.when(j > 0)(lambda: wide_copy(0, u).wait())
            lanes = pl.ds(pl.multiple_of(place, wide_cut), wide_cut)
            x = xs_ref[:, :, lanes].reshape(tokens, wide_cut).T
            for c in range(2):
                wide_stage[u, c] = dot_nn(x, grads_ref[c].reshape(tokens, hidden_units)).T.astype(jnp.bfloat16)
            wide_copy(place, u).start()

    def down_copy(place, size):
        return pltpu.make_async_copy(down_stage.at[:, pl.ds(0, size)], grad_down_ref.at[:, pl.ds(place, size)], down_sem)

    def down_gradient(index):
        place, size = places[index]
        if index > 0:
            down_copy(*places[index - 1]).wait()
        low = hidden_ref[:, :, place:place + size].reshape(tokens, size).T
        for a in range(0, width, cut):
            down_stage[a // depth, :size, a % depth:a % depth + cut] = dot_nn(low, cots_ref[:, :, a:a + cut].reshape(tokens, cut)).astype(jnp.bfloat16)
        down_copy(place, size).start()

    def two(j, _):
        k = near(n - 1 - j, m, n)
        partials(k, 1)
        pl.when(j < n - 1)(lambda: halves[1].pass_on(k, acc_ref.at[1, core]))
        for u in range(per):
            wide_gradient(u, j)
        for index in range(len(places)):
            pl.when(j == index)(functools.partial(down_gradient, index))
        return 0

    own = acc_ref.at[0, core]

    def settle(h):
        def consume(at, total):
            here = pl.ds(pl.multiple_of(h * half + at.start, at.size), at.size)
            back, gain, shift = norm_backward(middle_ref[here, :], norm_ref[2:3, :], total)
            grad_middle_ref[here, :] = cots_ref[g.t, here, :].astype(jnp.float32) + back
            sums_ref[0:1, :] += gain
            sums_ref[1:2, :] += shift

        halves[h].settle(acc_ref.at[h, core], consume)

    sums_ref[...] = jnp.zeros(sums_ref.shape, jnp.float32)
    settle(0)
    lax.fori_loop(0, n, two, 0)
    settle(1)
    for u in range(per):
        wide_copy(0, u).wait()
    down_copy(*places[-1]).wait()
    g.finish()

    def sent(k, _):
        halves[1].side(k).wait_send()
        for h in range(2):
            halves[h].finish_line(k)
        return 0

    lax.fori_loop(0, n, sent, 0)


def mlp(x, cots, gate_up, down, middle, norms, n, number, pieces=4):
    rows, width = x.shape
    group_count, hidden, depth = down.shape
    half, part = rows // 2, pieces // 2
    f32, low = jnp.float32, jnp.bfloat16
    shape = jax.ShapeDtypeStruct
    anywhere = pl.BlockSpec(memory_space=pl.ANY)
    wide_cut = min(256, depth)
    per = -(-(width // wide_cut) // n)
    dma = pltpu.SemaphoreType.DMA
    return pl.pallas_call(functools.partial(mlp_kernel, n, pieces),
        out_shape=(shape((2 * n, rows, hidden), low), shape((rows, width), f32),
                   shape((2, width), f32), shape(gate_up.shape, low), shape(down.shape, low)),
        in_specs=[VM] + [anywhere] * 4 + [VM], out_specs=(VM,) * 3 + (anywhere,) * 2,
        scratch_shapes=[
            pltpu.VMEM((2 * n, rows, width), low), pltpu.VMEM(gate_up.shape, low), pltpu.VMEM(down.shape, low), pltpu.VMEM((rows, width), f32),
            pltpu.VMEM((2 * n, rows, width), low), pltpu.VMEM((2, 2 * n, rows, hidden), low), dma((4,)),
            pltpu.VMEM((2, 2, half, width), f32), pltpu.VMEM((n, half, width), low), pltpu.VMEM((2, n, half, width), low),
            pltpu.VMEM((2, n + 1, half, width), low), dma((2, 2, n)), dma((2, n * part)), dma((2, (n + 1) * part)),
            dma((5, n * pieces)), pltpu.VMEM((per, 2, hidden, wide_cut), low), pltpu.VMEM((group_count, min(256, hidden), depth), low),
            dma((per,)), dma,
        ],
        compiler_params=params(number), cost_estimate=lasting(140), name="mlp")(x, cots, gate_up, down, middle, norms)


def down_kernel(n, pieces, hidden_ref, down_ref, middle_ref, grad_ref, out_ref, mixed_ref, wide_ref, low_ref, block_ref, back_ref, grad_out_ref, wide_parts, low_parts,
                local_sems, share_send, share_recv, xs_ref, x_ref, acc_ref, side_out, side_in, line_in, side_sems, line_send, line_recv, gather_sems):
    group_count, _, depth = down_ref.shape
    greet_all(n, group_count)
    grads = Exchange(group_count, ((wide_ref, wide_parts), (low_ref, low_parts)), local_sems, share_send, share_recv)
    g = Gather(n, x_ref, xs_ref, gather_sems, pieces)
    s = Scatter(n, pieces, side_out, side_in, line_in, side_sems, line_send, line_recv)
    x_ref[...] = grad_ref[...].astype(jnp.bfloat16)
    g.start()
    grads.start()
    xs_ref[g.t] = x_ref[...]
    m, core = s.m, s.core
    width = group_count * depth
    cut = min(512, depth)

    def one(j, _):
        k = near(n - 1 - j, m, n)
        for a in range(0, width, cut):
            s.side_out[k, :, a:a + cut] = dot_nn(hidden_ref[2 * k + 1 - core], down_ref[a // depth, :, a % depth:a % depth + cut]).astype(jnp.bfloat16)
        s.side(k).start()
        for a in range(0, width, cut):
            acc_ref[:, a:a + cut] = dot_nn(hidden_ref[2 * k + core], down_ref[a // depth, :, a % depth:a % depth + cut])
        pl.when(j < n - 1)(lambda: s.pass_on(k, acc_ref, lambda p: g.arrive(j + 1, (p,))))
        return 0

    lax.fori_loop(0, n, one, 0)

    def consume(at, total):
        block_ref[at, :] = (middle_ref[at, :] + total).astype(jnp.bfloat16)

    s.settle(acc_ref, consume)

    def last(k, _):
        g.side_wait(k)
        for c in range(2):
            back_ref[2 * k + c] = dot_nt(xs_ref[2 * k + c], out_ref[...]).astype(jnp.bfloat16)
        return 0

    lax.fori_loop(0, n, last, 0)
    flipped = mixed_ref[...].T
    for a in range(0, width, cut):
        grad_out_ref[a // depth, :, a % depth:a % depth + cut] = dot_nn(
            flipped, xs_ref[:, :, a:a + cut].reshape(mixed_ref.shape[0], cut)).astype(jnp.bfloat16)
    g.finish()
    s.finish()
    grads.finish()


def down_branch(hidden, down, middle, x, out, mixed, wide, narrow, n, number, pieces=4):
    rows, width = x.shape
    f32, low = jnp.float32, jnp.bfloat16
    return pl.pallas_call(functools.partial(down_kernel, n, pieces),
        out_shape=(jax.ShapeDtypeStruct((rows, width), low), jax.ShapeDtypeStruct((2 * n, rows, out.shape[0]), low),
                   jax.ShapeDtypeStruct((down.shape[0], out.shape[0], down.shape[2]), low),
                   jax.ShapeDtypeStruct(wide.shape, low), jax.ShapeDtypeStruct(narrow.shape, low)),
        in_specs=[VM] * 6 + [ANYWHERE] * 2, out_specs=(VM,) * 3 + (ANYWHERE,) * 2,
        scratch_shapes=exchange_scratch(2, down.shape[0]) + [pltpu.VMEM((2 * n, rows, width), low), pltpu.VMEM((rows, width), low), pltpu.VMEM((rows, width), f32)] + scatter_scratch(n, pieces, rows, width) + [pltpu.SemaphoreType.DMA((5, n * pieces))],
        compiler_params=params(number), cost_estimate=lasting(115), name="down_branch")(hidden, down, middle, x, out, mixed, wide, narrow)


def first_kernel(n, pieces, grad_ref, w_ref, x_ref, middle_ref, norm_ref, wide_ref, low_ref, result_ref, sums_ref, wide_parts, low_parts,
                 local_sems, share_send, share_recv, acc_ref, side_out, side_in, line_in, side_sems, line_send, line_recv):
    group_count = wide_ref.shape[0]
    greet_all(n, group_count)
    grads = Exchange(group_count, ((wide_ref, wide_parts), (low_ref, low_parts)), local_sems, share_send, share_recv)
    grads.start()
    s = Scatter(n, pieces, side_out, side_in, line_in, side_sems, line_send, line_recv)
    m, core = s.m, s.core
    width = w_ref.shape[1]
    part = w_ref.shape[2]
    cut = min(512, width)

    def one(j, _):
        k = near(n - 1 - j, m, n)

        def partial(slot, a):
            return sum(dot_nt(grad_ref[slot, :, c * part:(c + 1) * part], w_ref[c, a:a + cut, :]) for c in range(3))

        for a in range(0, width, cut):
            s.side_out[k, :, a:a + cut] = partial(2 * k + 1 - core, a).astype(jnp.bfloat16)
        s.side(k).start()
        for a in range(0, width, cut):
            acc_ref[:, a:a + cut] = partial(2 * k + core, a)
        pl.when(j < n - 1)(lambda: s.pass_on(k, acc_ref))
        return 0

    lax.fori_loop(0, n, one, 0)
    sums_ref[...] = jnp.zeros(sums_ref.shape, jnp.float32)

    def consume(at, total):
        back, gain, shift = norm_backward(x_ref[at, :].astype(jnp.float32), norm_ref[0:1, :], total)
        result_ref[at, :] = middle_ref[at, :] + back
        sums_ref[0:1, :] += gain
        sums_ref[1:2, :] += shift

    s.settle(acc_ref, consume)
    s.finish()
    grads.finish()


def first_branch(grad, w, x, grad_middle, norms, wide, narrow, n, number, pieces=4):
    rows, width = x.shape
    f32 = jnp.float32
    return pl.pallas_call(functools.partial(first_kernel, n, pieces),
        out_shape=(jax.ShapeDtypeStruct((rows, width), f32), jax.ShapeDtypeStruct((2, width), f32),
                   jax.ShapeDtypeStruct(wide.shape, wide.dtype), jax.ShapeDtypeStruct(narrow.shape, narrow.dtype)),
        in_specs=[VM] * 5 + [ANYWHERE] * 2, out_specs=(VM,) * 2 + (ANYWHERE,) * 2,
        scratch_shapes=exchange_scratch(2, wide.shape[0]) + [pltpu.VMEM((rows, width), f32)] + scatter_scratch(n, pieces, rows, width),
        compiler_params=params(number), cost_estimate=lasting(85), name="first_branch")(grad.reshape(2 * n, rows, grad.shape[1]), w, x, grad_middle, norms, wide, narrow)


def total_kernel(x_ref, bias_ref, out_ref, bias_out_ref, parts, groups, biases, send_one, recv_one, send_two, recv_two, send_three, recv_three, send_bias, recv_bias):
    t, g = lax.axis_index("tensor"), lax.axis_index("dp")
    count, group_count = parts.shape[0], groups.shape[0]
    barrier = pltpu.get_barrier_semaphore()
    for j in range(count):
        pl.when(j != t)(lambda: pl.semaphore_signal(barrier, inc=1, device_id={"tensor": j}, device_id_type=MESH))
    for i in range(group_count):
        pl.when(i != g)(lambda: pl.semaphore_signal(barrier, inc=1, device_id={"dp": i}, device_id_type=MESH))
    pl.semaphore_wait(barrier, count + group_count - 2)

    def spread(src, dst, send, recv, at, axis, peer):
        return pltpu.make_async_remote_copy(
            src_ref=src, dst_ref=dst, send_sem=send.at[peer], recv_sem=recv.at[at], device_id={axis: peer}, device_id_type=MESH)

    def exchange(me, size, make, stay):
        for j in range(size):
            pl.when(j != me)(lambda: make(j, me).start())
        stay()
        for j in range(size):
            pl.when(j != me)(lambda: make(j, j).wait_recv())
        for j in range(size):
            pl.when(j != me)(lambda: make(j, me).wait_send())

    def keep_one():
        parts[t] = x_ref[t]

    biases[g] = bias_ref[...]
    for i in range(group_count):
        pl.when(i != g)(lambda: spread(biases.at[g], biases.at[g], send_bias, recv_bias, g, "dp", i).start())

    def keep_two():
        groups[g] = sum_of(parts)

    def sum_of(ref):
        total = ref[0]
        for j in range(1, ref.shape[0]):
            total = total + ref[j]
        return total

    exchange(t, count, lambda j, at: spread(x_ref.at[j], parts.at[at], send_one, recv_one, at, "tensor", j), keep_one)
    keep_two()
    exchange(g, group_count, lambda j, at: spread(groups.at[g], groups.at[at], send_two, recv_two, at, "dp", j), lambda: None)
    out_ref[t] = sum_of(groups)
    for i in range(group_count):
        pl.when(i != g)(lambda: spread(biases.at[g], biases.at[i], send_bias, recv_bias, i, "dp", i).wait_recv())
    bias_out_ref[...] = sum_of(biases)
    for i in range(group_count):
        pl.when(i != g)(lambda: spread(biases.at[g], biases.at[g], send_bias, recv_bias, g, "dp", i).wait_send())
    exchange(t, count, lambda j, at: spread(out_ref.at[t], out_ref.at[at], send_three, recv_three, at, "tensor", j), lambda: None)


def total_over_all(x, bias, count, group_count, number):
    rows, width = x.shape
    piece = width // count
    shape = jax.ShapeDtypeStruct((count, rows, piece), x.dtype)
    bias_shape = jax.ShapeDtypeStruct(bias.shape, bias.dtype)
    out, bias_out = pl.pallas_call(
        total_kernel, out_shape=(shape, bias_shape), in_specs=[VM] * 2, out_specs=(VM,) * 2,
        scratch_shapes=[
            pltpu.VMEM((count, rows, piece), x.dtype), pltpu.VMEM((group_count, rows, piece), x.dtype),
            pltpu.VMEM((group_count,) + bias.shape, bias.dtype),
            pltpu.SemaphoreType.DMA((count,)), pltpu.SemaphoreType.DMA((count,)),
            pltpu.SemaphoreType.DMA((group_count,)), pltpu.SemaphoreType.DMA((group_count,)),
            pltpu.SemaphoreType.DMA((count,)), pltpu.SemaphoreType.DMA((count,)),
            pltpu.SemaphoreType.DMA((group_count,)), pltpu.SemaphoreType.DMA((group_count,)),
        ],
        compiler_params=params(number), cost_estimate=lasting(12), name="total_over_all",
    )(jnp.transpose(x.reshape(rows, count, piece), (1, 0, 2)), bias)
    return jnp.transpose(out, (1, 0, 2)).reshape(rows, width), bias_out


def local(
    inputs,
    cotangent,
    lengths,
    positions,
    qkv_master,
    gate_up_master,
    out_master,
    down_master,
    bias_master,
    norm_master,
    qkv_first,
    gate_up_first,
    out_first,
    down_first,
    bias_first,
    norm_first,
    qkv_second,
    gate_up_second,
    out_second,
    down_second,
    bias_second,
    norm_second,
):
    tensor_count = lax.axis_size("tensor")
    local_tokens = inputs.shape[0]
    group_tokens = local_tokens * tensor_count
    row_count = lengths.shape[0]
    row_length = group_tokens // row_count
    block_rows = min(512, row_length)
    heads_here = bias_master.shape[1]
    width_here = heads_here * HEAD_DIM
    own_start = lax.axis_index("tensor") * local_tokens
    chips = tensor_count // 2
    gate_up_copy, down_copy = (
        lax.all_gather(jnp.swapaxes(gate_up_master, 1, 2).astype(jnp.bfloat16), "dp", axis=0, tiled=False),
        lax.all_gather(down_master.astype(jnp.bfloat16), "dp", axis=0, tiled=False),
    )
    group = lax.axis_index("dp")
    group_count = lax.axis_size("dp")
    group_index = own_start + jnp.arange(local_tokens, dtype=jnp.int32)
    row_of = group_index // row_length
    slot_of = group_index % row_length
    row_match = row_of[:, None] == jnp.arange(row_count, dtype=jnp.int32)[None, :]
    length_of = jnp.sum(jnp.where(row_match, lengths[None, :], 0), axis=1)
    valid = slot_of < length_of
    grad_low = jnp.where(valid[:, None], cotangent, jnp.zeros_like(cotangent))
    own_dims = jnp.arange(HEAD_DIM) // (HEAD_DIM // group_count) == group
    bias_row = jnp.where(own_dims, jnp.tile(bias_master, (1, 1, group_count)), 0.0).reshape(3, width_here)
    bias_row = jnp.concatenate([bias_row, jnp.zeros((5, width_here), jnp.float32)], axis=0)
    (
        gathered_one, qkv_copy, out_copy, queries, keys, values, keys_flipped, mixed_low, log_totals,
        keep, ahead, behind, middle, normed_two, gathered_grad,
    ) = forward(
        lengths, positions, inputs, norm_master, qkv_master, out_master, bias_row, grad_low, chips, group_count, 0
    )
    gathered_one = gathered_one.reshape(group_tokens, D)
    hidden, grad_middle, sums_two, grad_gate_up_w, grad_down = mlp(
        normed_two, gathered_grad, gate_up_copy, down_copy, middle, norm_master, chips, 2
    )
    block_output, grad_mixed, grad_out_w, gate_up_parts, down_parts = down_branch(
        hidden, down_copy, middle, grad_middle, out_copy, mixed_low, grad_gate_up_w, grad_down, chips, 3
    )
    grad_mixed = grad_mixed.reshape(group_tokens, width_here)
    grad_projected, grad_bias = attention_backward(
        lengths, queries, keys, values, keys_flipped, mixed_low, log_totals, grad_mixed, keep, ahead, behind, block_rows
    )
    grad_qkv_w = lax.dot_general(
        gathered_one, grad_projected, (((0,), (0,)), ((), ())), preferred_element_type=jnp.float32
    )
    grad_qkv_w = grad_qkv_w.astype(jnp.bfloat16).reshape(group_count, D // group_count, 3 * width_here)
    input_grad, sums_one, qkv_parts, out_parts = first_branch(
        grad_projected, qkv_copy, inputs, grad_middle, norm_master, grad_qkv_w, grad_out_w, chips, 4
    )
    gate_up_grad, down_grad, out_grad = sum_parts(gate_up_parts), sum_parts(down_parts), sum_parts(out_parts)
    qkv_grad = jnp.transpose(sum_parts(qkv_parts).reshape(D // group_count, 3, width_here), (1, 0, 2))
    norm_grads, bias_grad = total_over_all(
        jnp.concatenate([sums_one, sums_two], axis=0), grad_bias, tensor_count, group_count, 5
    )
    bias_grad = lax.dynamic_slice_in_dim(
        bias_grad.reshape(3, heads_here, HEAD_DIM), group * bias_master.shape[2], bias_master.shape[2], axis=2
    )
    qkv_new = adamw(qkv_master, qkv_first, qkv_second, qkv_grad, 2.0 / math.sqrt(D), decay_rate)
    gate_up_new = tuple(
        jnp.swapaxes(item, 1, 2)
        for item in adamw(
            jnp.swapaxes(gate_up_master, 1, 2),
            jnp.swapaxes(gate_up_first, 1, 2),
            jnp.swapaxes(gate_up_second, 1, 2),
            gate_up_grad,
            2.0 / math.sqrt(D),
            decay_rate,
        )
    )
    out_new = adamw(
        out_master, out_first, out_second, out_grad, 16.0 / math.sqrt(HEADS * HEAD_DIM), decay_rate
    )
    down_new = adamw(
        down_master, down_first, down_second, down_grad, 6.0 / math.sqrt(FF), decay_rate
    )
    bias_new = adamw(bias_master, bias_first, bias_second, bias_grad, 1.5, 0.0)
    norm_new = adamw(norm_master, norm_first, norm_second, norm_grads, 0.7, 0.0)
    return (
        block_output,
        input_grad,
        qkv_new[0],
        qkv_new[1],
        qkv_new[2],
        gate_up_new[0],
        gate_up_new[1],
        gate_up_new[2],
        out_new[0],
        out_new[1],
        out_new[2],
        down_new[0],
        down_new[1],
        down_new[2],
        bias_new[0],
        bias_new[1],
        bias_new[2],
        norm_new[0],
        norm_new[1],
        norm_new[2],
    )


def solution(mesh):
    return jax.shard_map(
        local,
        mesh=mesh,
        in_specs=(
            P(("dp", "tensor"), None),
            P(("dp", "tensor"), None),
            P("dp"),
            P("dp"),
            P(None, "dp", "tensor"),
            P(None, "dp", "tensor"),
            P("tensor", "dp"),
            P("tensor", "dp"),
            P(None, "tensor", "dp"),
            P(),
            P(None, "dp", "tensor"),
            P(None, "dp", "tensor"),
            P("tensor", "dp"),
            P("tensor", "dp"),
            P(None, "tensor", "dp"),
            P(),
            P(None, "dp", "tensor"),
            P(None, "dp", "tensor"),
            P("tensor", "dp"),
            P("tensor", "dp"),
            P(None, "tensor", "dp"),
            P(),
        ),
        out_specs=(
            P(("dp", "tensor"), None),
            P(("dp", "tensor"), None),
            P(None, "dp", "tensor"),
            P(None, "dp", "tensor"),
            P(None, "dp", "tensor"),
            P(None, "dp", "tensor"),
            P(None, "dp", "tensor"),
            P(None, "dp", "tensor"),
            P("tensor", "dp"),
            P("tensor", "dp"),
            P("tensor", "dp"),
            P("tensor", "dp"),
            P("tensor", "dp"),
            P("tensor", "dp"),
            P(None, "tensor", "dp"),
            P(None, "tensor", "dp"),
            P(None, "tensor", "dp"),
            P(),
            P(),
            P(),
        ),
        check_vma=False,
    )
```

```python
import functools
import math

import jax
import jax.numpy as jnp
from jax import lax
from jax.experimental import pallas as pl
from jax.experimental.pallas import tpu as pltpu
from jax.sharding import PartitionSpec as P

D = 2048
HEADS = 32
HEAD_DIM = 64
ROTARY = 16
FF = 5632


norm_eps = 1e-05
beta_one = 0.9
beta_two = 0.95
adam_eps = 1e-08
adam_steps = 10
decay_rate = 0.1
rope_base = 10000.0
score_scale = 0.125
mask_fill = -1e30
log2_e = math.log2(math.e)
LANES = 128
VMEM_LIMIT = 62 * 1024 * 1024


def norm_forward(values, gain_row, shift_row):
    average = jnp.mean(values, axis=-1, keepdims=True)
    centred = values - average
    spread = jnp.mean(centred * centred, axis=-1, keepdims=True)
    return centred * lax.rsqrt(spread + norm_eps) * gain_row + shift_row


def norm_backward(values, gain_row, grad_rows):
    average = jnp.mean(values, axis=-1, keepdims=True)
    centred = values - average
    spread = jnp.mean(centred * centred, axis=-1, keepdims=True)
    inverse = lax.rsqrt(spread + norm_eps)
    normal = centred * inverse
    grad_normal = grad_rows * gain_row
    grad_values = inverse * (
        grad_normal
        - jnp.mean(grad_normal, axis=-1, keepdims=True)
        - normal * jnp.mean(grad_normal * normal, axis=-1, keepdims=True)
    )
    return (
        grad_values,
        jnp.sum(grad_rows * normal, axis=0, keepdims=True),
        jnp.sum(grad_rows, axis=0, keepdims=True),
    )


def sum_parts(parts):
    return sum(parts[i].astype(jnp.float32) for i in range(parts.shape[0]))


def adamw(weight_old, first_old, second_old, gradient, step_rate, decay_part):
    first_new = beta_one * first_old + (1.0 - beta_one) * gradient
    second_new = beta_two * second_old + (1.0 - beta_two) * gradient * gradient
    correct_one = 1.0 - beta_one**adam_steps
    correct_two = 1.0 - beta_two**adam_steps
    update = first_new / correct_one / (jnp.sqrt(second_new / correct_two) + adam_eps)
    return (weight_old - step_rate * (update + decay_part * weight_old), first_new, second_new)


def spin(x, keep, ahead, behind):
    return x * keep + pltpu.roll(x, LANES - ROTARY // 2, 1) * ahead + pltpu.roll(x, ROTARY // 2, 1) * behind


def dot_nt(a, b):
    return lax.dot_general(a, b, (((1,), (1,)), ((), ())), preferred_element_type=jnp.float32)


def dot_nn(a, b):
    return lax.dot_general(a, b, (((1,), (0,)), ((), ())), preferred_element_type=jnp.float32)


def masked_scores(s, key_start, query_start, length, causal):
    key_slots = key_start + lax.broadcasted_iota(jnp.int32, s.shape, 0)
    allowed = key_slots < length
    if causal:
        query_slots = query_start + lax.broadcasted_iota(jnp.int32, s.shape, 1)
        allowed = allowed & (key_slots <= query_slots)
    return jnp.where(allowed, s, mask_fill)


VM = pl.BlockSpec(memory_space=pltpu.VMEM)
ANYWHERE = pl.BlockSpec(memory_space=pl.ANY)
MESH = pl.DeviceIdType.MESH


def params(number):
    return pltpu.CompilerParams(collective_id=number, has_side_effects=True, vmem_limit_bytes=VMEM_LIMIT)


def lasting(us):
    return pl.CostEstimate(flops=int(us * 1.1e9), bytes_accessed=0, transcendentals=0)


def place():
    t = lax.axis_index("tensor")
    return t, lax.rem(t, 2), lax.div(t, 2)


def greet(n):
    t, core, chip = place()
    barrier = pltpu.get_barrier_semaphore()

    def hail(index):
        pl.semaphore_signal(barrier, inc=1, device_id={"tensor": index}, device_id_type=MESH)

    hail(t + 1 - 2 * core)
    pl.when(chip > 0)(lambda: hail(t - 2))
    pl.when(chip < n - 1)(lambda: hail(t + 2))
    pl.semaphore_wait(barrier, 1 + jnp.minimum(chip, 1) + jnp.minimum(n - 1 - chip, 1))


def near(j, m, n):
    below, above = m, n - 1 - m
    both = jnp.minimum(below, above)
    half = lax.div(j + 1, 2)
    inside = m + jnp.where(lax.rem(j, 2) == 1, -half, half)
    outside = m + jnp.where(above > below, j - both, both - j)
    return jnp.where(j <= 2 * both, inside, outside)


class Gather:
    def __init__(self, n, own, buf, sems, pieces):
        self.n, self.own, self.buf, self.pieces = n, own, buf, pieces
        self.up, self.down, self.side, self.line_in, self.side_in = [sems.at[i] for i in range(5)]
        self.t, self.core, self.m = place()
        self.sibling = self.t + 1 - 2 * self.core
        self.rows = own.shape[0] // pieces

    def copy(self, src, k, p, core, send, recv, target):
        at = pl.ds(pl.multiple_of(p * self.rows, self.rows), self.rows)
        index = k * self.pieces + p
        return pltpu.make_async_remote_copy(
            src_ref=src.at[at], dst_ref=self.buf.at[2 * k + core, at], send_sem=send.at[index],
            recv_sem=recv.at[index], device_id={"tensor": target}, device_id_type=MESH)

    def to_up(self, k, p, src):
        return self.copy(src, k, p, self.core, self.up, self.line_in, self.t + 2)

    def to_down(self, k, p, src):
        return self.copy(src, k, p, self.core, self.down, self.line_in, self.t - 2)

    def to_side(self, k, p, src):
        return self.copy(src, k, p, self.core, self.side, self.side_in, self.sibling)

    def start(self, which=None):
        m = self.m
        for p in range(self.pieces) if which is None else which:
            pl.when(m < self.n - 1)(lambda: self.to_up(m, p, self.own).start())
            pl.when(m > 0)(lambda: self.to_down(m, p, self.own).start())
            self.to_side(m, p, self.own).start()

    def arrive(self, d, which=None):
        m = self.m
        lo, hi = m - d, m + d
        for p in range(self.pieces) if which is None else which:
            @pl.when(lo >= 0)
            def _():
                src = self.buf.at[2 * lo + self.core]
                self.to_up(lo, p, src).wait_recv()
                pl.when(m < self.n - 1)(lambda: self.to_up(lo, p, src).start())
                self.to_side(lo, p, src).start()

            @pl.when(hi < self.n)
            def _():
                src = self.buf.at[2 * hi + self.core]
                self.to_down(hi, p, src).wait_recv()
                pl.when(m > 0)(lambda: self.to_down(hi, p, src).start())
                self.to_side(hi, p, src).start()

    def side_wait(self, k, which=None):
        for p in range(self.pieces) if which is None else which:
            self.copy(self.own, k, p, 1 - self.core, self.side, self.side_in, self.sibling).wait_recv()

    def finish(self):
        m = self.m

        def one(k, _):
            for p in range(self.pieces):
                pl.when((k <= m) & (m < self.n - 1))(lambda: self.to_up(k, p, self.own).wait_send())
                pl.when((k >= m) & (m > 0))(lambda: self.to_down(k, p, self.own).wait_send())
                self.to_side(k, p, self.own).wait_send()
            return 0

        lax.fori_loop(0, self.n, one, 0)


class Scatter:
    def __init__(self, n, pieces, side_out, side_in, line_in, side_sems, line_send, line_recv):
        self.n, self.pieces = n, pieces
        self.side_out, self.side_in, self.line_in = side_out, side_in, line_in
        self.side_send, self.side_recv = side_sems.at[0], side_sems.at[1]
        self.line_send, self.line_recv = line_send, line_recv
        self.t, self.core, self.m = place()
        self.sibling = self.t + 1 - 2 * self.core
        self.rows = side_out.shape[1] // pieces
        self.step = min(32, self.rows)

    def side(self, k):
        return pltpu.make_async_remote_copy(
            src_ref=self.side_out.at[k], dst_ref=self.side_in.at[k], send_sem=self.side_send.at[k],
            recv_sem=self.side_recv.at[k], device_id={"tensor": self.sibling}, device_id_type=MESH)

    def line(self, k, p, slot, target):
        at = pl.ds(pl.multiple_of(p * self.rows, self.rows), self.rows)
        return pltpu.make_async_remote_copy(
            src_ref=self.side_in.at[k, at], dst_ref=self.line_in.at[slot, at],
            send_sem=self.line_send.at[k * self.pieces + p], recv_sem=self.line_recv.at[slot * self.pieces + p],
            device_id={"tensor": target}, device_id_type=MESH)

    def each(self, p, body):
        def one(i, _):
            body(pl.ds(pl.multiple_of(p * self.rows + i * self.step, self.step), self.step))
            return 0

        lax.fori_loop(0, self.rows // self.step, one, 0)

    def pass_on(self, k, own, between=None):
        m, n = self.m, self.n
        self.side(k).wait_recv()
        inner = ((k > m) & (m > 0)) | ((k < m) & (m < n - 1))

        def one(p, _):
            @pl.when(inner)
            def _():
                self.line(k, p, k, self.t).wait_recv()

                def add(at):
                    total = own[at, :] + self.side_in[k, at, :].astype(jnp.float32) + self.line_in[k, at, :].astype(jnp.float32)
                    self.side_in[k, at, :] = total.astype(jnp.bfloat16)

                self.each(p, add)

            @pl.when(jnp.logical_not(inner))
            def _():
                def add(at):
                    self.side_in[k, at, :] = (own[at, :] + self.side_in[k, at, :].astype(jnp.float32)).astype(jnp.bfloat16)

                self.each(p, add)

            pl.when(k > m)(lambda: self.line(k, p, k, self.t + 2).start())
            pl.when(k < m)(lambda: self.line(k, p, jnp.where(k == m - 1, n, k), self.t - 2).start())
            if between is not None:
                between(p)
            return 0

        lax.fori_loop(0, self.pieces, one, 0)

    def settle(self, own, consume):
        m, n = self.m, self.n
        self.side(m).wait_recv()

        def one(p, _):
            def first(at):
                own[at, :] += self.side_in[m, at, :].astype(jnp.float32)

            self.each(p, first)

            def more(slot):
                self.line(m, p, slot, self.t).wait_recv()

                def add(at):
                    own[at, :] += self.line_in[slot, at, :].astype(jnp.float32)

                self.each(p, add)

            pl.when(m > 0)(lambda: more(m))
            pl.when(m < n - 1)(lambda: more(n))
            self.each(p, lambda at: consume(at, own[at, :]))
            return 0

        lax.fori_loop(0, self.pieces, one, 0)

    def finish(self):
        def one(k, _):
            self.side(k).wait_send()
            self.finish_line(k)
            return 0

        lax.fori_loop(0, self.n, one, 0)

    def finish_line(self, k):
        @pl.when(k != self.m)
        def _():
            for p in range(self.pieces):
                self.line(k, p, k, self.t).wait_send()


def scatter_scratch(n, pieces, rows, width):
    return [
        pltpu.VMEM((n, rows, width), jnp.bfloat16), pltpu.VMEM((n, rows, width), jnp.bfloat16),
        pltpu.VMEM((n + 1, rows, width), jnp.bfloat16),
        pltpu.SemaphoreType.DMA((2, n)), pltpu.SemaphoreType.DMA((n * pieces,)), pltpu.SemaphoreType.DMA(((n + 1) * pieces,)),
    ]


class Exchange:
    def __init__(self, group_count, pairs, local_sems, send, recv):
        self.group, self.count, self.pairs = lax.axis_index("dp"), group_count, pairs
        self.local_sems, self.send, self.recv = local_sems, send, recv

    def stay(self, index):
        src, dst = self.pairs[index]
        return pltpu.make_async_copy(src.at[self.group], dst.at[self.group], self.local_sems.at[index])

    def copy(self, index, peer, slot):
        src, dst = self.pairs[index]
        return pltpu.make_async_remote_copy(
            src_ref=src.at[peer], dst_ref=dst.at[slot], send_sem=self.send.at[index, peer],
            recv_sem=self.recv.at[index, slot], device_id={"dp": peer}, device_id_type=MESH)

    def others(self, body, which=None):
        for index in range(len(self.pairs)) if which is None else which:
            for i in range(self.count):
                pl.when(i != self.group)(lambda: body(index, i))

    def start(self, which=None):
        self.others(lambda index, i: self.copy(index, i, self.group).start(), which)
        for index in range(len(self.pairs)) if which is None else which:
            self.stay(index).start()

    def finish(self):
        for index in range(len(self.pairs)):
            self.stay(index).wait()
        self.others(lambda index, i: self.copy(index, i, i).wait_recv())
        self.others(lambda index, i: self.copy(index, i, self.group).wait_send())


def exchange_scratch(pairs, group_count):
    dma = pltpu.SemaphoreType.DMA
    return [dma((pairs,)), dma((pairs, group_count)), dma((pairs, group_count))]


def greet_all(n, group_count):
    t, core, chip = place()
    g = lax.axis_index("dp")
    barrier = pltpu.get_barrier_semaphore()

    def hail(index):
        pl.semaphore_signal(barrier, inc=1, device_id={"tensor": index}, device_id_type=MESH)

    hail(t + 1 - 2 * core)
    pl.when(chip > 0)(lambda: hail(t - 2))
    pl.when(chip < n - 1)(lambda: hail(t + 2))
    for i in range(group_count):
        pl.when(i != g)(lambda: pl.semaphore_signal(barrier, inc=1, device_id={"dp": i}, device_id_type=MESH))
    pl.semaphore_wait(barrier, group_count + jnp.minimum(chip, 1) + jnp.minimum(n - 1 - chip, 1))


def forward_kernel(n, group_count, pieces, length_ref, place_ref, frequency_ref, x_ref, norm_ref, qkv_ref, out_ref, bias_ref, cot_ref,
                   xs_ref, wq_ref, wo_ref, q_ref, k_ref, v_ref, kt_ref, mixed_ref, lse_ref, keep_ref, ahead_ref, behind_ref,
                   middle_ref, normed_ref, cots_ref,
                   vt_ref, biases_ref, acc_ref, side_out, side_in, line_in, side_sems, line_send, line_recv,
                   first_sems, cot_sems, share_send, share_recv):
    greet_all(n, group_count)
    heads, total_rows, _ = q_ref.shape
    rows, features = x_ref.shape
    width = heads * HEAD_DIM
    lane_groups = width // LANES
    per_group = LANES // HEAD_DIM
    block = rows
    length = length_ref[0]
    group = lax.axis_index("dp")
    t, core, m = place()
    first = Gather(n, xs_ref.at[t], xs_ref, first_sems, pieces)
    cots = Gather(n, cot_ref, cots_ref, cot_sems, pieces)
    s = Scatter(n, pieces, side_out, side_in, line_in, side_sems, line_send, line_recv)
    step = 32

    def first_norm(i, _):
        at = pl.ds(pl.multiple_of(i * step, step), step)
        xs_ref[t, at, :] = norm_forward(x_ref[at, :].astype(jnp.float32), norm_ref[0:1, :], norm_ref[1:2, :]).astype(jnp.bfloat16)
        return 0

    lax.fori_loop(0, rows // step, first_norm, 0)
    first.start()
    depth = features // group_count
    mine = pl.ds(pl.multiple_of(group * depth, depth), depth)
    for c in range(3):
        wq_ref[c, mine, :] = qkv_ref[c].astype(jnp.bfloat16)
    wo_ref[:, mine] = out_ref[...].astype(jnp.bfloat16)
    biases_ref[group] = bias_ref[...].astype(jnp.bfloat16).astype(jnp.float32)

    def share(kind, src, owner, peer):
        ref = src(owner)
        return pltpu.make_async_remote_copy(
            src_ref=ref, dst_ref=ref, send_sem=share_send.at[kind, peer], recv_sem=share_recv.at[kind, owner],
            device_id={"dp": peer}, device_id_type=MESH)

    def part(owner):
        return pl.ds(pl.multiple_of(owner * depth, depth), depth)

    kinds = (lambda o: wq_ref.at[:, part(o), :], lambda o: biases_ref.at[o], lambda o: wo_ref.at[:, part(o)])
    for kind in range(3):
        for i in range(group_count):
            pl.when(i != group)(lambda: share(kind, kinds[kind], group, i).start())

    def tables(i, _):
        at = pl.ds(pl.multiple_of(i * block, block), block)
        angles = jnp.broadcast_to(place_ref[:, at], (LANES, block)).T * frequency_ref[...]
        cosine, sine = jnp.cos(angles), jnp.sin(angles)
        dim = lax.rem(lax.broadcasted_iota(jnp.int32, (block, LANES), 1), HEAD_DIM)
        none = jnp.zeros((block, LANES), jnp.float32)
        keep_ref[at, :] = jnp.where(dim < ROTARY, cosine, 1.0)
        ahead_ref[at, :] = jnp.where(dim < ROTARY // 2, -sine, none)
        behind_ref[at, :] = jnp.where((dim >= ROTARY // 2) & (dim < ROTARY), sine, none)
        return 0

    lax.fori_loop(0, total_rows // block, tables, 0)
    def project(slot):
        at = pl.ds(pl.multiple_of(slot * block, block), block)
        keep, ahead, behind = keep_ref[at, :], ahead_ref[at, :], behind_ref[at, :]
        x = xs_ref[slot]
        for c in range(3):
            wide = dot_nn(x, wq_ref[c]) + biases_ref[group_count, c:c + 1, :]
            for a in range(lane_groups):
                lanes = slice(a * LANES, (a + 1) * LANES)
                part_wide = wide[:, lanes]
                if c < 2:
                    part_wide = spin(part_wide, keep, ahead, behind)
                if c == 1:
                    kt_ref[lanes, at] = part_wide.T.astype(jnp.bfloat16)
                if c == 2:
                    vt_ref[lanes, at] = part_wide.T.astype(jnp.bfloat16)
                for b in range(per_group):
                    (q_ref, k_ref, v_ref)[c][a * per_group + b, at, :] = part_wide[:, b * HEAD_DIM:(b + 1) * HEAD_DIM].astype(jnp.bfloat16)

    def ring(d, _):
        def one(q, _):
            other, above = lax.div(q, 2), lax.rem(q, 2)
            k = jnp.where(above == 1, m + d, m - d)

            @pl.when((k >= 0) & (k < n) & ((d > 0) | (above == 0)))
            def _():
                pl.when(other == 1)(lambda: first.side_wait(k))
                project(2 * k + jnp.where(other == 1, 1 - core, core))

            return 0

        lax.fori_loop(0, 4, one, 0)
        pl.when(d == n - 2)(lambda: first.arrive(n - 1))
        return 0

    for d in range(1, n - 1):
        first.arrive(d)
    for kind in range(3):
        for i in range(group_count):
            pl.when(i != group)(lambda: share(kind, kinds[kind], i, i).wait_recv())
    bias = biases_ref[0]
    for i in range(1, group_count):
        bias = bias + biases_ref[i]
    biases_ref[group_count] = bias

    lax.fori_loop(0, n, ring, 0)
    cots.start()
    cots_ref[t] = cot_ref[...]
    pair = 2 * block

    def attend(i):
        at = pl.ds(pl.multiple_of(i * pair, pair), pair)
        queries = [q_ref[h, at, :] for h in range(heads)]

        def key_block(j, carry, kind):
            key_start = pl.multiple_of(j * pair, pair)
            keys_at = pl.ds(key_start, pair)
            out = []
            for h in range(heads):
                top, total, mixed = carry[h]
                scores = dot_nt(k_ref[h, keys_at, :], queries[h]) * (score_scale * log2_e)
                if kind > 0:
                    scores = masked_scores(scores, key_start, i * pair, length, kind == 2)
                new_top = jnp.maximum(top, jnp.max(scores, axis=0, keepdims=True))
                shrink = jnp.exp2(top - new_top)
                p = jnp.exp2(scores - new_top)
                total = total * shrink + jnp.sum(p, axis=0, keepdims=True)
                mixed = mixed * shrink + dot_nn(
                    vt_ref[h * HEAD_DIM:(h + 1) * HEAD_DIM, keys_at], p.astype(jnp.bfloat16))
                out.append((new_top, total, mixed))
            return tuple(out)

        start = tuple(
            (jnp.full((1, pair), mask_fill, jnp.float32), jnp.zeros((1, pair), jnp.float32),
             jnp.zeros((HEAD_DIM, pair), jnp.float32)) for _ in range(heads))
        carry = lax.fori_loop(0, i, lambda j, c: key_block(j, c, 1), start)
        carry = key_block(i, carry, 2)
        for h in range(heads):
            top, total, mixed = carry[h]
            lse_ref[h:h + 1, at] = top + jnp.log2(total)
        for a in range(lane_groups):
            both = [carry[a * per_group + b][2] * (1.0 / carry[a * per_group + b][1]) for b in range(per_group)]
            mixed_ref[at, a * LANES:(a + 1) * LANES] = jnp.concatenate(both, axis=0).T.astype(jnp.bfloat16)

    cut = min(512, features)

    def branch(j, _):
        k = near(n - 1 - j, m, n)

        attend(k)

        def attended(slot):
            return mixed_ref[pl.ds(pl.multiple_of(slot * block, block), block), :]

        low = attended(2 * k + 1 - core)
        for a in range(0, features, cut):
            s.side_out[k, :, a:a + cut] = dot_nn(low, wo_ref[:, a:a + cut]).astype(jnp.bfloat16)
        s.side(k).start()
        low = attended(2 * k + core)
        for a in range(0, features, cut):
            acc_ref[:, a:a + cut] = dot_nn(low, wo_ref[:, a:a + cut])
        pl.when(j < n - 1)(lambda: s.pass_on(k, acc_ref, lambda p: cots.arrive(j + 1, (p,))))
        return 0

    lax.fori_loop(0, n, branch, 0)

    def consume(at, total):
        middle = x_ref[at, :].astype(jnp.float32) + total
        middle_ref[at, :] = middle
        normed_ref[at, :] = norm_forward(middle, norm_ref[2:3, :], norm_ref[3:4, :]).astype(jnp.bfloat16)

    s.settle(acc_ref, consume)
    for k in range(n):
        cots.side_wait(k)
    first.finish()
    cots.finish()
    s.finish()
    for kind in range(3):
        for i in range(group_count):
            pl.when(i != group)(lambda: share(kind, kinds[kind], group, i).wait_send())


def forward(lengths, positions, x, norms, qkv, out, bias, cot, n, group_count, number, pieces=4):
    rows, features = x.shape
    width = qkv.shape[2]
    heads = width // HEAD_DIM
    total_rows = 2 * n * rows
    f32, low = jnp.float32, jnp.bfloat16
    shape = jax.ShapeDtypeStruct
    half_rot = ROTARY // 2
    frequency = rope_base ** (-(2.0 * jnp.arange(half_rot, dtype=jnp.float32)) / ROTARY)
    split = shape((heads, total_rows, HEAD_DIM), low)
    table = shape((total_rows, LANES), f32)
    gathered = shape((2 * n, rows, features), low)
    return pl.pallas_call(
        functools.partial(forward_kernel, n, group_count, pieces),
        out_shape=(gathered, shape((3, features, width), low), shape((width, features), low), split, split, split,
                   shape((width, total_rows), low), shape((total_rows, width), low), shape((heads, total_rows), f32),
                   table, table, table, shape((rows, features), f32), shape((rows, features), low), gathered),
        in_specs=[pl.BlockSpec(memory_space=pltpu.SMEM)] + [VM] * 8, out_specs=(VM,) * 15,
        scratch_shapes=[
            pltpu.VMEM((width, total_rows), low), pltpu.VMEM((group_count + 1, 8, width), f32), pltpu.VMEM((rows, features), f32),
        ] + scatter_scratch(n, pieces, rows, features) + [
            pltpu.SemaphoreType.DMA((5, n * pieces)), pltpu.SemaphoreType.DMA((5, n * pieces)),
            pltpu.SemaphoreType.DMA((3, group_count)), pltpu.SemaphoreType.DMA((3, group_count)),
        ],
        compiler_params=params(number), cost_estimate=lasting(200), name="forward",
    )(lengths, positions.astype(f32).reshape(1, total_rows), jnp.tile(frequency, LANES // half_rot).reshape(1, LANES),
      x, norms, qkv, out, bias, cot)


def mlp_kernel(n, pieces, x_ref, cots_hbm, gate_up_hbm, down_hbm, middle_hbm, norm_ref,
               hidden_ref, grad_middle_ref, sums_ref, grad_gate_up_ref, grad_down_ref,
               cots_ref, gate_up_ref, down_ref, middle_ref, xs_ref, grads_ref, load_sems,
               acc_ref, side_out, side_in, line_in, side_sems, line_send, line_recv, gather_sems,
               wide_stage, down_stage, wide_sem, down_sem):
    loads = [
        pltpu.make_async_copy(src, dst, load_sems.at[i])
        for i, (src, dst) in enumerate(
            ((gate_up_hbm, gate_up_ref), (cots_hbm, cots_ref), (down_hbm, down_ref), (middle_hbm, middle_ref)))
    ]
    for load in loads:
        load.start()
    greet(n)
    g = Gather(n, x_ref, xs_ref, gather_sems, pieces)
    halves = tuple(
        Scatter(n, pieces // 2, side_out, side_in.at[h], line_in.at[h], side_sems.at[h], line_send.at[h], line_recv.at[h])
        for h in range(2))
    m, core = g.m, g.core
    rows, width = x_ref.shape
    half = rows // 2
    group_count, hidden_units, depth = down_ref.shape
    cut = min(512, depth)
    places = [(f, min(256, hidden_units - f)) for f in range(0, hidden_units, 256)]
    early, late = tuple(range(pieces // 2)), tuple(range(pieces // 2, pieces))
    g.start(early)
    xs_ref[g.t] = x_ref[...]
    for load in loads:
        load.wait()

    def work(k, h):
        both = pl.ds(2 * k, 2)
        at = slice(h * half, (h + 1) * half)
        x = xs_ref[both, at, :].reshape(2 * half, width)
        cot = cots_ref[both, at, :].reshape(2 * half, width)
        for place, size in places:
            units = slice(place, place + size)
            shape = (2, half, size)

            def product(left, right):
                return sum(dot_nt(left[:, o * depth:(o + 1) * depth], right(o)) for o in range(group_count))

            gate = product(x, lambda o: gate_up_ref[o, 0, units, :])
            up = product(x, lambda o: gate_up_ref[o, 1, units, :])
            grad_hidden = product(cot, lambda o: down_ref[o, units, :])
            sig = 1.0 / (1.0 + jnp.exp(-gate))
            silu = gate * sig
            hidden_ref[both, at, units] = (silu * up).astype(jnp.bfloat16).reshape(shape)
            grads_ref[0, both, at, units] = (grad_hidden * up * (sig * (1.0 + gate * (1.0 - sig)))).astype(jnp.bfloat16).reshape(shape)
            grads_ref[1, both, at, units] = (grad_hidden * silu).astype(jnp.bfloat16).reshape(shape)

    def work_at(d, h, which):
        def one(above, _):
            k = jnp.where(above == 1, m + d, m - d)

            @pl.when((k >= 0) & (k < n) & ((d > 0) | (above == 0)))
            def _():
                g.side_wait(k, which)
                work(k, h)

            return 0

        lax.fori_loop(0, 2, one, 0)

    def ring(d, _):
        pl.when(d > 0)(lambda: g.arrive(d, early))
        pl.when(d == n - 2)(lambda: g.start(late))
        work_at(d, 0, early)
        return 0

    lax.fori_loop(0, n, ring, 0)

    def partials(k, h):
        at = slice(h * half, (h + 1) * half)
        both = pl.ds(2 * k, 2)
        for a in range(0, width, cut):
            acc_ref[h, :, :, a:a + cut] = sum(
                dot_nn(grads_ref[c, both, at, :].reshape(2 * half, hidden_units), gate_up_ref[a // depth, c, :, a % depth:a % depth + cut])
                for c in range(2)
            ).reshape(2, half, cut)
        if h == 1:
            halves[0].side(k).wait_send()
        step = min(32, half)

        def lower(i, _):
            here = pl.ds(pl.multiple_of(i * step, step), step)
            side_out[k, here, :] = acc_ref[h, 1 - core, here, :].astype(jnp.bfloat16)
            return 0

        lax.fori_loop(0, half // step, lower, 0)
        halves[h].side(k).start()

    def one(j, _):
        k = near(n - 1 - j, m, n)
        partials(k, 0)
        pl.when(j < n - 1)(
            lambda: halves[0].pass_on(k, acc_ref.at[0, core], lambda p: g.arrive(j + 1, (late[0] + p,))))
        work_at(j, 1, late)
        return 0

    lax.fori_loop(0, n, one, 0)
    wide_cut = min(256, depth)
    per = -(-(width // wide_cut) // n)
    tokens = 2 * n * rows

    def wide_copy(place, slot):
        lanes = pl.ds(pl.multiple_of(lax.rem(place, depth), wide_cut), wide_cut)
        return pltpu.make_async_copy(
            wide_stage.at[slot], grad_gate_up_ref.at[lax.div(place, depth), :, :, lanes], wide_sem.at[slot])

    def wide_gradient(u, j):
        place = (j * per + u) * wide_cut

        @pl.when(place < width)
        def _():
            pl.when(j > 0)(lambda: wide_copy(0, u).wait())
            lanes = pl.ds(pl.multiple_of(place, wide_cut), wide_cut)
            x = xs_ref[:, :, lanes].reshape(tokens, wide_cut).T
            for c in range(2):
                wide_stage[u, c] = dot_nn(x, grads_ref[c].reshape(tokens, hidden_units)).T.astype(jnp.bfloat16)
            wide_copy(place, u).start()

    def down_copy(place, size):
        return pltpu.make_async_copy(down_stage.at[:, pl.ds(0, size)], grad_down_ref.at[:, pl.ds(place, size)], down_sem)

    def down_gradient(index):
        place, size = places[index]
        if index > 0:
            down_copy(*places[index - 1]).wait()
        low = hidden_ref[:, :, place:place + size].reshape(tokens, size).T
        for a in range(0, width, cut):
            down_stage[a // depth, :size, a % depth:a % depth + cut] = dot_nn(low, cots_ref[:, :, a:a + cut].reshape(tokens, cut)).astype(jnp.bfloat16)
        down_copy(place, size).start()

    def two(j, _):
        k = near(n - 1 - j, m, n)
        partials(k, 1)
        pl.when(j < n - 1)(lambda: halves[1].pass_on(k, acc_ref.at[1, core]))
        for u in range(per):
            wide_gradient(u, j)
        for index in range(len(places)):
            pl.when(j == index)(functools.partial(down_gradient, index))
        return 0

    own = acc_ref.at[0, core]

    def settle(h):
        def consume(at, total):
            here = pl.ds(pl.multiple_of(h * half + at.start, at.size), at.size)
            back, gain, shift = norm_backward(middle_ref[here, :], norm_ref[2:3, :], total)
            grad_middle_ref[here, :] = cots_ref[g.t, here, :].astype(jnp.float32) + back
            sums_ref[0:1, :] += gain
            sums_ref[1:2, :] += shift

        halves[h].settle(acc_ref.at[h, core], consume)

    sums_ref[...] = jnp.zeros(sums_ref.shape, jnp.float32)
    settle(0)
    lax.fori_loop(0, n, two, 0)
    settle(1)
    for u in range(per):
        wide_copy(0, u).wait()
    down_copy(*places[-1]).wait()
    g.finish()

    def sent(k, _):
        halves[1].side(k).wait_send()
        for h in range(2):
            halves[h].finish_line(k)
        return 0

    lax.fori_loop(0, n, sent, 0)


def mlp(x, cots, gate_up, down, middle, norms, n, number, pieces=4):
    rows, width = x.shape
    group_count, hidden, depth = down.shape
    half, part = rows // 2, pieces // 2
    f32, low = jnp.float32, jnp.bfloat16
    shape = jax.ShapeDtypeStruct
    anywhere = pl.BlockSpec(memory_space=pl.ANY)
    wide_cut = min(256, depth)
    per = -(-(width // wide_cut) // n)
    dma = pltpu.SemaphoreType.DMA
    return pl.pallas_call(functools.partial(mlp_kernel, n, pieces),
        out_shape=(shape((2 * n, rows, hidden), low), shape((rows, width), f32),
                   shape((2, width), f32), shape(gate_up.shape, low), shape(down.shape, low)),
        in_specs=[VM] + [anywhere] * 4 + [VM], out_specs=(VM,) * 3 + (anywhere,) * 2,
        scratch_shapes=[
            pltpu.VMEM((2 * n, rows, width), low), pltpu.VMEM(gate_up.shape, low), pltpu.VMEM(down.shape, low), pltpu.VMEM((rows, width), f32),
            pltpu.VMEM((2 * n, rows, width), low), pltpu.VMEM((2, 2 * n, rows, hidden), low), dma((4,)),
            pltpu.VMEM((2, 2, half, width), f32), pltpu.VMEM((n, half, width), low), pltpu.VMEM((2, n, half, width), low),
            pltpu.VMEM((2, n + 1, half, width), low), dma((2, 2, n)), dma((2, n * part)), dma((2, (n + 1) * part)),
            dma((5, n * pieces)), pltpu.VMEM((per, 2, hidden, wide_cut), low), pltpu.VMEM((group_count, min(256, hidden), depth), low),
            dma((per,)), dma,
        ],
        compiler_params=params(number), cost_estimate=lasting(140), name="mlp")(x, cots, gate_up, down, middle, norms)


def down_kernel(n, pieces, hidden_ref, down_ref, middle_ref, grad_ref, out_ref, mixed_ref, wide_ref, low_ref, block_ref, back_ref, grad_out_ref, wide_parts, low_parts,
                local_sems, share_send, share_recv, xs_ref, x_ref, acc_ref, side_out, side_in, line_in, side_sems, line_send, line_recv, gather_sems):
    group_count, _, depth = down_ref.shape
    greet_all(n, group_count)
    grads = Exchange(group_count, ((wide_ref, wide_parts), (low_ref, low_parts)), local_sems, share_send, share_recv)
    g = Gather(n, x_ref, xs_ref, gather_sems, pieces)
    s = Scatter(n, pieces, side_out, side_in, line_in, side_sems, line_send, line_recv)
    x_ref[...] = grad_ref[...].astype(jnp.bfloat16)
    g.start()
    grads.start()
    xs_ref[g.t] = x_ref[...]
    m, core = s.m, s.core
    width = group_count * depth
    cut = min(512, depth)

    def one(j, _):
        k = near(n - 1 - j, m, n)
        for a in range(0, width, cut):
            s.side_out[k, :, a:a + cut] = dot_nn(hidden_ref[2 * k + 1 - core], down_ref[a // depth, :, a % depth:a % depth + cut]).astype(jnp.bfloat16)
        s.side(k).start()
        for a in range(0, width, cut):
            acc_ref[:, a:a + cut] = dot_nn(hidden_ref[2 * k + core], down_ref[a // depth, :, a % depth:a % depth + cut])
        pl.when(j < n - 1)(lambda: s.pass_on(k, acc_ref, lambda p: g.arrive(j + 1, (p,))))
        return 0

    lax.fori_loop(0, n, one, 0)

    def consume(at, total):
        block_ref[at, :] = (middle_ref[at, :] + total).astype(jnp.bfloat16)

    s.settle(acc_ref, consume)

    def last(k, _):
        g.side_wait(k)
        for c in range(2):
            back_ref[2 * k + c] = dot_nt(xs_ref[2 * k + c], out_ref[...]).astype(jnp.bfloat16)
        return 0

    lax.fori_loop(0, n, last, 0)
    flipped = mixed_ref[...].T
    for a in range(0, width, cut):
        grad_out_ref[a // depth, :, a % depth:a % depth + cut] = dot_nn(
            flipped, xs_ref[:, :, a:a + cut].reshape(mixed_ref.shape[0], cut)).astype(jnp.bfloat16)
    g.finish()
    s.finish()
    grads.finish()


def down_branch(hidden, down, middle, x, out, mixed, wide, narrow, n, number, pieces=4):
    rows, width = x.shape
    f32, low = jnp.float32, jnp.bfloat16
    return pl.pallas_call(functools.partial(down_kernel, n, pieces),
        out_shape=(jax.ShapeDtypeStruct((rows, width), low), jax.ShapeDtypeStruct((2 * n, rows, out.shape[0]), low),
                   jax.ShapeDtypeStruct((down.shape[0], out.shape[0], down.shape[2]), low),
                   jax.ShapeDtypeStruct(wide.shape, low), jax.ShapeDtypeStruct(narrow.shape, low)),
        in_specs=[VM] * 6 + [ANYWHERE] * 2, out_specs=(VM,) * 3 + (ANYWHERE,) * 2,
        scratch_shapes=exchange_scratch(2, down.shape[0]) + [pltpu.VMEM((2 * n, rows, width), low), pltpu.VMEM((rows, width), low), pltpu.VMEM((rows, width), f32)] + scatter_scratch(n, pieces, rows, width) + [pltpu.SemaphoreType.DMA((5, n * pieces))],
        compiler_params=params(number), cost_estimate=lasting(115), name="down_branch")(hidden, down, middle, x, out, mixed, wide, narrow)


def backward_kernel(n, pieces, length_ref, q_ref, k_ref, v_ref, kt_ref, o_ref, lse_ref, do_ref,
                    keep_ref, ahead_ref, behind_ref, w_ref, x_ref, middle_ref, norm_ref, xs_hbm, low_ref,
                    result_ref, sums_ref, bias_ref, wide_parts, low_parts,
                    dos_ref, delta_ref, dqt_ref, dk_ref, dv_ref, grad_ref, wide_ref, strips_ref, acc_ref, side_out, side_in, line_in,
                    strip_sems, side_sems, line_send, line_recv, local_sems, share_send, share_recv):
    group_count = low_ref.shape[0]
    greet_all(n, group_count)
    heads, tokens, _ = q_ref.shape
    width = heads * HEAD_DIM
    rows, features = x_ref.shape
    lane_groups = width // LANES
    per_group = LANES // HEAD_DIM
    pair = 2 * rows
    depth = features // group_count
    length = length_ref[0]
    s = Scatter(n, pieces, side_out, side_in, line_in, side_sems, line_send, line_recv)
    m, core = s.m, s.core
    grads = Exchange(group_count, ((low_ref, low_parts), (wide_ref, wide_parts)), local_sems, share_send, share_recv)
    grads.start((0,))
    strip = min(256, depth)
    strip_count = features // strip

    def strip_copy(index, slot):
        return pltpu.make_async_copy(
            xs_hbm.at[:, :, pl.ds(pl.multiple_of(index * strip, strip), strip)], strips_ref.at[slot], strip_sems.at[slot])

    for slot in range(2):
        strip_copy(slot, slot).start()
    bias_ref[...] = jnp.zeros(bias_ref.shape, jnp.float32)
    sums_ref[...] = jnp.zeros(sums_ref.shape, jnp.float32)

    def prepare(i, _):
        at = pl.ds(pl.multiple_of(i * pair, pair), pair)
        for a in range(lane_groups):
            lanes = slice(a * LANES, (a + 1) * LANES)
            grad = do_ref[at, lanes]
            for b in range(per_group):
                dos_ref[a * per_group + b, at, :] = grad[:, b * HEAD_DIM:(b + 1) * HEAD_DIM]
            both = (grad.astype(jnp.float32) * o_ref[at, lanes].astype(jnp.float32)).T
            for b in range(per_group):
                h = a * per_group + b
                delta_ref[h:h + 1, at] = jnp.sum(both[b * HEAD_DIM:(b + 1) * HEAD_DIM], axis=0, keepdims=True)
        dqt_ref[:, at] = jnp.zeros((width, pair), jnp.float32)
        for h in range(heads):
            dk_ref[h, at, :] = jnp.zeros((pair, HEAD_DIM), jnp.float32)
            dv_ref[h, at, :] = jnp.zeros((pair, HEAD_DIM), jnp.float32)
        return 0

    lax.fori_loop(0, n, prepare, 0)

    falling = 2 * m < n - 1

    def order(step):
        return jnp.where(falling, n - 1 - step, step)

    def finish_block(step):
        j = order(step)

        def tile(i, j, causal):
            at = pl.ds(pl.multiple_of(i * pair, pair), pair)
            key_start = pl.multiple_of(j * pair, pair)
            keys_at = pl.ds(key_start, pair)
            for h in range(heads):
                keys, queries, grad = k_ref[h, keys_at, :], q_ref[h, at, :], dos_ref[h, at, :]
                scores = dot_nt(keys, queries) * (score_scale * log2_e)
                scores = masked_scores(scores, key_start, i * pair, length, causal)
                p = jnp.exp2(scores - lse_ref[h:h + 1, at])
                dp = dot_nt(v_ref[h, keys_at, :], grad)
                ds = (p * (dp - delta_ref[h:h + 1, at])).astype(jnp.bfloat16)
                dv_ref[h, keys_at, :] += dot_nn(p.astype(jnp.bfloat16), grad)
                dk_ref[h, keys_at, :] += dot_nn(ds, queries)
                here = slice(h * HEAD_DIM, (h + 1) * HEAD_DIM)
                dqt_ref[here, at] += dot_nn(kt_ref[here, keys_at], ds)

        def other(u, _):
            tile(jnp.where(falling, j, j + u), jnp.where(falling, j - u, j), False)
            return 0

        tile(j, j, True)
        lax.fori_loop(1, n - step, other, 0)
        keys_at = pl.ds(pl.multiple_of(j * pair, pair), pair)
        keep, ahead, behind = keep_ref[keys_at, :], -ahead_ref[keys_at, :], -behind_ref[keys_at, :]
        for a in range(lane_groups):
            lanes = slice(a * LANES, (a + 1) * LANES)
            heads_here = range(a * per_group, (a + 1) * per_group)
            dq = dqt_ref[lanes, keys_at].T
            dk = jnp.concatenate([dk_ref[h, keys_at, :] for h in heads_here], axis=1)
            dv = jnp.concatenate([dv_ref[h, keys_at, :] for h in heads_here], axis=1)
            parts = (spin(dq * score_scale, keep, ahead, behind), spin(dk * score_scale, keep, ahead, behind), dv)
            for c in range(3):
                low = parts[c].astype(jnp.bfloat16)
                place_here = slice(c * width + a * LANES, c * width + (a + 1) * LANES)
                grad_ref[keys_at, place_here] = low
                bias_ref[:, place_here] += jnp.sum(low.astype(jnp.float32), axis=0, keepdims=True)

    cut = min(512, features)

    def partial(slot, a):
        at = pl.ds(pl.multiple_of(slot * rows, rows), rows)
        return sum(dot_nt(grad_ref[at, c * width:(c + 1) * width], w_ref[c, a:a + cut, :]) for c in range(3))

    def own_partial(k):
        for a in range(0, features, cut):
            acc_ref[:, a:a + cut] = partial(2 * k + core, a)

    def strip_gradient(index, _):
        slot = lax.rem(index, 2)
        strip_copy(index, slot).wait()
        x = strips_ref[slot].reshape(tokens, strip).T
        owner = lax.div(index * strip, depth)
        at = pl.ds(pl.multiple_of(lax.rem(index * strip, depth), strip), strip)
        for c in range(3):
            wide_ref[owner, c, at, :] = dot_nn(x, grad_ref[:, c * width:(c + 1) * width]).astype(jnp.bfloat16)
        pl.when(index + 2 < strip_count)(lambda: strip_copy(index + 2, slot).start())
        return 0

    def step(j, _):
        @pl.when(j < n)
        def _():
            finish_block(j)
            k = order(j)
            for a in range(0, features, cut):
                s.side_out[k, :, a:a + cut] = partial(2 * k + 1 - core, a).astype(jnp.bfloat16)
            s.side(k).start()

        @pl.when(j == n - 1)
        def _():
            lax.fori_loop(0, strip_count, strip_gradient, 0)
            grads.start((1,))

        def one(late, _):
            turn = jnp.where(late == 1, j - 2, j)
            k = order(turn)
            inner = ((k > m) & (m > 0)) | ((k < m) & (m < n - 1))

            @pl.when((turn >= 0) & (turn < n) & (k != m) & (inner == (late == 1)))
            def _():
                own_partial(k)
                s.pass_on(k, acc_ref)

            return 0

        lax.fori_loop(0, 2, one, 0)
        return 0

    lax.fori_loop(0, n + 2, step, 0)
    own_partial(m)

    def consume(at, total):
        back, gain, shift = norm_backward(x_ref[at, :].astype(jnp.float32), norm_ref[0:1, :], total)
        result_ref[at, :] = middle_ref[at, :] + back
        sums_ref[0:1, :] += gain
        sums_ref[1:2, :] += shift

    s.settle(acc_ref, consume)
    s.finish()
    grads.finish()


def backward(lengths, q, k, v, kt, o, lse, grad, keep, ahead, behind, w, x, grad_middle, norms, xs, narrow, n, number, pieces=4):
    rows, features = x.shape
    heads, tokens, _ = q.shape
    width = heads * HEAD_DIM
    group_count = narrow.shape[0]
    depth = features // group_count
    f32, low = jnp.float32, jnp.bfloat16
    shape = jax.ShapeDtypeStruct
    wide = (group_count, 3, depth, width)
    strip = min(256, depth)
    scatter = scatter_scratch(n, pieces, rows, features)
    return pl.pallas_call(functools.partial(backward_kernel, n, pieces),
        out_shape=(shape((rows, features), f32), shape((2, features), f32), shape((1, 3 * width), f32),
                   shape(wide, low), shape(narrow.shape, low)),
        in_specs=[pl.BlockSpec(memory_space=pltpu.SMEM)] + [VM] * 14 + [ANYWHERE] * 2,
        out_specs=(VM,) * 3 + (ANYWHERE,) * 2,
        scratch_shapes=[
            pltpu.VMEM((heads, tokens, HEAD_DIM), low), pltpu.VMEM((heads, tokens), f32), pltpu.VMEM((width, tokens), f32),
            pltpu.VMEM((heads, tokens, HEAD_DIM), f32), pltpu.VMEM((heads, tokens, HEAD_DIM), f32),
            pltpu.VMEM((tokens, 3 * width), low), pltpu.VMEM(wide, low), pltpu.VMEM((2, 2 * n, rows, strip), low),
            pltpu.VMEM((rows, features), f32),
        ] + scatter[:3] + [pltpu.SemaphoreType.DMA((2,))] + scatter[3:] + exchange_scratch(2, group_count),
        compiler_params=params(number), cost_estimate=lasting(125), name="backward",
    )(lengths, q, k, v, kt, o, lse, grad, keep, ahead, behind, w, x, grad_middle, norms, xs, narrow)


def total_kernel(x_ref, bias_ref, out_ref, bias_out_ref, parts, groups, biases, send_one, recv_one, send_two, recv_two, send_three, recv_three, send_bias, recv_bias):
    t, g = lax.axis_index("tensor"), lax.axis_index("dp")
    count, group_count = parts.shape[0], groups.shape[0]
    barrier = pltpu.get_barrier_semaphore()
    for j in range(count):
        pl.when(j != t)(lambda: pl.semaphore_signal(barrier, inc=1, device_id={"tensor": j}, device_id_type=MESH))
    for i in range(group_count):
        pl.when(i != g)(lambda: pl.semaphore_signal(barrier, inc=1, device_id={"dp": i}, device_id_type=MESH))
    pl.semaphore_wait(barrier, count + group_count - 2)

    def spread(src, dst, send, recv, at, axis, peer):
        return pltpu.make_async_remote_copy(
            src_ref=src, dst_ref=dst, send_sem=send.at[peer], recv_sem=recv.at[at], device_id={axis: peer}, device_id_type=MESH)

    def exchange(me, size, make, stay):
        for j in range(size):
            pl.when(j != me)(lambda: make(j, me).start())
        stay()
        for j in range(size):
            pl.when(j != me)(lambda: make(j, j).wait_recv())
        for j in range(size):
            pl.when(j != me)(lambda: make(j, me).wait_send())

    def keep_one():
        parts[t] = x_ref[t]

    biases[g] = bias_ref[...]
    for i in range(group_count):
        pl.when(i != g)(lambda: spread(biases.at[g], biases.at[g], send_bias, recv_bias, g, "dp", i).start())

    def keep_two():
        groups[g] = sum_of(parts)

    def sum_of(ref):
        total = ref[0]
        for j in range(1, ref.shape[0]):
            total = total + ref[j]
        return total

    exchange(t, count, lambda j, at: spread(x_ref.at[j], parts.at[at], send_one, recv_one, at, "tensor", j), keep_one)
    keep_two()
    exchange(g, group_count, lambda j, at: spread(groups.at[g], groups.at[at], send_two, recv_two, at, "dp", j), lambda: None)
    out_ref[t] = sum_of(groups)
    for i in range(group_count):
        pl.when(i != g)(lambda: spread(biases.at[g], biases.at[i], send_bias, recv_bias, i, "dp", i).wait_recv())
    bias_out_ref[...] = sum_of(biases)
    for i in range(group_count):
        pl.when(i != g)(lambda: spread(biases.at[g], biases.at[g], send_bias, recv_bias, g, "dp", i).wait_send())
    exchange(t, count, lambda j, at: spread(out_ref.at[t], out_ref.at[at], send_three, recv_three, at, "tensor", j), lambda: None)


def total_over_all(x, bias, count, group_count, number):
    rows, width = x.shape
    piece = width // count
    shape = jax.ShapeDtypeStruct((count, rows, piece), x.dtype)
    bias_shape = jax.ShapeDtypeStruct(bias.shape, bias.dtype)
    out, bias_out = pl.pallas_call(
        total_kernel, out_shape=(shape, bias_shape), in_specs=[VM] * 2, out_specs=(VM,) * 2,
        scratch_shapes=[
            pltpu.VMEM((count, rows, piece), x.dtype), pltpu.VMEM((group_count, rows, piece), x.dtype),
            pltpu.VMEM((group_count,) + bias.shape, bias.dtype),
            pltpu.SemaphoreType.DMA((count,)), pltpu.SemaphoreType.DMA((count,)),
            pltpu.SemaphoreType.DMA((group_count,)), pltpu.SemaphoreType.DMA((group_count,)),
            pltpu.SemaphoreType.DMA((count,)), pltpu.SemaphoreType.DMA((count,)),
            pltpu.SemaphoreType.DMA((group_count,)), pltpu.SemaphoreType.DMA((group_count,)),
        ],
        compiler_params=params(number), cost_estimate=lasting(12), name="total_over_all",
    )(jnp.transpose(x.reshape(rows, count, piece), (1, 0, 2)), bias)
    return jnp.transpose(out, (1, 0, 2)).reshape(rows, width), bias_out


def local(
    inputs,
    cotangent,
    lengths,
    positions,
    qkv_master,
    gate_up_master,
    out_master,
    down_master,
    bias_master,
    norm_master,
    qkv_first,
    gate_up_first,
    out_first,
    down_first,
    bias_first,
    norm_first,
    qkv_second,
    gate_up_second,
    out_second,
    down_second,
    bias_second,
    norm_second,
):
    tensor_count = lax.axis_size("tensor")
    local_tokens = inputs.shape[0]
    group_tokens = local_tokens * tensor_count
    row_count = lengths.shape[0]
    row_length = group_tokens // row_count
    heads_here = bias_master.shape[1]
    width_here = heads_here * HEAD_DIM
    own_start = lax.axis_index("tensor") * local_tokens
    chips = tensor_count // 2
    gate_up_copy, down_copy = (
        lax.all_gather(jnp.swapaxes(gate_up_master, 1, 2).astype(jnp.bfloat16), "dp", axis=0, tiled=False),
        lax.all_gather(down_master.astype(jnp.bfloat16), "dp", axis=0, tiled=False),
    )
    group = lax.axis_index("dp")
    group_count = lax.axis_size("dp")
    group_index = own_start + jnp.arange(local_tokens, dtype=jnp.int32)
    row_of = group_index // row_length
    slot_of = group_index % row_length
    row_match = row_of[:, None] == jnp.arange(row_count, dtype=jnp.int32)[None, :]
    length_of = jnp.sum(jnp.where(row_match, lengths[None, :], 0), axis=1)
    valid = slot_of < length_of
    grad_low = jnp.where(valid[:, None], cotangent, jnp.zeros_like(cotangent))
    own_dims = jnp.arange(HEAD_DIM) // (HEAD_DIM // group_count) == group
    bias_row = jnp.where(own_dims, jnp.tile(bias_master, (1, 1, group_count)), 0.0).reshape(3, width_here)
    bias_row = jnp.concatenate([bias_row, jnp.zeros((5, width_here), jnp.float32)], axis=0)
    (
        gathered_one, qkv_copy, out_copy, queries, keys, values, keys_flipped, mixed_low, log_totals,
        keep, ahead, behind, middle, normed_two, gathered_grad,
    ) = forward(
        lengths, positions, inputs, norm_master, qkv_master, out_master, bias_row, grad_low, chips, group_count, 0
    )
    hidden, grad_middle, sums_two, grad_gate_up_w, grad_down = mlp(
        normed_two, gathered_grad, gate_up_copy, down_copy, middle, norm_master, chips, 2
    )
    block_output, grad_mixed, grad_out_w, gate_up_parts, down_parts = down_branch(
        hidden, down_copy, middle, grad_middle, out_copy, mixed_low, grad_gate_up_w, grad_down, chips, 3
    )
    grad_mixed = grad_mixed.reshape(group_tokens, width_here)
    input_grad, sums_one, grad_bias, qkv_parts, out_parts = backward(
        lengths, queries, keys, values, keys_flipped, mixed_low, log_totals, grad_mixed, keep, ahead, behind,
        qkv_copy, inputs, grad_middle, norm_master, gathered_one, grad_out_w, chips, 4
    )
    gate_up_grad, down_grad, out_grad = sum_parts(gate_up_parts), sum_parts(down_parts), sum_parts(out_parts)
    qkv_grad = sum_parts(qkv_parts)
    norm_grads, bias_grad = total_over_all(
        jnp.concatenate([sums_one, sums_two], axis=0), grad_bias, tensor_count, group_count, 5
    )
    bias_grad = lax.dynamic_slice_in_dim(
        bias_grad.reshape(3, heads_here, HEAD_DIM), group * bias_master.shape[2], bias_master.shape[2], axis=2
    )
    qkv_new = adamw(qkv_master, qkv_first, qkv_second, qkv_grad, 2.0 / math.sqrt(D), decay_rate)
    gate_up_new = tuple(
        jnp.swapaxes(item, 1, 2)
        for item in adamw(
            jnp.swapaxes(gate_up_master, 1, 2),
            jnp.swapaxes(gate_up_first, 1, 2),
            jnp.swapaxes(gate_up_second, 1, 2),
            gate_up_grad,
            2.0 / math.sqrt(D),
            decay_rate,
        )
    )
    out_new = adamw(
        out_master, out_first, out_second, out_grad, 16.0 / math.sqrt(HEADS * HEAD_DIM), decay_rate
    )
    down_new = adamw(
        down_master, down_first, down_second, down_grad, 6.0 / math.sqrt(FF), decay_rate
    )
    bias_new = adamw(bias_master, bias_first, bias_second, bias_grad, 1.5, 0.0)
    norm_new = adamw(norm_master, norm_first, norm_second, norm_grads, 0.7, 0.0)
    return (
        block_output,
        input_grad,
        qkv_new[0],
        qkv_new[1],
        qkv_new[2],
        gate_up_new[0],
        gate_up_new[1],
        gate_up_new[2],
        out_new[0],
        out_new[1],
        out_new[2],
        down_new[0],
        down_new[1],
        down_new[2],
        bias_new[0],
        bias_new[1],
        bias_new[2],
        norm_new[0],
        norm_new[1],
        norm_new[2],
    )


def solution(mesh):
    return jax.shard_map(
        local,
        mesh=mesh,
        in_specs=(
            P(("dp", "tensor"), None),
            P(("dp", "tensor"), None),
            P("dp"),
            P("dp"),
            P(None, "dp", "tensor"),
            P(None, "dp", "tensor"),
            P("tensor", "dp"),
            P("tensor", "dp"),
            P(None, "tensor", "dp"),
            P(),
            P(None, "dp", "tensor"),
            P(None, "dp", "tensor"),
            P("tensor", "dp"),
            P("tensor", "dp"),
            P(None, "tensor", "dp"),
            P(),
            P(None, "dp", "tensor"),
            P(None, "dp", "tensor"),
            P("tensor", "dp"),
            P("tensor", "dp"),
            P(None, "tensor", "dp"),
            P(),
        ),
        out_specs=(
            P(("dp", "tensor"), None),
            P(("dp", "tensor"), None),
            P(None, "dp", "tensor"),
            P(None, "dp", "tensor"),
            P(None, "dp", "tensor"),
            P(None, "dp", "tensor"),
            P(None, "dp", "tensor"),
            P(None, "dp", "tensor"),
            P("tensor", "dp"),
            P("tensor", "dp"),
            P("tensor", "dp"),
            P("tensor", "dp"),
            P("tensor", "dp"),
            P("tensor", "dp"),
            P(None, "tensor", "dp"),
            P(None, "tensor", "dp"),
            P(None, "tensor", "dp"),
            P(),
            P(),
            P(),
        ),
        check_vma=False,
    )
```

```python
import functools
import math

import jax
import jax.numpy as jnp
from jax import lax
from jax.experimental import pallas as pl
from jax.experimental.pallas import tpu as pltpu
from jax.sharding import PartitionSpec as P

D = 2048
HEADS = 32
HEAD_DIM = 64
ROTARY = 16
FF = 5632


norm_eps = 1e-05
beta_one = 0.9
beta_two = 0.95
adam_eps = 1e-08
adam_steps = 10
decay_rate = 0.1
rope_base = 10000.0
score_scale = 0.125
mask_fill = -1e30
log2_e = math.log2(math.e)
LANES = 128
VMEM_LIMIT = 62 * 1024 * 1024


def norm_forward(values, gain_row, shift_row):
    average = jnp.mean(values, axis=-1, keepdims=True)
    centred = values - average
    spread = jnp.mean(centred * centred, axis=-1, keepdims=True)
    return centred * lax.rsqrt(spread + norm_eps) * gain_row + shift_row


def norm_backward(values, gain_row, grad_rows):
    average = jnp.mean(values, axis=-1, keepdims=True)
    centred = values - average
    spread = jnp.mean(centred * centred, axis=-1, keepdims=True)
    inverse = lax.rsqrt(spread + norm_eps)
    normal = centred * inverse
    grad_normal = grad_rows * gain_row
    grad_values = inverse * (
        grad_normal
        - jnp.mean(grad_normal, axis=-1, keepdims=True)
        - normal * jnp.mean(grad_normal * normal, axis=-1, keepdims=True)
    )
    return (
        grad_values,
        jnp.sum(grad_rows * normal, axis=0, keepdims=True),
        jnp.sum(grad_rows, axis=0, keepdims=True),
    )


def adamw(weight_old, first_old, second_old, gradient, step_rate, decay_part):
    first_new = beta_one * first_old + (1.0 - beta_one) * gradient
    second_new = beta_two * second_old + (1.0 - beta_two) * gradient * gradient
    correct_one = 1.0 - beta_one**adam_steps
    correct_two = 1.0 - beta_two**adam_steps
    update = first_new / correct_one / (jnp.sqrt(second_new / correct_two) + adam_eps)
    return (weight_old - step_rate * (update + decay_part * weight_old), first_new, second_new)


def spin(x, keep, ahead, behind):
    return x * keep + pltpu.roll(x, LANES - ROTARY // 2, 1) * ahead + pltpu.roll(x, ROTARY // 2, 1) * behind


def dot_nt(a, b):
    return lax.dot_general(a, b, (((1,), (1,)), ((), ())), preferred_element_type=jnp.float32)


def dot_nn(a, b):
    return lax.dot_general(a, b, (((1,), (0,)), ((), ())), preferred_element_type=jnp.float32)


def masked_scores(s, key_start, query_start, length, causal):
    key_slots = key_start + lax.broadcasted_iota(jnp.int32, s.shape, 0)
    allowed = key_slots < length
    if causal:
        query_slots = query_start + lax.broadcasted_iota(jnp.int32, s.shape, 1)
        allowed = allowed & (key_slots <= query_slots)
    return jnp.where(allowed, s, mask_fill)


VM = pl.BlockSpec(memory_space=pltpu.VMEM)
ANYWHERE = pl.BlockSpec(memory_space=pl.ANY)
MESH = pl.DeviceIdType.MESH


def params(number):
    return pltpu.CompilerParams(collective_id=number, has_side_effects=True, vmem_limit_bytes=VMEM_LIMIT)


def lasting(us):
    return pl.CostEstimate(flops=int(us * 1.1e9), bytes_accessed=0, transcendentals=0)


def place():
    t = lax.axis_index("tensor")
    return t, lax.rem(t, 2), lax.div(t, 2)


def greet(n):
    t, core, chip = place()
    barrier = pltpu.get_barrier_semaphore()

    def hail(index):
        pl.semaphore_signal(barrier, inc=1, device_id={"tensor": index}, device_id_type=MESH)

    hail(t + 1 - 2 * core)
    pl.when(chip > 0)(lambda: hail(t - 2))
    pl.when(chip < n - 1)(lambda: hail(t + 2))
    pl.semaphore_wait(barrier, 1 + jnp.minimum(chip, 1) + jnp.minimum(n - 1 - chip, 1))


def near(j, m, n):
    below, above = m, n - 1 - m
    both = jnp.minimum(below, above)
    half = lax.div(j + 1, 2)
    inside = m + jnp.where(lax.rem(j, 2) == 1, -half, half)
    outside = m + jnp.where(above > below, j - both, both - j)
    return jnp.where(j <= 2 * both, inside, outside)


class Gather:
    def __init__(self, n, own, buf, sems, pieces):
        self.n, self.own, self.buf, self.pieces = n, own, buf, pieces
        self.up, self.down, self.side, self.line_in, self.side_in = [sems.at[i] for i in range(5)]
        self.t, self.core, self.m = place()
        self.sibling = self.t + 1 - 2 * self.core
        self.rows = own.shape[0] // pieces

    def copy(self, src, k, p, core, send, recv, target):
        at = pl.ds(pl.multiple_of(p * self.rows, self.rows), self.rows)
        index = k * self.pieces + p
        return pltpu.make_async_remote_copy(
            src_ref=src.at[at], dst_ref=self.buf.at[2 * k + core, at], send_sem=send.at[index],
            recv_sem=recv.at[index], device_id={"tensor": target}, device_id_type=MESH)

    def to_up(self, k, p, src):
        return self.copy(src, k, p, self.core, self.up, self.line_in, self.t + 2)

    def to_down(self, k, p, src):
        return self.copy(src, k, p, self.core, self.down, self.line_in, self.t - 2)

    def to_side(self, k, p, src):
        return self.copy(src, k, p, self.core, self.side, self.side_in, self.sibling)

    def start(self, which=None):
        m = self.m
        for p in range(self.pieces) if which is None else which:
            pl.when(m < self.n - 1)(lambda: self.to_up(m, p, self.own).start())
            pl.when(m > 0)(lambda: self.to_down(m, p, self.own).start())
            self.to_side(m, p, self.own).start()

    def arrive(self, d, which=None):
        m = self.m
        lo, hi = m - d, m + d
        for p in range(self.pieces) if which is None else which:
            @pl.when(lo >= 0)
            def _():
                src = self.buf.at[2 * lo + self.core]
                self.to_up(lo, p, src).wait_recv()
                pl.when(m < self.n - 1)(lambda: self.to_up(lo, p, src).start())
                self.to_side(lo, p, src).start()

            @pl.when(hi < self.n)
            def _():
                src = self.buf.at[2 * hi + self.core]
                self.to_down(hi, p, src).wait_recv()
                pl.when(m > 0)(lambda: self.to_down(hi, p, src).start())
                self.to_side(hi, p, src).start()

    def side_wait(self, k, which=None):
        for p in range(self.pieces) if which is None else which:
            self.copy(self.own, k, p, 1 - self.core, self.side, self.side_in, self.sibling).wait_recv()

    def finish(self):
        m = self.m

        def one(k, _):
            for p in range(self.pieces):
                pl.when((k <= m) & (m < self.n - 1))(lambda: self.to_up(k, p, self.own).wait_send())
                pl.when((k >= m) & (m > 0))(lambda: self.to_down(k, p, self.own).wait_send())
                self.to_side(k, p, self.own).wait_send()
            return 0

        lax.fori_loop(0, self.n, one, 0)


class Scatter:
    def __init__(self, n, pieces, side_out, side_in, line_in, side_sems, line_send, line_recv):
        self.n, self.pieces = n, pieces
        self.side_out, self.side_in, self.line_in = side_out, side_in, line_in
        self.side_send, self.side_recv = side_sems.at[0], side_sems.at[1]
        self.line_send, self.line_recv = line_send, line_recv
        self.t, self.core, self.m = place()
        self.sibling = self.t + 1 - 2 * self.core
        self.rows = side_out.shape[1] // pieces
        self.step = min(32, self.rows)

    def side(self, k):
        return pltpu.make_async_remote_copy(
            src_ref=self.side_out.at[k], dst_ref=self.side_in.at[k], send_sem=self.side_send.at[k],
            recv_sem=self.side_recv.at[k], device_id={"tensor": self.sibling}, device_id_type=MESH)

    def line(self, k, p, slot, target):
        at = pl.ds(pl.multiple_of(p * self.rows, self.rows), self.rows)
        return pltpu.make_async_remote_copy(
            src_ref=self.side_in.at[k, at], dst_ref=self.line_in.at[slot, at],
            send_sem=self.line_send.at[k * self.pieces + p], recv_sem=self.line_recv.at[slot * self.pieces + p],
            device_id={"tensor": target}, device_id_type=MESH)

    def each(self, p, body):
        def one(i, _):
            body(pl.ds(pl.multiple_of(p * self.rows + i * self.step, self.step), self.step))
            return 0

        lax.fori_loop(0, self.rows // self.step, one, 0)

    def pass_on(self, k, own, between=None):
        m, n = self.m, self.n
        self.side(k).wait_recv()
        inner = ((k > m) & (m > 0)) | ((k < m) & (m < n - 1))

        def one(p, _):
            @pl.when(inner)
            def _():
                self.line(k, p, k, self.t).wait_recv()

                def add(at):
                    total = own[at, :] + self.side_in[k, at, :].astype(jnp.float32) + self.line_in[k, at, :].astype(jnp.float32)
                    self.side_in[k, at, :] = total.astype(jnp.bfloat16)

                self.each(p, add)

            @pl.when(jnp.logical_not(inner))
            def _():
                def add(at):
                    self.side_in[k, at, :] = (own[at, :] + self.side_in[k, at, :].astype(jnp.float32)).astype(jnp.bfloat16)

                self.each(p, add)

            pl.when(k > m)(lambda: self.line(k, p, k, self.t + 2).start())
            pl.when(k < m)(lambda: self.line(k, p, jnp.where(k == m - 1, n, k), self.t - 2).start())
            if between is not None:
                between(p)
            return 0

        lax.fori_loop(0, self.pieces, one, 0)

    def settle(self, own, consume):
        m, n = self.m, self.n
        self.side(m).wait_recv()

        def one(p, _):
            def first(at):
                own[at, :] += self.side_in[m, at, :].astype(jnp.float32)

            self.each(p, first)

            def more(slot):
                self.line(m, p, slot, self.t).wait_recv()

                def add(at):
                    own[at, :] += self.line_in[slot, at, :].astype(jnp.float32)

                self.each(p, add)

            pl.when(m > 0)(lambda: more(m))
            pl.when(m < n - 1)(lambda: more(n))
            self.each(p, lambda at: consume(at, own[at, :]))
            return 0

        lax.fori_loop(0, self.pieces, one, 0)

    def finish(self):
        def one(k, _):
            self.side(k).wait_send()
            self.finish_line(k)
            return 0

        lax.fori_loop(0, self.n, one, 0)

    def finish_line(self, k):
        @pl.when(k != self.m)
        def _():
            for p in range(self.pieces):
                self.line(k, p, k, self.t).wait_send()


def scatter_scratch(n, pieces, rows, width):
    return [
        pltpu.VMEM((n, rows, width), jnp.bfloat16), pltpu.VMEM((n, rows, width), jnp.bfloat16),
        pltpu.VMEM((n + 1, rows, width), jnp.bfloat16),
        pltpu.SemaphoreType.DMA((2, n)), pltpu.SemaphoreType.DMA((n * pieces,)), pltpu.SemaphoreType.DMA(((n + 1) * pieces,)),
    ]


class Exchange:
    def __init__(self, group_count, pairs, local_sems, send, recv):
        self.group, self.count, self.pairs = lax.axis_index("dp"), group_count, pairs
        self.local_sems, self.send, self.recv = local_sems, send, recv

    def stay(self, index):
        src, dst = self.pairs[index]
        return pltpu.make_async_copy(src.at[self.group], dst.at[self.group], self.local_sems.at[index])

    def copy(self, index, peer, slot):
        src, dst = self.pairs[index]
        return pltpu.make_async_remote_copy(
            src_ref=src.at[peer], dst_ref=dst.at[slot], send_sem=self.send.at[index, peer],
            recv_sem=self.recv.at[index, slot], device_id={"dp": peer}, device_id_type=MESH)

    def others(self, body, which=None):
        for index in range(len(self.pairs)) if which is None else which:
            for i in range(self.count):
                pl.when(i != self.group)(lambda: body(index, i))

    def start(self, which=None):
        self.others(lambda index, i: self.copy(index, i, self.group).start(), which)
        for index in range(len(self.pairs)) if which is None else which:
            self.stay(index).start()

    def finish(self):
        for index in range(len(self.pairs)):
            self.stay(index).wait()
        self.others(lambda index, i: self.copy(index, i, i).wait_recv())
        self.others(lambda index, i: self.copy(index, i, self.group).wait_send())


def exchange_scratch(pairs, group_count):
    dma = pltpu.SemaphoreType.DMA
    return [dma((pairs,)), dma((pairs, group_count)), dma((pairs, group_count))]


def greet_all(n, group_count):
    t, core, chip = place()
    g = lax.axis_index("dp")
    barrier = pltpu.get_barrier_semaphore()

    def hail(index):
        pl.semaphore_signal(barrier, inc=1, device_id={"tensor": index}, device_id_type=MESH)

    hail(t + 1 - 2 * core)
    pl.when(chip > 0)(lambda: hail(t - 2))
    pl.when(chip < n - 1)(lambda: hail(t + 2))
    for i in range(group_count):
        pl.when(i != g)(lambda: pl.semaphore_signal(barrier, inc=1, device_id={"dp": i}, device_id_type=MESH))
    pl.semaphore_wait(barrier, group_count + jnp.minimum(chip, 1) + jnp.minimum(n - 1 - chip, 1))


def forward_kernel(n, group_count, pieces, length_ref, place_ref, frequency_ref, x_ref, norm_ref, qkv_ref, out_ref, bias_ref, cot_ref, wide_hbm, down_hbm,
                   xs_out, wq_out, wo_ref, q_out, k_out, v_out, kt_out, mixed_ref, lse_ref, keep_out, ahead_out, behind_out,
                   middle_ref, normed_ref, cots_ref, wide_copy, down_copy,
                   xs_ref, wq_ref, q_ref, k_ref, v_ref, kt_ref, keep_ref, ahead_ref, behind_ref, keep_sems,
                   wide_stage, low_stage, stage_sems, weight_send, weight_recv,
                   vt_ref, biases_ref, acc_ref, side_out, side_in, line_in, side_sems, line_send, line_recv,
                   first_sems, cot_sems, share_send, share_recv):
    greet_all(n, group_count)
    heads, total_rows, _ = q_ref.shape
    rows, features = x_ref.shape
    width = heads * HEAD_DIM
    lane_groups = width // LANES
    per_group = LANES // HEAD_DIM
    block = rows
    length = length_ref[0]
    group = lax.axis_index("dp")
    t, core, m = place()
    first = Gather(n, xs_ref.at[t], xs_ref, first_sems, pieces)
    cots = Gather(n, cot_ref, cots_ref, cot_sems, pieces)
    s = Scatter(n, pieces, side_out, side_in, line_in, side_sems, line_send, line_recv)
    step = 32

    def first_norm(i, _):
        at = pl.ds(pl.multiple_of(i * step, step), step)
        xs_ref[t, at, :] = norm_forward(x_ref[at, :].astype(jnp.float32), norm_ref[0:1, :], norm_ref[1:2, :]).astype(jnp.bfloat16)
        return 0

    lax.fori_loop(0, rows // step, first_norm, 0)
    first.start()
    depth = features // group_count
    mine = pl.ds(pl.multiple_of(group * depth, depth), depth)
    for c in range(3):
        wq_ref[c, mine, :] = qkv_ref[c].astype(jnp.bfloat16)
    wo_ref[:, mine] = out_ref[...].astype(jnp.bfloat16)
    biases_ref[group] = bias_ref[...].astype(jnp.bfloat16).astype(jnp.float32)

    def share(kind, src, owner, peer):
        ref = src(owner)
        return pltpu.make_async_remote_copy(
            src_ref=ref, dst_ref=ref, send_sem=share_send.at[kind, peer], recv_sem=share_recv.at[kind, owner],
            device_id={"dp": peer}, device_id_type=MESH)

    def part(owner):
        return pl.ds(pl.multiple_of(owner * depth, depth), depth)

    kinds = (lambda o: wq_ref.at[:, part(o), :], lambda o: biases_ref.at[o], lambda o: wo_ref.at[:, part(o)])
    for kind in range(3):
        for i in range(group_count):
            pl.when(i != group)(lambda: share(kind, kinds[kind], group, i).start())

    half_units = wide_stage.shape[0]
    units = wide_hbm.shape[1]
    chunks = [(wide_hbm.at[c], wide_copy.at[group, c], u) for c in range(2) for u in range(0, units, half_units)]
    chunks += [(down_hbm, down_copy.at[group], u) for u in range(0, units, half_units)]

    def chunk_in(index):
        src, _, u = chunks[index]
        return pltpu.make_async_copy(src.at[pl.ds(u, half_units)], wide_stage, stage_sems.at[0])

    def chunk_out(index):
        _, dst, u = chunks[index]
        return pltpu.make_async_copy(low_stage, dst.at[pl.ds(u, half_units)], stage_sems.at[1])

    chunk_in(0).start()
    for index in range(len(chunks)):
        chunk_in(index).wait()
        if index > 0:
            chunk_out(index - 1).wait()
        low_stage[...] = wide_stage[...].astype(jnp.bfloat16)
        if index + 1 < len(chunks):
            chunk_in(index + 1).start()
        chunk_out(index).start()
    chunk_out(len(chunks) - 1).wait()

    def weight(kind, peer, slot):
        ref = (wide_copy, down_copy)[kind]
        return pltpu.make_async_remote_copy(
            src_ref=ref.at[group], dst_ref=ref.at[slot], send_sem=weight_send.at[kind, peer],
            recv_sem=weight_recv.at[kind, slot], device_id={"dp": peer}, device_id_type=MESH)

    def weights(body):
        for kind in range(2):
            for i in range(group_count):
                pl.when(i != group)(lambda: body(kind, i))

    def tables(i, _):
        at = pl.ds(pl.multiple_of(i * block, block), block)
        angles = jnp.broadcast_to(place_ref[:, at], (LANES, block)).T * frequency_ref[...]
        cosine, sine = jnp.cos(angles), jnp.sin(angles)
        dim = lax.rem(lax.broadcasted_iota(jnp.int32, (block, LANES), 1), HEAD_DIM)
        none = jnp.zeros((block, LANES), jnp.float32)
        keep_ref[at, :] = jnp.where(dim < ROTARY, cosine, 1.0)
        ahead_ref[at, :] = jnp.where(dim < ROTARY // 2, -sine, none)
        behind_ref[at, :] = jnp.where((dim >= ROTARY // 2) & (dim < ROTARY), sine, none)
        return 0

    lax.fori_loop(0, total_rows // block, tables, 0)
    def project(slot):
        at = pl.ds(pl.multiple_of(slot * block, block), block)
        keep, ahead, behind = keep_ref[at, :], ahead_ref[at, :], behind_ref[at, :]
        x = xs_ref[slot]
        for c in range(3):
            wide = dot_nn(x, wq_ref[c]) + biases_ref[group_count, c:c + 1, :]
            for a in range(lane_groups):
                lanes = slice(a * LANES, (a + 1) * LANES)
                part_wide = wide[:, lanes]
                if c < 2:
                    part_wide = spin(part_wide, keep, ahead, behind)
                if c == 1:
                    kt_ref[lanes, at] = part_wide.T.astype(jnp.bfloat16)
                if c == 2:
                    vt_ref[lanes, at] = part_wide.T.astype(jnp.bfloat16)
                for b in range(per_group):
                    (q_ref, k_ref, v_ref)[c][a * per_group + b, at, :] = part_wide[:, b * HEAD_DIM:(b + 1) * HEAD_DIM].astype(jnp.bfloat16)

    def ring(d, _):
        def one(q, _):
            other, above = lax.div(q, 2), lax.rem(q, 2)
            k = jnp.where(above == 1, m + d, m - d)

            @pl.when((k >= 0) & (k < n) & ((d > 0) | (above == 0)))
            def _():
                pl.when(other == 1)(lambda: first.side_wait(k))
                project(2 * k + jnp.where(other == 1, 1 - core, core))

            return 0

        lax.fori_loop(0, 4, one, 0)
        pl.when(d == n - 2)(lambda: first.arrive(n - 1))
        return 0

    for d in range(1, n - 1):
        first.arrive(d)
    for kind in range(3):
        for i in range(group_count):
            pl.when(i != group)(lambda: share(kind, kinds[kind], i, i).wait_recv())
    bias = biases_ref[0]
    for i in range(1, group_count):
        bias = bias + biases_ref[i]
    biases_ref[group_count] = bias

    weights(lambda kind, i: weight(kind, i, group).start())
    lax.fori_loop(0, n, ring, 0)
    kept = [
        pltpu.make_async_copy(src, dst, keep_sems.at[index])
        for index, (src, dst) in enumerate((
            (xs_ref, xs_out), (wq_ref, wq_out), (q_ref, q_out), (k_ref, k_out), (v_ref, v_out), (kt_ref, kt_out),
            (keep_ref, keep_out), (ahead_ref, ahead_out), (behind_ref, behind_out)))
    ]
    for item in kept:
        item.start()
    cots.start()
    cots_ref[t] = cot_ref[...]
    pair = 2 * block

    def attend(i):
        at = pl.ds(pl.multiple_of(i * pair, pair), pair)
        queries = [q_ref[h, at, :] for h in range(heads)]

        def key_block(j, carry, kind):
            key_start = pl.multiple_of(j * pair, pair)
            keys_at = pl.ds(key_start, pair)
            out = []
            for h in range(heads):
                top, total, mixed = carry[h]
                scores = dot_nt(k_ref[h, keys_at, :], queries[h]) * (score_scale * log2_e)
                if kind > 0:
                    scores = masked_scores(scores, key_start, i * pair, length, kind == 2)
                new_top = jnp.maximum(top, jnp.max(scores, axis=0, keepdims=True))
                shrink = jnp.exp2(top - new_top)
                p = jnp.exp2(scores - new_top)
                total = total * shrink + jnp.sum(p, axis=0, keepdims=True)
                mixed = mixed * shrink + dot_nn(
                    vt_ref[h * HEAD_DIM:(h + 1) * HEAD_DIM, keys_at], p.astype(jnp.bfloat16))
                out.append((new_top, total, mixed))
            return tuple(out)

        start = tuple(
            (jnp.full((1, pair), mask_fill, jnp.float32), jnp.zeros((1, pair), jnp.float32),
             jnp.zeros((HEAD_DIM, pair), jnp.float32)) for _ in range(heads))
        carry = lax.fori_loop(0, i, lambda j, c: key_block(j, c, 1), start)
        carry = key_block(i, carry, 2)
        for h in range(heads):
            top, total, mixed = carry[h]
            lse_ref[h:h + 1, at] = top + jnp.log2(total)
        for a in range(lane_groups):
            both = [carry[a * per_group + b][2] * (1.0 / carry[a * per_group + b][1]) for b in range(per_group)]
            mixed_ref[at, a * LANES:(a + 1) * LANES] = jnp.concatenate(both, axis=0).T.astype(jnp.bfloat16)

    cut = min(512, features)

    def branch(j, _):
        k = near(n - 1 - j, m, n)

        attend(k)

        def attended(slot):
            return mixed_ref[pl.ds(pl.multiple_of(slot * block, block), block), :]

        low = attended(2 * k + 1 - core)
        for a in range(0, features, cut):
            s.side_out[k, :, a:a + cut] = dot_nn(low, wo_ref[:, a:a + cut]).astype(jnp.bfloat16)
        s.side(k).start()
        low = attended(2 * k + core)
        for a in range(0, features, cut):
            acc_ref[:, a:a + cut] = dot_nn(low, wo_ref[:, a:a + cut])
        pl.when(j < n - 1)(lambda: s.pass_on(k, acc_ref, lambda p: cots.arrive(j + 1, (p,))))
        return 0

    lax.fori_loop(0, n, branch, 0)

    def consume(at, total):
        middle = x_ref[at, :].astype(jnp.float32) + total
        middle_ref[at, :] = middle
        normed_ref[at, :] = norm_forward(middle, norm_ref[2:3, :], norm_ref[3:4, :]).astype(jnp.bfloat16)

    s.settle(acc_ref, consume)
    for k in range(n):
        cots.side_wait(k)
    first.finish()
    cots.finish()
    s.finish()
    for kind in range(3):
        for i in range(group_count):
            pl.when(i != group)(lambda: share(kind, kinds[kind], group, i).wait_send())
    for item in kept:
        item.wait()
    weights(lambda kind, i: weight(kind, i, i).wait_recv())
    weights(lambda kind, i: weight(kind, i, group).wait_send())


def forward(lengths, positions, x, norms, qkv, out, bias, cot, wide, down, n, group_count, number, pieces=4):
    rows, features = x.shape
    width = qkv.shape[2]
    heads = width // HEAD_DIM
    total_rows = 2 * n * rows
    f32, low = jnp.float32, jnp.bfloat16
    shape = jax.ShapeDtypeStruct
    half_rot = ROTARY // 2
    frequency = rope_base ** (-(2.0 * jnp.arange(half_rot, dtype=jnp.float32)) / ROTARY)
    split = shape((heads, total_rows, HEAD_DIM), low)
    table = shape((total_rows, LANES), f32)
    gathered = shape((2 * n, rows, features), low)
    return pl.pallas_call(
        functools.partial(forward_kernel, n, group_count, pieces),
        out_shape=(gathered, shape((3, features, width), low), shape((width, features), low), split, split, split,
                   shape((width, total_rows), low), shape((total_rows, width), low), shape((heads, total_rows), f32),
                   table, table, table, shape((rows, features), f32), shape((rows, features), low), gathered,
                   shape((group_count,) + wide.shape, low), shape((group_count,) + down.shape, low)),
        in_specs=[pl.BlockSpec(memory_space=pltpu.SMEM)] + [VM] * 8 + [ANYWHERE] * 2,
        out_specs=(ANYWHERE, ANYWHERE, VM) + (ANYWHERE,) * 4 + (VM, VM) + (ANYWHERE,) * 3 + (VM,) * 3 + (ANYWHERE,) * 2,
        scratch_shapes=[
            pltpu.VMEM(item.shape, item.dtype)
            for item in (gathered, shape((3, features, width), low), split, split, split, shape((width, total_rows), low), table, table, table)
        ] + [
            pltpu.SemaphoreType.DMA((9,)), pltpu.VMEM((down.shape[0] // 2, down.shape[1]), f32), pltpu.VMEM((down.shape[0] // 2, down.shape[1]), low),
            pltpu.SemaphoreType.DMA((2,)), pltpu.SemaphoreType.DMA((2, group_count)), pltpu.SemaphoreType.DMA((2, group_count)),
            pltpu.VMEM((width, total_rows), low), pltpu.VMEM((group_count + 1, 8, width), f32), pltpu.VMEM((rows, features), f32),
        ] + scatter_scratch(n, pieces, rows, features) + [
            pltpu.SemaphoreType.DMA((5, n * pieces)), pltpu.SemaphoreType.DMA((5, n * pieces)),
            pltpu.SemaphoreType.DMA((3, group_count)), pltpu.SemaphoreType.DMA((3, group_count)),
        ],
        compiler_params=params(number), cost_estimate=lasting(200), name="forward",
    )(lengths, positions.astype(f32).reshape(1, total_rows), jnp.tile(frequency, LANES // half_rot).reshape(1, LANES),
      x, norms, qkv, out, bias, cot, wide, down)


def mlp_kernel(n, pieces, x_ref, cots_hbm, gate_up_hbm, down_hbm, middle_hbm, norm_ref,
               hidden_ref, grad_middle_ref, sums_ref, grad_gate_up_ref, grad_down_ref,
               cots_ref, gate_up_ref, down_ref, middle_ref, xs_ref, grads_ref, load_sems,
               acc_ref, side_out, side_in, line_in, side_sems, line_send, line_recv, gather_sems,
               wide_stage, down_stage, wide_sem, down_sem):
    loads = [
        pltpu.make_async_copy(src, dst, load_sems.at[i])
        for i, (src, dst) in enumerate(
            ((gate_up_hbm, gate_up_ref), (cots_hbm, cots_ref), (down_hbm, down_ref), (middle_hbm, middle_ref)))
    ]
    for load in loads:
        load.start()
    greet(n)
    g = Gather(n, x_ref, xs_ref, gather_sems, pieces)
    halves = tuple(
        Scatter(n, pieces // 2, side_out, side_in.at[h], line_in.at[h], side_sems.at[h], line_send.at[h], line_recv.at[h])
        for h in range(2))
    m, core = g.m, g.core
    rows, width = x_ref.shape
    half = rows // 2
    group_count, hidden_units, depth = down_ref.shape
    cut = min(512, depth)
    places = [(f, min(256, hidden_units - f)) for f in range(0, hidden_units, 256)]
    early, late = tuple(range(pieces // 2)), tuple(range(pieces // 2, pieces))
    g.start(early)
    xs_ref[g.t] = x_ref[...]
    for load in loads:
        load.wait()

    def work(k, h):
        both = pl.ds(2 * k, 2)
        at = slice(h * half, (h + 1) * half)
        x = xs_ref[both, at, :].reshape(2 * half, width)
        cot = cots_ref[both, at, :].reshape(2 * half, width)
        for place, size in places:
            units = slice(place, place + size)
            shape = (2, half, size)

            def product(left, right):
                return sum(dot_nt(left[:, o * depth:(o + 1) * depth], right(o)) for o in range(group_count))

            gate = product(x, lambda o: gate_up_ref[o, 0, units, :])
            up = product(x, lambda o: gate_up_ref[o, 1, units, :])
            grad_hidden = product(cot, lambda o: down_ref[o, units, :])
            sig = 1.0 / (1.0 + jnp.exp(-gate))
            silu = gate * sig
            hidden_ref[both, at, units] = (silu * up).astype(jnp.bfloat16).reshape(shape)
            grads_ref[0, both, at, units] = (grad_hidden * up * (sig * (1.0 + gate * (1.0 - sig)))).astype(jnp.bfloat16).reshape(shape)
            grads_ref[1, both, at, units] = (grad_hidden * silu).astype(jnp.bfloat16).reshape(shape)

    def work_at(d, h, which):
        def one(above, _):
            k = jnp.where(above == 1, m + d, m - d)

            @pl.when((k >= 0) & (k < n) & ((d > 0) | (above == 0)))
            def _():
                g.side_wait(k, which)
                work(k, h)

            return 0

        lax.fori_loop(0, 2, one, 0)

    def ring(d, _):
        pl.when(d > 0)(lambda: g.arrive(d, early))
        pl.when(d == n - 2)(lambda: g.start(late))
        work_at(d, 0, early)
        return 0

    lax.fori_loop(0, n, ring, 0)

    def partials(k, h):
        at = slice(h * half, (h + 1) * half)
        both = pl.ds(2 * k, 2)
        for a in range(0, width, cut):
            acc_ref[h, :, :, a:a + cut] = sum(
                dot_nn(grads_ref[c, both, at, :].reshape(2 * half, hidden_units), gate_up_ref[a // depth, c, :, a % depth:a % depth + cut])
                for c in range(2)
            ).reshape(2, half, cut)
        if h == 1:
            halves[0].side(k).wait_send()
        step = min(32, half)

        def lower(i, _):
            here = pl.ds(pl.multiple_of(i * step, step), step)
            side_out[k, here, :] = acc_ref[h, 1 - core, here, :].astype(jnp.bfloat16)
            return 0

        lax.fori_loop(0, half // step, lower, 0)
        halves[h].side(k).start()

    def one(j, _):
        k = near(n - 1 - j, m, n)
        partials(k, 0)
        pl.when(j < n - 1)(
            lambda: halves[0].pass_on(k, acc_ref.at[0, core], lambda p: g.arrive(j + 1, (late[0] + p,))))
        work_at(j, 1, late)
        return 0

    lax.fori_loop(0, n, one, 0)
    wide_cut = min(256, depth)
    per = -(-(width // wide_cut) // n)
    tokens = 2 * n * rows

    def wide_copy(place, slot):
        lanes = pl.ds(pl.multiple_of(lax.rem(place, depth), wide_cut), wide_cut)
        return pltpu.make_async_copy(
            wide_stage.at[slot], grad_gate_up_ref.at[lax.div(place, depth), :, :, lanes], wide_sem.at[slot])

    def wide_gradient(u, j):
        place = (j * per + u) * wide_cut

        @pl.when(place < width)
        def _():
            pl.when(j > 0)(lambda: wide_copy(0, u).wait())
            lanes = pl.ds(pl.multiple_of(place, wide_cut), wide_cut)
            x = xs_ref[:, :, lanes].reshape(tokens, wide_cut).T
            for c in range(2):
                wide_stage[u, c] = dot_nn(x, grads_ref[c].reshape(tokens, hidden_units)).T.astype(jnp.bfloat16)
            wide_copy(place, u).start()

    def down_copy(place, size):
        return pltpu.make_async_copy(down_stage.at[:, pl.ds(0, size)], grad_down_ref.at[:, pl.ds(place, size)], down_sem)

    def down_gradient(index):
        place, size = places[index]
        if index > 0:
            down_copy(*places[index - 1]).wait()
        low = hidden_ref[:, :, place:place + size].reshape(tokens, size).T
        for a in range(0, width, cut):
            down_stage[a // depth, :size, a % depth:a % depth + cut] = dot_nn(low, cots_ref[:, :, a:a + cut].reshape(tokens, cut)).astype(jnp.bfloat16)
        down_copy(place, size).start()

    def two(j, _):
        k = near(n - 1 - j, m, n)
        partials(k, 1)
        pl.when(j < n - 1)(lambda: halves[1].pass_on(k, acc_ref.at[1, core]))
        for u in range(per):
            wide_gradient(u, j)
        for index in range(len(places)):
            pl.when(j == index)(functools.partial(down_gradient, index))
        return 0

    own = acc_ref.at[0, core]

    def settle(h):
        def consume(at, total):
            here = pl.ds(pl.multiple_of(h * half + at.start, at.size), at.size)
            back, gain, shift = norm_backward(middle_ref[here, :], norm_ref[2:3, :], total)
            grad_middle_ref[here, :] = cots_ref[g.t, here, :].astype(jnp.float32) + back
            sums_ref[0:1, :] += gain
            sums_ref[1:2, :] += shift

        halves[h].settle(acc_ref.at[h, core], consume)

    sums_ref[...] = jnp.zeros(sums_ref.shape, jnp.float32)
    settle(0)
    lax.fori_loop(0, n, two, 0)
    settle(1)
    for u in range(per):
        wide_copy(0, u).wait()
    down_copy(*places[-1]).wait()
    g.finish()

    def sent(k, _):
        halves[1].side(k).wait_send()
        for h in range(2):
            halves[h].finish_line(k)
        return 0

    lax.fori_loop(0, n, sent, 0)


def mlp(x, cots, gate_up, down, middle, norms, n, number, pieces=4):
    rows, width = x.shape
    group_count, hidden, depth = down.shape
    half, part = rows // 2, pieces // 2
    f32, low = jnp.float32, jnp.bfloat16
    shape = jax.ShapeDtypeStruct
    anywhere = pl.BlockSpec(memory_space=pl.ANY)
    wide_cut = min(256, depth)
    per = -(-(width // wide_cut) // n)
    dma = pltpu.SemaphoreType.DMA
    return pl.pallas_call(functools.partial(mlp_kernel, n, pieces),
        out_shape=(shape((2 * n, rows, hidden), low), shape((rows, width), f32),
                   shape((2, width), f32), shape(gate_up.shape, low), shape(down.shape, low)),
        in_specs=[VM] + [anywhere] * 4 + [VM], out_specs=(VM,) * 3 + (anywhere,) * 2,
        scratch_shapes=[
            pltpu.VMEM((2 * n, rows, width), low), pltpu.VMEM(gate_up.shape, low), pltpu.VMEM(down.shape, low), pltpu.VMEM((rows, width), f32),
            pltpu.VMEM((2 * n, rows, width), low), pltpu.VMEM((2, 2 * n, rows, hidden), low), dma((4,)),
            pltpu.VMEM((2, 2, half, width), f32), pltpu.VMEM((n, half, width), low), pltpu.VMEM((2, n, half, width), low),
            pltpu.VMEM((2, n + 1, half, width), low), dma((2, 2, n)), dma((2, n * part)), dma((2, (n + 1) * part)),
            dma((5, n * pieces)), pltpu.VMEM((per, 2, hidden, wide_cut), low), pltpu.VMEM((group_count, min(256, hidden), depth), low),
            dma((per,)), dma,
        ],
        compiler_params=params(number), cost_estimate=lasting(140), name="mlp")(x, cots, gate_up, down, middle, norms)


def down_kernel(n, pieces, hidden_ref, down_ref, middle_ref, grad_ref, out_ref, mixed_ref, wide_ref, low_ref, block_ref, back_ref, grad_out_ref, wide_parts, low_parts,
                local_sems, share_send, share_recv, xs_ref, x_ref, acc_ref, side_out, side_in, line_in, side_sems, line_send, line_recv, gather_sems):
    group_count, _, depth = down_ref.shape
    greet_all(n, group_count)
    grads = Exchange(group_count, ((wide_ref, wide_parts), (low_ref, low_parts)), local_sems, share_send, share_recv)
    g = Gather(n, x_ref, xs_ref, gather_sems, pieces)
    s = Scatter(n, pieces, side_out, side_in, line_in, side_sems, line_send, line_recv)
    x_ref[...] = grad_ref[...].astype(jnp.bfloat16)
    g.start()
    grads.start()
    xs_ref[g.t] = x_ref[...]
    m, core = s.m, s.core
    width = group_count * depth
    cut = min(512, depth)

    def one(j, _):
        k = near(n - 1 - j, m, n)
        for a in range(0, width, cut):
            s.side_out[k, :, a:a + cut] = dot_nn(hidden_ref[2 * k + 1 - core], down_ref[a // depth, :, a % depth:a % depth + cut]).astype(jnp.bfloat16)
        s.side(k).start()
        for a in range(0, width, cut):
            acc_ref[:, a:a + cut] = dot_nn(hidden_ref[2 * k + core], down_ref[a // depth, :, a % depth:a % depth + cut])
        pl.when(j < n - 1)(lambda: s.pass_on(k, acc_ref, lambda p: g.arrive(j + 1, (p,))))
        return 0

    lax.fori_loop(0, n, one, 0)

    def consume(at, total):
        block_ref[at, :] = (middle_ref[at, :] + total).astype(jnp.bfloat16)

    s.settle(acc_ref, consume)

    def last(k, _):
        g.side_wait(k)
        for c in range(2):
            back_ref[2 * k + c] = dot_nt(xs_ref[2 * k + c], out_ref[...]).astype(jnp.bfloat16)
        return 0

    lax.fori_loop(0, n, last, 0)
    flipped = mixed_ref[...].T
    for a in range(0, width, cut):
        grad_out_ref[a // depth, :, a % depth:a % depth + cut] = dot_nn(
            flipped, xs_ref[:, :, a:a + cut].reshape(mixed_ref.shape[0], cut)).astype(jnp.bfloat16)
    g.finish()
    s.finish()
    grads.finish()


def down_branch(hidden, down, middle, x, out, mixed, wide, narrow, n, number, pieces=4):
    rows, width = x.shape
    f32, low = jnp.float32, jnp.bfloat16
    return pl.pallas_call(functools.partial(down_kernel, n, pieces),
        out_shape=(jax.ShapeDtypeStruct((rows, width), low), jax.ShapeDtypeStruct((2 * n, rows, out.shape[0]), low),
                   jax.ShapeDtypeStruct((down.shape[0], out.shape[0], down.shape[2]), low),
                   jax.ShapeDtypeStruct(wide.shape, low), jax.ShapeDtypeStruct(narrow.shape, low)),
        in_specs=[VM] * 6 + [ANYWHERE] * 2, out_specs=(VM,) * 3 + (ANYWHERE,) * 2,
        scratch_shapes=exchange_scratch(2, down.shape[0]) + [pltpu.VMEM((2 * n, rows, width), low), pltpu.VMEM((rows, width), low), pltpu.VMEM((rows, width), f32)] + scatter_scratch(n, pieces, rows, width) + [pltpu.SemaphoreType.DMA((5, n * pieces))],
        compiler_params=params(number), cost_estimate=lasting(115), name="down_branch")(hidden, down, middle, x, out, mixed, wide, narrow)


def greet_everyone(count, group_count):
    t, g = lax.axis_index("tensor"), lax.axis_index("dp")
    barrier = pltpu.get_barrier_semaphore()
    for j in range(count):
        pl.when(j != t)(lambda: pl.semaphore_signal(barrier, inc=1, device_id={"tensor": j}, device_id_type=MESH))
    for i in range(group_count):
        pl.when(i != g)(lambda: pl.semaphore_signal(barrier, inc=1, device_id={"dp": i}, device_id_type=MESH))
    pl.semaphore_wait(barrier, count + group_count - 2)


class Totals:
    def __init__(self, sums, total, parts, groups, biases, near_send, near_recv, far_send, far_recv):
        self.sums, self.total, self.parts, self.groups, self.biases = sums, total, parts, groups, biases
        self.near_send, self.near_recv, self.far_send, self.far_recv = near_send, near_recv, far_send, far_recv
        self.t, self.g = lax.axis_index("tensor"), lax.axis_index("dp")
        self.count, self.group_count = parts.shape[0], groups.shape[0]
        self.piece = parts.shape[2]

    def columns(self, ref, j):
        return ref.at[:, pl.ds(pl.multiple_of(j * self.piece, self.piece), self.piece)]

    def near(self, kind, src, dst, peer, slot):
        return pltpu.make_async_remote_copy(
            src_ref=src, dst_ref=dst, send_sem=self.near_send.at[kind, peer], recv_sem=self.near_recv.at[kind, slot],
            device_id={"tensor": peer}, device_id_type=MESH)

    def far(self, kind, ref, peer, slot):
        return pltpu.make_async_remote_copy(
            src_ref=ref.at[self.g], dst_ref=ref.at[slot], send_sem=self.far_send.at[kind, peer], recv_sem=self.far_recv.at[kind, slot],
            device_id={"dp": peer}, device_id_type=MESH)

    def first(self, peer, slot):
        return self.near(0, self.columns(self.sums, peer), self.parts.at[slot], peer, slot)

    def last(self, peer, slot):
        return self.near(1, self.columns(self.total, self.t), self.columns(self.total, slot), peer, slot)

    def each_near(self, body):
        for j in range(self.count):
            pl.when(j != self.t)(lambda: body(j))

    def each_far(self, body):
        for i in range(self.group_count):
            pl.when(i != self.g)(lambda: body(i))

    def start_bias(self, bias):
        self.biases[self.g] = bias[...]
        self.each_far(lambda i: self.far(1, self.biases, i, self.g).start())

    def run(self, bias_total):
        def added(ref):
            total = ref[0]
            for j in range(1, ref.shape[0]):
                total = total + ref[j]
            return total

        here = pl.ds(pl.multiple_of(self.t * self.piece, self.piece), self.piece)
        self.each_near(lambda j: self.first(j, self.t).start())
        self.parts[self.t] = self.sums[:, here]
        self.each_near(lambda j: self.first(j, j).wait_recv())
        self.groups[self.g] = added(self.parts)
        self.each_far(lambda i: self.far(0, self.groups, i, self.g).start())
        self.each_far(lambda i: self.far(1, self.biases, i, i).wait_recv())
        bias_total[...] = added(self.biases)
        self.each_far(lambda i: self.far(0, self.groups, i, i).wait_recv())
        self.total[:, here] = added(self.groups)
        self.each_near(lambda j: self.last(j, self.t).start())
        self.each_near(lambda j: self.last(j, j).wait_recv())

    def finish(self):
        self.each_near(lambda j: self.first(j, self.t).wait_send())
        self.each_far(lambda i: self.far(0, self.groups, i, self.g).wait_send())
        self.each_far(lambda i: self.far(1, self.biases, i, self.g).wait_send())
        self.each_near(lambda j: self.last(j, self.t).wait_send())


def backward_kernel(n, pieces, length_ref, q_ref, k_ref, v_ref, kt_ref, o_ref, lse_ref, do_ref,
                    keep_hbm, ahead_hbm, behind_hbm, w_hbm, x_hbm, middle_hbm, norm_ref, sums_two_ref, xs_hbm, low_ref,
                    result_ref, total_ref, bias_total_ref, wide_parts, low_parts,
                    keep_ref, ahead_ref, behind_ref, w_ref, x_ref, middle_ref, late_sems,
                    dos_ref, delta_ref, dqt_ref, dk_ref, dv_ref, grad_ref, wide_ref, strips_ref, acc_ref, sums_ref, bias_ref, pieces_ref, groups_ref, biases_ref, side_out, side_in, line_in,
                    strip_sems, side_sems, line_send, line_recv, local_sems, share_send, share_recv, near_send, near_recv, far_send, far_recv):
    group_count = low_ref.shape[0]
    late = [
        pltpu.make_async_copy(src, dst, late_sems.at[index])
        for index, (src, dst) in enumerate((
            (keep_hbm, keep_ref), (ahead_hbm, ahead_ref), (behind_hbm, behind_ref), (w_hbm, w_ref), (x_hbm, x_ref), (middle_hbm, middle_ref)))
    ]
    for item in late:
        item.start()
    greet_everyone(2 * n, group_count)
    heads, tokens, _ = q_ref.shape
    width = heads * HEAD_DIM
    rows, features = x_ref.shape
    lane_groups = width // LANES
    per_group = LANES // HEAD_DIM
    pair = 2 * rows
    depth = features // group_count
    length = length_ref[0]
    s = Scatter(n, pieces, side_out, side_in, line_in, side_sems, line_send, line_recv)
    m, core = s.m, s.core
    grads = Exchange(group_count, ((low_ref, low_parts), (wide_ref, wide_parts)), local_sems, share_send, share_recv)
    grads.start((0,))
    strip = min(256, depth)
    strip_count = features // strip

    def strip_copy(index, slot):
        return pltpu.make_async_copy(
            xs_hbm.at[:, :, pl.ds(pl.multiple_of(index * strip, strip), strip)], strips_ref.at[slot], strip_sems.at[slot])

    for slot in range(2):
        strip_copy(slot, slot).start()
    bias_ref[...] = jnp.zeros(bias_ref.shape, jnp.float32)
    sums_ref[0:2, :] = jnp.zeros((2, features), jnp.float32)
    sums_ref[2:4, :] = sums_two_ref[...]
    totals = Totals(sums_ref, total_ref, pieces_ref, groups_ref, biases_ref, near_send, near_recv, far_send, far_recv)

    def prepare(i, _):
        at = pl.ds(pl.multiple_of(i * pair, pair), pair)
        for a in range(lane_groups):
            lanes = slice(a * LANES, (a + 1) * LANES)
            grad = do_ref[at, lanes]
            for b in range(per_group):
                dos_ref[a * per_group + b, at, :] = grad[:, b * HEAD_DIM:(b + 1) * HEAD_DIM]
            both = (grad.astype(jnp.float32) * o_ref[at, lanes].astype(jnp.float32)).T
            for b in range(per_group):
                h = a * per_group + b
                delta_ref[h:h + 1, at] = jnp.sum(both[b * HEAD_DIM:(b + 1) * HEAD_DIM], axis=0, keepdims=True)
        dqt_ref[:, at] = jnp.zeros((width, pair), jnp.float32)
        for h in range(heads):
            dk_ref[h, at, :] = jnp.zeros((pair, HEAD_DIM), jnp.float32)
            dv_ref[h, at, :] = jnp.zeros((pair, HEAD_DIM), jnp.float32)
        return 0

    lax.fori_loop(0, n, prepare, 0)
    for item in late:
        item.wait()

    falling = 2 * m < n - 1

    def order(step):
        return jnp.where(falling, n - 1 - step, step)

    def finish_block(step):
        j = order(step)

        def tile(i, j, causal):
            at = pl.ds(pl.multiple_of(i * pair, pair), pair)
            key_start = pl.multiple_of(j * pair, pair)
            keys_at = pl.ds(key_start, pair)
            for h in range(heads):
                keys, queries, grad = k_ref[h, keys_at, :], q_ref[h, at, :], dos_ref[h, at, :]
                scores = dot_nt(keys, queries) * (score_scale * log2_e)
                scores = masked_scores(scores, key_start, i * pair, length, causal)
                p = jnp.exp2(scores - lse_ref[h:h + 1, at])
                dp = dot_nt(v_ref[h, keys_at, :], grad)
                ds = (p * (dp - delta_ref[h:h + 1, at])).astype(jnp.bfloat16)
                dv_ref[h, keys_at, :] += dot_nn(p.astype(jnp.bfloat16), grad)
                dk_ref[h, keys_at, :] += dot_nn(ds, queries)
                here = slice(h * HEAD_DIM, (h + 1) * HEAD_DIM)
                dqt_ref[here, at] += dot_nn(kt_ref[here, keys_at], ds)

        def other(u, _):
            tile(jnp.where(falling, j, j + u), jnp.where(falling, j - u, j), False)
            return 0

        tile(j, j, True)
        lax.fori_loop(1, n - step, other, 0)
        keys_at = pl.ds(pl.multiple_of(j * pair, pair), pair)
        keep, ahead, behind = keep_ref[keys_at, :], -ahead_ref[keys_at, :], -behind_ref[keys_at, :]
        for a in range(lane_groups):
            lanes = slice(a * LANES, (a + 1) * LANES)
            heads_here = range(a * per_group, (a + 1) * per_group)
            dq = dqt_ref[lanes, keys_at].T
            dk = jnp.concatenate([dk_ref[h, keys_at, :] for h in heads_here], axis=1)
            dv = jnp.concatenate([dv_ref[h, keys_at, :] for h in heads_here], axis=1)
            parts = (spin(dq * score_scale, keep, ahead, behind), spin(dk * score_scale, keep, ahead, behind), dv)
            for c in range(3):
                low = parts[c].astype(jnp.bfloat16)
                place_here = slice(c * width + a * LANES, c * width + (a + 1) * LANES)
                grad_ref[keys_at, place_here] = low
                bias_ref[:, place_here] += jnp.sum(low.astype(jnp.float32), axis=0, keepdims=True)

    cut = min(512, features)

    def partial(slot, a):
        at = pl.ds(pl.multiple_of(slot * rows, rows), rows)
        return sum(dot_nt(grad_ref[at, c * width:(c + 1) * width], w_ref[c, a:a + cut, :]) for c in range(3))

    def own_partial(k):
        for a in range(0, features, cut):
            acc_ref[:, a:a + cut] = partial(2 * k + core, a)

    def strip_gradient(index, _):
        slot = lax.rem(index, 2)
        strip_copy(index, slot).wait()
        x = strips_ref[slot].reshape(tokens, strip).T
        owner = lax.div(index * strip, depth)
        at = pl.ds(pl.multiple_of(lax.rem(index * strip, depth), strip), strip)
        for c in range(3):
            wide_ref[owner, c, at, :] = dot_nn(x, grad_ref[:, c * width:(c + 1) * width]).astype(jnp.bfloat16)
        pl.when(index + 2 < strip_count)(lambda: strip_copy(index + 2, slot).start())
        return 0

    def step(j, _):
        @pl.when(j < n)
        def _():
            finish_block(j)
            k = order(j)
            for a in range(0, features, cut):
                s.side_out[k, :, a:a + cut] = partial(2 * k + 1 - core, a).astype(jnp.bfloat16)
            s.side(k).start()

        @pl.when(j == n - 1)
        def _():
            lax.fori_loop(0, strip_count, strip_gradient, 0)
            grads.start((1,))
            totals.start_bias(bias_ref)

        def one(late, _):
            turn = jnp.where(late == 1, j - 2, j)
            k = order(turn)
            inner = ((k > m) & (m > 0)) | ((k < m) & (m < n - 1))

            @pl.when((turn >= 0) & (turn < n) & (k != m) & (inner == (late == 1)))
            def _():
                own_partial(k)
                s.pass_on(k, acc_ref)

            return 0

        lax.fori_loop(0, 2, one, 0)
        return 0

    lax.fori_loop(0, n + 2, step, 0)
    own_partial(m)

    def consume(at, total):
        back, gain, shift = norm_backward(x_ref[at, :].astype(jnp.float32), norm_ref[0:1, :], total)
        result_ref[at, :] = middle_ref[at, :] + back
        sums_ref[0:1, :] += gain
        sums_ref[1:2, :] += shift

    s.settle(acc_ref, consume)
    totals.run(bias_total_ref)
    s.finish()
    grads.finish()
    totals.finish()


def backward(lengths, q, k, v, kt, o, lse, grad, keep, ahead, behind, w, x, grad_middle, norms, sums_two, xs, narrow, n, number, pieces=4):
    rows, features = x.shape
    heads, tokens, _ = q.shape
    width = heads * HEAD_DIM
    group_count = narrow.shape[0]
    depth = features // group_count
    f32, low = jnp.float32, jnp.bfloat16
    shape = jax.ShapeDtypeStruct
    wide = (group_count, 3, depth, width)
    strip = min(256, depth)
    dma = pltpu.SemaphoreType.DMA
    scatter = scatter_scratch(n, pieces, rows, features)
    return pl.pallas_call(functools.partial(backward_kernel, n, pieces),
        out_shape=(shape((rows, features), f32), shape((4, features), f32), shape((1, 3 * width), f32),
                   shape(wide, low), shape(narrow.shape, low)),
        in_specs=[pl.BlockSpec(memory_space=pltpu.SMEM)] + [VM] * 7 + [ANYWHERE] * 6 + [VM] * 2 + [ANYWHERE] * 2,
        out_specs=(VM,) * 3 + (ANYWHERE,) * 2,
        scratch_shapes=[pltpu.VMEM(item.shape, item.dtype) for item in (keep, ahead, behind, w, x, grad_middle)] + [
            dma((6,)),
            pltpu.VMEM((heads, tokens, HEAD_DIM), low), pltpu.VMEM((heads, tokens), f32), pltpu.VMEM((width, tokens), f32),
            pltpu.VMEM((heads, tokens, HEAD_DIM), f32), pltpu.VMEM((heads, tokens, HEAD_DIM), f32),
            pltpu.VMEM((tokens, 3 * width), low), pltpu.VMEM(wide, low), pltpu.VMEM((2, 2 * n, rows, strip), low),
            pltpu.VMEM((rows, features), f32), pltpu.VMEM((4, features), f32), pltpu.VMEM((1, 3 * width), f32),
            pltpu.VMEM((2 * n, 4, features // (2 * n)), f32), pltpu.VMEM((group_count, 4, features // (2 * n)), f32),
            pltpu.VMEM((group_count, 1, 3 * width), f32),
        ] + scatter[:3] + [pltpu.SemaphoreType.DMA((2,))] + scatter[3:] + exchange_scratch(2, group_count)
        + [dma((2, 2 * n)), dma((2, 2 * n)), dma((2, group_count)), dma((2, group_count))],
        compiler_params=params(number), cost_estimate=lasting(125), name="backward",
    )(lengths, q, k, v, kt, o, lse, grad, keep, ahead, behind, w, x, grad_middle, norms, sums_two, xs, narrow)


def update_kernel(rates, *refs):
    kinds = len(rates)
    ins, outs, refs = refs[:4 * kinds], refs[4 * kinds:7 * kinds], refs[7 * kinds:]
    holds, held_parts, refs = refs[:kinds], refs[kinds:2 * kinds], refs[2 * kinds:]
    load_sems, part_sems, store_sems = refs

    def load(kind, i):
        return pltpu.make_async_copy(ins[4 * kind + i], holds[kind].at[i], load_sems.at[kind, i])

    def load_parts(kind):
        return pltpu.make_async_copy(ins[4 * kind + 3], held_parts[kind], part_sems.at[kind])

    def store(kind, i):
        return pltpu.make_async_copy(holds[kind].at[i], outs[3 * kind + i], store_sems.at[kind, i])

    for kind in range(kinds):
        for i in range(3):
            load(kind, i).start()
        load_parts(kind).start()
    for kind in range(kinds):
        for i in range(3):
            load(kind, i).wait()
        load_parts(kind).wait()
        hold, part = holds[kind], held_parts[kind]
        step = min(32, hold.shape[1])

        def one(i, _):
            at = pl.ds(pl.multiple_of(i * step, step), step)
            gradient = part[0, at, :].astype(jnp.float32)
            for owner in range(1, part.shape[0]):
                gradient = gradient + part[owner, at, :].astype(jnp.float32)
            new = adamw(hold[0, at, :], hold[1, at, :], hold[2, at, :], gradient, *rates[kind])
            for index in range(3):
                hold[index, at, :] = new[index]
            return 0

        lax.fori_loop(0, hold.shape[1] // step, one, 0)
        for i in range(3):
            store(kind, i).start()
    for kind in range(kinds):
        for i in range(3):
            store(kind, i).wait()


def update(params_in, rates):
    f32 = jnp.float32
    kinds = len(rates)
    dma = pltpu.SemaphoreType.DMA
    flat = [array for group in params_in for array in group]
    results = pl.pallas_call(
        functools.partial(update_kernel, rates),
        out_shape=tuple(jax.ShapeDtypeStruct(group[0].shape, f32) for group in params_in for _ in range(3)),
        in_specs=[ANYWHERE] * len(flat), out_specs=(ANYWHERE,) * (3 * kinds),
        scratch_shapes=[pltpu.VMEM((3,) + group[0].shape, f32) for group in params_in]
        + [pltpu.VMEM(group[3].shape, group[3].dtype) for group in params_in]
        + [dma((kinds, 3)), dma((kinds,)), dma((kinds, 3))],
        compiler_params=pltpu.CompilerParams(vmem_limit_bytes=VMEM_LIMIT), cost_estimate=lasting(20), name="update",
    )(*flat)
    return tuple(results[3 * i:3 * i + 3] for i in range(kinds))


def local(
    inputs,
    cotangent,
    lengths,
    positions,
    qkv_master,
    gate_up_master,
    out_master,
    down_master,
    bias_master,
    norm_master,
    qkv_first,
    gate_up_first,
    out_first,
    down_first,
    bias_first,
    norm_first,
    qkv_second,
    gate_up_second,
    out_second,
    down_second,
    bias_second,
    norm_second,
):
    tensor_count = lax.axis_size("tensor")
    local_tokens = inputs.shape[0]
    group_tokens = local_tokens * tensor_count
    row_count = lengths.shape[0]
    row_length = group_tokens // row_count
    heads_here = bias_master.shape[1]
    width_here = heads_here * HEAD_DIM
    own_start = lax.axis_index("tensor") * local_tokens
    chips = tensor_count // 2
    group = lax.axis_index("dp")
    group_count = lax.axis_size("dp")
    group_index = own_start + jnp.arange(local_tokens, dtype=jnp.int32)
    row_of = group_index // row_length
    slot_of = group_index % row_length
    row_match = row_of[:, None] == jnp.arange(row_count, dtype=jnp.int32)[None, :]
    length_of = jnp.sum(jnp.where(row_match, lengths[None, :], 0), axis=1)
    valid = slot_of < length_of
    grad_low = jnp.where(valid[:, None], cotangent, jnp.zeros_like(cotangent))
    own_dims = jnp.arange(HEAD_DIM) // (HEAD_DIM // group_count) == group
    bias_row = jnp.where(own_dims, jnp.tile(bias_master, (1, 1, group_count)), 0.0).reshape(3, width_here)
    bias_row = jnp.concatenate([bias_row, jnp.zeros((5, width_here), jnp.float32)], axis=0)
    (
        gathered_one, qkv_copy, out_copy, queries, keys, values, keys_flipped, mixed_low, log_totals,
        keep, ahead, behind, middle, normed_two, gathered_grad, gate_up_copy, down_copy,
    ) = forward(
        lengths, positions, inputs, norm_master, qkv_master, out_master, bias_row, grad_low,
        jnp.swapaxes(gate_up_master, 1, 2), down_master, chips, group_count, 0
    )
    hidden, grad_middle, sums_two, grad_gate_up_w, grad_down = mlp(
        normed_two, gathered_grad, gate_up_copy, down_copy, middle, norm_master, chips, 2
    )
    block_output, grad_mixed, grad_out_w, gate_up_parts, down_parts = down_branch(
        hidden, down_copy, middle, grad_middle, out_copy, mixed_low, grad_gate_up_w, grad_down, chips, 3
    )
    grad_mixed = grad_mixed.reshape(group_tokens, width_here)
    input_grad, norm_grads, bias_grad, qkv_parts, out_parts = backward(
        lengths, queries, keys, values, keys_flipped, mixed_low, log_totals, grad_mixed, keep, ahead, behind,
        qkv_copy, inputs, grad_middle, norm_master, sums_two, gathered_one, grad_out_w, chips, 4
    )

    def level(array):
        return array.reshape(-1, array.shape[-1])

    def level_parts(array):
        return array.reshape(group_count, -1, array.shape[-1])

    def turned(array):
        return level(jnp.swapaxes(array, 1, 2))

    gate_up_new, down_new, out_new, qkv_new = update(
        (
            (turned(gate_up_master), turned(gate_up_first), turned(gate_up_second), level_parts(gate_up_parts)),
            (down_master, down_first, down_second, down_parts),
            (out_master, out_first, out_second, out_parts),
            (level(qkv_master), level(qkv_first), level(qkv_second), level_parts(qkv_parts)),
        ),
        (
            (2.0 / math.sqrt(D), decay_rate),
            (6.0 / math.sqrt(FF), decay_rate),
            (16.0 / math.sqrt(HEADS * HEAD_DIM), decay_rate),
            (2.0 / math.sqrt(D), decay_rate),
        ),
    )
    turned_shape = (2, gate_up_master.shape[2], gate_up_master.shape[1])
    gate_up_new = tuple(jnp.swapaxes(item.reshape(turned_shape), 1, 2) for item in gate_up_new)
    qkv_new = tuple(item.reshape(qkv_master.shape) for item in qkv_new)
    bias_grad = lax.dynamic_slice_in_dim(
        bias_grad.reshape(3, heads_here, HEAD_DIM), group * bias_master.shape[2], bias_master.shape[2], axis=2
    )
    bias_new = adamw(bias_master, bias_first, bias_second, bias_grad, 1.5, 0.0)
    norm_new = adamw(norm_master, norm_first, norm_second, norm_grads, 0.7, 0.0)
    return (
        block_output,
        input_grad,
        qkv_new[0],
        qkv_new[1],
        qkv_new[2],
        gate_up_new[0],
        gate_up_new[1],
        gate_up_new[2],
        out_new[0],
        out_new[1],
        out_new[2],
        down_new[0],
        down_new[1],
        down_new[2],
        bias_new[0],
        bias_new[1],
        bias_new[2],
        norm_new[0],
        norm_new[1],
        norm_new[2],
    )


def solution(mesh):
    return jax.shard_map(
        local,
        mesh=mesh,
        in_specs=(
            P(("dp", "tensor"), None),
            P(("dp", "tensor"), None),
            P("dp"),
            P("dp"),
            P(None, "dp", "tensor"),
            P(None, "dp", "tensor"),
            P("tensor", "dp"),
            P("tensor", "dp"),
            P(None, "tensor", "dp"),
            P(),
            P(None, "dp", "tensor"),
            P(None, "dp", "tensor"),
            P("tensor", "dp"),
            P("tensor", "dp"),
            P(None, "tensor", "dp"),
            P(),
            P(None, "dp", "tensor"),
            P(None, "dp", "tensor"),
            P("tensor", "dp"),
            P("tensor", "dp"),
            P(None, "tensor", "dp"),
            P(),
        ),
        out_specs=(
            P(("dp", "tensor"), None),
            P(("dp", "tensor"), None),
            P(None, "dp", "tensor"),
            P(None, "dp", "tensor"),
            P(None, "dp", "tensor"),
            P(None, "dp", "tensor"),
            P(None, "dp", "tensor"),
            P(None, "dp", "tensor"),
            P("tensor", "dp"),
            P("tensor", "dp"),
            P("tensor", "dp"),
            P("tensor", "dp"),
            P("tensor", "dp"),
            P("tensor", "dp"),
            P(None, "tensor", "dp"),
            P(None, "tensor", "dp"),
            P(None, "tensor", "dp"),
            P(),
            P(),
            P(),
        ),
        check_vma=False,
    )
```

```python
import functools
import math

import jax
import jax.numpy as jnp
from jax import lax
from jax.experimental import pallas as pl
from jax.experimental.pallas import tpu as pltpu
from jax.sharding import PartitionSpec as P

D = 2048
HEADS = 32
HEAD_DIM = 64
ROTARY = 16
FF = 5632


norm_eps = 1e-05
beta_one = 0.9
beta_two = 0.95
adam_eps = 1e-08
adam_steps = 10
decay_rate = 0.1
rope_base = 10000.0
score_scale = 0.125
mask_fill = -1e30
log2_e = math.log2(math.e)
LANES = 128
VMEM_LIMIT = 62 * 1024 * 1024


def norm_forward(values, gain_row, shift_row):
    average = jnp.mean(values, axis=-1, keepdims=True)
    centred = values - average
    spread = jnp.mean(centred * centred, axis=-1, keepdims=True)
    return centred * lax.rsqrt(spread + norm_eps) * gain_row + shift_row


def norm_backward(values, gain_row, grad_rows):
    average = jnp.mean(values, axis=-1, keepdims=True)
    centred = values - average
    spread = jnp.mean(centred * centred, axis=-1, keepdims=True)
    inverse = lax.rsqrt(spread + norm_eps)
    normal = centred * inverse
    grad_normal = grad_rows * gain_row
    grad_values = inverse * (
        grad_normal
        - jnp.mean(grad_normal, axis=-1, keepdims=True)
        - normal * jnp.mean(grad_normal * normal, axis=-1, keepdims=True)
    )
    return (
        grad_values,
        jnp.sum(grad_rows * normal, axis=0, keepdims=True),
        jnp.sum(grad_rows, axis=0, keepdims=True),
    )


def adamw(weight_old, first_old, second_old, gradient, step_rate, decay_part):
    first_new = beta_one * first_old + (1.0 - beta_one) * gradient
    second_new = beta_two * second_old + (1.0 - beta_two) * gradient * gradient
    correct_one = 1.0 - beta_one**adam_steps
    correct_two = 1.0 - beta_two**adam_steps
    update = first_new / correct_one / (jnp.sqrt(second_new / correct_two) + adam_eps)
    return (weight_old - step_rate * (update + decay_part * weight_old), first_new, second_new)


def spin(x, keep, ahead, behind):
    return x * keep + pltpu.roll(x, LANES - ROTARY // 2, 1) * ahead + pltpu.roll(x, ROTARY // 2, 1) * behind


def dot_nt(a, b):
    return lax.dot_general(a, b, (((1,), (1,)), ((), ())), preferred_element_type=jnp.float32)


def dot_nn(a, b):
    return lax.dot_general(a, b, (((1,), (0,)), ((), ())), preferred_element_type=jnp.float32)


def masked_scores(s, key_start, query_start, length, causal):
    key_slots = key_start + lax.broadcasted_iota(jnp.int32, s.shape, 0)
    allowed = key_slots < length
    if causal:
        query_slots = query_start + lax.broadcasted_iota(jnp.int32, s.shape, 1)
        allowed = allowed & (key_slots <= query_slots)
    return jnp.where(allowed, s, mask_fill)


VM = pl.BlockSpec(memory_space=pltpu.VMEM)
ANYWHERE = pl.BlockSpec(memory_space=pl.ANY)
MESH = pl.DeviceIdType.MESH


def params(number):
    return pltpu.CompilerParams(collective_id=number, has_side_effects=True, vmem_limit_bytes=VMEM_LIMIT)


def lasting(us):
    return pl.CostEstimate(flops=int(us * 1.1e9), bytes_accessed=0, transcendentals=0)


def place():
    t = lax.axis_index("tensor")
    return t, lax.rem(t, 2), lax.div(t, 2)


def greet(n):
    t, core, chip = place()
    barrier = pltpu.get_barrier_semaphore()

    def hail(index):
        pl.semaphore_signal(barrier, inc=1, device_id={"tensor": index}, device_id_type=MESH)

    hail(t + 1 - 2 * core)
    pl.when(chip > 0)(lambda: hail(t - 2))
    pl.when(chip < n - 1)(lambda: hail(t + 2))
    pl.semaphore_wait(barrier, 1 + jnp.minimum(chip, 1) + jnp.minimum(n - 1 - chip, 1))


def near(j, m, n):
    below, above = m, n - 1 - m
    both = jnp.minimum(below, above)
    half = lax.div(j + 1, 2)
    inside = m + jnp.where((lax.rem(j, 2) == 1) == (2 * m < n - 1), half, -half)
    outside = m + jnp.where(above > below, j - both, both - j)
    return jnp.where(j <= 2 * both, inside, outside)


class Gather:
    def __init__(self, n, own, buf, sems, pieces):
        self.n, self.own, self.buf, self.pieces = n, own, buf, pieces
        self.up, self.down, self.side, self.line_in, self.side_in = [sems.at[i] for i in range(5)]
        self.t, self.core, self.m = place()
        self.sibling = self.t + 1 - 2 * self.core
        self.rows = own.shape[0] // pieces

    def copy(self, src, k, p, core, send, recv, target):
        at = pl.ds(pl.multiple_of(p * self.rows, self.rows), self.rows)
        index = k * self.pieces + p
        return pltpu.make_async_remote_copy(
            src_ref=src.at[at], dst_ref=self.buf.at[2 * k + core, at], send_sem=send.at[index],
            recv_sem=recv.at[index], device_id={"tensor": target}, device_id_type=MESH)

    def to_up(self, k, p, src):
        return self.copy(src, k, p, self.core, self.up, self.line_in, self.t + 2)

    def to_down(self, k, p, src):
        return self.copy(src, k, p, self.core, self.down, self.line_in, self.t - 2)

    def to_side(self, k, p, src):
        return self.copy(src, k, p, self.core, self.side, self.side_in, self.sibling)

    def start(self, which=None, inward=True, outward=True):
        m = self.m
        low = 2 * m < self.n - 1
        for p in range(self.pieces) if which is None else which:
            if inward and outward:
                pl.when(m < self.n - 1)(lambda: self.to_up(m, p, self.own).start())
                pl.when(m > 0)(lambda: self.to_down(m, p, self.own).start())
            else:
                pl.when((m < self.n - 1) & (low == inward))(lambda: self.to_up(m, p, self.own).start())
                pl.when((m > 0) & (low != inward))(lambda: self.to_down(m, p, self.own).start())
            if outward:
                self.to_side(m, p, self.own).start()

    def arrive(self, d, which=None):
        m = self.m
        lo, hi = m - d, m + d
        for p in range(self.pieces) if which is None else which:
            @pl.when(lo >= 0)
            def _():
                src = self.buf.at[2 * lo + self.core]
                self.to_up(lo, p, src).wait_recv()
                pl.when(m < self.n - 1)(lambda: self.to_up(lo, p, src).start())
                self.to_side(lo, p, src).start()

            @pl.when(hi < self.n)
            def _():
                src = self.buf.at[2 * hi + self.core]
                self.to_down(hi, p, src).wait_recv()
                pl.when(m > 0)(lambda: self.to_down(hi, p, src).start())
                self.to_side(hi, p, src).start()

    def side_wait(self, k, which=None):
        for p in range(self.pieces) if which is None else which:
            self.copy(self.own, k, p, 1 - self.core, self.side, self.side_in, self.sibling).wait_recv()

    def finish(self):
        m = self.m

        def one(k, _):
            for p in range(self.pieces):
                pl.when((k <= m) & (m < self.n - 1))(lambda: self.to_up(k, p, self.own).wait_send())
                pl.when((k >= m) & (m > 0))(lambda: self.to_down(k, p, self.own).wait_send())
                self.to_side(k, p, self.own).wait_send()
            return 0

        lax.fori_loop(0, self.n, one, 0)


class Scatter:
    def __init__(self, n, pieces, side_out, side_in, line_in, side_sems, line_send, line_recv):
        self.n, self.pieces = n, pieces
        self.side_out, self.side_in, self.line_in = side_out, side_in, line_in
        self.side_send, self.side_recv = side_sems.at[0], side_sems.at[1]
        self.line_send, self.line_recv = line_send, line_recv
        self.t, self.core, self.m = place()
        self.sibling = self.t + 1 - 2 * self.core
        self.rows = side_out.shape[1] // pieces
        self.step = min(32, self.rows)

    def side(self, k):
        return pltpu.make_async_remote_copy(
            src_ref=self.side_out.at[k], dst_ref=self.side_in.at[k], send_sem=self.side_send.at[k],
            recv_sem=self.side_recv.at[k], device_id={"tensor": self.sibling}, device_id_type=MESH)

    def line(self, k, p, slot, target):
        at = pl.ds(pl.multiple_of(p * self.rows, self.rows), self.rows)
        return pltpu.make_async_remote_copy(
            src_ref=self.side_in.at[k, at], dst_ref=self.line_in.at[slot, at],
            send_sem=self.line_send.at[k * self.pieces + p], recv_sem=self.line_recv.at[slot * self.pieces + p],
            device_id={"tensor": target}, device_id_type=MESH)

    def each(self, p, body):
        def one(i, _):
            body(pl.ds(pl.multiple_of(p * self.rows + i * self.step, self.step), self.step))
            return 0

        lax.fori_loop(0, self.rows // self.step, one, 0)

    def inner(self, k):
        return ((k > self.m) & (self.m > 0)) | ((k < self.m) & (self.m < self.n - 1))

    def pass_on(self, k, own, between=None):
        m, n = self.m, self.n
        self.side(k).wait_recv()
        inner = self.inner(k)

        def one(p, _):
            @pl.when(inner)
            def _():
                self.line(k, p, k, self.t).wait_recv()

                def add(at):
                    total = own[at, :] + self.side_in[k, at, :].astype(jnp.float32) + self.line_in[k, at, :].astype(jnp.float32)
                    self.side_in[k, at, :] = total.astype(jnp.bfloat16)

                self.each(p, add)

            @pl.when(jnp.logical_not(inner))
            def _():
                def add(at):
                    self.side_in[k, at, :] = (own[at, :] + self.side_in[k, at, :].astype(jnp.float32)).astype(jnp.bfloat16)

                self.each(p, add)

            pl.when(k > m)(lambda: self.line(k, p, k, self.t + 2).start())
            pl.when(k < m)(lambda: self.line(k, p, jnp.where(k == m - 1, n, k), self.t - 2).start())
            if between is not None:
                between(p)
            return 0

        lax.fori_loop(0, self.pieces, one, 0)

    def settle(self, own, consume):
        m, n = self.m, self.n
        self.side(m).wait_recv()

        def one(p, _):
            def first(at):
                own[at, :] += self.side_in[m, at, :].astype(jnp.float32)

            self.each(p, first)

            def more(slot):
                self.line(m, p, slot, self.t).wait_recv()

                def add(at):
                    own[at, :] += self.line_in[slot, at, :].astype(jnp.float32)

                self.each(p, add)

            pl.when(m > 0)(lambda: more(m))
            pl.when(m < n - 1)(lambda: more(n))
            self.each(p, lambda at: consume(at, own[at, :]))
            return 0

        lax.fori_loop(0, self.pieces, one, 0)

    def finish(self):
        def one(k, _):
            self.side(k).wait_send()
            self.finish_line(k)
            return 0

        lax.fori_loop(0, self.n, one, 0)

    def finish_line(self, k):
        @pl.when(k != self.m)
        def _():
            for p in range(self.pieces):
                self.line(k, p, k, self.t).wait_send()


def scatter_scratch(n, pieces, rows, width):
    return [
        pltpu.VMEM((n, rows, width), jnp.bfloat16), pltpu.VMEM((n, rows, width), jnp.bfloat16),
        pltpu.VMEM((n + 1, rows, width), jnp.bfloat16),
        pltpu.SemaphoreType.DMA((2, n)), pltpu.SemaphoreType.DMA((n * pieces,)), pltpu.SemaphoreType.DMA(((n + 1) * pieces,)),
    ]


class Exchange:
    def __init__(self, group_count, pairs, local_sems, send, recv):
        self.group, self.count, self.pairs = lax.axis_index("dp"), group_count, pairs
        self.local_sems, self.send, self.recv = local_sems, send, recv

    def stay(self, index):
        src, dst = self.pairs[index]
        return pltpu.make_async_copy(src.at[self.group], dst.at[self.group], self.local_sems.at[index])

    def copy(self, index, peer, slot):
        src, dst = self.pairs[index]
        return pltpu.make_async_remote_copy(
            src_ref=src.at[peer], dst_ref=dst.at[slot], send_sem=self.send.at[index, peer],
            recv_sem=self.recv.at[index, slot], device_id={"dp": peer}, device_id_type=MESH)

    def others(self, body, which=None):
        for index in range(len(self.pairs)) if which is None else which:
            for i in range(self.count):
                pl.when(i != self.group)(lambda: body(index, i))

    def start(self, which=None):
        self.others(lambda index, i: self.copy(index, i, self.group).start(), which)
        for index in range(len(self.pairs)) if which is None else which:
            self.stay(index).start()

    def finish(self):
        for index in range(len(self.pairs)):
            self.stay(index).wait()
        self.others(lambda index, i: self.copy(index, i, i).wait_recv())
        self.others(lambda index, i: self.copy(index, i, self.group).wait_send())


def exchange_scratch(pairs, group_count):
    dma = pltpu.SemaphoreType.DMA
    return [dma((pairs,)), dma((pairs, group_count)), dma((pairs, group_count))]


def greet_all(n, group_count):
    t, core, chip = place()
    g = lax.axis_index("dp")
    barrier = pltpu.get_barrier_semaphore()

    def hail(index):
        pl.semaphore_signal(barrier, inc=1, device_id={"tensor": index}, device_id_type=MESH)

    hail(t + 1 - 2 * core)
    pl.when(chip > 0)(lambda: hail(t - 2))
    pl.when(chip < n - 1)(lambda: hail(t + 2))
    for i in range(group_count):
        pl.when(i != g)(lambda: pl.semaphore_signal(barrier, inc=1, device_id={"dp": i}, device_id_type=MESH))
    pl.semaphore_wait(barrier, group_count + jnp.minimum(chip, 1) + jnp.minimum(n - 1 - chip, 1))


def forward_kernel(n, group_count, pieces, length_ref, place_ref, frequency_ref, x_ref, norm_ref, qkv_ref, out_ref, bias_ref, cot_ref, wide_hbm, down_hbm,
                   xs_out, wq_out, wo_ref, q_out, k_out, v_out, kt_out, mixed_ref, lse_ref, keep_out, ahead_out, behind_out,
                   middle_ref, normed_ref, cots_ref, wide_copy, down_copy,
                   xs_ref, wq_ref, q_ref, k_ref, v_ref, kt_ref, keep_ref, ahead_ref, behind_ref, keep_sems,
                   wide_stage, low_stage, stage_sems, weight_send, weight_recv,
                   vt_ref, biases_ref, acc_ref, side_out, side_in, line_in, side_sems, line_send, line_recv,
                   first_sems, cot_sems, share_send, share_recv):
    greet_all(n, group_count)
    heads, total_rows, _ = q_ref.shape
    rows, features = x_ref.shape
    width = heads * HEAD_DIM
    lane_groups = width // LANES
    per_group = LANES // HEAD_DIM
    block = rows
    length = length_ref[0]
    group = lax.axis_index("dp")
    t, core, m = place()
    first = Gather(n, xs_ref.at[t], xs_ref, first_sems, pieces)
    cots = Gather(n, cot_ref, cots_ref, cot_sems, pieces)
    s = Scatter(n, pieces, side_out, side_in, line_in, side_sems, line_send, line_recv)
    step = 32

    def first_norm(i, _):
        at = pl.ds(pl.multiple_of(i * step, step), step)
        xs_ref[t, at, :] = norm_forward(x_ref[at, :].astype(jnp.float32), norm_ref[0:1, :], norm_ref[1:2, :]).astype(jnp.bfloat16)
        return 0

    lax.fori_loop(0, rows // step, first_norm, 0)
    first.start()
    depth = features // group_count
    mine = pl.ds(pl.multiple_of(group * depth, depth), depth)
    for c in range(3):
        wq_ref[c, mine, :] = qkv_ref[c].astype(jnp.bfloat16)
    wo_ref[:, mine] = out_ref[...].astype(jnp.bfloat16)
    biases_ref[group] = bias_ref[...].astype(jnp.bfloat16).astype(jnp.float32)

    def share(kind, src, owner, peer):
        ref = src(owner)
        return pltpu.make_async_remote_copy(
            src_ref=ref, dst_ref=ref, send_sem=share_send.at[kind, peer], recv_sem=share_recv.at[kind, owner],
            device_id={"dp": peer}, device_id_type=MESH)

    def part(owner):
        return pl.ds(pl.multiple_of(owner * depth, depth), depth)

    kinds = (lambda o: wq_ref.at[:, part(o), :], lambda o: biases_ref.at[o], lambda o: wo_ref.at[:, part(o)])
    for kind in range(3):
        for i in range(group_count):
            pl.when(i != group)(lambda: share(kind, kinds[kind], group, i).start())

    half_units = wide_stage.shape[0]
    units = wide_hbm.shape[1]
    chunks = [(wide_hbm.at[c], wide_copy.at[group, c], u) for c in range(2) for u in range(0, units, half_units)]
    chunks += [(down_hbm, down_copy.at[group], u) for u in range(0, units, half_units)]

    def chunk_in(index):
        src, _, u = chunks[index]
        return pltpu.make_async_copy(src.at[pl.ds(u, half_units)], wide_stage, stage_sems.at[0])

    def chunk_out(index):
        _, dst, u = chunks[index]
        return pltpu.make_async_copy(low_stage, dst.at[pl.ds(u, half_units)], stage_sems.at[1])

    chunk_in(0).start()
    for index in range(len(chunks)):
        chunk_in(index).wait()
        if index > 0:
            chunk_out(index - 1).wait()
        low_stage[...] = wide_stage[...].astype(jnp.bfloat16)
        if index + 1 < len(chunks):
            chunk_in(index + 1).start()
        chunk_out(index).start()
    chunk_out(len(chunks) - 1).wait()

    def weight(kind, peer, slot):
        ref = (wide_copy, down_copy)[kind]
        return pltpu.make_async_remote_copy(
            src_ref=ref.at[group], dst_ref=ref.at[slot], send_sem=weight_send.at[kind, peer],
            recv_sem=weight_recv.at[kind, slot], device_id={"dp": peer}, device_id_type=MESH)

    def weights(body):
        for kind in range(2):
            for i in range(group_count):
                pl.when(i != group)(lambda: body(kind, i))

    def tables(i, _):
        at = pl.ds(pl.multiple_of(i * block, block), block)
        angles = jnp.broadcast_to(place_ref[:, at], (LANES, block)).T * frequency_ref[...]
        cosine, sine = jnp.cos(angles), jnp.sin(angles)
        dim = lax.rem(lax.broadcasted_iota(jnp.int32, (block, LANES), 1), HEAD_DIM)
        none = jnp.zeros((block, LANES), jnp.float32)
        keep_ref[at, :] = jnp.where(dim < ROTARY, cosine, 1.0)
        ahead_ref[at, :] = jnp.where(dim < ROTARY // 2, -sine, none)
        behind_ref[at, :] = jnp.where((dim >= ROTARY // 2) & (dim < ROTARY), sine, none)
        return 0

    lax.fori_loop(0, total_rows // block, tables, 0)
    def project(slot):
        at = pl.ds(pl.multiple_of(slot * block, block), block)
        keep, ahead, behind = keep_ref[at, :], ahead_ref[at, :], behind_ref[at, :]
        x = xs_ref[slot]
        for c in range(3):
            wide = dot_nn(x, wq_ref[c]) + biases_ref[group_count, c:c + 1, :]
            for a in range(lane_groups):
                lanes = slice(a * LANES, (a + 1) * LANES)
                part_wide = wide[:, lanes]
                if c < 2:
                    part_wide = spin(part_wide, keep, ahead, behind)
                if c == 1:
                    kt_ref[lanes, at] = part_wide.T.astype(jnp.bfloat16)
                if c == 2:
                    vt_ref[lanes, at] = part_wide.T.astype(jnp.bfloat16)
                for b in range(per_group):
                    (q_ref, k_ref, v_ref)[c][a * per_group + b, at, :] = part_wide[:, b * HEAD_DIM:(b + 1) * HEAD_DIM].astype(jnp.bfloat16)

    def ring(d, _):
        def one(q, _):
            other, above = lax.div(q, 2), lax.rem(q, 2)
            k = jnp.where(above == 1, m + d, m - d)

            @pl.when((k >= 0) & (k < n) & ((d > 0) | (above == 0)))
            def _():
                pl.when(other == 1)(lambda: first.side_wait(k))
                project(2 * k + jnp.where(other == 1, 1 - core, core))

            return 0

        lax.fori_loop(0, 4, one, 0)
        pl.when(d == n - 2)(lambda: first.arrive(n - 1))
        return 0

    for d in range(1, n - 1):
        first.arrive(d)
    cots.start(outward=False)
    for kind in range(3):
        for i in range(group_count):
            pl.when(i != group)(lambda: share(kind, kinds[kind], i, i).wait_recv())
    bias = biases_ref[0]
    for i in range(1, group_count):
        bias = bias + biases_ref[i]
    biases_ref[group_count] = bias

    weights(lambda kind, i: weight(kind, i, group).start())
    lax.fori_loop(0, n, ring, 0)
    kept = [
        pltpu.make_async_copy(src, dst, keep_sems.at[index])
        for index, (src, dst) in enumerate((
            (xs_ref, xs_out), (wq_ref, wq_out), (q_ref, q_out), (k_ref, k_out), (v_ref, v_out), (kt_ref, kt_out),
            (keep_ref, keep_out), (ahead_ref, ahead_out), (behind_ref, behind_out)))
    ]
    for item in kept:
        item.start()
    cots.start(inward=False)
    cots_ref[t] = cot_ref[...]
    pair = 2 * block

    def attend(i):
        at = pl.ds(pl.multiple_of(i * pair, pair), pair)
        queries = [q_ref[h, at, :] for h in range(heads)]

        def key_block(j, carry, kind):
            key_start = pl.multiple_of(j * pair, pair)
            keys_at = pl.ds(key_start, pair)
            out = []
            for h in range(heads):
                top, total, mixed = carry[h]
                scores = dot_nt(k_ref[h, keys_at, :], queries[h]) * (score_scale * log2_e)
                if kind > 0:
                    scores = masked_scores(scores, key_start, i * pair, length, kind == 2)
                new_top = jnp.maximum(top, jnp.max(scores, axis=0, keepdims=True))
                shrink = jnp.exp2(top - new_top)
                p = jnp.exp2(scores - new_top)
                total = total * shrink + jnp.sum(p, axis=0, keepdims=True)
                mixed = mixed * shrink + dot_nn(
                    vt_ref[h * HEAD_DIM:(h + 1) * HEAD_DIM, keys_at], p.astype(jnp.bfloat16))
                out.append((new_top, total, mixed))
            return tuple(out)

        start = tuple(
            (jnp.full((1, pair), mask_fill, jnp.float32), jnp.zeros((1, pair), jnp.float32),
             jnp.zeros((HEAD_DIM, pair), jnp.float32)) for _ in range(heads))
        carry = lax.fori_loop(0, i, lambda j, c: key_block(j, c, 1), start)
        carry = key_block(i, carry, 2)
        for h in range(heads):
            top, total, mixed = carry[h]
            lse_ref[h:h + 1, at] = top + jnp.log2(total)
        for a in range(lane_groups):
            both = [carry[a * per_group + b][2] * (1.0 / carry[a * per_group + b][1]) for b in range(per_group)]
            mixed_ref[at, a * LANES:(a + 1) * LANES] = jnp.concatenate(both, axis=0).T.astype(jnp.bfloat16)

    cut = min(512, features)

    def branch(j, _):
        k = near(n - 1 - j, m, n)

        attend(k)

        def attended(slot):
            return mixed_ref[pl.ds(pl.multiple_of(slot * block, block), block), :]

        low = attended(2 * k + 1 - core)
        for a in range(0, features, cut):
            s.side_out[k, :, a:a + cut] = dot_nn(low, wo_ref[:, a:a + cut]).astype(jnp.bfloat16)
        s.side(k).start()
        low = attended(2 * k + core)
        for a in range(0, features, cut):
            acc_ref[:, a:a + cut] = dot_nn(low, wo_ref[:, a:a + cut])
        pl.when(j < n - 1)(lambda: s.pass_on(k, acc_ref, lambda p: cots.arrive(j + 1, (p,))))
        return 0

    lax.fori_loop(0, n, branch, 0)

    def consume(at, total):
        middle = x_ref[at, :].astype(jnp.float32) + total
        middle_ref[at, :] = middle
        normed_ref[at, :] = norm_forward(middle, norm_ref[2:3, :], norm_ref[3:4, :]).astype(jnp.bfloat16)

    s.settle(acc_ref, consume)
    for k in range(n):
        cots.side_wait(k)
    first.finish()
    cots.finish()
    s.finish()
    for kind in range(3):
        for i in range(group_count):
            pl.when(i != group)(lambda: share(kind, kinds[kind], group, i).wait_send())
    for item in kept:
        item.wait()
    weights(lambda kind, i: weight(kind, i, i).wait_recv())
    weights(lambda kind, i: weight(kind, i, group).wait_send())


def forward(lengths, positions, x, norms, qkv, out, bias, cot, wide, down, n, group_count, number, pieces=4):
    rows, features = x.shape
    width = qkv.shape[2]
    heads = width // HEAD_DIM
    total_rows = 2 * n * rows
    f32, low = jnp.float32, jnp.bfloat16
    shape = jax.ShapeDtypeStruct
    half_rot = ROTARY // 2
    frequency = rope_base ** (-(2.0 * jnp.arange(half_rot, dtype=jnp.float32)) / ROTARY)
    split = shape((heads, total_rows, HEAD_DIM), low)
    table = shape((total_rows, LANES), f32)
    gathered = shape((2 * n, rows, features), low)
    return pl.pallas_call(
        functools.partial(forward_kernel, n, group_count, pieces),
        out_shape=(gathered, shape((3, features, width), low), shape((width, features), low), split, split, split,
                   shape((width, total_rows), low), shape((total_rows, width), low), shape((heads, total_rows), f32),
                   table, table, table, shape((rows, features), f32), shape((rows, features), low), gathered,
                   shape((group_count,) + wide.shape, low), shape((group_count,) + down.shape, low)),
        in_specs=[pl.BlockSpec(memory_space=pltpu.SMEM)] + [VM] * 8 + [ANYWHERE] * 2,
        out_specs=(ANYWHERE, ANYWHERE, VM) + (ANYWHERE,) * 4 + (VM, VM) + (ANYWHERE,) * 3 + (VM,) * 3 + (ANYWHERE,) * 2,
        scratch_shapes=[
            pltpu.VMEM(item.shape, item.dtype)
            for item in (gathered, shape((3, features, width), low), split, split, split, shape((width, total_rows), low), table, table, table)
        ] + [
            pltpu.SemaphoreType.DMA((9,)), pltpu.VMEM((down.shape[0] // 2, down.shape[1]), f32), pltpu.VMEM((down.shape[0] // 2, down.shape[1]), low),
            pltpu.SemaphoreType.DMA((2,)), pltpu.SemaphoreType.DMA((2, group_count)), pltpu.SemaphoreType.DMA((2, group_count)),
            pltpu.VMEM((width, total_rows), low), pltpu.VMEM((group_count + 1, 8, width), f32), pltpu.VMEM((rows, features), f32),
        ] + scatter_scratch(n, pieces, rows, features) + [
            pltpu.SemaphoreType.DMA((5, n * pieces)), pltpu.SemaphoreType.DMA((5, n * pieces)),
            pltpu.SemaphoreType.DMA((3, group_count)), pltpu.SemaphoreType.DMA((3, group_count)),
        ],
        compiler_params=params(number), cost_estimate=lasting(200), name="forward",
    )(lengths, positions.astype(f32).reshape(1, total_rows), jnp.tile(frequency, LANES // half_rot).reshape(1, LANES),
      x, norms, qkv, out, bias, cot, wide, down)


def mlp_kernel(n, pieces, x_ref, cots_hbm, gate_up_hbm, down_hbm, middle_hbm, norm_ref,
               hidden_ref, grad_middle_ref, sums_ref, grad_gate_up_ref, grad_down_ref,
               cots_ref, gate_up_ref, down_ref, middle_ref, xs_ref, grads_ref, load_sems,
               acc_ref, side_out, side_in, line_in, side_sems, line_send, line_recv, gather_sems,
               wide_stage, down_stage, wide_sem, down_sem):
    loads = [
        pltpu.make_async_copy(src, dst, load_sems.at[i])
        for i, (src, dst) in enumerate(
            ((gate_up_hbm, gate_up_ref), (cots_hbm, cots_ref), (down_hbm, down_ref), (middle_hbm, middle_ref)))
    ]
    for load in loads:
        load.start()
    greet(n)
    g = Gather(n, x_ref, xs_ref, gather_sems, pieces)
    halves = tuple(
        Scatter(n, pieces // 2, side_out, side_in.at[h], line_in.at[h], side_sems.at[h], line_send.at[h], line_recv.at[h])
        for h in range(2))
    m, core = g.m, g.core
    rows, width = x_ref.shape
    half = rows // 2
    group_count, hidden_units, depth = down_ref.shape
    cut = min(512, depth)
    places = [(f, min(256, hidden_units - f)) for f in range(0, hidden_units, 256)]
    early, late = tuple(range(pieces // 2)), tuple(range(pieces // 2, pieces))
    g.start(early)
    g.start(late, outward=False)
    xs_ref[g.t] = x_ref[...]
    for load in loads:
        load.wait()

    def work(k, h):
        both = pl.ds(2 * k, 2)
        at = slice(h * half, (h + 1) * half)
        x = xs_ref[both, at, :].reshape(2 * half, width)
        cot = cots_ref[both, at, :].reshape(2 * half, width)
        for place, size in places:
            units = slice(place, place + size)
            shape = (2, half, size)

            def product(left, right):
                return sum(dot_nt(left[:, o * depth:(o + 1) * depth], right(o)) for o in range(group_count))

            gate = product(x, lambda o: gate_up_ref[o, 0, units, :])
            up = product(x, lambda o: gate_up_ref[o, 1, units, :])
            grad_hidden = product(cot, lambda o: down_ref[o, units, :])
            sig = 1.0 / (1.0 + jnp.exp(-gate))
            silu = gate * sig
            hidden_ref[both, at, units] = (silu * up).astype(jnp.bfloat16).reshape(shape)
            grads_ref[0, both, at, units] = (grad_hidden * up * (sig * (1.0 + gate * (1.0 - sig)))).astype(jnp.bfloat16).reshape(shape)
            grads_ref[1, both, at, units] = (grad_hidden * silu).astype(jnp.bfloat16).reshape(shape)

    def work_at(d, h, which):
        def one(above, _):
            k = jnp.where(above == 1, m + d, m - d)

            @pl.when((k >= 0) & (k < n) & ((d > 0) | (above == 0)))
            def _():
                g.side_wait(k, which)
                work(k, h)

            return 0

        lax.fori_loop(0, 2, one, 0)

    def ring(d, _):
        pl.when(d > 0)(lambda: g.arrive(d, early))
        pl.when(d == n - 2)(lambda: g.start(late, inward=False))
        work_at(d, 0, early)
        return 0

    lax.fori_loop(0, n, ring, 0)

    def partials(k, h):
        at = slice(h * half, (h + 1) * half)
        both = pl.ds(2 * k, 2)
        for a in range(0, width, cut):
            acc_ref[h, :, :, a:a + cut] = sum(
                dot_nn(grads_ref[c, both, at, :].reshape(2 * half, hidden_units), gate_up_ref[a // depth, c, :, a % depth:a % depth + cut])
                for c in range(2)
            ).reshape(2, half, cut)
        if h == 1:
            halves[0].side(k).wait_send()
        step = min(32, half)

        def lower(i, _):
            here = pl.ds(pl.multiple_of(i * step, step), step)
            side_out[k, here, :] = acc_ref[h, 1 - core, here, :].astype(jnp.bfloat16)
            return 0

        lax.fori_loop(0, half // step, lower, 0)
        halves[h].side(k).start()

    def one(j, _):
        k = near(n - 1 - j, m, n)
        partials(k, 0)

        def send():
            halves[0].pass_on(k, acc_ref.at[0, core], lambda p: g.arrive(j + 1, (late[0] + p,)))

        pl.when((j < n - 1) & jnp.logical_not(halves[0].inner(k)))(send)
        work_at(j, 1, late)
        pl.when((j < n - 1) & halves[0].inner(k))(send)
        return 0

    lax.fori_loop(0, n, one, 0)
    wide_cut = min(256, depth)
    per = -(-(width // wide_cut) // n)
    tokens = 2 * n * rows

    def wide_copy(place, slot):
        lanes = pl.ds(pl.multiple_of(lax.rem(place, depth), wide_cut), wide_cut)
        return pltpu.make_async_copy(
            wide_stage.at[slot], grad_gate_up_ref.at[lax.div(place, depth), :, :, lanes], wide_sem.at[slot])

    def wide_gradient(u, j):
        place = (j * per + u) * wide_cut

        @pl.when(place < width)
        def _():
            pl.when(j > 0)(lambda: wide_copy(0, u).wait())
            lanes = pl.ds(pl.multiple_of(place, wide_cut), wide_cut)
            x = xs_ref[:, :, lanes].reshape(tokens, wide_cut).T
            for c in range(2):
                wide_stage[u, c] = dot_nn(x, grads_ref[c].reshape(tokens, hidden_units)).T.astype(jnp.bfloat16)
            wide_copy(place, u).start()

    def down_copy(place, size):
        return pltpu.make_async_copy(down_stage.at[:, pl.ds(0, size)], grad_down_ref.at[:, pl.ds(place, size)], down_sem)

    def down_gradient(index):
        place, size = places[index]
        if index > 0:
            down_copy(*places[index - 1]).wait()
        low = hidden_ref[:, :, place:place + size].reshape(tokens, size).T
        for a in range(0, width, cut):
            down_stage[a // depth, :size, a % depth:a % depth + cut] = dot_nn(low, cots_ref[:, :, a:a + cut].reshape(tokens, cut)).astype(jnp.bfloat16)
        down_copy(place, size).start()

    def two(j, _):
        k = near(n - 1 - j, m, n)
        partials(k, 1)

        def send():
            halves[1].pass_on(k, acc_ref.at[1, core])

        pl.when((j < n - 1) & jnp.logical_not(halves[1].inner(k)))(send)
        for u in range(per):
            wide_gradient(u, j)
        for index in range(len(places)):
            pl.when(j == index)(functools.partial(down_gradient, index))
        pl.when((j < n - 1) & halves[1].inner(k))(send)
        return 0

    def settle(h):
        def consume(at, total):
            here = pl.ds(pl.multiple_of(h * half + at.start, at.size), at.size)
            back, gain, shift = norm_backward(middle_ref[here, :], norm_ref[2:3, :], total)
            grad_middle_ref[here, :] = cots_ref[g.t, here, :].astype(jnp.float32) + back
            sums_ref[0:1, :] += gain
            sums_ref[1:2, :] += shift

        halves[h].settle(acc_ref.at[h, core], consume)

    sums_ref[...] = jnp.zeros(sums_ref.shape, jnp.float32)
    settle(0)
    lax.fori_loop(0, n, two, 0)
    settle(1)
    for u in range(per):
        wide_copy(0, u).wait()
    down_copy(*places[-1]).wait()
    g.finish()

    def sent(k, _):
        halves[1].side(k).wait_send()
        for h in range(2):
            halves[h].finish_line(k)
        return 0

    lax.fori_loop(0, n, sent, 0)


def mlp(x, cots, gate_up, down, middle, norms, n, number, pieces=8):
    rows, width = x.shape
    group_count, hidden, depth = down.shape
    half, part = rows // 2, pieces // 2
    f32, low = jnp.float32, jnp.bfloat16
    shape = jax.ShapeDtypeStruct
    anywhere = pl.BlockSpec(memory_space=pl.ANY)
    wide_cut = min(256, depth)
    per = -(-(width // wide_cut) // n)
    dma = pltpu.SemaphoreType.DMA
    return pl.pallas_call(functools.partial(mlp_kernel, n, pieces),
        out_shape=(shape((2 * n, rows, hidden), low), shape((rows, width), f32),
                   shape((2, width), f32), shape(gate_up.shape, low), shape(down.shape, low)),
        in_specs=[VM] + [anywhere] * 4 + [VM], out_specs=(VM,) * 3 + (anywhere,) * 2,
        scratch_shapes=[
            pltpu.VMEM((2 * n, rows, width), low), pltpu.VMEM(gate_up.shape, low), pltpu.VMEM(down.shape, low), pltpu.VMEM((rows, width), f32),
            pltpu.VMEM((2 * n, rows, width), low), pltpu.VMEM((2, 2 * n, rows, hidden), low), dma((4,)),
            pltpu.VMEM((2, 2, half, width), f32), pltpu.VMEM((n, half, width), low), pltpu.VMEM((2, n, half, width), low),
            pltpu.VMEM((2, n + 1, half, width), low), dma((2, 2, n)), dma((2, n * part)), dma((2, (n + 1) * part)),
            dma((5, n * pieces)), pltpu.VMEM((per, 2, hidden, wide_cut), low), pltpu.VMEM((group_count, min(256, hidden), depth), low),
            dma((per,)), dma,
        ],
        compiler_params=params(number), cost_estimate=lasting(140), name="mlp")(x, cots, gate_up, down, middle, norms)


def down_kernel(n, pieces, hidden_ref, down_ref, middle_ref, grad_ref, out_ref, mixed_ref, wide_ref, low_ref, block_ref, back_ref, grad_out_ref, wide_parts, low_parts,
                local_sems, share_send, share_recv, xs_ref, x_ref, acc_ref, side_out, side_in, line_in, side_sems, line_send, line_recv, gather_sems):
    group_count, _, depth = down_ref.shape
    greet_all(n, group_count)
    grads = Exchange(group_count, ((wide_ref, wide_parts), (low_ref, low_parts)), local_sems, share_send, share_recv)
    g = Gather(n, x_ref, xs_ref, gather_sems, pieces)
    s = Scatter(n, pieces, side_out, side_in, line_in, side_sems, line_send, line_recv)
    x_ref[...] = grad_ref[...].astype(jnp.bfloat16)
    g.start()
    grads.start()
    xs_ref[g.t] = x_ref[...]
    m, core = s.m, s.core
    width = group_count * depth
    cut = min(512, depth)

    def one(j, _):
        k = near(n - 1 - j, m, n)
        for a in range(0, width, cut):
            s.side_out[k, :, a:a + cut] = dot_nn(hidden_ref[2 * k + 1 - core], down_ref[a // depth, :, a % depth:a % depth + cut]).astype(jnp.bfloat16)
        s.side(k).start()
        for a in range(0, width, cut):
            acc_ref[:, a:a + cut] = dot_nn(hidden_ref[2 * k + core], down_ref[a // depth, :, a % depth:a % depth + cut])
        pl.when(j < n - 1)(lambda: s.pass_on(k, acc_ref, lambda p: g.arrive(j + 1, (p,))))
        return 0

    lax.fori_loop(0, n, one, 0)

    def consume(at, total):
        block_ref[at, :] = (middle_ref[at, :] + total).astype(jnp.bfloat16)

    def last(k, _):
        g.side_wait(k)
        for c in range(2):
            back_ref[2 * k + c] = dot_nt(xs_ref[2 * k + c], out_ref[...]).astype(jnp.bfloat16)
        return 0

    lax.fori_loop(0, n, last, 0)
    flipped = mixed_ref[...].T
    for a in range(0, width, cut):
        grad_out_ref[a // depth, :, a % depth:a % depth + cut] = dot_nn(
            flipped, xs_ref[:, :, a:a + cut].reshape(mixed_ref.shape[0], cut)).astype(jnp.bfloat16)
    s.settle(acc_ref, consume)

    g.finish()
    s.finish()
    grads.finish()


def down_branch(hidden, down, middle, x, out, mixed, wide, narrow, n, number, pieces=8):
    rows, width = x.shape
    f32, low = jnp.float32, jnp.bfloat16
    return pl.pallas_call(functools.partial(down_kernel, n, pieces),
        out_shape=(jax.ShapeDtypeStruct((rows, width), low), jax.ShapeDtypeStruct((2 * n, rows, out.shape[0]), low),
                   jax.ShapeDtypeStruct((down.shape[0], out.shape[0], down.shape[2]), low),
                   jax.ShapeDtypeStruct(wide.shape, low), jax.ShapeDtypeStruct(narrow.shape, low)),
        in_specs=[VM] * 6 + [ANYWHERE] * 2, out_specs=(VM,) * 3 + (ANYWHERE,) * 2,
        scratch_shapes=exchange_scratch(2, down.shape[0]) + [pltpu.VMEM((2 * n, rows, width), low), pltpu.VMEM((rows, width), low), pltpu.VMEM((rows, width), f32)] + scatter_scratch(n, pieces, rows, width) + [pltpu.SemaphoreType.DMA((5, n * pieces))],
        compiler_params=params(number), cost_estimate=lasting(115), name="down_branch")(hidden, down, middle, x, out, mixed, wide, narrow)


def greet_everyone(count, group_count):
    t, g = lax.axis_index("tensor"), lax.axis_index("dp")
    barrier = pltpu.get_barrier_semaphore()
    for j in range(count):
        pl.when(j != t)(lambda: pl.semaphore_signal(barrier, inc=1, device_id={"tensor": j}, device_id_type=MESH))
    for i in range(group_count):
        pl.when(i != g)(lambda: pl.semaphore_signal(barrier, inc=1, device_id={"dp": i}, device_id_type=MESH))
    pl.semaphore_wait(barrier, count + group_count - 2)


class Totals:
    def __init__(self, sums, total, parts, groups, biases, near_send, near_recv, far_send, far_recv):
        self.sums, self.total, self.parts, self.groups, self.biases = sums, total, parts, groups, biases
        self.near_send, self.near_recv, self.far_send, self.far_recv = near_send, near_recv, far_send, far_recv
        self.t, self.g = lax.axis_index("tensor"), lax.axis_index("dp")
        self.count, self.group_count = parts.shape[0], groups.shape[0]
        self.piece = parts.shape[2]

    def columns(self, ref, j):
        return ref.at[:, pl.ds(pl.multiple_of(j * self.piece, self.piece), self.piece)]

    def near(self, kind, src, dst, peer, slot):
        return pltpu.make_async_remote_copy(
            src_ref=src, dst_ref=dst, send_sem=self.near_send.at[kind, peer], recv_sem=self.near_recv.at[kind, slot],
            device_id={"tensor": peer}, device_id_type=MESH)

    def far(self, kind, ref, peer, slot):
        return pltpu.make_async_remote_copy(
            src_ref=ref.at[self.g], dst_ref=ref.at[slot], send_sem=self.far_send.at[kind, peer], recv_sem=self.far_recv.at[kind, slot],
            device_id={"dp": peer}, device_id_type=MESH)

    def first(self, peer, slot):
        return self.near(0, self.columns(self.sums, peer), self.parts.at[slot], peer, slot)

    def last(self, peer, slot):
        return self.near(1, self.columns(self.total, self.t), self.columns(self.total, slot), peer, slot)

    def each_near(self, body):
        for j in range(self.count):
            pl.when(j != self.t)(lambda: body(j))

    def each_far(self, body):
        for i in range(self.group_count):
            pl.when(i != self.g)(lambda: body(i))

    def start_bias(self, bias):
        self.biases[self.g] = bias[...]
        self.each_far(lambda i: self.far(1, self.biases, i, self.g).start())

    def run(self, bias_total):
        def added(ref):
            total = ref[0]
            for j in range(1, ref.shape[0]):
                total = total + ref[j]
            return total

        here = pl.ds(pl.multiple_of(self.t * self.piece, self.piece), self.piece)
        self.each_near(lambda j: self.first(j, self.t).start())
        self.parts[self.t] = self.sums[:, here]
        self.each_near(lambda j: self.first(j, j).wait_recv())
        self.groups[self.g] = added(self.parts)
        self.each_far(lambda i: self.far(0, self.groups, i, self.g).start())
        self.each_far(lambda i: self.far(1, self.biases, i, i).wait_recv())
        bias_total[...] = added(self.biases)
        self.each_far(lambda i: self.far(0, self.groups, i, i).wait_recv())
        self.total[:, here] = added(self.groups)
        self.each_near(lambda j: self.last(j, self.t).start())
        self.each_near(lambda j: self.last(j, j).wait_recv())

    def finish(self):
        self.each_near(lambda j: self.first(j, self.t).wait_send())
        self.each_far(lambda i: self.far(0, self.groups, i, self.g).wait_send())
        self.each_far(lambda i: self.far(1, self.biases, i, self.g).wait_send())
        self.each_near(lambda j: self.last(j, self.t).wait_send())


def backward_kernel(n, pieces, length_ref, q_ref, k_ref, v_ref, kt_ref, o_ref, lse_ref, do_ref,
                    keep_hbm, ahead_hbm, behind_hbm, w_hbm, x_hbm, middle_hbm, norm_ref, sums_two_ref, xs_hbm, low_ref,
                    result_ref, total_ref, bias_total_ref, wide_parts, low_parts,
                    keep_ref, ahead_ref, behind_ref, w_ref, x_ref, middle_ref, late_sems,
                    dos_ref, delta_ref, dqt_ref, dk_ref, dv_ref, grad_ref, wide_ref, strips_ref, acc_ref, sums_ref, bias_ref, pieces_ref, groups_ref, biases_ref, side_out, side_in, line_in,
                    strip_sems, side_sems, line_send, line_recv, local_sems, share_send, share_recv, near_send, near_recv, far_send, far_recv):
    group_count = low_ref.shape[0]
    late = [
        pltpu.make_async_copy(src, dst, late_sems.at[index])
        for index, (src, dst) in enumerate((
            (keep_hbm, keep_ref), (ahead_hbm, ahead_ref), (behind_hbm, behind_ref), (w_hbm, w_ref), (x_hbm, x_ref), (middle_hbm, middle_ref)))
    ]
    for item in late:
        item.start()
    greet_everyone(2 * n, group_count)
    heads, tokens, _ = q_ref.shape
    width = heads * HEAD_DIM
    rows, features = x_ref.shape
    lane_groups = width // LANES
    per_group = LANES // HEAD_DIM
    pair = 2 * rows
    depth = features // group_count
    length = length_ref[0]
    s = Scatter(n, pieces, side_out, side_in, line_in, side_sems, line_send, line_recv)
    m, core = s.m, s.core
    grads = Exchange(group_count, ((low_ref, low_parts), (wide_ref, wide_parts)), local_sems, share_send, share_recv)
    grads.start((0,))
    strip = min(256, depth)
    strip_count = features // strip

    def strip_copy(index, slot):
        return pltpu.make_async_copy(
            xs_hbm.at[:, :, pl.ds(pl.multiple_of(index * strip, strip), strip)], strips_ref.at[slot], strip_sems.at[slot])

    for slot in range(2):
        strip_copy(slot, slot).start()
    bias_ref[...] = jnp.zeros(bias_ref.shape, jnp.float32)
    sums_ref[0:2, :] = jnp.zeros((2, features), jnp.float32)
    sums_ref[2:4, :] = sums_two_ref[...]
    totals = Totals(sums_ref, total_ref, pieces_ref, groups_ref, biases_ref, near_send, near_recv, far_send, far_recv)

    def prepare(i, _):
        at = pl.ds(pl.multiple_of(i * pair, pair), pair)
        for a in range(lane_groups):
            lanes = slice(a * LANES, (a + 1) * LANES)
            grad = do_ref[at, lanes]
            for b in range(per_group):
                dos_ref[a * per_group + b, at, :] = grad[:, b * HEAD_DIM:(b + 1) * HEAD_DIM]
            both = (grad.astype(jnp.float32) * o_ref[at, lanes].astype(jnp.float32)).T
            for b in range(per_group):
                h = a * per_group + b
                delta_ref[h:h + 1, at] = jnp.sum(both[b * HEAD_DIM:(b + 1) * HEAD_DIM], axis=0, keepdims=True)
        dqt_ref[:, at] = jnp.zeros((width, pair), jnp.float32)
        for h in range(heads):
            dk_ref[h, at, :] = jnp.zeros((pair, HEAD_DIM), jnp.float32)
            dv_ref[h, at, :] = jnp.zeros((pair, HEAD_DIM), jnp.float32)
        return 0

    lax.fori_loop(0, n, prepare, 0)
    for item in late:
        item.wait()

    falling = 2 * m < n - 1

    def order(step):
        return jnp.where(falling, n - 1 - step, step)

    def finish_block(step):
        j = order(step)

        def tile(i, j, causal):
            at = pl.ds(pl.multiple_of(i * pair, pair), pair)
            key_start = pl.multiple_of(j * pair, pair)
            keys_at = pl.ds(key_start, pair)
            for h in range(heads):
                keys, queries, grad = k_ref[h, keys_at, :], q_ref[h, at, :], dos_ref[h, at, :]
                scores = dot_nt(keys, queries) * (score_scale * log2_e)
                scores = masked_scores(scores, key_start, i * pair, length, causal)
                p = jnp.exp2(scores - lse_ref[h:h + 1, at])
                dp = dot_nt(v_ref[h, keys_at, :], grad)
                ds = (p * (dp - delta_ref[h:h + 1, at])).astype(jnp.bfloat16)
                dv_ref[h, keys_at, :] += dot_nn(p.astype(jnp.bfloat16), grad)
                dk_ref[h, keys_at, :] += dot_nn(ds, queries)
                here = slice(h * HEAD_DIM, (h + 1) * HEAD_DIM)
                dqt_ref[here, at] += dot_nn(kt_ref[here, keys_at], ds)

        def other(u, _):
            tile(jnp.where(falling, j, j + u), jnp.where(falling, j - u, j), False)
            return 0

        tile(j, j, True)
        lax.fori_loop(1, n - step, other, 0)
        keys_at = pl.ds(pl.multiple_of(j * pair, pair), pair)
        keep, ahead, behind = keep_ref[keys_at, :], -ahead_ref[keys_at, :], -behind_ref[keys_at, :]
        for a in range(lane_groups):
            lanes = slice(a * LANES, (a + 1) * LANES)
            heads_here = range(a * per_group, (a + 1) * per_group)
            dq = dqt_ref[lanes, keys_at].T
            dk = jnp.concatenate([dk_ref[h, keys_at, :] for h in heads_here], axis=1)
            dv = jnp.concatenate([dv_ref[h, keys_at, :] for h in heads_here], axis=1)
            parts = (spin(dq * score_scale, keep, ahead, behind), spin(dk * score_scale, keep, ahead, behind), dv)
            for c in range(3):
                low = parts[c].astype(jnp.bfloat16)
                place_here = slice(c * width + a * LANES, c * width + (a + 1) * LANES)
                grad_ref[keys_at, place_here] = low
                bias_ref[:, place_here] += jnp.sum(low.astype(jnp.float32), axis=0, keepdims=True)

    cut = min(512, features)

    def partial(slot, a):
        at = pl.ds(pl.multiple_of(slot * rows, rows), rows)
        return sum(dot_nt(grad_ref[at, c * width:(c + 1) * width], w_ref[c, a:a + cut, :]) for c in range(3))

    def own_partial(k):
        for a in range(0, features, cut):
            acc_ref[:, a:a + cut] = partial(2 * k + core, a)

    def strip_gradient(index, _):
        slot = lax.rem(index, 2)
        strip_copy(index, slot).wait()
        x = strips_ref[slot].reshape(tokens, strip).T
        owner = lax.div(index * strip, depth)
        at = pl.ds(pl.multiple_of(lax.rem(index * strip, depth), strip), strip)
        for c in range(3):
            wide_ref[owner, c, at, :] = dot_nn(x, grad_ref[:, c * width:(c + 1) * width]).astype(jnp.bfloat16)
        pl.when(index + 2 < strip_count)(lambda: strip_copy(index + 2, slot).start())
        return 0

    def step(j, _):
        @pl.when(j < n)
        def _():
            finish_block(j)
            k = order(j)
            for a in range(0, features, cut):
                s.side_out[k, :, a:a + cut] = partial(2 * k + 1 - core, a).astype(jnp.bfloat16)
            s.side(k).start()

        @pl.when(j == n - 1)
        def _():
            lax.fori_loop(0, strip_count, strip_gradient, 0)
            grads.start((1,))
            totals.start_bias(bias_ref)

        def one(late, _):
            turn = jnp.where(late == 1, j - 2, j)
            k = order(turn)
            inner = ((k > m) & (m > 0)) | ((k < m) & (m < n - 1))

            @pl.when((turn >= 0) & (turn < n) & (k != m) & (inner == (late == 1)))
            def _():
                own_partial(k)
                s.pass_on(k, acc_ref)

            return 0

        lax.fori_loop(0, 2, one, 0)
        return 0

    lax.fori_loop(0, n + 2, step, 0)
    own_partial(m)

    def consume(at, total):
        back, gain, shift = norm_backward(x_ref[at, :].astype(jnp.float32), norm_ref[0:1, :], total)
        result_ref[at, :] = middle_ref[at, :] + back
        sums_ref[0:1, :] += gain
        sums_ref[1:2, :] += shift

    s.settle(acc_ref, consume)
    totals.run(bias_total_ref)
    s.finish()
    grads.finish()
    totals.finish()


def backward(lengths, q, k, v, kt, o, lse, grad, keep, ahead, behind, w, x, grad_middle, norms, sums_two, xs, narrow, n, number, pieces=4):
    rows, features = x.shape
    heads, tokens, _ = q.shape
    width = heads * HEAD_DIM
    group_count = narrow.shape[0]
    depth = features // group_count
    f32, low = jnp.float32, jnp.bfloat16
    shape = jax.ShapeDtypeStruct
    wide = (group_count, 3, depth, width)
    strip = min(256, depth)
    dma = pltpu.SemaphoreType.DMA
    scatter = scatter_scratch(n, pieces, rows, features)
    return pl.pallas_call(functools.partial(backward_kernel, n, pieces),
        out_shape=(shape((rows, features), f32), shape((4, features), f32), shape((1, 3 * width), f32),
                   shape(wide, low), shape(narrow.shape, low)),
        in_specs=[pl.BlockSpec(memory_space=pltpu.SMEM)] + [VM] * 7 + [ANYWHERE] * 6 + [VM] * 2 + [ANYWHERE] * 2,
        out_specs=(VM,) * 3 + (ANYWHERE,) * 2,
        scratch_shapes=[pltpu.VMEM(item.shape, item.dtype) for item in (keep, ahead, behind, w, x, grad_middle)] + [
            dma((6,)),
            pltpu.VMEM((heads, tokens, HEAD_DIM), low), pltpu.VMEM((heads, tokens), f32), pltpu.VMEM((width, tokens), f32),
            pltpu.VMEM((heads, tokens, HEAD_DIM), f32), pltpu.VMEM((heads, tokens, HEAD_DIM), f32),
            pltpu.VMEM((tokens, 3 * width), low), pltpu.VMEM(wide, low), pltpu.VMEM((2, 2 * n, rows, strip), low),
            pltpu.VMEM((rows, features), f32), pltpu.VMEM((4, features), f32), pltpu.VMEM((1, 3 * width), f32),
            pltpu.VMEM((2 * n, 4, features // (2 * n)), f32), pltpu.VMEM((group_count, 4, features // (2 * n)), f32),
            pltpu.VMEM((group_count, 1, 3 * width), f32),
        ] + scatter[:3] + [pltpu.SemaphoreType.DMA((2,))] + scatter[3:] + exchange_scratch(2, group_count)
        + [dma((2, 2 * n)), dma((2, 2 * n)), dma((2, group_count)), dma((2, group_count))],
        compiler_params=params(number), cost_estimate=lasting(125), name="backward",
    )(lengths, q, k, v, kt, o, lse, grad, keep, ahead, behind, w, x, grad_middle, norms, sums_two, xs, narrow)


def update_kernel(rates, *refs):
    kinds = len(rates)
    ins, outs, refs = refs[:4 * kinds], refs[4 * kinds:7 * kinds], refs[7 * kinds:]
    holds, held_parts, refs = refs[:kinds], refs[kinds:2 * kinds], refs[2 * kinds:]
    load_sems, part_sems, store_sems = refs

    def load(kind, i):
        return pltpu.make_async_copy(ins[4 * kind + i], holds[kind].at[i], load_sems.at[kind, i])

    def load_parts(kind):
        return pltpu.make_async_copy(ins[4 * kind + 3], held_parts[kind], part_sems.at[kind])

    def store(kind, i):
        return pltpu.make_async_copy(holds[kind].at[i], outs[3 * kind + i], store_sems.at[kind, i])

    for kind in range(kinds):
        for i in range(3):
            load(kind, i).start()
        load_parts(kind).start()
    for kind in range(kinds):
        for i in range(3):
            load(kind, i).wait()
        load_parts(kind).wait()
        hold, part = holds[kind], held_parts[kind]
        step = min(32, hold.shape[1])

        def one(i, _):
            at = pl.ds(pl.multiple_of(i * step, step), step)
            gradient = part[0, at, :].astype(jnp.float32)
            for owner in range(1, part.shape[0]):
                gradient = gradient + part[owner, at, :].astype(jnp.float32)
            new = adamw(hold[0, at, :], hold[1, at, :], hold[2, at, :], gradient, *rates[kind])
            for index in range(3):
                hold[index, at, :] = new[index]
            return 0

        lax.fori_loop(0, hold.shape[1] // step, one, 0)
        for i in range(3):
            store(kind, i).start()
    for kind in range(kinds):
        for i in range(3):
            store(kind, i).wait()


def update(params_in, rates):
    f32 = jnp.float32
    kinds = len(rates)
    dma = pltpu.SemaphoreType.DMA
    flat = [array for group in params_in for array in group]
    results = pl.pallas_call(
        functools.partial(update_kernel, rates),
        out_shape=tuple(jax.ShapeDtypeStruct(group[0].shape, f32) for group in params_in for _ in range(3)),
        in_specs=[ANYWHERE] * len(flat), out_specs=(ANYWHERE,) * (3 * kinds),
        scratch_shapes=[pltpu.VMEM((3,) + group[0].shape, f32) for group in params_in]
        + [pltpu.VMEM(group[3].shape, group[3].dtype) for group in params_in]
        + [dma((kinds, 3)), dma((kinds,)), dma((kinds, 3))],
        compiler_params=pltpu.CompilerParams(vmem_limit_bytes=VMEM_LIMIT), cost_estimate=lasting(20), name="update",
    )(*flat)
    return tuple(results[3 * i:3 * i + 3] for i in range(kinds))


def local(
    inputs,
    cotangent,
    lengths,
    positions,
    qkv_master,
    gate_up_master,
    out_master,
    down_master,
    bias_master,
    norm_master,
    qkv_first,
    gate_up_first,
    out_first,
    down_first,
    bias_first,
    norm_first,
    qkv_second,
    gate_up_second,
    out_second,
    down_second,
    bias_second,
    norm_second,
):
    tensor_count = lax.axis_size("tensor")
    local_tokens = inputs.shape[0]
    group_tokens = local_tokens * tensor_count
    row_count = lengths.shape[0]
    row_length = group_tokens // row_count
    heads_here = bias_master.shape[1]
    width_here = heads_here * HEAD_DIM
    own_start = lax.axis_index("tensor") * local_tokens
    chips = tensor_count // 2
    group = lax.axis_index("dp")
    group_count = lax.axis_size("dp")
    group_index = own_start + jnp.arange(local_tokens, dtype=jnp.int32)
    row_of = group_index // row_length
    slot_of = group_index % row_length
    row_match = row_of[:, None] == jnp.arange(row_count, dtype=jnp.int32)[None, :]
    length_of = jnp.sum(jnp.where(row_match, lengths[None, :], 0), axis=1)
    valid = slot_of < length_of
    grad_low = jnp.where(valid[:, None], cotangent, jnp.zeros_like(cotangent))
    own_dims = jnp.arange(HEAD_DIM) // (HEAD_DIM // group_count) == group
    bias_row = jnp.where(own_dims, jnp.tile(bias_master, (1, 1, group_count)), 0.0).reshape(3, width_here)
    bias_row = jnp.concatenate([bias_row, jnp.zeros((5, width_here), jnp.float32)], axis=0)
    (
        gathered_one, qkv_copy, out_copy, queries, keys, values, keys_flipped, mixed_low, log_totals,
        keep, ahead, behind, middle, normed_two, gathered_grad, gate_up_copy, down_copy,
    ) = forward(
        lengths, positions, inputs, norm_master, qkv_master, out_master, bias_row, grad_low,
        jnp.swapaxes(gate_up_master, 1, 2), down_master, chips, group_count, 0
    )
    hidden, grad_middle, sums_two, grad_gate_up_w, grad_down = mlp(
        normed_two, gathered_grad, gate_up_copy, down_copy, middle, norm_master, chips, 2
    )
    block_output, grad_mixed, grad_out_w, gate_up_parts, down_parts = down_branch(
        hidden, down_copy, middle, grad_middle, out_copy, mixed_low, grad_gate_up_w, grad_down, chips, 3
    )
    grad_mixed = grad_mixed.reshape(group_tokens, width_here)
    input_grad, norm_grads, bias_grad, qkv_parts, out_parts = backward(
        lengths, queries, keys, values, keys_flipped, mixed_low, log_totals, grad_mixed, keep, ahead, behind,
        qkv_copy, inputs, grad_middle, norm_master, sums_two, gathered_one, grad_out_w, chips, 4
    )

    def level(array):
        return array.reshape(-1, array.shape[-1])

    def level_parts(array):
        return array.reshape(group_count, -1, array.shape[-1])

    def turned(array):
        return level(jnp.swapaxes(array, 1, 2))

    gate_up_new, down_new, out_new, qkv_new = update(
        (
            (turned(gate_up_master), turned(gate_up_first), turned(gate_up_second), level_parts(gate_up_parts)),
            (down_master, down_first, down_second, down_parts),
            (out_master, out_first, out_second, out_parts),
            (level(qkv_master), level(qkv_first), level(qkv_second), level_parts(qkv_parts)),
        ),
        (
            (2.0 / math.sqrt(D), decay_rate),
            (6.0 / math.sqrt(FF), decay_rate),
            (16.0 / math.sqrt(HEADS * HEAD_DIM), decay_rate),
            (2.0 / math.sqrt(D), decay_rate),
        ),
    )
    turned_shape = (2, gate_up_master.shape[2], gate_up_master.shape[1])
    gate_up_new = tuple(jnp.swapaxes(item.reshape(turned_shape), 1, 2) for item in gate_up_new)
    qkv_new = tuple(item.reshape(qkv_master.shape) for item in qkv_new)
    bias_grad = lax.dynamic_slice_in_dim(
        bias_grad.reshape(3, heads_here, HEAD_DIM), group * bias_master.shape[2], bias_master.shape[2], axis=2
    )
    bias_new = adamw(bias_master, bias_first, bias_second, bias_grad, 1.5, 0.0)
    norm_new = adamw(norm_master, norm_first, norm_second, norm_grads, 0.7, 0.0)
    return (
        block_output,
        input_grad,
        qkv_new[0],
        qkv_new[1],
        qkv_new[2],
        gate_up_new[0],
        gate_up_new[1],
        gate_up_new[2],
        out_new[0],
        out_new[1],
        out_new[2],
        down_new[0],
        down_new[1],
        down_new[2],
        bias_new[0],
        bias_new[1],
        bias_new[2],
        norm_new[0],
        norm_new[1],
        norm_new[2],
    )


def solution(mesh):
    return jax.shard_map(
        local,
        mesh=mesh,
        in_specs=(
            P(("dp", "tensor"), None),
            P(("dp", "tensor"), None),
            P("dp"),
            P("dp"),
            P(None, "dp", "tensor"),
            P(None, "dp", "tensor"),
            P("tensor", "dp"),
            P("tensor", "dp"),
            P(None, "tensor", "dp"),
            P(),
            P(None, "dp", "tensor"),
            P(None, "dp", "tensor"),
            P("tensor", "dp"),
            P("tensor", "dp"),
            P(None, "tensor", "dp"),
            P(),
            P(None, "dp", "tensor"),
            P(None, "dp", "tensor"),
            P("tensor", "dp"),
            P("tensor", "dp"),
            P(None, "tensor", "dp"),
            P(),
        ),
        out_specs=(
            P(("dp", "tensor"), None),
            P(("dp", "tensor"), None),
            P(None, "dp", "tensor"),
            P(None, "dp", "tensor"),
            P(None, "dp", "tensor"),
            P(None, "dp", "tensor"),
            P(None, "dp", "tensor"),
            P(None, "dp", "tensor"),
            P("tensor", "dp"),
            P("tensor", "dp"),
            P("tensor", "dp"),
            P("tensor", "dp"),
            P("tensor", "dp"),
            P("tensor", "dp"),
            P(None, "tensor", "dp"),
            P(None, "tensor", "dp"),
            P(None, "tensor", "dp"),
            P(),
            P(),
            P(),
        ),
        check_vma=False,
    )
```

```python
import functools
import math

import jax
import jax.numpy as jnp
import numpy as np
from jax import lax
from jax.experimental import pallas as pl
from jax.experimental.pallas import tpu as pltpu
from jax.sharding import PartitionSpec as P

D = 2048
HEADS = 32
HEAD_DIM = 64
ROTARY = 16
FF = 5632


norm_eps = 1e-05
beta_one = 0.9
beta_two = 0.95
adam_eps = 1e-08
adam_steps = 10
decay_rate = 0.1
rope_base = 10000.0
score_scale = 0.125
mask_fill = -1e30
log2_e = math.log2(math.e)
LANES = 128
VMEM_LIMIT = 62 * 1024 * 1024


def norm_forward(values, gain_row, shift_row):
    average = jnp.mean(values, axis=-1, keepdims=True)
    centred = values - average
    spread = jnp.mean(centred * centred, axis=-1, keepdims=True)
    return centred * lax.rsqrt(spread + norm_eps) * gain_row + shift_row


def norm_backward(values, gain_row, grad_rows):
    average = jnp.mean(values, axis=-1, keepdims=True)
    centred = values - average
    spread = jnp.mean(centred * centred, axis=-1, keepdims=True)
    inverse = lax.rsqrt(spread + norm_eps)
    normal = centred * inverse
    grad_normal = grad_rows * gain_row
    grad_values = inverse * (
        grad_normal
        - jnp.mean(grad_normal, axis=-1, keepdims=True)
        - normal * jnp.mean(grad_normal * normal, axis=-1, keepdims=True)
    )
    return (
        grad_values,
        jnp.sum(grad_rows * normal, axis=0, keepdims=True),
        jnp.sum(grad_rows, axis=0, keepdims=True),
    )


def adamw(weight_old, first_old, second_old, gradient, step_rate, decay_part):
    first_new = beta_one * first_old + (1.0 - beta_one) * gradient
    second_new = beta_two * second_old + (1.0 - beta_two) * gradient * gradient
    correct_one = 1.0 - beta_one**adam_steps
    correct_two = 1.0 - beta_two**adam_steps
    update = first_new / correct_one / (jnp.sqrt(second_new / correct_two) + adam_eps)
    return (weight_old - step_rate * (update + decay_part * weight_old), first_new, second_new)


def spin(x, keep, ahead, behind):
    return x * keep + pltpu.roll(x, LANES - ROTARY // 2, 1) * ahead + pltpu.roll(x, ROTARY // 2, 1) * behind


def dot_nt(a, b):
    return lax.dot_general(a, b, (((1,), (1,)), ((), ())), preferred_element_type=jnp.float32)


def dot_nn(a, b):
    return lax.dot_general(a, b, (((1,), (0,)), ((), ())), preferred_element_type=jnp.float32)


def masked_scores(s, key_start, query_start, length, causal):
    key_slots = key_start + lax.broadcasted_iota(jnp.int32, s.shape, 0)
    allowed = key_slots < length
    if causal:
        query_slots = query_start + lax.broadcasted_iota(jnp.int32, s.shape, 1)
        allowed = allowed & (key_slots <= query_slots)
    return jnp.where(allowed, s, mask_fill)


VM = pl.BlockSpec(memory_space=pltpu.VMEM)
ANYWHERE = pl.BlockSpec(memory_space=pl.ANY)
MESH = pl.DeviceIdType.MESH


def params(number):
    return pltpu.CompilerParams(collective_id=number, has_side_effects=True, vmem_limit_bytes=VMEM_LIMIT)


def lasting(us):
    return pl.CostEstimate(flops=int(us * 1.1e9), bytes_accessed=0, transcendentals=0)


def place():
    t = lax.axis_index("tensor")
    return t, lax.rem(t, 2), lax.div(t, 2)


def greet(n):
    t, core, chip = place()
    barrier = pltpu.get_barrier_semaphore()

    def hail(index):
        pl.semaphore_signal(barrier, inc=1, device_id={"tensor": index}, device_id_type=MESH)

    hail(t + 1 - 2 * core)
    pl.when(chip > 0)(lambda: hail(t - 2))
    pl.when(chip < n - 1)(lambda: hail(t + 2))
    pl.semaphore_wait(barrier, 1 + jnp.minimum(chip, 1) + jnp.minimum(n - 1 - chip, 1))


def near(j, m, n):
    below, above = m, n - 1 - m
    both = jnp.minimum(below, above)
    half = lax.div(j + 1, 2)
    inside = m + jnp.where((lax.rem(j, 2) == 1) == (2 * m < n - 1), half, -half)
    outside = m + jnp.where(above > below, j - both, both - j)
    return jnp.where(j <= 2 * both, inside, outside)


class Gather:
    def __init__(self, n, own, buf, sems, pieces):
        self.n, self.own, self.buf, self.pieces = n, own, buf, pieces
        self.up, self.down, self.side, self.line_in, self.side_in = [sems.at[i] for i in range(5)]
        self.t, self.core, self.m = place()
        self.sibling = self.t + 1 - 2 * self.core
        self.rows = own.shape[0] // pieces

    def copy(self, src, k, p, core, send, recv, target):
        at = pl.ds(pl.multiple_of(p * self.rows, self.rows), self.rows)
        index = k * self.pieces + p
        return pltpu.make_async_remote_copy(
            src_ref=src.at[at], dst_ref=self.buf.at[2 * k + core, at], send_sem=send.at[index],
            recv_sem=recv.at[index], device_id={"tensor": target}, device_id_type=MESH)

    def to_up(self, k, p, src):
        return self.copy(src, k, p, self.core, self.up, self.line_in, self.t + 2)

    def to_down(self, k, p, src):
        return self.copy(src, k, p, self.core, self.down, self.line_in, self.t - 2)

    def to_side(self, k, p, src):
        return self.copy(src, k, p, self.core, self.side, self.side_in, self.sibling)

    def start(self, which=None, inward=True, outward=True):
        m = self.m
        low = 2 * m < self.n - 1
        for p in range(self.pieces) if which is None else which:
            if inward and outward:
                pl.when(m < self.n - 1)(lambda: self.to_up(m, p, self.own).start())
                pl.when(m > 0)(lambda: self.to_down(m, p, self.own).start())
            else:
                pl.when((m < self.n - 1) & (low == inward))(lambda: self.to_up(m, p, self.own).start())
                pl.when((m > 0) & (low != inward))(lambda: self.to_down(m, p, self.own).start())
            if outward:
                self.to_side(m, p, self.own).start()

    def arrive(self, d, which=None):
        m = self.m
        lo, hi = m - d, m + d
        for p in range(self.pieces) if which is None else which:
            @pl.when(lo >= 0)
            def _():
                src = self.buf.at[2 * lo + self.core]
                self.to_up(lo, p, src).wait_recv()
                pl.when(m < self.n - 1)(lambda: self.to_up(lo, p, src).start())
                self.to_side(lo, p, src).start()

            @pl.when(hi < self.n)
            def _():
                src = self.buf.at[2 * hi + self.core]
                self.to_down(hi, p, src).wait_recv()
                pl.when(m > 0)(lambda: self.to_down(hi, p, src).start())
                self.to_side(hi, p, src).start()

    def side_wait(self, k, which=None):
        for p in range(self.pieces) if which is None else which:
            self.copy(self.own, k, p, 1 - self.core, self.side, self.side_in, self.sibling).wait_recv()

    def finish(self):
        m = self.m

        def one(k, _):
            for p in range(self.pieces):
                pl.when((k <= m) & (m < self.n - 1))(lambda: self.to_up(k, p, self.own).wait_send())
                pl.when((k >= m) & (m > 0))(lambda: self.to_down(k, p, self.own).wait_send())
                self.to_side(k, p, self.own).wait_send()
            return 0

        lax.fori_loop(0, self.n, one, 0)


class Scatter:
    def __init__(self, n, pieces, side_out, side_in, line_in, side_sems, line_send, line_recv):
        self.n, self.pieces = n, pieces
        self.side_out, self.side_in, self.line_in = side_out, side_in, line_in
        self.side_send, self.side_recv = side_sems.at[0], side_sems.at[1]
        self.line_send, self.line_recv = line_send, line_recv
        self.t, self.core, self.m = place()
        self.sibling = self.t + 1 - 2 * self.core
        self.rows = side_out.shape[1] // pieces
        self.step = min(32, self.rows)

    def side(self, k):
        return pltpu.make_async_remote_copy(
            src_ref=self.side_out.at[k], dst_ref=self.side_in.at[k], send_sem=self.side_send.at[k],
            recv_sem=self.side_recv.at[k], device_id={"tensor": self.sibling}, device_id_type=MESH)

    def line(self, k, p, slot, target):
        at = pl.ds(pl.multiple_of(p * self.rows, self.rows), self.rows)
        return pltpu.make_async_remote_copy(
            src_ref=self.side_in.at[k, at], dst_ref=self.line_in.at[slot, at],
            send_sem=self.line_send.at[k * self.pieces + p], recv_sem=self.line_recv.at[slot * self.pieces + p],
            device_id={"tensor": target}, device_id_type=MESH)

    def each(self, p, body):
        def one(i, _):
            body(pl.ds(pl.multiple_of(p * self.rows + i * self.step, self.step), self.step))
            return 0

        lax.fori_loop(0, self.rows // self.step, one, 0)

    def inner(self, k):
        return ((k > self.m) & (self.m > 0)) | ((k < self.m) & (self.m < self.n - 1))

    def pass_on(self, k, own, between=None):
        m, n = self.m, self.n
        self.side(k).wait_recv()
        inner = self.inner(k)

        def one(p, _):
            @pl.when(inner)
            def _():
                self.line(k, p, k, self.t).wait_recv()

                def add(at):
                    total = own[at, :] + self.side_in[k, at, :].astype(jnp.float32) + self.line_in[k, at, :].astype(jnp.float32)
                    self.side_in[k, at, :] = total.astype(jnp.bfloat16)

                self.each(p, add)

            @pl.when(jnp.logical_not(inner))
            def _():
                def add(at):
                    self.side_in[k, at, :] = (own[at, :] + self.side_in[k, at, :].astype(jnp.float32)).astype(jnp.bfloat16)

                self.each(p, add)

            pl.when(k > m)(lambda: self.line(k, p, k, self.t + 2).start())
            pl.when(k < m)(lambda: self.line(k, p, jnp.where(k == m - 1, n, k), self.t - 2).start())
            if between is not None:
                between(p)
            return 0

        lax.fori_loop(0, self.pieces, one, 0)

    def settle(self, own, consume):
        m, n = self.m, self.n
        self.side(m).wait_recv()

        def one(p, _):
            def first(at):
                own[at, :] += self.side_in[m, at, :].astype(jnp.float32)

            self.each(p, first)

            def more(slot):
                self.line(m, p, slot, self.t).wait_recv()

                def add(at):
                    own[at, :] += self.line_in[slot, at, :].astype(jnp.float32)

                self.each(p, add)

            pl.when(m > 0)(lambda: more(m))
            pl.when(m < n - 1)(lambda: more(n))
            self.each(p, lambda at: consume(at, own[at, :]))
            return 0

        lax.fori_loop(0, self.pieces, one, 0)

    def finish(self):
        def one(k, _):
            self.side(k).wait_send()
            self.finish_line(k)
            return 0

        lax.fori_loop(0, self.n, one, 0)

    def finish_line(self, k):
        @pl.when(k != self.m)
        def _():
            for p in range(self.pieces):
                self.line(k, p, k, self.t).wait_send()


def scatter_scratch(n, pieces, rows, width):
    return [
        pltpu.VMEM((n, rows, width), jnp.bfloat16), pltpu.VMEM((n, rows, width), jnp.bfloat16),
        pltpu.VMEM((n + 1, rows, width), jnp.bfloat16),
        pltpu.SemaphoreType.DMA((2, n)), pltpu.SemaphoreType.DMA((n * pieces,)), pltpu.SemaphoreType.DMA(((n + 1) * pieces,)),
    ]


class Exchange:
    def __init__(self, group_count, pairs, local_sems, send, recv):
        self.group, self.count, self.pairs = lax.axis_index("dp"), group_count, pairs
        self.local_sems, self.send, self.recv = local_sems, send, recv

    def stay(self, index):
        src, dst = self.pairs[index]
        return pltpu.make_async_copy(src.at[self.group], dst.at[self.group], self.local_sems.at[index])

    def copy(self, index, peer, slot):
        src, dst = self.pairs[index]
        return pltpu.make_async_remote_copy(
            src_ref=src.at[peer], dst_ref=dst.at[slot], send_sem=self.send.at[index, peer],
            recv_sem=self.recv.at[index, slot], device_id={"dp": peer}, device_id_type=MESH)

    def others(self, body, which=None):
        for index in range(len(self.pairs)) if which is None else which:
            for i in range(self.count):
                pl.when(i != self.group)(lambda: body(index, i))

    def start(self, which=None):
        self.others(lambda index, i: self.copy(index, i, self.group).start(), which)
        for index in range(len(self.pairs)) if which is None else which:
            self.stay(index).start()

    def finish(self):
        for index in range(len(self.pairs)):
            self.stay(index).wait()
        self.others(lambda index, i: self.copy(index, i, i).wait_recv())
        self.others(lambda index, i: self.copy(index, i, self.group).wait_send())


def exchange_scratch(pairs, group_count):
    dma = pltpu.SemaphoreType.DMA
    return [dma((pairs,)), dma((pairs, group_count)), dma((pairs, group_count))]


def greet_all(n, group_count):
    t, core, chip = place()
    g = lax.axis_index("dp")
    barrier = pltpu.get_barrier_semaphore()

    def hail(index):
        pl.semaphore_signal(barrier, inc=1, device_id={"tensor": index}, device_id_type=MESH)

    hail(t + 1 - 2 * core)
    pl.when(chip > 0)(lambda: hail(t - 2))
    pl.when(chip < n - 1)(lambda: hail(t + 2))
    for i in range(group_count):
        pl.when(i != g)(lambda: pl.semaphore_signal(barrier, inc=1, device_id={"dp": i}, device_id_type=MESH))
    pl.semaphore_wait(barrier, group_count + jnp.minimum(chip, 1) + jnp.minimum(n - 1 - chip, 1))


def forward_kernel(n, group_count, pieces, length_ref, place_ref, frequency_ref, x_ref, norm_ref, qkv_ref, out_ref, bias_ref, cot_ref, wide_hbm, down_hbm,
                   xs_out, wq_out, wo_ref, q_out, k_out, v_out, kt_out, mixed_ref, lse_ref, keep_out, ahead_out, behind_out,
                   middle_ref, normed_ref, cots_out, wide_copy, down_copy,
                   cots_ref, xs_ref, wq_ref, q_ref, k_ref, v_ref, kt_ref, keep_ref, ahead_ref, behind_ref, keep_sems,
                   wide_stage, low_stage, stage_sems, weight_send, weight_recv,
                   vt_ref, biases_ref, acc_ref, side_out, side_in, line_in, side_sems, line_send, line_recv,
                   first_sems, cot_sems, share_send, share_recv):
    greet_all(n, group_count)
    heads, total_rows, _ = q_ref.shape
    rows, features = x_ref.shape
    width = heads * HEAD_DIM
    lane_groups = width // LANES
    per_group = LANES // HEAD_DIM
    block = rows
    length = length_ref[0]
    group = lax.axis_index("dp")
    t, core, m = place()
    first = Gather(n, xs_ref.at[t], xs_ref, first_sems, pieces)
    cots = Gather(n, cots_ref.at[t], cots_ref, cot_sems, pieces)
    s = Scatter(n, pieces, side_out, side_in, line_in, side_sems, line_send, line_recv)
    step = 32

    def first_norm(i, _):
        at = pl.ds(pl.multiple_of(i * step, step), step)
        xs_ref[t, at, :] = norm_forward(x_ref[at, :].astype(jnp.float32), norm_ref[0:1, :], norm_ref[1:2, :]).astype(jnp.bfloat16)
        return 0

    lax.fori_loop(0, rows // step, first_norm, 0)
    first.start()

    def mask(i, _):
        start = pl.multiple_of(i * step, step)
        at = pl.ds(start, step)
        slots = t * rows + start + lax.broadcasted_iota(jnp.int32, (step, features), 0)
        cots_ref[t, at, :] = jnp.where(slots < length, cot_ref[at, :].astype(jnp.float32), 0.0).astype(jnp.bfloat16)
        return 0

    lax.fori_loop(0, rows // step, mask, 0)
    depth = features // group_count
    mine = pl.ds(pl.multiple_of(group * depth, depth), depth)
    for c in range(3):
        wq_ref[c, mine, :] = qkv_ref[c].astype(jnp.bfloat16)
    wo_ref[:, mine] = out_ref[...].astype(jnp.bfloat16)
    biases_ref[group] = bias_ref[...].astype(jnp.bfloat16).astype(jnp.float32)

    def share(kind, src, owner, peer):
        ref = src(owner)
        return pltpu.make_async_remote_copy(
            src_ref=ref, dst_ref=ref, send_sem=share_send.at[kind, peer], recv_sem=share_recv.at[kind, owner],
            device_id={"dp": peer}, device_id_type=MESH)

    def part(owner):
        return pl.ds(pl.multiple_of(owner * depth, depth), depth)

    kinds = (lambda o: wq_ref.at[:, part(o), :], lambda o: biases_ref.at[o], lambda o: wo_ref.at[:, part(o)])
    for kind in range(3):
        for i in range(group_count):
            pl.when(i != group)(lambda: share(kind, kinds[kind], group, i).start())

    half_units = wide_stage.shape[0]
    units = wide_hbm.shape[1]
    chunks = [(wide_hbm.at[c], wide_copy.at[group, c], u) for c in range(2) for u in range(0, units, half_units)]
    chunks += [(down_hbm, down_copy.at[group], u) for u in range(0, units, half_units)]

    def chunk_in(index):
        src, _, u = chunks[index]
        return pltpu.make_async_copy(src.at[pl.ds(u, half_units)], wide_stage, stage_sems.at[0])

    def chunk_out(index):
        _, dst, u = chunks[index]
        return pltpu.make_async_copy(low_stage, dst.at[pl.ds(u, half_units)], stage_sems.at[1])

    chunk_in(0).start()
    for index in range(len(chunks)):
        chunk_in(index).wait()
        if index > 0:
            chunk_out(index - 1).wait()
        low_stage[...] = wide_stage[...].astype(jnp.bfloat16)
        if index + 1 < len(chunks):
            chunk_in(index + 1).start()
        chunk_out(index).start()
    chunk_out(len(chunks) - 1).wait()

    def weight(kind, peer, slot):
        ref = (wide_copy, down_copy)[kind]
        return pltpu.make_async_remote_copy(
            src_ref=ref.at[group], dst_ref=ref.at[slot], send_sem=weight_send.at[kind, peer],
            recv_sem=weight_recv.at[kind, slot], device_id={"dp": peer}, device_id_type=MESH)

    def weights(body):
        for kind in range(2):
            for i in range(group_count):
                pl.when(i != group)(lambda: body(kind, i))

    def tables(i, _):
        at = pl.ds(pl.multiple_of(i * block, block), block)
        angles = jnp.broadcast_to(place_ref[:, at].astype(jnp.float32), (LANES, block)).T * frequency_ref[...]
        cosine, sine = jnp.cos(angles), jnp.sin(angles)
        dim = lax.rem(lax.broadcasted_iota(jnp.int32, (block, LANES), 1), HEAD_DIM)
        none = jnp.zeros((block, LANES), jnp.float32)
        keep_ref[at, :] = jnp.where(dim < ROTARY, cosine, 1.0)
        ahead_ref[at, :] = jnp.where(dim < ROTARY // 2, -sine, none)
        behind_ref[at, :] = jnp.where((dim >= ROTARY // 2) & (dim < ROTARY), sine, none)
        return 0

    lax.fori_loop(0, total_rows // block, tables, 0)
    def project(slot):
        at = pl.ds(pl.multiple_of(slot * block, block), block)
        keep, ahead, behind = keep_ref[at, :], ahead_ref[at, :], behind_ref[at, :]
        x = xs_ref[slot]
        for c in range(3):
            wide = dot_nn(x, wq_ref[c]) + biases_ref[group_count, c:c + 1, :]
            for a in range(lane_groups):
                lanes = slice(a * LANES, (a + 1) * LANES)
                part_wide = wide[:, lanes]
                if c < 2:
                    part_wide = spin(part_wide, keep, ahead, behind)
                if c == 1:
                    kt_ref[lanes, at] = part_wide.T.astype(jnp.bfloat16)
                if c == 2:
                    vt_ref[lanes, at] = part_wide.T.astype(jnp.bfloat16)
                for b in range(per_group):
                    (q_ref, k_ref, v_ref)[c][a * per_group + b, at, :] = part_wide[:, b * HEAD_DIM:(b + 1) * HEAD_DIM].astype(jnp.bfloat16)

    def ring(d, _):
        def one(q, _):
            other, above = lax.div(q, 2), lax.rem(q, 2)
            k = jnp.where(above == 1, m + d, m - d)

            @pl.when((k >= 0) & (k < n) & ((d > 0) | (above == 0)))
            def _():
                pl.when(other == 1)(lambda: first.side_wait(k))
                project(2 * k + jnp.where(other == 1, 1 - core, core))

            return 0

        lax.fori_loop(0, 4, one, 0)
        pl.when(d == n - 2)(lambda: first.arrive(n - 1))
        return 0

    for d in range(1, n - 1):
        first.arrive(d)
    cots.start(outward=False)
    for kind in range(3):
        for i in range(group_count):
            pl.when(i != group)(lambda: share(kind, kinds[kind], i, i).wait_recv())
    bias = biases_ref[0]
    for i in range(1, group_count):
        bias = bias + biases_ref[i]
    biases_ref[group_count] = bias

    weights(lambda kind, i: weight(kind, i, group).start())
    lax.fori_loop(0, n, ring, 0)
    kept = [
        pltpu.make_async_copy(src, dst, keep_sems.at[index])
        for index, (src, dst) in enumerate((
            (xs_ref, xs_out), (wq_ref, wq_out), (q_ref, q_out), (k_ref, k_out), (v_ref, v_out), (kt_ref, kt_out),
            (keep_ref, keep_out), (ahead_ref, ahead_out), (behind_ref, behind_out)))
    ]
    for item in kept:
        item.start()
    cots.start(inward=False)
    pair = 2 * block

    def attend(i):
        at = pl.ds(pl.multiple_of(i * pair, pair), pair)
        queries = [q_ref[h, at, :] for h in range(heads)]

        def key_block(j, carry, kind):
            key_start = pl.multiple_of(j * pair, pair)
            keys_at = pl.ds(key_start, pair)
            out = []
            for h in range(heads):
                top, total, mixed = carry[h]
                scores = dot_nt(k_ref[h, keys_at, :], queries[h]) * (score_scale * log2_e)
                if kind > 0:
                    scores = masked_scores(scores, key_start, i * pair, length, kind == 2)
                new_top = jnp.maximum(top, jnp.max(scores, axis=0, keepdims=True))
                shrink = jnp.exp2(top - new_top)
                p = jnp.exp2(scores - new_top)
                total = total * shrink + jnp.sum(p, axis=0, keepdims=True)
                mixed = mixed * shrink + dot_nn(
                    vt_ref[h * HEAD_DIM:(h + 1) * HEAD_DIM, keys_at], p.astype(jnp.bfloat16))
                out.append((new_top, total, mixed))
            return tuple(out)

        start = tuple(
            (jnp.full((1, pair), mask_fill, jnp.float32), jnp.zeros((1, pair), jnp.float32),
             jnp.zeros((HEAD_DIM, pair), jnp.float32)) for _ in range(heads))
        carry = lax.fori_loop(0, i, lambda j, c: key_block(j, c, 1), start)
        carry = key_block(i, carry, 2)
        for h in range(heads):
            top, total, mixed = carry[h]
            lse_ref[h:h + 1, at] = top + jnp.log2(total)
        for a in range(lane_groups):
            both = [carry[a * per_group + b][2] * (1.0 / carry[a * per_group + b][1]) for b in range(per_group)]
            mixed_ref[at, a * LANES:(a + 1) * LANES] = jnp.concatenate(both, axis=0).T.astype(jnp.bfloat16)

    cut = min(512, features)

    def branch(j, _):
        k = near(n - 1 - j, m, n)

        attend(k)

        def attended(slot):
            return mixed_ref[pl.ds(pl.multiple_of(slot * block, block), block), :]

        low = attended(2 * k + 1 - core)
        for a in range(0, features, cut):
            s.side_out[k, :, a:a + cut] = dot_nn(low, wo_ref[:, a:a + cut]).astype(jnp.bfloat16)
        s.side(k).start()
        low = attended(2 * k + core)
        for a in range(0, features, cut):
            acc_ref[:, a:a + cut] = dot_nn(low, wo_ref[:, a:a + cut])
        pl.when(j < n - 1)(lambda: s.pass_on(k, acc_ref, lambda p: cots.arrive(j + 1, (p,))))
        return 0

    lax.fori_loop(0, n, branch, 0)

    def consume(at, total):
        middle = x_ref[at, :].astype(jnp.float32) + total
        middle_ref[at, :] = middle
        normed_ref[at, :] = norm_forward(middle, norm_ref[2:3, :], norm_ref[3:4, :]).astype(jnp.bfloat16)

    for k in range(n):
        cots.side_wait(k)
    kept.append(pltpu.make_async_copy(cots_ref, cots_out, keep_sems.at[len(kept)]))
    kept[-1].start()
    s.settle(acc_ref, consume)
    first.finish()
    cots.finish()
    s.finish()
    for kind in range(3):
        for i in range(group_count):
            pl.when(i != group)(lambda: share(kind, kinds[kind], group, i).wait_send())
    for item in kept:
        item.wait()
    weights(lambda kind, i: weight(kind, i, i).wait_recv())
    weights(lambda kind, i: weight(kind, i, group).wait_send())


def forward(lengths, positions, x, norms, qkv, out, bias, cot, wide, down, n, group_count, number, pieces=4):
    rows, features = x.shape
    width = qkv.shape[2]
    heads = width // HEAD_DIM
    total_rows = 2 * n * rows
    f32, low = jnp.float32, jnp.bfloat16
    shape = jax.ShapeDtypeStruct
    half_rot = ROTARY // 2
    frequency = np.tile(rope_base ** (-(2.0 * np.arange(half_rot)) / ROTARY), LANES // half_rot)
    split = shape((heads, total_rows, HEAD_DIM), low)
    table = shape((total_rows, LANES), f32)
    gathered = shape((2 * n, rows, features), low)
    return pl.pallas_call(
        functools.partial(forward_kernel, n, group_count, pieces),
        out_shape=(gathered, shape((3, features, width), low), shape((width, features), low), split, split, split,
                   shape((width, total_rows), low), shape((total_rows, width), low), shape((heads, total_rows), f32),
                   table, table, table, shape((rows, features), f32), shape((rows, features), low), gathered,
                   shape((group_count,) + wide.shape, low), shape((group_count,) + down.shape, low)),
        in_specs=[pl.BlockSpec(memory_space=pltpu.SMEM)] + [VM] * 8 + [ANYWHERE] * 2,
        out_specs=(ANYWHERE, ANYWHERE, VM) + (ANYWHERE,) * 4 + (VM, VM) + (ANYWHERE,) * 3 + (VM,) * 2 + (ANYWHERE,) * 3,
        scratch_shapes=[
            pltpu.VMEM(item.shape, item.dtype)
            for item in (gathered, gathered, shape((3, features, width), low), split, split, split, shape((width, total_rows), low), table, table, table)
        ] + [
            pltpu.SemaphoreType.DMA((10,)), pltpu.VMEM((down.shape[0] // 2, down.shape[1]), f32), pltpu.VMEM((down.shape[0] // 2, down.shape[1]), low),
            pltpu.SemaphoreType.DMA((2,)), pltpu.SemaphoreType.DMA((2, group_count)), pltpu.SemaphoreType.DMA((2, group_count)),
            pltpu.VMEM((width, total_rows), low), pltpu.VMEM((group_count + 1, 8, width), f32), pltpu.VMEM((rows, features), f32),
        ] + scatter_scratch(n, pieces, rows, features) + [
            pltpu.SemaphoreType.DMA((5, n * pieces)), pltpu.SemaphoreType.DMA((5, n * pieces)),
            pltpu.SemaphoreType.DMA((3, group_count)), pltpu.SemaphoreType.DMA((3, group_count)),
        ],
        compiler_params=params(number), cost_estimate=lasting(200), name="forward",
    )(lengths, positions.reshape(1, total_rows), jnp.asarray(frequency.reshape(1, LANES), f32),
      x, norms, qkv, out, bias, cot, wide, down)


def mlp_kernel(n, pieces, x_ref, cots_hbm, gate_up_hbm, down_hbm, middle_hbm, norm_ref,
               hidden_ref, grad_middle_ref, sums_ref, grad_gate_up_ref, grad_down_ref,
               cots_ref, gate_up_ref, down_ref, middle_ref, xs_ref, grads_ref, load_sems,
               acc_ref, side_out, side_in, line_in, side_sems, line_send, line_recv, gather_sems,
               wide_stage, down_stage, wide_sem, down_sem):
    loads = [
        pltpu.make_async_copy(src, dst, load_sems.at[i])
        for i, (src, dst) in enumerate(
            ((gate_up_hbm, gate_up_ref), (cots_hbm, cots_ref), (down_hbm, down_ref), (middle_hbm, middle_ref)))
    ]
    for load in loads:
        load.start()
    greet(n)
    g = Gather(n, x_ref, xs_ref, gather_sems, pieces)
    halves = tuple(
        Scatter(n, pieces // 2, side_out, side_in.at[h], line_in.at[h], side_sems.at[h], line_send.at[h], line_recv.at[h])
        for h in range(2))
    m, core = g.m, g.core
    rows, width = x_ref.shape
    half = rows // 2
    group_count, hidden_units, depth = down_ref.shape
    cut = min(512, depth)
    places = [(f, min(256, hidden_units - f)) for f in range(0, hidden_units, 256)]
    early, late = tuple(range(pieces // 2)), tuple(range(pieces // 2, pieces))
    g.start(early)
    g.start(late, outward=False)
    xs_ref[g.t] = x_ref[...]
    for load in loads:
        load.wait()

    def work(k, h):
        both = pl.ds(2 * k, 2)
        at = slice(h * half, (h + 1) * half)
        x = xs_ref[both, at, :].reshape(2 * half, width)
        cot = cots_ref[both, at, :].reshape(2 * half, width)
        for place, size in places:
            units = slice(place, place + size)
            shape = (2, half, size)

            def product(left, right):
                return sum(dot_nt(left[:, o * depth:(o + 1) * depth], right(o)) for o in range(group_count))

            gate = product(x, lambda o: gate_up_ref[o, 0, units, :])
            up = product(x, lambda o: gate_up_ref[o, 1, units, :])
            grad_hidden = product(cot, lambda o: down_ref[o, units, :])
            sig = 1.0 / (1.0 + jnp.exp(-gate))
            silu = gate * sig
            hidden_ref[both, at, units] = (silu * up).astype(jnp.bfloat16).reshape(shape)
            grads_ref[0, both, at, units] = (grad_hidden * up * (sig * (1.0 + gate * (1.0 - sig)))).astype(jnp.bfloat16).reshape(shape)
            grads_ref[1, both, at, units] = (grad_hidden * silu).astype(jnp.bfloat16).reshape(shape)

    def work_at(d, h, which):
        def one(above, _):
            k = jnp.where(above == 1, m + d, m - d)

            @pl.when((k >= 0) & (k < n) & ((d > 0) | (above == 0)))
            def _():
                g.side_wait(k, which)
                work(k, h)

            return 0

        lax.fori_loop(0, 2, one, 0)

    def ring(d, _):
        pl.when(d > 0)(lambda: g.arrive(d, early))
        pl.when(d == n - 2)(lambda: g.start(late, inward=False))
        work_at(d, 0, early)
        return 0

    lax.fori_loop(0, n, ring, 0)

    def partials(k, h):
        at = slice(h * half, (h + 1) * half)
        both = pl.ds(2 * k, 2)
        for a in range(0, width, cut):
            acc_ref[h, :, :, a:a + cut] = sum(
                dot_nn(grads_ref[c, both, at, :].reshape(2 * half, hidden_units), gate_up_ref[a // depth, c, :, a % depth:a % depth + cut])
                for c in range(2)
            ).reshape(2, half, cut)
        if h == 1:
            halves[0].side(k).wait_send()
        step = min(32, half)

        def lower(i, _):
            here = pl.ds(pl.multiple_of(i * step, step), step)
            side_out[k, here, :] = acc_ref[h, 1 - core, here, :].astype(jnp.bfloat16)
            return 0

        lax.fori_loop(0, half // step, lower, 0)
        halves[h].side(k).start()

    def one(j, _):
        k = near(n - 1 - j, m, n)
        partials(k, 0)

        def send():
            halves[0].pass_on(k, acc_ref.at[0, core], lambda p: g.arrive(j + 1, (late[0] + p,)))

        pl.when((j < n - 1) & jnp.logical_not(halves[0].inner(k)))(send)
        work_at(j, 1, late)
        pl.when((j < n - 1) & halves[0].inner(k))(send)
        return 0

    lax.fori_loop(0, n, one, 0)
    wide_cut = min(256, depth)
    per = -(-(width // wide_cut) // n)
    tokens = 2 * n * rows

    def wide_copy(place, slot):
        lanes = pl.ds(pl.multiple_of(lax.rem(place, depth), wide_cut), wide_cut)
        return pltpu.make_async_copy(
            wide_stage.at[slot], grad_gate_up_ref.at[lax.div(place, depth), :, :, lanes], wide_sem.at[slot])

    def wide_gradient(u, j):
        place = (j * per + u) * wide_cut

        @pl.when(place < width)
        def _():
            pl.when(j > 0)(lambda: wide_copy(0, u).wait())
            lanes = pl.ds(pl.multiple_of(place, wide_cut), wide_cut)
            x = xs_ref[:, :, lanes].reshape(tokens, wide_cut).T
            for c in range(2):
                wide_stage[u, c] = dot_nn(x, grads_ref[c].reshape(tokens, hidden_units)).T.astype(jnp.bfloat16)
            wide_copy(place, u).start()

    def down_copy(place, size):
        return pltpu.make_async_copy(down_stage.at[:, pl.ds(0, size)], grad_down_ref.at[:, pl.ds(place, size)], down_sem)

    def down_gradient(index):
        place, size = places[index]
        if index > 0:
            down_copy(*places[index - 1]).wait()
        low = hidden_ref[:, :, place:place + size].reshape(tokens, size).T
        for a in range(0, width, cut):
            down_stage[a // depth, :size, a % depth:a % depth + cut] = dot_nn(low, cots_ref[:, :, a:a + cut].reshape(tokens, cut)).astype(jnp.bfloat16)
        down_copy(place, size).start()

    def two(j, _):
        k = near(n - 1 - j, m, n)
        partials(k, 1)

        def send():
            halves[1].pass_on(k, acc_ref.at[1, core])

        pl.when((j < n - 1) & jnp.logical_not(halves[1].inner(k)))(send)
        for u in range(per):
            wide_gradient(u, j)
        for index in range(len(places)):
            pl.when(j == index)(functools.partial(down_gradient, index))
        pl.when((j < n - 1) & halves[1].inner(k))(send)
        return 0

    def settle(h):
        def consume(at, total):
            here = pl.ds(pl.multiple_of(h * half + at.start, at.size), at.size)
            back, gain, shift = norm_backward(middle_ref[here, :], norm_ref[2:3, :], total)
            grad_middle_ref[here, :] = cots_ref[g.t, here, :].astype(jnp.float32) + back
            sums_ref[0:1, :] += gain
            sums_ref[1:2, :] += shift

        halves[h].settle(acc_ref.at[h, core], consume)

    sums_ref[...] = jnp.zeros(sums_ref.shape, jnp.float32)
    settle(0)
    lax.fori_loop(0, n, two, 0)
    settle(1)
    for u in range(per):
        wide_copy(0, u).wait()
    down_copy(*places[-1]).wait()
    g.finish()

    def sent(k, _):
        halves[1].side(k).wait_send()
        for h in range(2):
            halves[h].finish_line(k)
        return 0

    lax.fori_loop(0, n, sent, 0)


def mlp(x, cots, gate_up, down, middle, norms, n, number, pieces=8):
    rows, width = x.shape
    group_count, hidden, depth = down.shape
    half, part = rows // 2, pieces // 2
    f32, low = jnp.float32, jnp.bfloat16
    shape = jax.ShapeDtypeStruct
    anywhere = pl.BlockSpec(memory_space=pl.ANY)
    wide_cut = min(256, depth)
    per = -(-(width // wide_cut) // n)
    dma = pltpu.SemaphoreType.DMA
    return pl.pallas_call(functools.partial(mlp_kernel, n, pieces),
        out_shape=(shape((2 * n, rows, hidden), low), shape((rows, width), f32),
                   shape((2, width), f32), shape(gate_up.shape, low), shape(down.shape, low)),
        in_specs=[VM] + [anywhere] * 4 + [VM], out_specs=(VM,) * 3 + (anywhere,) * 2,
        scratch_shapes=[
            pltpu.VMEM((2 * n, rows, width), low), pltpu.VMEM(gate_up.shape, low), pltpu.VMEM(down.shape, low), pltpu.VMEM((rows, width), f32),
            pltpu.VMEM((2 * n, rows, width), low), pltpu.VMEM((2, 2 * n, rows, hidden), low), dma((4,)),
            pltpu.VMEM((2, 2, half, width), f32), pltpu.VMEM((n, half, width), low), pltpu.VMEM((2, n, half, width), low),
            pltpu.VMEM((2, n + 1, half, width), low), dma((2, 2, n)), dma((2, n * part)), dma((2, (n + 1) * part)),
            dma((5, n * pieces)), pltpu.VMEM((per, 2, hidden, wide_cut), low), pltpu.VMEM((group_count, min(256, hidden), depth), low),
            dma((per,)), dma,
        ],
        compiler_params=params(number), cost_estimate=lasting(140), name="mlp")(x, cots, gate_up, down, middle, norms)


def down_kernel(n, pieces, hidden_ref, down_ref, middle_hbm, grad_ref, out_hbm, mixed_hbm, wide_ref, low_ref, block_ref, back_ref, grad_out_ref, wide_parts, low_parts,
                middle_ref, out_ref, mixed_ref, late_sems, local_sems, share_send, share_recv, xs_ref, x_ref, acc_ref, side_out, side_in, line_in, side_sems, line_send, line_recv, gather_sems):
    group_count, _, depth = down_ref.shape
    greet_all(n, group_count)
    grads = Exchange(group_count, ((wide_ref, wide_parts), (low_ref, low_parts)), local_sems, share_send, share_recv)
    g = Gather(n, x_ref, xs_ref, gather_sems, pieces)
    s = Scatter(n, pieces, side_out, side_in, line_in, side_sems, line_send, line_recv)
    x_ref[...] = grad_ref[...].astype(jnp.bfloat16)
    g.start()
    grads.start()
    late = [
        pltpu.make_async_copy(src, dst, late_sems.at[index])
        for index, (src, dst) in enumerate(((middle_hbm, middle_ref), (out_hbm, out_ref), (mixed_hbm, mixed_ref)))
    ]
    for item in late:
        item.start()
    xs_ref[g.t] = x_ref[...]
    m, core = s.m, s.core
    width = group_count * depth
    cut = min(512, depth)

    def one(j, _):
        k = near(n - 1 - j, m, n)
        for a in range(0, width, cut):
            s.side_out[k, :, a:a + cut] = dot_nn(hidden_ref[2 * k + 1 - core], down_ref[a // depth, :, a % depth:a % depth + cut]).astype(jnp.bfloat16)
        s.side(k).start()
        for a in range(0, width, cut):
            acc_ref[:, a:a + cut] = dot_nn(hidden_ref[2 * k + core], down_ref[a // depth, :, a % depth:a % depth + cut])
        pl.when(j < n - 1)(lambda: s.pass_on(k, acc_ref, lambda p: g.arrive(j + 1, (p,))))
        return 0

    lax.fori_loop(0, n, one, 0)

    def consume(at, total):
        block_ref[at, :] = (middle_ref[at, :] + total).astype(jnp.bfloat16)

    for item in late:
        item.wait()

    def last(k, _):
        g.side_wait(k)
        for c in range(2):
            back_ref[2 * k + c] = dot_nt(xs_ref[2 * k + c], out_ref[...]).astype(jnp.bfloat16)
        return 0

    lax.fori_loop(0, n, last, 0)
    flipped = mixed_ref[...].T
    for a in range(0, width, cut):
        grad_out_ref[a // depth, :, a % depth:a % depth + cut] = dot_nn(
            flipped, xs_ref[:, :, a:a + cut].reshape(mixed_ref.shape[0], cut)).astype(jnp.bfloat16)
    s.settle(acc_ref, consume)

    g.finish()
    s.finish()
    grads.finish()


def down_branch(hidden, down, middle, x, out, mixed, wide, narrow, n, number, pieces=8):
    rows, width = x.shape
    f32, low = jnp.float32, jnp.bfloat16
    return pl.pallas_call(functools.partial(down_kernel, n, pieces),
        out_shape=(jax.ShapeDtypeStruct((rows, width), low), jax.ShapeDtypeStruct((2 * n, rows, out.shape[0]), low),
                   jax.ShapeDtypeStruct((down.shape[0], out.shape[0], down.shape[2]), low),
                   jax.ShapeDtypeStruct(wide.shape, low), jax.ShapeDtypeStruct(narrow.shape, low)),
        in_specs=[VM, VM, ANYWHERE, VM] + [ANYWHERE] * 4, out_specs=(VM,) * 3 + (ANYWHERE,) * 2,
        scratch_shapes=[pltpu.VMEM(item.shape, item.dtype) for item in (middle, out, mixed)] + [pltpu.SemaphoreType.DMA((3,))] + exchange_scratch(2, down.shape[0]) + [pltpu.VMEM((2 * n, rows, width), low), pltpu.VMEM((rows, width), low), pltpu.VMEM((rows, width), f32)] + scatter_scratch(n, pieces, rows, width) + [pltpu.SemaphoreType.DMA((5, n * pieces))],
        compiler_params=params(number), cost_estimate=lasting(115), name="down_branch")(hidden, down, middle, x, out, mixed, wide, narrow)


def greet_everyone(count, group_count):
    t, g = lax.axis_index("tensor"), lax.axis_index("dp")
    barrier = pltpu.get_barrier_semaphore()
    for j in range(count):
        pl.when(j != t)(lambda: pl.semaphore_signal(barrier, inc=1, device_id={"tensor": j}, device_id_type=MESH))
    for i in range(group_count):
        pl.when(i != g)(lambda: pl.semaphore_signal(barrier, inc=1, device_id={"dp": i}, device_id_type=MESH))
    pl.semaphore_wait(barrier, count + group_count - 2)


class Totals:
    def __init__(self, sums, total, parts, groups, biases, near_send, near_recv, far_send, far_recv):
        self.sums, self.total, self.parts, self.groups, self.biases = sums, total, parts, groups, biases
        self.near_send, self.near_recv, self.far_send, self.far_recv = near_send, near_recv, far_send, far_recv
        self.t, self.g = lax.axis_index("tensor"), lax.axis_index("dp")
        self.count, self.group_count = parts.shape[0], groups.shape[0]
        self.piece = parts.shape[2]

    def columns(self, ref, j):
        return ref.at[:, pl.ds(pl.multiple_of(j * self.piece, self.piece), self.piece)]

    def near(self, kind, src, dst, peer, slot):
        return pltpu.make_async_remote_copy(
            src_ref=src, dst_ref=dst, send_sem=self.near_send.at[kind, peer], recv_sem=self.near_recv.at[kind, slot],
            device_id={"tensor": peer}, device_id_type=MESH)

    def far(self, kind, ref, peer, slot):
        return pltpu.make_async_remote_copy(
            src_ref=ref.at[self.g], dst_ref=ref.at[slot], send_sem=self.far_send.at[kind, peer], recv_sem=self.far_recv.at[kind, slot],
            device_id={"dp": peer}, device_id_type=MESH)

    def first(self, peer, slot):
        return self.near(0, self.columns(self.sums, peer), self.parts.at[slot], peer, slot)

    def last(self, peer, slot):
        return self.near(1, self.columns(self.total, self.t), self.columns(self.total, slot), peer, slot)

    def each_near(self, body):
        for j in range(self.count):
            pl.when(j != self.t)(lambda: body(j))

    def each_far(self, body):
        for i in range(self.group_count):
            pl.when(i != self.g)(lambda: body(i))

    def start_bias(self, bias):
        self.biases[self.g] = bias[...]
        self.each_far(lambda i: self.far(1, self.biases, i, self.g).start())

    def run(self, bias_total):
        def added(ref):
            total = ref[0]
            for j in range(1, ref.shape[0]):
                total = total + ref[j]
            return total

        here = pl.ds(pl.multiple_of(self.t * self.piece, self.piece), self.piece)
        self.each_near(lambda j: self.first(j, self.t).start())
        self.parts[self.t] = self.sums[:, here]
        self.each_near(lambda j: self.first(j, j).wait_recv())
        self.groups[self.g] = added(self.parts)
        self.each_far(lambda i: self.far(0, self.groups, i, self.g).start())
        self.each_far(lambda i: self.far(1, self.biases, i, i).wait_recv())
        bias_total[...] = added(self.biases)
        self.each_far(lambda i: self.far(0, self.groups, i, i).wait_recv())
        self.total[:, here] = added(self.groups)
        self.each_near(lambda j: self.last(j, self.t).start())
        self.each_near(lambda j: self.last(j, j).wait_recv())

    def finish(self):
        self.each_near(lambda j: self.first(j, self.t).wait_send())
        self.each_far(lambda i: self.far(0, self.groups, i, self.g).wait_send())
        self.each_far(lambda i: self.far(1, self.biases, i, self.g).wait_send())
        self.each_near(lambda j: self.last(j, self.t).wait_send())


def backward_kernel(n, pieces, length_ref, q_ref, k_ref, v_ref, kt_ref, o_ref, lse_ref, do_ref,
                    keep_hbm, ahead_hbm, behind_hbm, w_hbm, x_hbm, middle_hbm, norm_ref, sums_two_ref, xs_hbm, low_ref,
                    result_ref, total_ref, bias_total_ref, wide_parts, low_parts,
                    keep_ref, ahead_ref, behind_ref, w_ref, x_ref, middle_ref, late_sems,
                    dos_ref, delta_ref, dqt_ref, dk_ref, dv_ref, grad_ref, wide_ref, strips_ref, acc_ref, sums_ref, bias_ref, pieces_ref, groups_ref, biases_ref, side_out, side_in, line_in,
                    strip_sems, side_sems, line_send, line_recv, local_sems, share_send, share_recv, near_send, near_recv, far_send, far_recv):
    group_count = low_ref.shape[0]
    late = [
        pltpu.make_async_copy(src, dst, late_sems.at[index])
        for index, (src, dst) in enumerate((
            (keep_hbm, keep_ref), (ahead_hbm, ahead_ref), (behind_hbm, behind_ref), (w_hbm, w_ref), (x_hbm, x_ref), (middle_hbm, middle_ref)))
    ]
    for item in late:
        item.start()
    greet_everyone(2 * n, group_count)
    heads, tokens, _ = q_ref.shape
    width = heads * HEAD_DIM
    rows, features = x_ref.shape
    lane_groups = width // LANES
    per_group = LANES // HEAD_DIM
    pair = 2 * rows
    depth = features // group_count
    length = length_ref[0]
    s = Scatter(n, pieces, side_out, side_in, line_in, side_sems, line_send, line_recv)
    m, core = s.m, s.core
    grads = Exchange(group_count, ((low_ref, low_parts), (wide_ref, wide_parts)), local_sems, share_send, share_recv)
    grads.start((0,))
    strip = min(256, depth)
    strip_count = features // strip

    def strip_copy(index, slot):
        return pltpu.make_async_copy(
            xs_hbm.at[:, :, pl.ds(pl.multiple_of(index * strip, strip), strip)], strips_ref.at[slot], strip_sems.at[slot])

    for slot in range(2):
        strip_copy(slot, slot).start()
    bias_ref[...] = jnp.zeros(bias_ref.shape, jnp.float32)
    sums_ref[0:2, :] = jnp.zeros((2, features), jnp.float32)
    sums_ref[2:4, :] = sums_two_ref[...]
    totals = Totals(sums_ref, total_ref, pieces_ref, groups_ref, biases_ref, near_send, near_recv, far_send, far_recv)

    def prepare(i, _):
        at = pl.ds(pl.multiple_of(i * pair, pair), pair)
        for a in range(lane_groups):
            lanes = slice(a * LANES, (a + 1) * LANES)
            grad = do_ref[at, lanes]
            for b in range(per_group):
                dos_ref[a * per_group + b, at, :] = grad[:, b * HEAD_DIM:(b + 1) * HEAD_DIM]
            both = (grad.astype(jnp.float32) * o_ref[at, lanes].astype(jnp.float32)).T
            for b in range(per_group):
                h = a * per_group + b
                delta_ref[h:h + 1, at] = jnp.sum(both[b * HEAD_DIM:(b + 1) * HEAD_DIM], axis=0, keepdims=True)
        dqt_ref[:, at] = jnp.zeros((width, pair), jnp.float32)
        for h in range(heads):
            dk_ref[h, at, :] = jnp.zeros((pair, HEAD_DIM), jnp.float32)
            dv_ref[h, at, :] = jnp.zeros((pair, HEAD_DIM), jnp.float32)
        return 0

    lax.fori_loop(0, n, prepare, 0)
    for item in late:
        item.wait()

    falling = 2 * m < n - 1

    def order(step):
        return jnp.where(falling, n - 1 - step, step)

    def finish_block(step):
        j = order(step)

        def tile(i, j, causal):
            at = pl.ds(pl.multiple_of(i * pair, pair), pair)
            key_start = pl.multiple_of(j * pair, pair)
            keys_at = pl.ds(key_start, pair)
            for h in range(heads):
                keys, queries, grad = k_ref[h, keys_at, :], q_ref[h, at, :], dos_ref[h, at, :]
                scores = dot_nt(keys, queries) * (score_scale * log2_e)
                scores = masked_scores(scores, key_start, i * pair, length, causal)
                p = jnp.exp2(scores - lse_ref[h:h + 1, at])
                dp = dot_nt(v_ref[h, keys_at, :], grad)
                ds = (p * (dp - delta_ref[h:h + 1, at])).astype(jnp.bfloat16)
                dv_ref[h, keys_at, :] += dot_nn(p.astype(jnp.bfloat16), grad)
                dk_ref[h, keys_at, :] += dot_nn(ds, queries)
                here = slice(h * HEAD_DIM, (h + 1) * HEAD_DIM)
                dqt_ref[here, at] += dot_nn(kt_ref[here, keys_at], ds)

        def other(u, _):
            tile(jnp.where(falling, j, j + u), jnp.where(falling, j - u, j), False)
            return 0

        tile(j, j, True)
        lax.fori_loop(1, n - step, other, 0)
        keys_at = pl.ds(pl.multiple_of(j * pair, pair), pair)
        keep, ahead, behind = keep_ref[keys_at, :], -ahead_ref[keys_at, :], -behind_ref[keys_at, :]
        for a in range(lane_groups):
            lanes = slice(a * LANES, (a + 1) * LANES)
            heads_here = range(a * per_group, (a + 1) * per_group)
            dq = dqt_ref[lanes, keys_at].T
            dk = jnp.concatenate([dk_ref[h, keys_at, :] for h in heads_here], axis=1)
            dv = jnp.concatenate([dv_ref[h, keys_at, :] for h in heads_here], axis=1)
            parts = (spin(dq * score_scale, keep, ahead, behind), spin(dk * score_scale, keep, ahead, behind), dv)
            for c in range(3):
                low = parts[c].astype(jnp.bfloat16)
                place_here = slice(c * width + a * LANES, c * width + (a + 1) * LANES)
                grad_ref[keys_at, place_here] = low
                bias_ref[:, place_here] += jnp.sum(low.astype(jnp.float32), axis=0, keepdims=True)

    cut = min(512, features)

    def partial(slot, a):
        at = pl.ds(pl.multiple_of(slot * rows, rows), rows)
        return sum(dot_nt(grad_ref[at, c * width:(c + 1) * width], w_ref[c, a:a + cut, :]) for c in range(3))

    def own_partial(k):
        for a in range(0, features, cut):
            acc_ref[:, a:a + cut] = partial(2 * k + core, a)

    def strip_gradient(index, _):
        slot = lax.rem(index, 2)
        strip_copy(index, slot).wait()
        x = strips_ref[slot].reshape(tokens, strip).T
        owner = lax.div(index * strip, depth)
        at = pl.ds(pl.multiple_of(lax.rem(index * strip, depth), strip), strip)
        for c in range(3):
            wide_ref[owner, c, at, :] = dot_nn(x, grad_ref[:, c * width:(c + 1) * width]).astype(jnp.bfloat16)
        pl.when(index + 2 < strip_count)(lambda: strip_copy(index + 2, slot).start())
        return 0

    def step(j, _):
        @pl.when(j < n)
        def _():
            finish_block(j)
            k = order(j)
            for a in range(0, features, cut):
                s.side_out[k, :, a:a + cut] = partial(2 * k + 1 - core, a).astype(jnp.bfloat16)
            s.side(k).start()

        @pl.when(j == n - 1)
        def _():
            lax.fori_loop(0, strip_count, strip_gradient, 0)
            grads.start((1,))
            totals.start_bias(bias_ref)

        def one(late, _):
            turn = jnp.where(late == 1, j - 2, j)
            k = order(turn)
            inner = ((k > m) & (m > 0)) | ((k < m) & (m < n - 1))

            @pl.when((turn >= 0) & (turn < n) & (k != m) & (inner == (late == 1)))
            def _():
                own_partial(k)
                s.pass_on(k, acc_ref)

            return 0

        lax.fori_loop(0, 2, one, 0)
        return 0

    lax.fori_loop(0, n + 2, step, 0)
    own_partial(m)

    def consume(at, total):
        back, gain, shift = norm_backward(x_ref[at, :].astype(jnp.float32), norm_ref[0:1, :], total)
        result_ref[at, :] = middle_ref[at, :] + back
        sums_ref[0:1, :] += gain
        sums_ref[1:2, :] += shift

    s.settle(acc_ref, consume)
    totals.run(bias_total_ref)
    s.finish()
    grads.finish()
    totals.finish()


def backward(lengths, q, k, v, kt, o, lse, grad, keep, ahead, behind, w, x, grad_middle, norms, sums_two, xs, narrow, n, number, pieces=4):
    rows, features = x.shape
    heads, tokens, _ = q.shape
    width = heads * HEAD_DIM
    group_count = narrow.shape[0]
    depth = features // group_count
    f32, low = jnp.float32, jnp.bfloat16
    shape = jax.ShapeDtypeStruct
    wide = (group_count, 3, depth, width)
    strip = min(256, depth)
    dma = pltpu.SemaphoreType.DMA
    scatter = scatter_scratch(n, pieces, rows, features)
    return pl.pallas_call(functools.partial(backward_kernel, n, pieces),
        out_shape=(shape((rows, features), f32), shape((4, features), f32), shape((1, 3 * width), f32),
                   shape(wide, low), shape(narrow.shape, low)),
        in_specs=[pl.BlockSpec(memory_space=pltpu.SMEM)] + [VM] * 7 + [ANYWHERE] * 6 + [VM] * 2 + [ANYWHERE] * 2,
        out_specs=(VM,) * 3 + (ANYWHERE,) * 2,
        scratch_shapes=[pltpu.VMEM(item.shape, item.dtype) for item in (keep, ahead, behind, w, x, grad_middle)] + [
            dma((6,)),
            pltpu.VMEM((heads, tokens, HEAD_DIM), low), pltpu.VMEM((heads, tokens), f32), pltpu.VMEM((width, tokens), f32),
            pltpu.VMEM((heads, tokens, HEAD_DIM), f32), pltpu.VMEM((heads, tokens, HEAD_DIM), f32),
            pltpu.VMEM((tokens, 3 * width), low), pltpu.VMEM(wide, low), pltpu.VMEM((2, 2 * n, rows, strip), low),
            pltpu.VMEM((rows, features), f32), pltpu.VMEM((4, features), f32), pltpu.VMEM((1, 3 * width), f32),
            pltpu.VMEM((2 * n, 4, features // (2 * n)), f32), pltpu.VMEM((group_count, 4, features // (2 * n)), f32),
            pltpu.VMEM((group_count, 1, 3 * width), f32),
        ] + scatter[:3] + [pltpu.SemaphoreType.DMA((2,))] + scatter[3:] + exchange_scratch(2, group_count)
        + [dma((2, 2 * n)), dma((2, 2 * n)), dma((2, group_count)), dma((2, group_count))],
        compiler_params=params(number), cost_estimate=lasting(125), name="backward",
    )(lengths, q, k, v, kt, o, lse, grad, keep, ahead, behind, w, x, grad_middle, norms, sums_two, xs, narrow)


def update_kernel(rates, *refs):
    kinds = len(rates)
    ins, outs, refs = refs[:4 * kinds], refs[4 * kinds:7 * kinds], refs[7 * kinds:]
    holds, held_parts, refs = refs[:kinds], refs[kinds:2 * kinds], refs[2 * kinds:]
    load_sems, part_sems, store_sems = refs

    def load(kind, i):
        return pltpu.make_async_copy(ins[4 * kind + i], holds[kind].at[i], load_sems.at[kind, i])

    def load_parts(kind):
        return pltpu.make_async_copy(ins[4 * kind + 3], held_parts[kind], part_sems.at[kind])

    def store(kind, i):
        return pltpu.make_async_copy(holds[kind].at[i], outs[3 * kind + i], store_sems.at[kind, i])

    for kind in range(kinds):
        for i in range(3):
            load(kind, i).start()
        load_parts(kind).start()
    for kind in range(kinds):
        for i in range(3):
            load(kind, i).wait()
        load_parts(kind).wait()
        hold, part = holds[kind], held_parts[kind]
        step = min(32, hold.shape[1])

        def one(i, _):
            at = pl.ds(pl.multiple_of(i * step, step), step)
            gradient = part[0, at, :].astype(jnp.float32)
            for owner in range(1, part.shape[0]):
                gradient = gradient + part[owner, at, :].astype(jnp.float32)
            new = adamw(hold[0, at, :], hold[1, at, :], hold[2, at, :], gradient, *rates[kind])
            for index in range(3):
                hold[index, at, :] = new[index]
            return 0

        lax.fori_loop(0, hold.shape[1] // step, one, 0)
        for i in range(3):
            store(kind, i).start()
    for kind in range(kinds):
        for i in range(3):
            store(kind, i).wait()


def update(params_in, rates):
    f32 = jnp.float32
    kinds = len(rates)
    dma = pltpu.SemaphoreType.DMA
    flat = [array for group in params_in for array in group]
    results = pl.pallas_call(
        functools.partial(update_kernel, rates),
        out_shape=tuple(jax.ShapeDtypeStruct(group[0].shape, f32) for group in params_in for _ in range(3)),
        in_specs=[ANYWHERE] * len(flat), out_specs=(ANYWHERE,) * (3 * kinds),
        scratch_shapes=[pltpu.VMEM((3,) + group[0].shape, f32) for group in params_in]
        + [pltpu.VMEM(group[3].shape, group[3].dtype) for group in params_in]
        + [dma((kinds, 3)), dma((kinds,)), dma((kinds, 3))],
        compiler_params=pltpu.CompilerParams(vmem_limit_bytes=VMEM_LIMIT), cost_estimate=lasting(20), name="update",
    )(*flat)
    return tuple(results[3 * i:3 * i + 3] for i in range(kinds))


def local(
    inputs,
    cotangent,
    lengths,
    positions,
    qkv_master,
    gate_up_master,
    out_master,
    down_master,
    bias_master,
    norm_master,
    qkv_first,
    gate_up_first,
    out_first,
    down_first,
    bias_first,
    norm_first,
    qkv_second,
    gate_up_second,
    out_second,
    down_second,
    bias_second,
    norm_second,
):
    tensor_count = lax.axis_size("tensor")
    local_tokens = inputs.shape[0]
    group_tokens = local_tokens * tensor_count
    row_count = lengths.shape[0]
    row_length = group_tokens // row_count
    heads_here = bias_master.shape[1]
    width_here = heads_here * HEAD_DIM
    chips = tensor_count // 2
    group = lax.axis_index("dp")
    group_count = lax.axis_size("dp")
    own_dims = jnp.arange(HEAD_DIM) // (HEAD_DIM // group_count) == group
    bias_row = jnp.where(own_dims, jnp.tile(bias_master, (1, 1, group_count)), 0.0).reshape(3, width_here)
    bias_row = jnp.concatenate([bias_row, jnp.zeros((5, width_here), jnp.float32)], axis=0)
    (
        gathered_one, qkv_copy, out_copy, queries, keys, values, keys_flipped, mixed_low, log_totals,
        keep, ahead, behind, middle, normed_two, gathered_grad, gate_up_copy, down_copy,
    ) = forward(
        lengths, positions, inputs, norm_master, qkv_master, out_master, bias_row, cotangent,
        jnp.swapaxes(gate_up_master, 1, 2), down_master, chips, group_count, 0
    )
    hidden, grad_middle, sums_two, grad_gate_up_w, grad_down = mlp(
        normed_two, gathered_grad, gate_up_copy, down_copy, middle, norm_master, chips, 2
    )
    block_output, grad_mixed, grad_out_w, gate_up_parts, down_parts = down_branch(
        hidden, down_copy, middle, grad_middle, out_copy, mixed_low, grad_gate_up_w, grad_down, chips, 3
    )
    grad_mixed = grad_mixed.reshape(group_tokens, width_here)
    input_grad, norm_grads, bias_grad, qkv_parts, out_parts = backward(
        lengths, queries, keys, values, keys_flipped, mixed_low, log_totals, grad_mixed, keep, ahead, behind,
        qkv_copy, inputs, grad_middle, norm_master, sums_two, gathered_one, grad_out_w, chips, 4
    )

    def level(array):
        return array.reshape(-1, array.shape[-1])

    def level_parts(array):
        return array.reshape(group_count, -1, array.shape[-1])

    def turned(array):
        return level(jnp.swapaxes(array, 1, 2))

    gate_up_new, down_new, out_new, qkv_new = update(
        (
            (turned(gate_up_master), turned(gate_up_first), turned(gate_up_second), level_parts(gate_up_parts)),
            (down_master, down_first, down_second, down_parts),
            (out_master, out_first, out_second, out_parts),
            (level(qkv_master), level(qkv_first), level(qkv_second), level_parts(qkv_parts)),
        ),
        (
            (2.0 / math.sqrt(D), decay_rate),
            (6.0 / math.sqrt(FF), decay_rate),
            (16.0 / math.sqrt(HEADS * HEAD_DIM), decay_rate),
            (2.0 / math.sqrt(D), decay_rate),
        ),
    )
    turned_shape = (2, gate_up_master.shape[2], gate_up_master.shape[1])
    gate_up_new = tuple(jnp.swapaxes(item.reshape(turned_shape), 1, 2) for item in gate_up_new)
    qkv_new = tuple(item.reshape(qkv_master.shape) for item in qkv_new)
    bias_grad = lax.dynamic_slice_in_dim(
        bias_grad.reshape(3, heads_here, HEAD_DIM), group * bias_master.shape[2], bias_master.shape[2], axis=2
    )
    bias_new = adamw(bias_master, bias_first, bias_second, bias_grad, 1.5, 0.0)
    norm_new = adamw(norm_master, norm_first, norm_second, norm_grads, 0.7, 0.0)
    return (
        block_output,
        input_grad,
        qkv_new[0],
        qkv_new[1],
        qkv_new[2],
        gate_up_new[0],
        gate_up_new[1],
        gate_up_new[2],
        out_new[0],
        out_new[1],
        out_new[2],
        down_new[0],
        down_new[1],
        down_new[2],
        bias_new[0],
        bias_new[1],
        bias_new[2],
        norm_new[0],
        norm_new[1],
        norm_new[2],
    )


def solution(mesh):
    return jax.shard_map(
        local,
        mesh=mesh,
        in_specs=(
            P(("dp", "tensor"), None),
            P(("dp", "tensor"), None),
            P("dp"),
            P("dp"),
            P(None, "dp", "tensor"),
            P(None, "dp", "tensor"),
            P("tensor", "dp"),
            P("tensor", "dp"),
            P(None, "tensor", "dp"),
            P(),
            P(None, "dp", "tensor"),
            P(None, "dp", "tensor"),
            P("tensor", "dp"),
            P("tensor", "dp"),
            P(None, "tensor", "dp"),
            P(),
            P(None, "dp", "tensor"),
            P(None, "dp", "tensor"),
            P("tensor", "dp"),
            P("tensor", "dp"),
            P(None, "tensor", "dp"),
            P(),
        ),
        out_specs=(
            P(("dp", "tensor"), None),
            P(("dp", "tensor"), None),
            P(None, "dp", "tensor"),
            P(None, "dp", "tensor"),
            P(None, "dp", "tensor"),
            P(None, "dp", "tensor"),
            P(None, "dp", "tensor"),
            P(None, "dp", "tensor"),
            P("tensor", "dp"),
            P("tensor", "dp"),
            P("tensor", "dp"),
            P("tensor", "dp"),
            P("tensor", "dp"),
            P("tensor", "dp"),
            P(None, "tensor", "dp"),
            P(None, "tensor", "dp"),
            P(None, "tensor", "dp"),
            P(),
            P(),
            P(),
        ),
        check_vma=False,
    )
```

```python
import functools
import math

import jax
import jax.numpy as jnp
import numpy as np
from jax import lax
from jax.experimental import pallas as pl
from jax.experimental.pallas import tpu as pltpu
from jax.sharding import PartitionSpec as P

D = 2048
HEADS = 32
HEAD_DIM = 64
ROTARY = 16
FF = 5632


norm_eps = 1e-05
beta_one = 0.9
beta_two = 0.95
adam_eps = 1e-08
adam_steps = 10
decay_rate = 0.1
rope_base = 10000.0
score_scale = 0.125
mask_fill = -1e30
log2_e = math.log2(math.e)
LANES = 128
VMEM_LIMIT = 62 * 1024 * 1024


def norm_forward(values, gain_row, shift_row):
    average = jnp.mean(values, axis=-1, keepdims=True)
    centred = values - average
    spread = jnp.mean(centred * centred, axis=-1, keepdims=True)
    return centred * lax.rsqrt(spread + norm_eps) * gain_row + shift_row


def norm_backward(values, gain_row, grad_rows):
    average = jnp.mean(values, axis=-1, keepdims=True)
    centred = values - average
    spread = jnp.mean(centred * centred, axis=-1, keepdims=True)
    inverse = lax.rsqrt(spread + norm_eps)
    normal = centred * inverse
    grad_normal = grad_rows * gain_row
    grad_values = inverse * (
        grad_normal
        - jnp.mean(grad_normal, axis=-1, keepdims=True)
        - normal * jnp.mean(grad_normal * normal, axis=-1, keepdims=True)
    )
    return (
        grad_values,
        jnp.sum(grad_rows * normal, axis=0, keepdims=True),
        jnp.sum(grad_rows, axis=0, keepdims=True),
    )


def adamw(weight_old, first_old, second_old, gradient, step_rate, decay_part):
    first_new = beta_one * first_old + (1.0 - beta_one) * gradient
    second_new = beta_two * second_old + (1.0 - beta_two) * gradient * gradient
    correct_one = 1.0 - beta_one**adam_steps
    correct_two = 1.0 - beta_two**adam_steps
    update = first_new / correct_one / (jnp.sqrt(second_new / correct_two) + adam_eps)
    return (weight_old - step_rate * (update + decay_part * weight_old), first_new, second_new)


def spin(x, keep, ahead, behind):
    return x * keep + pltpu.roll(x, LANES - ROTARY // 2, 1) * ahead + pltpu.roll(x, ROTARY // 2, 1) * behind


def dot_nt(a, b):
    return lax.dot_general(a, b, (((1,), (1,)), ((), ())), preferred_element_type=jnp.float32)


def dot_nn(a, b):
    return lax.dot_general(a, b, (((1,), (0,)), ((), ())), preferred_element_type=jnp.float32)


def masked_scores(s, key_start, query_start, length, causal):
    key_slots = key_start + lax.broadcasted_iota(jnp.int32, s.shape, 0)
    allowed = key_slots < length
    if causal:
        query_slots = query_start + lax.broadcasted_iota(jnp.int32, s.shape, 1)
        allowed = allowed & (key_slots <= query_slots)
    return jnp.where(allowed, s, mask_fill)


VM = pl.BlockSpec(memory_space=pltpu.VMEM)
ANYWHERE = pl.BlockSpec(memory_space=pl.ANY)
MESH = pl.DeviceIdType.MESH


def params(number):
    return pltpu.CompilerParams(collective_id=number, has_side_effects=True, vmem_limit_bytes=VMEM_LIMIT)


def lasting(us):
    return pl.CostEstimate(flops=int(us * 1.1e9), bytes_accessed=0, transcendentals=0)


def place():
    t = lax.axis_index("tensor")
    return t, lax.rem(t, 2), lax.div(t, 2)


def greet(n):
    t, core, chip = place()
    barrier = pltpu.get_barrier_semaphore()

    def hail(index):
        pl.semaphore_signal(barrier, inc=1, device_id={"tensor": index}, device_id_type=MESH)

    hail(t + 1 - 2 * core)
    pl.when(chip > 0)(lambda: hail(t - 2))
    pl.when(chip < n - 1)(lambda: hail(t + 2))
    pl.semaphore_wait(barrier, 1 + jnp.minimum(chip, 1) + jnp.minimum(n - 1 - chip, 1))


def near(j, m, n):
    below, above = m, n - 1 - m
    both = jnp.minimum(below, above)
    half = lax.div(j + 1, 2)
    inside = m + jnp.where((lax.rem(j, 2) == 1) == (2 * m < n - 1), half, -half)
    outside = m + jnp.where(above > below, j - both, both - j)
    return jnp.where(j <= 2 * both, inside, outside)


class Gather:
    def __init__(self, n, own, buf, sems, pieces):
        self.n, self.own, self.buf, self.pieces = n, own, buf, pieces
        self.up, self.down, self.side, self.line_in, self.side_in = [sems.at[i] for i in range(5)]
        self.t, self.core, self.m = place()
        self.sibling = self.t + 1 - 2 * self.core
        self.rows = own.shape[0] // pieces

    def copy(self, src, k, p, core, send, recv, target):
        at = pl.ds(pl.multiple_of(p * self.rows, self.rows), self.rows)
        index = k * self.pieces + p
        return pltpu.make_async_remote_copy(
            src_ref=src.at[at], dst_ref=self.buf.at[2 * k + core, at], send_sem=send.at[index],
            recv_sem=recv.at[index], device_id={"tensor": target}, device_id_type=MESH)

    def to_up(self, k, p, src):
        return self.copy(src, k, p, self.core, self.up, self.line_in, self.t + 2)

    def to_down(self, k, p, src):
        return self.copy(src, k, p, self.core, self.down, self.line_in, self.t - 2)

    def to_side(self, k, p, src):
        return self.copy(src, k, p, self.core, self.side, self.side_in, self.sibling)

    def start(self, which=None, inward=True, outward=True):
        m = self.m
        low = 2 * m < self.n - 1
        for p in range(self.pieces) if which is None else which:
            if inward and outward:
                pl.when(m < self.n - 1)(lambda: self.to_up(m, p, self.own).start())
                pl.when(m > 0)(lambda: self.to_down(m, p, self.own).start())
            else:
                pl.when((m < self.n - 1) & (low == inward))(lambda: self.to_up(m, p, self.own).start())
                pl.when((m > 0) & (low != inward))(lambda: self.to_down(m, p, self.own).start())
            if outward:
                self.to_side(m, p, self.own).start()

    def arrive(self, d, which=None):
        m = self.m
        lo, hi = m - d, m + d
        for p in range(self.pieces) if which is None else which:
            @pl.when(lo >= 0)
            def _():
                src = self.buf.at[2 * lo + self.core]
                self.to_up(lo, p, src).wait_recv()
                pl.when(m < self.n - 1)(lambda: self.to_up(lo, p, src).start())
                self.to_side(lo, p, src).start()

            @pl.when(hi < self.n)
            def _():
                src = self.buf.at[2 * hi + self.core]
                self.to_down(hi, p, src).wait_recv()
                pl.when(m > 0)(lambda: self.to_down(hi, p, src).start())
                self.to_side(hi, p, src).start()

    def side_wait(self, k, which=None):
        for p in range(self.pieces) if which is None else which:
            self.copy(self.own, k, p, 1 - self.core, self.side, self.side_in, self.sibling).wait_recv()

    def finish(self):
        m = self.m

        def one(k, _):
            for p in range(self.pieces):
                pl.when((k <= m) & (m < self.n - 1))(lambda: self.to_up(k, p, self.own).wait_send())
                pl.when((k >= m) & (m > 0))(lambda: self.to_down(k, p, self.own).wait_send())
                self.to_side(k, p, self.own).wait_send()
            return 0

        lax.fori_loop(0, self.n, one, 0)


class Scatter:
    def __init__(self, n, pieces, side_out, side_in, line_in, side_sems, line_send, line_recv):
        self.n, self.pieces = n, pieces
        self.side_out, self.side_in, self.line_in = side_out, side_in, line_in
        self.side_send, self.side_recv = side_sems.at[0], side_sems.at[1]
        self.line_send, self.line_recv = line_send, line_recv
        self.t, self.core, self.m = place()
        self.sibling = self.t + 1 - 2 * self.core
        self.rows = side_out.shape[1] // pieces
        self.step = min(32, self.rows)

    def side(self, k):
        return pltpu.make_async_remote_copy(
            src_ref=self.side_out.at[k], dst_ref=self.side_in.at[k], send_sem=self.side_send.at[k],
            recv_sem=self.side_recv.at[k], device_id={"tensor": self.sibling}, device_id_type=MESH)

    def line(self, k, p, slot, target):
        at = pl.ds(pl.multiple_of(p * self.rows, self.rows), self.rows)
        return pltpu.make_async_remote_copy(
            src_ref=self.side_in.at[k, at], dst_ref=self.line_in.at[slot, at],
            send_sem=self.line_send.at[k * self.pieces + p], recv_sem=self.line_recv.at[slot * self.pieces + p],
            device_id={"tensor": target}, device_id_type=MESH)

    def each(self, p, body):
        def one(i, _):
            body(pl.ds(pl.multiple_of(p * self.rows + i * self.step, self.step), self.step))
            return 0

        lax.fori_loop(0, self.rows // self.step, one, 0)

    def inner(self, k):
        return ((k > self.m) & (self.m > 0)) | ((k < self.m) & (self.m < self.n - 1))

    def pass_on(self, k, own, between=None):
        m, n = self.m, self.n
        self.side(k).wait_recv()
        inner = self.inner(k)

        def one(p, _):
            @pl.when(inner)
            def _():
                self.line(k, p, k, self.t).wait_recv()

                def add(at):
                    total = own[at, :] + self.side_in[k, at, :].astype(jnp.float32) + self.line_in[k, at, :].astype(jnp.float32)
                    self.side_in[k, at, :] = total.astype(jnp.bfloat16)

                self.each(p, add)

            @pl.when(jnp.logical_not(inner))
            def _():
                def add(at):
                    self.side_in[k, at, :] = (own[at, :] + self.side_in[k, at, :].astype(jnp.float32)).astype(jnp.bfloat16)

                self.each(p, add)

            pl.when(k > m)(lambda: self.line(k, p, k, self.t + 2).start())
            pl.when(k < m)(lambda: self.line(k, p, jnp.where(k == m - 1, n, k), self.t - 2).start())
            if between is not None:
                between(p)
            return 0

        lax.fori_loop(0, self.pieces, one, 0)

    def settle(self, own, consume):
        m, n = self.m, self.n
        self.side(m).wait_recv()

        def one(p, _):
            def first(at):
                own[at, :] += self.side_in[m, at, :].astype(jnp.float32)

            self.each(p, first)

            def more(slot):
                self.line(m, p, slot, self.t).wait_recv()

                def add(at):
                    own[at, :] += self.line_in[slot, at, :].astype(jnp.float32)

                self.each(p, add)

            pl.when(m > 0)(lambda: more(m))
            pl.when(m < n - 1)(lambda: more(n))
            self.each(p, lambda at: consume(at, own[at, :]))
            return 0

        lax.fori_loop(0, self.pieces, one, 0)

    def finish(self):
        def one(k, _):
            self.side(k).wait_send()
            self.finish_line(k)
            return 0

        lax.fori_loop(0, self.n, one, 0)

    def finish_line(self, k):
        @pl.when(k != self.m)
        def _():
            for p in range(self.pieces):
                self.line(k, p, k, self.t).wait_send()


def scatter_scratch(n, pieces, rows, width):
    return [
        pltpu.VMEM((n, rows, width), jnp.bfloat16), pltpu.VMEM((n, rows, width), jnp.bfloat16),
        pltpu.VMEM((n + 1, rows, width), jnp.bfloat16),
        pltpu.SemaphoreType.DMA((2, n)), pltpu.SemaphoreType.DMA((n * pieces,)), pltpu.SemaphoreType.DMA(((n + 1) * pieces,)),
    ]


class Exchange:
    def __init__(self, group_count, pairs, local_sems, send, recv):
        self.group, self.count, self.pairs = lax.axis_index("dp"), group_count, pairs
        self.local_sems, self.send, self.recv = local_sems, send, recv

    def stay(self, index):
        src, dst = self.pairs[index]
        return pltpu.make_async_copy(src.at[self.group], dst.at[self.group], self.local_sems.at[index])

    def copy(self, index, peer, slot):
        src, dst = self.pairs[index]
        return pltpu.make_async_remote_copy(
            src_ref=src.at[peer], dst_ref=dst.at[slot], send_sem=self.send.at[index, peer],
            recv_sem=self.recv.at[index, slot], device_id={"dp": peer}, device_id_type=MESH)

    def others(self, body, which=None):
        for index in range(len(self.pairs)) if which is None else which:
            for i in range(self.count):
                pl.when(i != self.group)(lambda: body(index, i))

    def start(self, which=None):
        self.others(lambda index, i: self.copy(index, i, self.group).start(), which)
        for index in range(len(self.pairs)) if which is None else which:
            self.stay(index).start()

    def finish(self):
        for index in range(len(self.pairs)):
            self.stay(index).wait()
        self.others(lambda index, i: self.copy(index, i, i).wait_recv())
        self.others(lambda index, i: self.copy(index, i, self.group).wait_send())


def exchange_scratch(pairs, group_count):
    dma = pltpu.SemaphoreType.DMA
    return [dma((pairs,)), dma((pairs, group_count)), dma((pairs, group_count))]


def greet_all(n, group_count):
    t, core, chip = place()
    g = lax.axis_index("dp")
    barrier = pltpu.get_barrier_semaphore()

    def hail(index):
        pl.semaphore_signal(barrier, inc=1, device_id={"tensor": index}, device_id_type=MESH)

    hail(t + 1 - 2 * core)
    pl.when(chip > 0)(lambda: hail(t - 2))
    pl.when(chip < n - 1)(lambda: hail(t + 2))
    for i in range(group_count):
        pl.when(i != g)(lambda: pl.semaphore_signal(barrier, inc=1, device_id={"dp": i}, device_id_type=MESH))
    pl.semaphore_wait(barrier, group_count + jnp.minimum(chip, 1) + jnp.minimum(n - 1 - chip, 1))


def forward_kernel(n, group_count, pieces, length_ref, place_ref, frequency_ref, x_ref, norm_ref, qkv_ref, out_ref, bias_ref, cot_ref, wide_hbm, down_hbm,
                   xs_out, wq_out, wo_ref, q_out, k_out, v_out, kt_out, mixed_ref, lse_ref, keep_out, ahead_out, behind_out,
                   middle_ref, normed_ref, cots_out, wide_copy, down_copy,
                   cots_ref, xs_ref, wq_ref, q_ref, k_ref, v_ref, kt_ref, keep_ref, ahead_ref, behind_ref, keep_sems,
                   wide_stage, low_stage, stage_sems, weight_send, weight_recv,
                   vt_ref, biases_ref, acc_ref, side_out, side_in, line_in, side_sems, line_send, line_recv,
                   first_sems, cot_sems, share_send, share_recv):
    greet_all(n, group_count)
    heads, total_rows, _ = q_ref.shape
    rows, features = x_ref.shape
    width = heads * HEAD_DIM
    lane_groups = width // LANES
    per_group = LANES // HEAD_DIM
    block = rows
    length = length_ref[0]
    group = lax.axis_index("dp")
    t, core, m = place()
    first = Gather(n, xs_ref.at[t], xs_ref, first_sems, pieces)
    cots = Gather(n, cots_ref.at[t], cots_ref, cot_sems, pieces)
    s = Scatter(n, pieces, side_out, side_in, line_in, side_sems, line_send, line_recv)
    step = 32

    def first_norm(i, _):
        at = pl.ds(pl.multiple_of(i * step, step), step)
        xs_ref[t, at, :] = norm_forward(x_ref[at, :].astype(jnp.float32), norm_ref[0:1, :], norm_ref[1:2, :]).astype(jnp.bfloat16)
        return 0

    lax.fori_loop(0, rows // step, first_norm, 0)
    first.start()

    def mask(i, _):
        start = pl.multiple_of(i * step, step)
        at = pl.ds(start, step)
        slots = t * rows + start + lax.broadcasted_iota(jnp.int32, (step, features), 0)
        cots_ref[t, at, :] = jnp.where(slots < length, cot_ref[at, :].astype(jnp.float32), 0.0).astype(jnp.bfloat16)
        return 0

    lax.fori_loop(0, rows // step, mask, 0)
    depth = features // group_count
    mine = pl.ds(pl.multiple_of(group * depth, depth), depth)
    for c in range(3):
        wq_ref[c, mine, :] = qkv_ref[c].astype(jnp.bfloat16)
    wo_ref[:, mine] = out_ref[...].astype(jnp.bfloat16)
    biases_ref[group] = bias_ref[...].astype(jnp.bfloat16).astype(jnp.float32)

    def share(kind, src, owner, peer):
        ref = src(owner)
        return pltpu.make_async_remote_copy(
            src_ref=ref, dst_ref=ref, send_sem=share_send.at[kind, peer], recv_sem=share_recv.at[kind, owner],
            device_id={"dp": peer}, device_id_type=MESH)

    def part(owner):
        return pl.ds(pl.multiple_of(owner * depth, depth), depth)

    kinds = (lambda o: wq_ref.at[:, part(o), :], lambda o: biases_ref.at[o], lambda o: wo_ref.at[:, part(o)])
    for kind in range(3):
        for i in range(group_count):
            pl.when(i != group)(lambda: share(kind, kinds[kind], group, i).start())

    half_units = wide_stage.shape[0]
    units = wide_hbm.shape[1]
    chunks = [(wide_hbm.at[c], wide_copy.at[group, c], u) for c in range(2) for u in range(0, units, half_units)]
    chunks += [(down_hbm, down_copy.at[group], u) for u in range(0, units, half_units)]

    def chunk_in(index):
        src, _, u = chunks[index]
        return pltpu.make_async_copy(src.at[pl.ds(u, half_units)], wide_stage, stage_sems.at[0])

    def chunk_out(index):
        _, dst, u = chunks[index]
        return pltpu.make_async_copy(low_stage, dst.at[pl.ds(u, half_units)], stage_sems.at[1])

    chunk_in(0).start()
    for index in range(len(chunks)):
        chunk_in(index).wait()
        if index > 0:
            chunk_out(index - 1).wait()
        low_stage[...] = wide_stage[...].astype(jnp.bfloat16)
        if index + 1 < len(chunks):
            chunk_in(index + 1).start()
        chunk_out(index).start()
    chunk_out(len(chunks) - 1).wait()

    def weight(kind, peer, slot):
        ref = (wide_copy, down_copy)[kind]
        return pltpu.make_async_remote_copy(
            src_ref=ref.at[group], dst_ref=ref.at[slot], send_sem=weight_send.at[kind, peer],
            recv_sem=weight_recv.at[kind, slot], device_id={"dp": peer}, device_id_type=MESH)

    def weights(body):
        for kind in range(2):
            for i in range(group_count):
                pl.when(i != group)(lambda: body(kind, i))

    def tables(i, _):
        at = pl.ds(pl.multiple_of(i * block, block), block)
        angles = jnp.broadcast_to(place_ref[:, at].astype(jnp.float32), (LANES, block)).T * frequency_ref[...]
        cosine, sine = jnp.cos(angles), jnp.sin(angles)
        dim = lax.rem(lax.broadcasted_iota(jnp.int32, (block, LANES), 1), HEAD_DIM)
        none = jnp.zeros((block, LANES), jnp.float32)
        keep_ref[at, :] = jnp.where(dim < ROTARY, cosine, 1.0)
        ahead_ref[at, :] = jnp.where(dim < ROTARY // 2, -sine, none)
        behind_ref[at, :] = jnp.where((dim >= ROTARY // 2) & (dim < ROTARY), sine, none)
        return 0

    lax.fori_loop(0, total_rows // block, tables, 0)
    def project(slot):
        at = pl.ds(pl.multiple_of(slot * block, block), block)
        keep, ahead, behind = keep_ref[at, :], ahead_ref[at, :], behind_ref[at, :]
        x = xs_ref[slot]
        for c in range(3):
            wide = dot_nn(x, wq_ref[c]) + biases_ref[group_count, c:c + 1, :]
            for a in range(lane_groups):
                lanes = slice(a * LANES, (a + 1) * LANES)
                part_wide = wide[:, lanes]
                if c < 2:
                    part_wide = spin(part_wide, keep, ahead, behind)
                if c == 1:
                    kt_ref[lanes, at] = part_wide.T.astype(jnp.bfloat16)
                if c == 2:
                    vt_ref[lanes, at] = part_wide.T.astype(jnp.bfloat16)
                for b in range(per_group):
                    (q_ref, k_ref, v_ref)[c][a * per_group + b, at, :] = part_wide[:, b * HEAD_DIM:(b + 1) * HEAD_DIM].astype(jnp.bfloat16)

    def ring(d, _):
        def one(q, _):
            other, above = lax.div(q, 2), lax.rem(q, 2)
            k = jnp.where(above == 1, m + d, m - d)

            @pl.when((k >= 0) & (k < n) & ((d > 0) | (above == 0)))
            def _():
                pl.when(other == 1)(lambda: first.side_wait(k))
                project(2 * k + jnp.where(other == 1, 1 - core, core))

            return 0

        lax.fori_loop(0, 4, one, 0)
        pl.when(d == n - 2)(lambda: first.arrive(n - 1))
        return 0

    for d in range(1, n - 1):
        first.arrive(d)
    cots.start(outward=False)
    for kind in range(3):
        for i in range(group_count):
            pl.when(i != group)(lambda: share(kind, kinds[kind], i, i).wait_recv())
    bias = biases_ref[0]
    for i in range(1, group_count):
        bias = bias + biases_ref[i]
    biases_ref[group_count] = bias

    weights(lambda kind, i: weight(kind, i, group).start())
    lax.fori_loop(0, n, ring, 0)
    kept = [
        pltpu.make_async_copy(src, dst, keep_sems.at[index])
        for index, (src, dst) in enumerate((
            (xs_ref, xs_out), (wq_ref, wq_out), (q_ref, q_out), (k_ref, k_out), (v_ref, v_out), (kt_ref, kt_out),
            (keep_ref, keep_out), (ahead_ref, ahead_out), (behind_ref, behind_out)))
    ]
    for item in kept:
        item.start()
    cots.start(inward=False)
    pair = 2 * block

    def attend(i):
        at = pl.ds(pl.multiple_of(i * pair, pair), pair)
        queries = [q_ref[h, at, :] for h in range(heads)]

        def key_block(j, carry, kind):
            key_start = pl.multiple_of(j * pair, pair)
            keys_at = pl.ds(key_start, pair)
            out = []
            for h in range(heads):
                top, total, mixed = carry[h]
                scores = dot_nt(k_ref[h, keys_at, :], queries[h]) * (score_scale * log2_e)
                if kind > 0:
                    scores = masked_scores(scores, key_start, i * pair, length, kind == 2)
                new_top = jnp.maximum(top, jnp.max(scores, axis=0, keepdims=True))
                shrink = jnp.exp2(top - new_top)
                p = jnp.exp2(scores - new_top)
                total = total * shrink + jnp.sum(p, axis=0, keepdims=True)
                mixed = mixed * shrink + dot_nn(
                    vt_ref[h * HEAD_DIM:(h + 1) * HEAD_DIM, keys_at], p.astype(jnp.bfloat16))
                out.append((new_top, total, mixed))
            return tuple(out)

        start = tuple(
            (jnp.full((1, pair), mask_fill, jnp.float32), jnp.zeros((1, pair), jnp.float32),
             jnp.zeros((HEAD_DIM, pair), jnp.float32)) for _ in range(heads))
        carry = lax.fori_loop(0, i, lambda j, c: key_block(j, c, 1), start)
        carry = key_block(i, carry, 2)
        for h in range(heads):
            top, total, mixed = carry[h]
            lse_ref[h:h + 1, at] = top + jnp.log2(total)
        for a in range(lane_groups):
            both = [carry[a * per_group + b][2] * (1.0 / carry[a * per_group + b][1]) for b in range(per_group)]
            mixed_ref[at, a * LANES:(a + 1) * LANES] = jnp.concatenate(both, axis=0).T.astype(jnp.bfloat16)

    cut = min(512, features)

    def branch(j, _):
        k = near(n - 1 - j, m, n)

        attend(k)

        def attended(slot):
            return mixed_ref[pl.ds(pl.multiple_of(slot * block, block), block), :]

        low = attended(2 * k + 1 - core)
        for a in range(0, features, cut):
            s.side_out[k, :, a:a + cut] = dot_nn(low, wo_ref[:, a:a + cut]).astype(jnp.bfloat16)
        s.side(k).start()
        low = attended(2 * k + core)
        for a in range(0, features, cut):
            acc_ref[:, a:a + cut] = dot_nn(low, wo_ref[:, a:a + cut])
        pl.when(j < n - 1)(lambda: s.pass_on(k, acc_ref, lambda p: cots.arrive(j + 1, (p,))))
        return 0

    lax.fori_loop(0, n, branch, 0)

    def consume(at, total):
        middle = x_ref[at, :].astype(jnp.float32) + total
        middle_ref[at, :] = middle
        normed_ref[at, :] = norm_forward(middle, norm_ref[2:3, :], norm_ref[3:4, :]).astype(jnp.bfloat16)

    for k in range(n):
        cots.side_wait(k)
    kept.append(pltpu.make_async_copy(cots_ref, cots_out, keep_sems.at[len(kept)]))
    kept[-1].start()
    s.settle(acc_ref, consume)
    first.finish()
    cots.finish()
    s.finish()
    for kind in range(3):
        for i in range(group_count):
            pl.when(i != group)(lambda: share(kind, kinds[kind], group, i).wait_send())
    for item in kept:
        item.wait()
    weights(lambda kind, i: weight(kind, i, i).wait_recv())
    weights(lambda kind, i: weight(kind, i, group).wait_send())


def forward(lengths, positions, x, norms, qkv, out, bias, cot, wide, down, n, group_count, number, pieces=4):
    rows, features = x.shape
    width = qkv.shape[2]
    heads = width // HEAD_DIM
    total_rows = 2 * n * rows
    f32, low = jnp.float32, jnp.bfloat16
    shape = jax.ShapeDtypeStruct
    half_rot = ROTARY // 2
    frequency = np.tile(rope_base ** (-(2.0 * np.arange(half_rot)) / ROTARY), LANES // half_rot)
    split = shape((heads, total_rows, HEAD_DIM), low)
    table = shape((total_rows, LANES), f32)
    gathered = shape((2 * n, rows, features), low)
    return pl.pallas_call(
        functools.partial(forward_kernel, n, group_count, pieces),
        out_shape=(gathered, shape((3, features, width), low), shape((width, features), low), split, split, split,
                   shape((width, total_rows), low), shape((total_rows, width), low), shape((heads, total_rows), f32),
                   table, table, table, shape((rows, features), f32), shape((rows, features), low), gathered,
                   shape((group_count,) + wide.shape, low), shape((group_count,) + down.shape, low)),
        in_specs=[pl.BlockSpec(memory_space=pltpu.SMEM)] + [VM] * 8 + [ANYWHERE] * 2,
        out_specs=(ANYWHERE, ANYWHERE, VM) + (ANYWHERE,) * 4 + (VM, VM) + (ANYWHERE,) * 3 + (VM,) * 2 + (ANYWHERE,) * 3,
        scratch_shapes=[
            pltpu.VMEM(item.shape, item.dtype)
            for item in (gathered, gathered, shape((3, features, width), low), split, split, split, shape((width, total_rows), low), table, table, table)
        ] + [
            pltpu.SemaphoreType.DMA((10,)), pltpu.VMEM((down.shape[0] // 2, down.shape[1]), f32), pltpu.VMEM((down.shape[0] // 2, down.shape[1]), low),
            pltpu.SemaphoreType.DMA((2,)), pltpu.SemaphoreType.DMA((2, group_count)), pltpu.SemaphoreType.DMA((2, group_count)),
            pltpu.VMEM((width, total_rows), low), pltpu.VMEM((group_count + 1, 8, width), f32), pltpu.VMEM((rows, features), f32),
        ] + scatter_scratch(n, pieces, rows, features) + [
            pltpu.SemaphoreType.DMA((5, n * pieces)), pltpu.SemaphoreType.DMA((5, n * pieces)),
            pltpu.SemaphoreType.DMA((3, group_count)), pltpu.SemaphoreType.DMA((3, group_count)),
        ],
        compiler_params=params(number), cost_estimate=lasting(200), name="forward",
    )(lengths, positions.reshape(1, total_rows), jnp.asarray(frequency.reshape(1, LANES), f32),
      x, norms, qkv, out, bias, cot, wide, down)


def mlp_kernel(n, pieces, x_ref, cots_hbm, gate_up_hbm, down_hbm, middle_hbm, norm_ref,
               hidden_ref, grad_middle_ref, sums_ref, grad_gate_up_ref, grad_down_ref,
               cots_ref, gate_up_ref, down_ref, middle_ref, xs_ref, grads_ref, load_sems,
               acc_ref, side_out, side_in, line_in, side_sems, line_send, line_recv, gather_sems,
               wide_stage, down_stage, wide_sem, down_sem):
    loads = [
        pltpu.make_async_copy(src, dst, load_sems.at[i])
        for i, (src, dst) in enumerate(
            ((gate_up_hbm, gate_up_ref), (cots_hbm, cots_ref), (down_hbm, down_ref), (middle_hbm, middle_ref)))
    ]
    for load in loads:
        load.start()
    greet(n)
    g = Gather(n, x_ref, xs_ref, gather_sems, pieces)
    halves = tuple(
        Scatter(n, pieces // 2, side_out, side_in.at[h], line_in.at[h], side_sems.at[h], line_send.at[h], line_recv.at[h])
        for h in range(2))
    m, core = g.m, g.core
    rows, width = x_ref.shape
    half = rows // 2
    group_count, hidden_units, depth = down_ref.shape
    cut = min(512, depth)
    places = [(f, min(256, hidden_units - f)) for f in range(0, hidden_units, 256)]
    early, late = tuple(range(pieces // 2)), tuple(range(pieces // 2, pieces))
    g.start(early)
    g.start(late, outward=False)
    xs_ref[g.t] = x_ref[...]
    for load in loads:
        load.wait()

    def work(k, h):
        both = pl.ds(2 * k, 2)
        at = slice(h * half, (h + 1) * half)
        x = xs_ref[both, at, :].reshape(2 * half, width)
        cot = cots_ref[both, at, :].reshape(2 * half, width)
        for place, size in places:
            units = slice(place, place + size)
            shape = (2, half, size)

            def product(left, right):
                return sum(dot_nt(left[:, o * depth:(o + 1) * depth], right(o)) for o in range(group_count))

            gate = product(x, lambda o: gate_up_ref[o, 0, units, :])
            up = product(x, lambda o: gate_up_ref[o, 1, units, :])
            grad_hidden = product(cot, lambda o: down_ref[o, units, :])
            sig = 1.0 / (1.0 + jnp.exp(-gate))
            silu = gate * sig
            hidden_ref[both, at, units] = (silu * up).astype(jnp.bfloat16).reshape(shape)
            grads_ref[0, both, at, units] = (grad_hidden * up * (sig * (1.0 + gate * (1.0 - sig)))).astype(jnp.bfloat16).reshape(shape)
            grads_ref[1, both, at, units] = (grad_hidden * silu).astype(jnp.bfloat16).reshape(shape)

    def work_at(d, h, which):
        def one(above, _):
            k = jnp.where(above == 1, m + d, m - d)

            @pl.when((k >= 0) & (k < n) & ((d > 0) | (above == 0)))
            def _():
                g.side_wait(k, which)
                work(k, h)

            return 0

        lax.fori_loop(0, 2, one, 0)

    def ring(d, _):
        pl.when(d > 0)(lambda: g.arrive(d, early))
        pl.when(d == n - 2)(lambda: g.start(late, inward=False))
        work_at(d, 0, early)
        return 0

    lax.fori_loop(0, n, ring, 0)

    def partials(k, h):
        at = slice(h * half, (h + 1) * half)
        both = pl.ds(2 * k, 2)
        for a in range(0, width, cut):
            acc_ref[h, :, :, a:a + cut] = sum(
                dot_nn(grads_ref[c, both, at, :].reshape(2 * half, hidden_units), gate_up_ref[a // depth, c, :, a % depth:a % depth + cut])
                for c in range(2)
            ).reshape(2, half, cut)
        if h == 1:
            halves[0].side(k).wait_send()
        step = min(32, half)

        def lower(i, _):
            here = pl.ds(pl.multiple_of(i * step, step), step)
            side_out[k, here, :] = acc_ref[h, 1 - core, here, :].astype(jnp.bfloat16)
            return 0

        lax.fori_loop(0, half // step, lower, 0)
        halves[h].side(k).start()

    def one(j, _):
        k = near(n - 1 - j, m, n)
        partials(k, 0)

        def send():
            halves[0].pass_on(k, acc_ref.at[0, core], lambda p: g.arrive(j + 1, (late[0] + p,)))

        pl.when((j < n - 1) & jnp.logical_not(halves[0].inner(k)))(send)
        work_at(j, 1, late)
        pl.when((j < n - 1) & halves[0].inner(k))(send)
        return 0

    lax.fori_loop(0, n, one, 0)
    wide_cut = min(256, depth)
    per = -(-(width // wide_cut) // n)
    tokens = 2 * n * rows

    def wide_copy(place, slot):
        lanes = pl.ds(pl.multiple_of(lax.rem(place, depth), wide_cut), wide_cut)
        return pltpu.make_async_copy(
            wide_stage.at[slot], grad_gate_up_ref.at[lax.div(place, depth), :, :, lanes], wide_sem.at[slot])

    def wide_gradient(u, j):
        place = (j * per + u) * wide_cut

        @pl.when(place < width)
        def _():
            pl.when(j > 0)(lambda: wide_copy(0, u).wait())
            lanes = pl.ds(pl.multiple_of(place, wide_cut), wide_cut)
            x = xs_ref[:, :, lanes].reshape(tokens, wide_cut).T
            for c in range(2):
                wide_stage[u, c] = dot_nn(x, grads_ref[c].reshape(tokens, hidden_units)).T.astype(jnp.bfloat16)
            wide_copy(place, u).start()

    def down_copy(place, size):
        return pltpu.make_async_copy(down_stage.at[:, pl.ds(0, size)], grad_down_ref.at[:, pl.ds(place, size)], down_sem)

    def down_gradient(index):
        place, size = places[index]
        if index > 0:
            down_copy(*places[index - 1]).wait()
        low = hidden_ref[:, :, place:place + size].reshape(tokens, size).T
        for a in range(0, width, cut):
            down_stage[a // depth, :size, a % depth:a % depth + cut] = dot_nn(low, cots_ref[:, :, a:a + cut].reshape(tokens, cut)).astype(jnp.bfloat16)
        down_copy(place, size).start()

    def two(j, _):
        k = near(n - 1 - j, m, n)
        partials(k, 1)

        def send():
            halves[1].pass_on(k, acc_ref.at[1, core])

        pl.when((j < n - 1) & jnp.logical_not(halves[1].inner(k)))(send)
        for u in range(per):
            wide_gradient(u, j)
        for index in range(len(places)):
            pl.when(j == index)(functools.partial(down_gradient, index))
        pl.when((j < n - 1) & halves[1].inner(k))(send)
        return 0

    def settle(h):
        def consume(at, total):
            here = pl.ds(pl.multiple_of(h * half + at.start, at.size), at.size)
            back, gain, shift = norm_backward(middle_ref[here, :], norm_ref[2:3, :], total)
            grad_middle_ref[here, :] = cots_ref[g.t, here, :].astype(jnp.float32) + back
            sums_ref[0:1, :] += gain
            sums_ref[1:2, :] += shift

        halves[h].settle(acc_ref.at[h, core], consume)

    sums_ref[...] = jnp.zeros(sums_ref.shape, jnp.float32)
    settle(0)
    lax.fori_loop(0, n, two, 0)
    settle(1)
    for u in range(per):
        wide_copy(0, u).wait()
    down_copy(*places[-1]).wait()
    g.finish()

    def sent(k, _):
        halves[1].side(k).wait_send()
        for h in range(2):
            halves[h].finish_line(k)
        return 0

    lax.fori_loop(0, n, sent, 0)


def mlp(x, cots, gate_up, down, middle, norms, n, number, pieces=8):
    rows, width = x.shape
    group_count, hidden, depth = down.shape
    half, part = rows // 2, pieces // 2
    f32, low = jnp.float32, jnp.bfloat16
    shape = jax.ShapeDtypeStruct
    anywhere = pl.BlockSpec(memory_space=pl.ANY)
    wide_cut = min(256, depth)
    per = -(-(width // wide_cut) // n)
    dma = pltpu.SemaphoreType.DMA
    return pl.pallas_call(functools.partial(mlp_kernel, n, pieces),
        out_shape=(shape((2 * n, rows, hidden), low), shape((rows, width), f32),
                   shape((2, width), f32), shape(gate_up.shape, low), shape(down.shape, low)),
        in_specs=[VM] + [anywhere] * 4 + [VM], out_specs=(VM,) * 3 + (anywhere,) * 2,
        scratch_shapes=[
            pltpu.VMEM((2 * n, rows, width), low), pltpu.VMEM(gate_up.shape, low), pltpu.VMEM(down.shape, low), pltpu.VMEM((rows, width), f32),
            pltpu.VMEM((2 * n, rows, width), low), pltpu.VMEM((2, 2 * n, rows, hidden), low), dma((4,)),
            pltpu.VMEM((2, 2, half, width), f32), pltpu.VMEM((n, half, width), low), pltpu.VMEM((2, n, half, width), low),
            pltpu.VMEM((2, n + 1, half, width), low), dma((2, 2, n)), dma((2, n * part)), dma((2, (n + 1) * part)),
            dma((5, n * pieces)), pltpu.VMEM((per, 2, hidden, wide_cut), low), pltpu.VMEM((group_count, min(256, hidden), depth), low),
            dma((per,)), dma,
        ],
        compiler_params=params(number), cost_estimate=lasting(140), name="mlp")(x, cots, gate_up, down, middle, norms)


def down_kernel(n, pieces, hidden_ref, down_ref, middle_hbm, grad_ref, out_hbm, mixed_hbm, wide_ref, low_ref, block_ref, back_ref, grad_out_ref, wide_parts, low_parts,
                middle_ref, out_ref, mixed_ref, late_sems, local_sems, share_send, share_recv, xs_ref, x_ref, acc_ref, side_out, side_in, line_in, side_sems, line_send, line_recv, gather_sems):
    group_count, _, depth = down_ref.shape
    greet_all(n, group_count)
    grads = Exchange(group_count, ((wide_ref, wide_parts), (low_ref, low_parts)), local_sems, share_send, share_recv)
    g = Gather(n, x_ref, xs_ref, gather_sems, pieces)
    s = Scatter(n, pieces, side_out, side_in, line_in, side_sems, line_send, line_recv)
    x_ref[...] = grad_ref[...].astype(jnp.bfloat16)
    g.start()
    grads.start()
    late = [
        pltpu.make_async_copy(src, dst, late_sems.at[index])
        for index, (src, dst) in enumerate(((middle_hbm, middle_ref), (out_hbm, out_ref), (mixed_hbm, mixed_ref)))
    ]
    for item in late:
        item.start()
    xs_ref[g.t] = x_ref[...]
    m, core = s.m, s.core
    width = group_count * depth
    cut = min(512, depth)

    def one(j, _):
        k = near(n - 1 - j, m, n)
        for a in range(0, width, cut):
            s.side_out[k, :, a:a + cut] = dot_nn(hidden_ref[2 * k + 1 - core], down_ref[a // depth, :, a % depth:a % depth + cut]).astype(jnp.bfloat16)
        s.side(k).start()
        for a in range(0, width, cut):
            acc_ref[:, a:a + cut] = dot_nn(hidden_ref[2 * k + core], down_ref[a // depth, :, a % depth:a % depth + cut])
        pl.when(j < n - 1)(lambda: s.pass_on(k, acc_ref, lambda p: g.arrive(j + 1, (p,))))
        return 0

    lax.fori_loop(0, n, one, 0)

    def consume(at, total):
        block_ref[at, :] = (middle_ref[at, :] + total).astype(jnp.bfloat16)

    for item in late:
        item.wait()

    def last(k, _):
        g.side_wait(k)
        for c in range(2):
            back_ref[2 * k + c] = dot_nt(xs_ref[2 * k + c], out_ref[...]).astype(jnp.bfloat16)
        return 0

    lax.fori_loop(0, n, last, 0)
    flipped = mixed_ref[...].T
    for a in range(0, width, cut):
        grad_out_ref[a // depth, :, a % depth:a % depth + cut] = dot_nn(
            flipped, xs_ref[:, :, a:a + cut].reshape(mixed_ref.shape[0], cut)).astype(jnp.bfloat16)
    s.settle(acc_ref, consume)

    g.finish()
    s.finish()
    grads.finish()


def down_branch(hidden, down, middle, x, out, mixed, wide, narrow, n, number, pieces=8):
    rows, width = x.shape
    f32, low = jnp.float32, jnp.bfloat16
    return pl.pallas_call(functools.partial(down_kernel, n, pieces),
        out_shape=(jax.ShapeDtypeStruct((rows, width), low), jax.ShapeDtypeStruct((2 * n, rows, out.shape[0]), low),
                   jax.ShapeDtypeStruct((down.shape[0], out.shape[0], down.shape[2]), low),
                   jax.ShapeDtypeStruct(wide.shape, low), jax.ShapeDtypeStruct(narrow.shape, low)),
        in_specs=[VM, VM, ANYWHERE, VM] + [ANYWHERE] * 4, out_specs=(VM,) * 3 + (ANYWHERE,) * 2,
        scratch_shapes=[pltpu.VMEM(item.shape, item.dtype) for item in (middle, out, mixed)] + [pltpu.SemaphoreType.DMA((3,))] + exchange_scratch(2, down.shape[0]) + [pltpu.VMEM((2 * n, rows, width), low), pltpu.VMEM((rows, width), low), pltpu.VMEM((rows, width), f32)] + scatter_scratch(n, pieces, rows, width) + [pltpu.SemaphoreType.DMA((5, n * pieces))],
        compiler_params=params(number), cost_estimate=lasting(115), name="down_branch")(hidden, down, middle, x, out, mixed, wide, narrow)


def greet_everyone(count, group_count):
    t, g = lax.axis_index("tensor"), lax.axis_index("dp")
    barrier = pltpu.get_barrier_semaphore()
    for j in range(count):
        pl.when(j != t)(lambda: pl.semaphore_signal(barrier, inc=1, device_id={"tensor": j}, device_id_type=MESH))
    for i in range(group_count):
        pl.when(i != g)(lambda: pl.semaphore_signal(barrier, inc=1, device_id={"dp": i}, device_id_type=MESH))
    pl.semaphore_wait(barrier, count + group_count - 2)


class Totals:
    def __init__(self, sums, total, parts, groups, biases, near_send, near_recv, far_send, far_recv):
        self.sums, self.total, self.parts, self.groups, self.biases = sums, total, parts, groups, biases
        self.near_send, self.near_recv, self.far_send, self.far_recv = near_send, near_recv, far_send, far_recv
        self.t, self.g = lax.axis_index("tensor"), lax.axis_index("dp")
        self.count, self.group_count = parts.shape[0], groups.shape[0]
        self.piece = parts.shape[2]

    def columns(self, ref, j):
        return ref.at[:, pl.ds(pl.multiple_of(j * self.piece, self.piece), self.piece)]

    def near(self, kind, src, dst, peer, slot):
        return pltpu.make_async_remote_copy(
            src_ref=src, dst_ref=dst, send_sem=self.near_send.at[kind, peer], recv_sem=self.near_recv.at[kind, slot],
            device_id={"tensor": peer}, device_id_type=MESH)

    def far(self, kind, ref, peer, slot):
        return pltpu.make_async_remote_copy(
            src_ref=ref.at[self.g], dst_ref=ref.at[slot], send_sem=self.far_send.at[kind, peer], recv_sem=self.far_recv.at[kind, slot],
            device_id={"dp": peer}, device_id_type=MESH)

    def first(self, peer, slot):
        return self.near(0, self.columns(self.sums, peer), self.parts.at[slot], peer, slot)

    def last(self, peer, slot):
        return self.near(1, self.columns(self.total, self.t), self.columns(self.total, slot), peer, slot)

    def each_near(self, body):
        for j in range(self.count):
            pl.when(j != self.t)(lambda: body(j))

    def each_far(self, body):
        for i in range(self.group_count):
            pl.when(i != self.g)(lambda: body(i))

    def start_bias(self, bias):
        self.biases[self.g] = bias[...]
        self.each_far(lambda i: self.far(1, self.biases, i, self.g).start())

    def run(self, bias_total):
        def added(ref):
            total = ref[0]
            for j in range(1, ref.shape[0]):
                total = total + ref[j]
            return total

        here = pl.ds(pl.multiple_of(self.t * self.piece, self.piece), self.piece)
        self.each_near(lambda j: self.first(j, self.t).start())
        self.parts[self.t] = self.sums[:, here]
        self.each_near(lambda j: self.first(j, j).wait_recv())
        self.groups[self.g] = added(self.parts)
        self.each_far(lambda i: self.far(0, self.groups, i, self.g).start())
        self.each_far(lambda i: self.far(1, self.biases, i, i).wait_recv())
        bias_total[...] = added(self.biases)
        self.each_far(lambda i: self.far(0, self.groups, i, i).wait_recv())
        self.total[:, here] = added(self.groups)
        self.each_near(lambda j: self.last(j, self.t).start())
        self.each_near(lambda j: self.last(j, j).wait_recv())

    def finish(self):
        self.each_near(lambda j: self.first(j, self.t).wait_send())
        self.each_far(lambda i: self.far(0, self.groups, i, self.g).wait_send())
        self.each_far(lambda i: self.far(1, self.biases, i, self.g).wait_send())
        self.each_near(lambda j: self.last(j, self.t).wait_send())


def backward_kernel(n, pieces, length_ref, q_ref, k_ref, v_ref, kt_ref, o_ref, lse_ref, do_ref,
                    keep_hbm, ahead_hbm, behind_hbm, w_hbm, x_hbm, middle_hbm, norm_ref, sums_two_ref, xs_hbm, low_ref,
                    result_ref, total_ref, bias_total_ref, wide_parts, low_parts,
                    keep_ref, ahead_ref, behind_ref, w_ref, x_ref, middle_ref, late_sems,
                    dos_ref, delta_ref, dqt_ref, dk_ref, dv_ref, grad_ref, wide_ref, strips_ref, acc_ref, sums_ref, bias_ref, pieces_ref, groups_ref, biases_ref, side_out, side_in, line_in,
                    strip_sems, side_sems, line_send, line_recv, local_sems, share_send, share_recv, near_send, near_recv, far_send, far_recv):
    group_count = low_ref.shape[0]
    late = [
        pltpu.make_async_copy(src, dst, late_sems.at[index])
        for index, (src, dst) in enumerate((
            (keep_hbm, keep_ref), (ahead_hbm, ahead_ref), (behind_hbm, behind_ref), (w_hbm, w_ref), (x_hbm, x_ref), (middle_hbm, middle_ref)))
    ]
    for item in late:
        item.start()
    greet_everyone(2 * n, group_count)
    heads, tokens, _ = q_ref.shape
    width = heads * HEAD_DIM
    rows, features = x_ref.shape
    lane_groups = width // LANES
    per_group = LANES // HEAD_DIM
    pair = 2 * rows
    depth = features // group_count
    length = length_ref[0]
    s = Scatter(n, pieces, side_out, side_in, line_in, side_sems, line_send, line_recv)
    m, core = s.m, s.core
    grads = Exchange(group_count, ((low_ref, low_parts), (wide_ref, wide_parts)), local_sems, share_send, share_recv)
    grads.start((0,))
    strip = min(256, depth)
    strip_count = features // strip

    def strip_copy(index, slot):
        return pltpu.make_async_copy(
            xs_hbm.at[:, :, pl.ds(pl.multiple_of(index * strip, strip), strip)], strips_ref.at[slot], strip_sems.at[slot])

    for slot in range(2):
        strip_copy(slot, slot).start()
    bias_ref[...] = jnp.zeros(bias_ref.shape, jnp.float32)
    sums_ref[0:2, :] = jnp.zeros((2, features), jnp.float32)
    sums_ref[2:4, :] = sums_two_ref[...]
    totals = Totals(sums_ref, total_ref, pieces_ref, groups_ref, biases_ref, near_send, near_recv, far_send, far_recv)

    def prepare(i, _):
        at = pl.ds(pl.multiple_of(i * pair, pair), pair)
        for a in range(lane_groups):
            lanes = slice(a * LANES, (a + 1) * LANES)
            grad = do_ref[at, lanes]
            for b in range(per_group):
                dos_ref[a * per_group + b, at, :] = grad[:, b * HEAD_DIM:(b + 1) * HEAD_DIM]
            both = (grad.astype(jnp.float32) * o_ref[at, lanes].astype(jnp.float32)).T
            for b in range(per_group):
                h = a * per_group + b
                delta_ref[h:h + 1, at] = jnp.sum(both[b * HEAD_DIM:(b + 1) * HEAD_DIM], axis=0, keepdims=True)
        dqt_ref[:, at] = jnp.zeros((width, pair), jnp.float32)
        for h in range(heads):
            dk_ref[h, at, :] = jnp.zeros((pair, HEAD_DIM), jnp.float32)
            dv_ref[h, at, :] = jnp.zeros((pair, HEAD_DIM), jnp.float32)
        return 0

    lax.fori_loop(0, n, prepare, 0)
    for item in late:
        item.wait()

    falling = 2 * m < n - 1

    def order(step):
        return jnp.where(falling, n - 1 - step, step)

    def finish_block(step):
        j = order(step)

        def tile(i, j, causal):
            at = pl.ds(pl.multiple_of(i * pair, pair), pair)
            key_start = pl.multiple_of(j * pair, pair)
            keys_at = pl.ds(key_start, pair)
            for h in range(heads):
                keys, queries, grad = k_ref[h, keys_at, :], q_ref[h, at, :], dos_ref[h, at, :]
                scores = dot_nt(keys, queries) * (score_scale * log2_e)
                scores = masked_scores(scores, key_start, i * pair, length, causal)
                p = jnp.exp2(scores - lse_ref[h:h + 1, at])
                dp = dot_nt(v_ref[h, keys_at, :], grad)
                ds = (p * (dp - delta_ref[h:h + 1, at])).astype(jnp.bfloat16)
                dv_ref[h, keys_at, :] += dot_nn(p.astype(jnp.bfloat16), grad)
                dk_ref[h, keys_at, :] += dot_nn(ds, queries)
                here = slice(h * HEAD_DIM, (h + 1) * HEAD_DIM)
                dqt_ref[here, at] += dot_nn(kt_ref[here, keys_at], ds)

        def other(u, _):
            tile(jnp.where(falling, j, j + u), jnp.where(falling, j - u, j), False)
            return 0

        tile(j, j, True)
        lax.fori_loop(1, n - step, other, 0)
        keys_at = pl.ds(pl.multiple_of(j * pair, pair), pair)
        keep, ahead, behind = keep_ref[keys_at, :], -ahead_ref[keys_at, :], -behind_ref[keys_at, :]
        for a in range(lane_groups):
            lanes = slice(a * LANES, (a + 1) * LANES)
            heads_here = range(a * per_group, (a + 1) * per_group)
            dq = dqt_ref[lanes, keys_at].T
            dk = jnp.concatenate([dk_ref[h, keys_at, :] for h in heads_here], axis=1)
            dv = jnp.concatenate([dv_ref[h, keys_at, :] for h in heads_here], axis=1)
            parts = (spin(dq * score_scale, keep, ahead, behind), spin(dk * score_scale, keep, ahead, behind), dv)
            for c in range(3):
                low = parts[c].astype(jnp.bfloat16)
                place_here = slice(c * width + a * LANES, c * width + (a + 1) * LANES)
                grad_ref[keys_at, place_here] = low
                bias_ref[:, place_here] += jnp.sum(low.astype(jnp.float32), axis=0, keepdims=True)

    cut = min(512, features)

    def partial(slot, a):
        at = pl.ds(pl.multiple_of(slot * rows, rows), rows)
        return sum(dot_nt(grad_ref[at, c * width:(c + 1) * width], w_ref[c, a:a + cut, :]) for c in range(3))

    def own_partial(k):
        for a in range(0, features, cut):
            acc_ref[:, a:a + cut] = partial(2 * k + core, a)

    def strip_gradient(index, _):
        slot = lax.rem(index, 2)
        strip_copy(index, slot).wait()
        x = strips_ref[slot].reshape(tokens, strip).T
        owner = lax.div(index * strip, depth)
        at = pl.ds(pl.multiple_of(lax.rem(index * strip, depth), strip), strip)
        for c in range(3):
            wide_ref[owner, c, at, :] = dot_nn(x, grad_ref[:, c * width:(c + 1) * width]).astype(jnp.bfloat16)
        pl.when(index + 2 < strip_count)(lambda: strip_copy(index + 2, slot).start())
        return 0

    def step(j, _):
        @pl.when(j < n)
        def _():
            finish_block(j)
            k = order(j)
            for a in range(0, features, cut):
                s.side_out[k, :, a:a + cut] = partial(2 * k + 1 - core, a).astype(jnp.bfloat16)
            s.side(k).start()

        @pl.when(j == n - 1)
        def _():
            lax.fori_loop(0, strip_count, strip_gradient, 0)
            grads.start((1,))
            totals.start_bias(bias_ref)

        def one(late, _):
            turn = jnp.where(late == 1, j - 2, j)
            k = order(turn)
            inner = ((k > m) & (m > 0)) | ((k < m) & (m < n - 1))

            @pl.when((turn >= 0) & (turn < n) & (k != m) & (inner == (late == 1)))
            def _():
                own_partial(k)
                s.pass_on(k, acc_ref)

            return 0

        lax.fori_loop(0, 2, one, 0)
        return 0

    lax.fori_loop(0, n + 2, step, 0)
    own_partial(m)

    def consume(at, total):
        back, gain, shift = norm_backward(x_ref[at, :].astype(jnp.float32), norm_ref[0:1, :], total)
        result_ref[at, :] = middle_ref[at, :] + back
        sums_ref[0:1, :] += gain
        sums_ref[1:2, :] += shift

    s.settle(acc_ref, consume)
    totals.run(bias_total_ref)
    s.finish()
    grads.finish()
    totals.finish()


def backward(lengths, q, k, v, kt, o, lse, grad, keep, ahead, behind, w, x, grad_middle, norms, sums_two, xs, narrow, n, number, pieces=4):
    rows, features = x.shape
    heads, tokens, _ = q.shape
    width = heads * HEAD_DIM
    group_count = narrow.shape[0]
    depth = features // group_count
    f32, low = jnp.float32, jnp.bfloat16
    shape = jax.ShapeDtypeStruct
    wide = (group_count, 3, depth, width)
    strip = min(256, depth)
    dma = pltpu.SemaphoreType.DMA
    scatter = scatter_scratch(n, pieces, rows, features)
    return pl.pallas_call(functools.partial(backward_kernel, n, pieces),
        out_shape=(shape((rows, features), f32), shape((4, features), f32), shape((1, 3 * width), f32),
                   shape(wide, low), shape(narrow.shape, low)),
        in_specs=[pl.BlockSpec(memory_space=pltpu.SMEM)] + [VM] * 7 + [ANYWHERE] * 6 + [VM] * 2 + [ANYWHERE] * 2,
        out_specs=(VM,) * 3 + (ANYWHERE,) * 2,
        scratch_shapes=[pltpu.VMEM(item.shape, item.dtype) for item in (keep, ahead, behind, w, x, grad_middle)] + [
            dma((6,)),
            pltpu.VMEM((heads, tokens, HEAD_DIM), low), pltpu.VMEM((heads, tokens), f32), pltpu.VMEM((width, tokens), f32),
            pltpu.VMEM((heads, tokens, HEAD_DIM), f32), pltpu.VMEM((heads, tokens, HEAD_DIM), f32),
            pltpu.VMEM((tokens, 3 * width), low), pltpu.VMEM(wide, low), pltpu.VMEM((2, 2 * n, rows, strip), low),
            pltpu.VMEM((rows, features), f32), pltpu.VMEM((4, features), f32), pltpu.VMEM((1, 3 * width), f32),
            pltpu.VMEM((2 * n, 4, features // (2 * n)), f32), pltpu.VMEM((group_count, 4, features // (2 * n)), f32),
            pltpu.VMEM((group_count, 1, 3 * width), f32),
        ] + scatter[:3] + [pltpu.SemaphoreType.DMA((2,))] + scatter[3:] + exchange_scratch(2, group_count)
        + [dma((2, 2 * n)), dma((2, 2 * n)), dma((2, group_count)), dma((2, group_count))],
        compiler_params=params(number), cost_estimate=lasting(125), name="backward",
    )(lengths, q, k, v, kt, o, lse, grad, keep, ahead, behind, w, x, grad_middle, norms, sums_two, xs, narrow)


def update_kernel(rates, *refs):
    kinds = len(rates)
    ins, outs, refs = refs[:4 * kinds], refs[4 * kinds:7 * kinds], refs[7 * kinds:]
    holds, held_parts, refs = refs[:kinds], refs[kinds:2 * kinds], refs[2 * kinds:]
    load_sems, part_sems, store_sems = refs

    def load(kind, i):
        return pltpu.make_async_copy(ins[4 * kind + i], holds[kind].at[i], load_sems.at[kind, i])

    def load_parts(kind):
        return pltpu.make_async_copy(ins[4 * kind + 3], held_parts[kind], part_sems.at[kind])

    def store(kind, i):
        return pltpu.make_async_copy(holds[kind].at[i], outs[3 * kind + i], store_sems.at[kind, i])

    for kind in range(kinds):
        for i in range(3):
            load(kind, i).start()
        load_parts(kind).start()
    for kind in range(kinds):
        for i in range(3):
            load(kind, i).wait()
        load_parts(kind).wait()
        hold, part = holds[kind], held_parts[kind]
        step = min(32, hold.shape[1])

        def one(i, _):
            at = pl.ds(pl.multiple_of(i * step, step), step)
            gradient = part[0, at, :].astype(jnp.float32)
            for owner in range(1, part.shape[0]):
                gradient = gradient + part[owner, at, :].astype(jnp.float32)
            new = adamw(hold[0, at, :], hold[1, at, :], hold[2, at, :], gradient, *rates[kind])
            for index in range(3):
                hold[index, at, :] = new[index]
            return 0

        lax.fori_loop(0, hold.shape[1] // step, one, 0)
        for i in range(3):
            store(kind, i).start()
    for kind in range(kinds):
        for i in range(3):
            store(kind, i).wait()


def update(params_in, rates):
    f32 = jnp.float32
    kinds = len(rates)
    dma = pltpu.SemaphoreType.DMA
    flat = [array for group in params_in for array in group]
    results = pl.pallas_call(
        functools.partial(update_kernel, rates),
        out_shape=tuple(jax.ShapeDtypeStruct(group[0].shape, f32) for group in params_in for _ in range(3)),
        in_specs=[ANYWHERE] * len(flat), out_specs=(ANYWHERE,) * (3 * kinds),
        scratch_shapes=[pltpu.VMEM((3,) + group[0].shape, f32) for group in params_in]
        + [pltpu.VMEM(group[3].shape, group[3].dtype) for group in params_in]
        + [dma((kinds, 3)), dma((kinds,)), dma((kinds, 3))],
        compiler_params=pltpu.CompilerParams(vmem_limit_bytes=VMEM_LIMIT), cost_estimate=lasting(20), name="update",
    )(*flat)
    return tuple(results[3 * i:3 * i + 3] for i in range(kinds))


def local(
    inputs,
    cotangent,
    lengths,
    positions,
    qkv_master,
    gate_up_master,
    out_master,
    down_master,
    bias_master,
    norm_master,
    qkv_first,
    gate_up_first,
    out_first,
    down_first,
    bias_first,
    norm_first,
    qkv_second,
    gate_up_second,
    out_second,
    down_second,
    bias_second,
    norm_second,
):
    tensor_count = lax.axis_size("tensor")
    local_tokens = inputs.shape[0]
    group_tokens = local_tokens * tensor_count
    row_count = lengths.shape[0]
    row_length = group_tokens // row_count
    heads_here = bias_master.shape[1]
    width_here = heads_here * HEAD_DIM
    chips = tensor_count // 2
    group = lax.axis_index("dp")
    group_count = lax.axis_size("dp")
    own_dims = jnp.arange(HEAD_DIM) // (HEAD_DIM // group_count) == group
    bias_row = jnp.where(own_dims, jnp.tile(bias_master, (1, 1, group_count)), 0.0).reshape(3, width_here)
    bias_row = jnp.concatenate([bias_row, jnp.zeros((5, width_here), jnp.float32)], axis=0)
    (
        gathered_one, qkv_copy, out_copy, queries, keys, values, keys_flipped, mixed_low, log_totals,
        keep, ahead, behind, middle, normed_two, gathered_grad, gate_up_copy, down_copy,
    ) = forward(
        lengths, positions, inputs, norm_master, qkv_master, out_master, bias_row, cotangent,
        jnp.swapaxes(gate_up_master, 1, 2), down_master, chips, group_count, 0
    )
    hidden, grad_middle, sums_two, grad_gate_up_w, grad_down = mlp(
        normed_two, gathered_grad, gate_up_copy, down_copy, middle, norm_master, chips, 2
    )
    block_output, grad_mixed, grad_out_w, gate_up_parts, down_parts = down_branch(
        hidden, down_copy, middle, grad_middle, out_copy, mixed_low, grad_gate_up_w, grad_down, chips, 3
    )
    grad_mixed = grad_mixed.reshape(group_tokens, width_here)
    input_grad, norm_grads, bias_grad, qkv_parts, out_parts = backward(
        lengths, queries, keys, values, keys_flipped, mixed_low, log_totals, grad_mixed, keep, ahead, behind,
        qkv_copy, inputs, grad_middle, norm_master, sums_two, gathered_one, grad_out_w, chips, 4
    )

    def level(array):
        return array.reshape(-1, array.shape[-1])

    def level_parts(array):
        return array.reshape(group_count, -1, array.shape[-1])

    def turned(array):
        return level(jnp.swapaxes(array, 1, 2))

    out_new, down_new, gate_up_new, qkv_new = update(
        (
            (out_master, out_first, out_second, out_parts),
            (down_master, down_first, down_second, down_parts),
            (turned(gate_up_master), turned(gate_up_first), turned(gate_up_second), level_parts(gate_up_parts)),
            (level(qkv_master), level(qkv_first), level(qkv_second), level_parts(qkv_parts)),
        ),
        (
            (16.0 / math.sqrt(HEADS * HEAD_DIM), decay_rate),
            (6.0 / math.sqrt(FF), decay_rate),
            (2.0 / math.sqrt(D), decay_rate),
            (2.0 / math.sqrt(D), decay_rate),
        ),
    )
    turned_shape = (2, gate_up_master.shape[2], gate_up_master.shape[1])
    gate_up_new = tuple(jnp.swapaxes(item.reshape(turned_shape), 1, 2) for item in gate_up_new)
    qkv_new = tuple(item.reshape(qkv_master.shape) for item in qkv_new)
    bias_grad = lax.dynamic_slice_in_dim(
        bias_grad.reshape(3, heads_here, HEAD_DIM), group * bias_master.shape[2], bias_master.shape[2], axis=2
    )
    bias_new = adamw(bias_master, bias_first, bias_second, bias_grad, 1.5, 0.0)
    norm_new = adamw(norm_master, norm_first, norm_second, norm_grads, 0.7, 0.0)
    return (
        block_output,
        input_grad,
        qkv_new[0],
        qkv_new[1],
        qkv_new[2],
        gate_up_new[0],
        gate_up_new[1],
        gate_up_new[2],
        out_new[0],
        out_new[1],
        out_new[2],
        down_new[0],
        down_new[1],
        down_new[2],
        bias_new[0],
        bias_new[1],
        bias_new[2],
        norm_new[0],
        norm_new[1],
        norm_new[2],
    )


def solution(mesh):
    return jax.shard_map(
        local,
        mesh=mesh,
        in_specs=(
            P(("dp", "tensor"), None),
            P(("dp", "tensor"), None),
            P("dp"),
            P("dp"),
            P(None, "dp", "tensor"),
            P(None, "dp", "tensor"),
            P("tensor", "dp"),
            P("tensor", "dp"),
            P(None, "tensor", "dp"),
            P(),
            P(None, "dp", "tensor"),
            P(None, "dp", "tensor"),
            P("tensor", "dp"),
            P("tensor", "dp"),
            P(None, "tensor", "dp"),
            P(),
            P(None, "dp", "tensor"),
            P(None, "dp", "tensor"),
            P("tensor", "dp"),
            P("tensor", "dp"),
            P(None, "tensor", "dp"),
            P(),
        ),
        out_specs=(
            P(("dp", "tensor"), None),
            P(("dp", "tensor"), None),
            P(None, "dp", "tensor"),
            P(None, "dp", "tensor"),
            P(None, "dp", "tensor"),
            P(None, "dp", "tensor"),
            P(None, "dp", "tensor"),
            P(None, "dp", "tensor"),
            P("tensor", "dp"),
            P("tensor", "dp"),
            P("tensor", "dp"),
            P("tensor", "dp"),
            P("tensor", "dp"),
            P("tensor", "dp"),
            P(None, "tensor", "dp"),
            P(None, "tensor", "dp"),
            P(None, "tensor", "dp"),
            P(),
            P(),
            P(),
        ),
        check_vma=False,
    )
```
